32 devices in a mesh: bucket: 8 (over y, x, core), seq: 4 (over z).
Axes of the slice: x: 2, y: 2, z: 4, core: 2. Of those that a mesh axis runs over, the one named last changes fastest.
Arguments:
- tokens: bfloat16 [8192, 1536], P(('bucket', 'seq')), may hold values from -6 to 6
- cotangent: bfloat16 [8192, 1536], P(('bucket', 'seq')), may hold values from -6 to 6
- step_embed: bfloat16 [8, 4, 1024], P('bucket'), may hold values from -6 to 6
- caption: bfloat16 [8, 4, 256, 4096], P('bucket', None, 'seq'), may hold values from -6 to 6
- lengths: int32 [8, 4], P('bucket'), may hold values from 32 to 928, as said below
- group_bucket: int32 [8], P('bucket'), may hold values from 0 to 3, as said below
- null_mask: int32 [8, 4], P('bucket'), may hold values 0 or 1
- w_qkv: bfloat16 [1536, 4608], P('seq'), may hold values from -0.15625 to 0.15625
- w_out: bfloat16 [1536, 1536], P('seq'), may hold values from -0.625 to 0.625
- w_capkv: bfloat16 [4096, 3072], P('seq'), may hold values from -0.09375 to 0.09375
- w_gateup: bfloat16 [1536, 8192], P('seq'), may hold values from -0.15625 to 0.15625
- w_down: bfloat16 [4096, 1536], P('seq'), may hold values from -0.09375 to 0.09375
- w_mod: bfloat16 [1024, 6144], P('seq'), may hold values from -0.1875 to 0.1875
- b_mod: float32 [6144], replicated, may hold values from -3 to 3
- gain_attn: float32 [1536], replicated, may hold values from 0.5 to 1.5
- gain_ffn: float32 [1536], replicated, may hold values from 0.5 to 1.5
- gain_query: float32 [1536], replicated, may hold values from 0.5 to 1.5
- gain_key: float32 [1536], replicated, may hold values from 0.5 to 1.5
- gain_capkey: float32 [1536], replicated, may hold values from 0.5 to 1.5
- gate_head: float32 [24], replicated, may hold values from -1.5 to 1.5
- null_embed: bfloat16 [4096], replicated, may hold values from -6 to 6
Outputs:
- mixed: bfloat16 [8192, 1536], P(('bucket', 'seq'))
- input_grad: bfloat16 [8192, 1536], P(('bucket', 'seq'))
- grad_qkv: float32 [1536, 4608], P('seq')
- grad_out: float32 [1536, 1536], P('seq')
- grad_capkv: float32 [4096, 3072], P('seq')
- grad_gateup: float32 [1536, 8192], P('seq')
- grad_down: float32 [4096, 1536], P('seq')
- grad_mod: float32 [1024, 6144], P('seq')
- grad_bias_mod: float32 [6144], replicated
- grad_gain_attn: float32 [1536], replicated
- grad_gain_ffn: float32 [1536], replicated
- grad_gain_query: float32 [1536], replicated
- grad_gain_key: float32 [1536], replicated
- grad_gain_capkey: float32 [1536], replicated
- grad_gate_head: float32 [24], replicated
- grad_null: float32 [4096], replicated
The draws below stay inside these ranges and needn't reach their ends.
Inputs may be any that keep to these rules, and one draw needn't show every extreme that they name: In each group one document, at a place drawn from the seed, starts on the group's first device and ends on its last; the others hold 32 to 84 tokens; a group's lengths sum to more than 768, the rest is padding. `group_bucket`: bucket numbers never fall along the groups, the first group has 0, and each of the 4 buckets owns at least one group.
All inputs are finite; a program needn't handle non-finite values. No bound on the sum of `null_mask` on one device may be relied on, other than what follows from the above.
Results may differ from the reference program's by a relative error of at most 0.02.
Values may be sent and summed in bfloat16 or wider, within the bound.
A program may use at most 448 MiB of HBM per device.

```python
import jax
import jax.numpy as jnp
from jax import lax

D = 1536
HEADS = 24
HDIM = 64
FF = 4096
CTX = 4096
TD = 1024
CAP = 256
DOCS = 4
RES = 4
TOK_DEV = 256
GTOK = 1024
TOKENS = 8192
N_BUCKET = 8


def draw_lengths(key, part):
    key = jax.random.fold_in(key, 7)
    key_short, key_pad, key_slot = jax.random.split(key, 3)
    shorts = jax.random.randint(key_short, (N_BUCKET, DOCS - 1), TOK_DEV // 8, TOK_DEV // 3)
    spare = TOK_DEV - jnp.sum(shorts, axis=1)
    padding = jax.random.randint(key_pad, (N_BUCKET,), 0, 1 << 20) % spare
    longest = GTOK - jnp.sum(shorts, axis=1) - padding
    chosen = jax.random.randint(key_slot, (N_BUCKET, 1), 0, DOCS)
    slots = jnp.arange(DOCS)[None, :]
    before = jnp.concatenate([shorts, shorts[:, :1]], axis=1)
    after = jnp.concatenate([shorts[:, :1], shorts], axis=1)
    result = jnp.where(slots < chosen, before, jnp.where(slots == chosen, longest[:, None], after))
    return result.astype(jnp.int32)


def draw_group_bucket(key, part):
    key = jax.random.fold_in(key, 11)
    order = jax.random.permutation(key, N_BUCKET - 1) + 1
    cuts = order[:RES - 1]
    groups = jnp.arange(N_BUCKET)
    return jnp.sum((groups[:, None] >= cuts[None, :]).astype(jnp.int32), axis=1).astype(jnp.int32)


def plant(values, rng, low, top_value):
    spot = [jax.random.randint(jax.random.fold_in(rng, axis), (), 0, length) for axis, length in enumerate(values.shape)]
    main_axis = values.shape.index(max(values.shape))
    neighbour = spot[:main_axis] + [(spot[main_axis] + 1) % values.shape[main_axis]] + spot[main_axis + 1:]
    return values.at[tuple(spot)].set(low).at[tuple(neighbour)].set(top_value)


def steps_of(rng, shape, cuts, least, top_value):
    level = 1.0
    for dim, shards_of in cuts:
        steps = jax.random.uniform(jax.random.fold_in(jax.random.fold_in(rng, 6), dim), (shards_of,), jnp.float32, least / len(cuts), top_value / len(cuts))
        level = level * jnp.repeat(jnp.exp(steps), shape[dim] // shards_of).reshape((-1,) + (1,) * (len(shape) - 1 - dim))
    return level


def scatter_about(stream_key, shape, deviation, reach, pieces=(), kind=jnp.bfloat16):
    drawn = deviation * jax.random.normal(stream_key, shape, jnp.float32)
    if pieces:
        drawn = drawn * steps_of(stream_key, shape, pieces, -0.22, 0.18)
    return jnp.clip(drawn, -reach, reach).astype(kind)


def setup_inputs(seed: int = 0) -> dict:
    arg_keys = jax.random.split(jax.random.key(seed), 22)
    tokens = scatter_about(arg_keys[0], (TOKENS, D), 1.0, 6.0, ((0, 32),))
    cotangent = scatter_about(arg_keys[1], (TOKENS, D), 1.0, 6.0, ((0, 32),))
    step_embed = scatter_about(arg_keys[2], (N_BUCKET, DOCS, TD), 1.0, 6.0, ((0, 8),))
    caption = scatter_about(arg_keys[3], (N_BUCKET, DOCS, CAP, CTX), 1.0, 6.0, ((0, 8), (2, 4)))
    lengths = draw_lengths(jax.random.fold_in(arg_keys[21], 71), 0)
    group_bucket = draw_group_bucket(jax.random.fold_in(arg_keys[21], 71), 0)
    null_mask = plant((jax.random.randint(arg_keys[6], (N_BUCKET, DOCS), 0, 4) < 1).astype(jnp.int32), jax.random.fold_in(arg_keys[6], 1), 0, 1)
    w_qkv = scatter_about(arg_keys[7], (D, 3 * D), D ** -0.5, 0.15625, ((0, 4),))
    w_out = scatter_about(arg_keys[8], (D, D), (D // 16) ** -0.5, 0.625, ((0, 4),))
    w_capkv = scatter_about(arg_keys[9], (CTX, 2 * D), CTX ** -0.5, 0.09375, ((0, 4),))
    w_gateup = scatter_about(arg_keys[10], (D, 2 * FF), D ** -0.5, 0.15625, ((0, 4),))
    w_down = scatter_about(arg_keys[11], (FF, D), FF ** -0.5, 0.09375, ((0, 4),))
    w_mod = scatter_about(arg_keys[12], (TD, 4 * D), TD ** -0.5, 0.1875, ((0, 4),))
    b_mod = scatter_about(arg_keys[13], (4 * D,), 0.3, 3.0, (), jnp.float32)
    gain_attn = jnp.clip(1.0 + 0.1 * jax.random.normal(arg_keys[14], (D,), jnp.float32), 0.5, 1.5)
    gain_ffn = jnp.clip(1.0 + 0.1 * jax.random.normal(arg_keys[15], (D,), jnp.float32), 0.5, 1.5)
    gain_query = jnp.clip(1.0 + 0.1 * jax.random.normal(arg_keys[16], (D,), jnp.float32), 0.5, 1.5)
    gain_key = jnp.clip(1.0 + 0.1 * jax.random.normal(arg_keys[17], (D,), jnp.float32), 0.5, 1.5)
    gain_capkey = jnp.clip(1.0 + 0.1 * jax.random.normal(arg_keys[18], (D,), jnp.float32), 0.5, 1.5)
    gate_head = jnp.clip(jax.random.uniform(arg_keys[19], (HEADS,), jnp.float32, -1.5, 1.5), -1.5, 1.5)
    null_embed = scatter_about(arg_keys[20], (CTX,), 1.0, 6.0)
    return {"tokens": tokens, "cotangent": cotangent, "step_embed": step_embed, "caption": caption, "lengths": lengths, "group_bucket": group_bucket, "null_mask": null_mask, "w_qkv": w_qkv, "w_out": w_out, "w_capkv": w_capkv, "w_gateup": w_gateup, "w_down": w_down, "w_mod": w_mod, "b_mod": b_mod, "gain_attn": gain_attn, "gain_ffn": gain_ffn, "gain_query": gain_query, "gain_key": gain_key, "gain_capkey": gain_capkey, "gate_head": gate_head, "null_embed": null_embed}


@jax.custom_vjp
def low(v):
    return lax.optimization_barrier(v.astype(jnp.bfloat16)).astype(jnp.float32)

@jax.custom_vjp
def low_back(v):
    return v

def low_keep(v):
    return (low(v), None)

def low_pass(kept, grad):
    return (grad,)

def back_keep(v):
    return (v, None)

def back_low(kept, grad):
    return (low(grad),)
low.defvjp(low_keep, low_pass)
low_back.defvjp(back_keep, back_low)
eps = 1e-06
head_block = 4

def highest_dot(left, right):
    return jnp.dot(left, right, precision=lax.Precision.HIGHEST)

def row_norm(values):
    return values * lax.rsqrt(lax.optimization_barrier(jnp.mean(values * values, axis=-1, keepdims=True)) + eps)

def head_norm(values):
    shaped = values.reshape(values.shape[0], HEADS, HDIM)
    return row_norm(shaped).reshape(values.shape)

def rotary(values, row_pos, col_pos, direction):
    quarter = HDIM // 4
    freqs = 10000.0 ** (-jnp.arange(quarter, dtype=jnp.float32) / quarter)
    angles = jnp.concatenate([row_pos[:, None] * freqs, col_pos[:, None] * freqs], axis=1)
    cosine = jnp.cos(angles)[:, None, :]
    sine = direction * jnp.sin(angles)[:, None, :]
    shaped = values.reshape(values.shape[0], HEADS, HDIM)
    first_half = shaped[..., :HDIM // 2]
    second_half = shaped[..., HDIM // 2:]
    turned = jnp.concatenate([first_half * cosine - second_half * sine, second_half * cosine + first_half * sine], axis=-1)
    return turned.reshape(values.shape)

def layout(doc_lengths, bucket, positions):
    doc_ends = jnp.cumsum(doc_lengths).astype(jnp.int32)
    starts = doc_ends - doc_lengths
    segment = lax.optimization_barrier(jnp.sum((positions[:, None] >= doc_ends[None, :]).astype(jnp.int32), axis=1)).astype(jnp.int32)
    matches = segment[:, None] == jnp.arange(DOCS, dtype=jnp.int32)[None, :]
    offset = lax.optimization_barrier(jnp.sum(jnp.where(matches, starts[None, :], 0), axis=1)).astype(jnp.int32)
    within = positions - offset
    stride = 32 * (bucket + 1)
    return (segment, (within // stride).astype(jnp.float32), (within % stride).astype(jnp.float32))

def head_groups(values):
    return values.reshape(values.shape[0], HEADS // head_block, head_block, HDIM).transpose(1, 0, 2, 3)

def attend(query, keys, values, allowed):
    scale = HDIM ** (-0.5)

    def block(block_args):
        part_q, part_k, part_v = block_args
        scores = jnp.einsum('qhd,khd->hqk', part_q, part_k, precision=lax.Precision.HIGHEST) * scale
        scores = jnp.where(allowed[None], low_back(scores), -1e+30)
        attn_probs = jax.nn.softmax(scores, axis=-1)
        return jnp.einsum('hqk,khd->qhd', low(attn_probs), part_v, precision=lax.Precision.HIGHEST)
    blocks = lax.map(jax.checkpoint(block), (head_groups(query), head_groups(keys), head_groups(values)))
    return blocks.transpose(1, 0, 2, 3).reshape(query.shape[0], HEADS * HDIM)

def group_forward(params, group_args):
    w_qkv, w_out, w_capkv, w_gateup, w_down, w_mod, b_mod, gain_attn, gain_ffn, gain_query, gain_key, gain_capkey, gate_head, null_embed = params
    inputs, step_rows, captions, doc_lengths, bucket, nulls = group_args
    positions = jnp.arange(GTOK, dtype=jnp.int32)
    segment, row_pos, col_pos = layout(doc_lengths, bucket, positions)
    document = jnp.minimum(segment, DOCS - 1)
    doc_pick = (document[:, None] == jnp.arange(DOCS, dtype=jnp.int32)[None, :]).astype(jnp.float32)
    condition = low(jax.nn.silu(step_rows))
    modulation = highest_dot(doc_pick, highest_dot(condition, w_mod) + b_mod)
    scale_a, gate_a, scale_f, gate_f = jnp.split(modulation, 4, axis=1)
    hidden1 = low(row_norm(inputs) * gain_attn * (1.0 + scale_a))
    projected = low_back(highest_dot(hidden1, w_qkv))
    query_raw, key_raw, value_raw = jnp.split(projected, 3, axis=1)
    query = low(rotary(head_norm(query_raw) * gain_query, row_pos, col_pos, 1.0))
    keys = low(rotary(head_norm(key_raw) * gain_key, row_pos, col_pos, 1.0))
    values = low(value_raw)
    capmix = jnp.where(nulls[:, None, None] > 0, null_embed[None, None, :], captions)
    cap_proj = low_back(highest_dot(capmix.reshape(DOCS * CAP, CTX), w_capkv))
    capkey_raw, capval_raw = jnp.split(cap_proj, 2, axis=1)
    capkeys = low(head_norm(capkey_raw) * gain_capkey)
    capvals = low(capval_raw)
    cap_segment = jnp.repeat(jnp.arange(DOCS, dtype=jnp.int32), CAP)
    own_out = low_back(attend(query, keys, values, segment[:, None] == segment[None, :]))
    cross_out = low_back(attend(query, capkeys, capvals, document[:, None] == cap_segment[None, :]))
    head_gate = jnp.repeat(jnp.tanh(gate_head), HDIM)[None, :]
    mixed_attn = low(own_out + head_gate * cross_out)
    attn_out = low_back(highest_dot(mixed_attn, w_out))
    residual = inputs + jnp.tanh(gate_a) * attn_out
    hidden2 = low(row_norm(residual) * gain_ffn * (1.0 + scale_f))
    gate_up = low_back(highest_dot(hidden2, w_gateup))
    gate_part, up_part = jnp.split(gate_up, 2, axis=1)
    hidden_ffn = low(jax.nn.silu(gate_part) * up_part)
    down_out = low_back(highest_dot(hidden_ffn, w_down))
    return residual + jnp.tanh(gate_f) * down_out

def forward(params, token_groups, step_embed, caption, lengths, group_bucket, null_mask):

    def one_group(group_args):
        return group_forward(params, group_args)
    return lax.map(jax.checkpoint(one_group), (token_groups, step_embed, caption, lengths, group_bucket, null_mask))

def reference(tokens, cotangent, step_embed, caption, lengths, group_bucket, null_mask, w_qkv, w_out, w_capkv, w_gateup, w_down, w_mod, b_mod, gain_attn, gain_ffn, gain_query, gain_key, gain_capkey, gate_head, null_embed):
    counts = lax.optimization_barrier(jnp.sum(lengths, axis=1)).astype(jnp.float32)
    member = (group_bucket[:, None] == jnp.arange(RES, dtype=jnp.int32)[None, :]).astype(jnp.float32)
    per_bucket = lax.optimization_barrier(jnp.sum(counts[:, None] * member, axis=0))
    scale_loss = jnp.sum(counts) / (RES * lax.optimization_barrier(jnp.sum(member * per_bucket[None, :], axis=1)))
    positions = jnp.arange(GTOK, dtype=jnp.int32)
    is_valid = positions[None, :] < lax.optimization_barrier(jnp.sum(lengths, axis=1))[:, None]
    token_weight = jnp.where(is_valid, scale_loss[:, None], 0.0)
    cot_groups = cotangent.astype(jnp.float32).reshape(N_BUCKET, GTOK, D) * token_weight[..., None]
    token_groups = tokens.astype(jnp.float32).reshape(N_BUCKET, GTOK, D)
    params = (w_qkv.astype(jnp.float32), w_out.astype(jnp.float32), w_capkv.astype(jnp.float32), w_gateup.astype(jnp.float32), w_down.astype(jnp.float32), w_mod.astype(jnp.float32), b_mod, gain_attn, gain_ffn, gain_query, gain_key, gain_capkey, gate_head, null_embed.astype(jnp.float32))
    step_f = step_embed.astype(jnp.float32)
    caption_f = caption.astype(jnp.float32)

    def run(param_set, token_set):
        return forward(param_set, token_set, step_f, caption_f, lengths, group_bucket, null_mask)
    outputs, pullback = jax.vjp(run, params, token_groups)
    param_grads, token_grads = pullback(cot_groups)
    return (outputs.reshape(TOKENS, D).astype(jnp.bfloat16), token_grads.reshape(TOKENS, D).astype(jnp.bfloat16), param_grads[0], param_grads[1], param_grads[2], param_grads[3], param_grads[4], param_grads[5], param_grads[6], param_grads[7], param_grads[8], param_grads[9], param_grads[10], param_grads[11], param_grads[12], param_grads[13])
```

```python
import jax
import jax.numpy as jnp
from jax import lax
from jax.sharding import Mesh, PartitionSpec as P

HEADS = 24
HDIM = 64
DOCS = 4
RES = 4


eps = 1e-06


def row_stats(values):
    inverse = lax.rsqrt(jnp.mean(values * values, axis=-1, keepdims=True) + eps)
    return (values * inverse, inverse)


def norm_back(grad_normed, normed, inverse):
    inner_mean = jnp.mean(grad_normed * normed, axis=-1, keepdims=True)
    return inverse * (grad_normed - normed * inner_mean)


def head_stats(values):
    shaped = values.reshape(values.shape[0], -1, HDIM)
    normed, inverse = row_stats(shaped)
    return (normed.reshape(values.shape), inverse)


def head_back(grad_normed, normed, inverse):
    shaped_grad = grad_normed.reshape(grad_normed.shape[0], -1, HDIM)
    shaped_norm = normed.reshape(normed.shape[0], -1, HDIM)
    return norm_back(shaped_grad, shaped_norm, inverse).reshape(grad_normed.shape)


def rotary(values, row_pos, col_pos, direction):
    quarter = HDIM // 4
    freqs = 10000.0 ** (-jnp.arange(quarter, dtype=jnp.float32) / quarter)
    angles = jnp.concatenate([row_pos[:, None] * freqs, col_pos[:, None] * freqs], axis=1)
    cosine = jnp.cos(angles)[:, None, :]
    sine = direction * jnp.sin(angles)[:, None, :]
    shaped = values.reshape(values.shape[0], -1, HDIM)
    first_half = shaped[..., : HDIM // 2]
    second_half = shaped[..., HDIM // 2 :]
    turned = jnp.concatenate(
        [first_half * cosine - second_half * sine, second_half * cosine + first_half * sine],
        axis=-1,
    )
    return turned.reshape(values.shape)


def layout(doc_lengths, bucket, positions):
    doc_ends = jnp.cumsum(doc_lengths)
    starts = doc_ends - doc_lengths
    segment = jnp.sum((positions[:, None] >= doc_ends[None, :]).astype(jnp.int32), axis=1)
    matches = segment[:, None] == jnp.arange(DOCS, dtype=jnp.int32)[None, :]
    offset = jnp.sum(jnp.where(matches, starts[None, :], 0), axis=1)
    within = positions - offset
    stride = 32 * (bucket + 1)
    return (segment, (within // stride).astype(jnp.float32), (within % stride).astype(jnp.float32))


def by_head(values):
    return values.reshape(values.shape[0], -1, 1, HDIM).transpose(1, 0, 2, 3)


def from_heads(blocks):
    return blocks.transpose(1, 0, 2, 3).reshape(blocks.shape[1], -1)


def attend_forward(query, keys, values, allowed):
    scale = HDIM ** (-0.5)

    def block(block_args):
        part_q, part_k, part_v = block_args
        scores = (
            jnp.einsum("qhd,khd->hqk", part_q, part_k, preferred_element_type=jnp.float32) * scale
        )
        scores = jnp.where(allowed[None], scores, -1e30)
        row_peak = jnp.max(scores, axis=-1, keepdims=True)
        exp_scores = jnp.exp(scores - row_peak)
        exp_total = jnp.sum(exp_scores, axis=-1, keepdims=True)
        attn_probs = (exp_scores / exp_total).astype(jnp.bfloat16)
        attn_block = jnp.einsum(
            "hqk,khd->qhd", attn_probs, part_v, preferred_element_type=jnp.float32
        )
        return (attn_block, row_peak[..., 0] + jnp.log(exp_total[..., 0]))

    blocks, log_total = lax.map(block, (by_head(query), by_head(keys), by_head(values)))
    return (from_heads(blocks), log_total)


def attend_backward(query, keys, values, allowed, log_total, grad_out):
    scale = HDIM ** (-0.5)

    def block(block_args):
        part_q, part_k, part_v, part_log, part_grad = block_args
        scores = (
            jnp.einsum("qhd,khd->hqk", part_q, part_k, preferred_element_type=jnp.float32) * scale
        )
        scores = jnp.where(allowed[None], scores, -1e30)
        attn_probs = jnp.exp(scores - part_log[..., None])
        grad_probs = jnp.einsum(
            "qhd,khd->hqk", part_grad, part_v, preferred_element_type=jnp.float32
        )
        row_delta = jnp.sum(attn_probs * grad_probs, axis=-1, keepdims=True)
        grad_scores = (attn_probs * (grad_probs - row_delta)).astype(jnp.bfloat16)
        grad_query = (
            jnp.einsum("hqk,khd->qhd", grad_scores, part_k, preferred_element_type=jnp.float32)
            * scale
        )
        grad_keys = (
            jnp.einsum("hqk,qhd->khd", grad_scores, part_q, preferred_element_type=jnp.float32)
            * scale
        )
        grad_values = jnp.einsum(
            "hqk,qhd->khd",
            attn_probs.astype(jnp.bfloat16),
            part_grad,
            preferred_element_type=jnp.float32,
        )
        return (grad_query, grad_keys, grad_values)

    grad_query, grad_keys, grad_values = lax.map(
        block,
        (by_head(query), by_head(keys), by_head(values), log_total, by_head(grad_out)),
    )
    return (from_heads(grad_query), from_heads(grad_keys), from_heads(grad_values))


def matmul(left, right):
    return jnp.dot(left, right, preferred_element_type=jnp.float32)


def contract_right(left, weight):
    return lax.dot_general(
        left, weight, (((1,), (1,)), ((), ())), preferred_element_type=jnp.float32
    )


def contract_rows(left, right):
    return lax.dot_general(
        left, right, (((0,), (0,)), ((), ())), preferred_element_type=jnp.float32
    )


def pick(values, index, axis):
    return lax.dynamic_index_in_dim(values, index, axis, keepdims=False)


def to_plane(values):
    ways = lax.axis_size("tp")
    parts = values.reshape((ways, values.shape[0] // ways) + values.shape[1:])
    parts = lax.all_to_all(parts, "tp", 0, 0, tiled=True)
    parts = lax.all_to_all(parts, "seq", 0, 0, tiled=True)
    return parts.reshape(values.shape)


def from_plane(values):
    ways = lax.axis_size("tp")
    parts = values.reshape((ways, values.shape[0] // ways) + values.shape[1:])
    parts = lax.all_to_all(parts, "seq", 0, 0, tiled=True)
    parts = lax.all_to_all(parts, "tp", 0, 0, tiled=True)
    return parts.reshape(values.shape)


def gather_rows(part):
    whole = lax.all_gather(part, "seq", axis=0, tiled=False)
    whole = lax.all_gather(whole, "core", axis=1, tiled=False)
    return whole.reshape((-1,) + part.shape[1:])


def scatter_rows(term):
    cores, planes = lax.axis_size("core"), lax.axis_size("seq")
    shaped = term.astype(jnp.bfloat16).reshape(planes, cores, -1, term.shape[-1])
    half = lax.psum_scatter(shaped, "core", scatter_dimension=1, tiled=False)
    return lax.psum_scatter(half, "seq", scatter_dimension=0, tiled=False)


def plane_gather(values):
    return lax.all_gather(values, "tp", axis=0, tiled=True)


def plane_scatter(values):
    return lax.psum_scatter(
        values.astype(jnp.bfloat16), "tp", scatter_dimension=0, tiled=True
    ).astype(jnp.float32)


def shards(
    tokens,
    cotangent,
    step_embed,
    caption,
    lengths,
    group_bucket,
    null_mask,
    w_qkv,
    w_out,
    w_capkv,
    w_gateup,
    w_down,
    w_mod,
    b_mod,
    gain_attn,
    gain_ffn,
    gain_query,
    gain_key,
    gain_capkey,
    gate_head,
    null_embed,
):
    tp, cores, planes = lax.axis_size("tp"), lax.axis_size("core"), lax.axis_size("seq")
    me_t, me_c, me_z = lax.axis_index("tp"), lax.axis_index("core"), lax.axis_index("seq")
    groups = tp * cores
    rows, width = tokens.shape
    piece = rows // tp
    local_heads = HEADS // tp
    local = local_heads * HDIM
    cap_dev = caption.shape[2]
    ctx = caption.shape[3]
    my_group = me_z * cores + me_c

    numbers = jnp.concatenate([lengths[0], group_bucket, null_mask[0]])
    numbers = lax.all_gather(numbers, ("tp", "core"), axis=0, tiled=False).reshape(groups, -1)
    counts = jnp.sum(numbers[:, :DOCS], axis=1).astype(jnp.float32)
    mine = pick(numbers, my_group, 0)
    doc_lengths, bucket, nulls = mine[:DOCS], mine[DOCS], mine[DOCS + 1 :]
    bucket_count = jnp.sum(jnp.where(numbers[:, DOCS] == bucket, counts, 0.0))
    scale_loss = jnp.sum(counts) / (RES * bucket_count)

    steps = lax.all_gather(step_embed[0], ("tp", "core"), axis=0, tiled=True)
    condition = jax.nn.silu(steps.astype(jnp.float32)).astype(jnp.bfloat16)
    mod_rows = w_mod.shape[0]
    cond_mine = lax.dynamic_slice_in_dim(condition, me_z * mod_rows, mod_rows, 1)
    mod_all = matmul(cond_mine, w_mod).reshape(planes, cores * DOCS, -1)
    mod_plane = lax.psum_scatter(mod_all, "seq", scatter_dimension=0, tiled=False)
    mod_doc = pick(mod_plane.reshape(cores, DOCS, -1), me_c, 0) + b_mod

    qkv_part = pick(w_qkv.reshape(-1, 3, tp, local), me_t, 2).reshape(cores, -1, 3 * local)
    full_qkv = gather_rows(pick(qkv_part, me_c, 0))
    capkv_part = pick(w_capkv.reshape(-1, 2, tp, local), me_t, 2).reshape(cores, -1, 2 * local)
    full_capkv = gather_rows(pick(capkv_part, me_c, 0))
    gateup_part = pick(
        w_gateup.reshape(w_gateup.shape[0], 2 * planes, tp, -1), me_t, 2
    ).reshape(cores, w_gateup.shape[0] // cores, -1)
    full_gateup = gather_rows(pick(gateup_part, me_c, 0))
    down_part = pick(w_down.reshape(tp, cores, -1, width), me_t, 0)
    full_down = gather_rows(pick(down_part, me_c, 0))
    out_part = pick(w_out.reshape(w_out.shape[0], groups, -1), me_t * cores + me_c, 1)
    out_part = lax.all_gather(out_part, "seq", axis=0, tiled=False)
    out_part = lax.all_to_all(out_part, "tp", 0, 0, tiled=True)
    out_part = lax.all_gather(out_part, "core", axis=1, tiled=False)
    full_out = out_part.transpose(2, 0, 1, 3).reshape(local, width)

    inputs = to_plane(tokens).astype(jnp.float32)
    row = jnp.arange(rows, dtype=jnp.int32)
    spread = (row // piece) * rows + row % piece
    positions = spread + me_t * piece
    all_positions = (jnp.arange(tp, dtype=jnp.int32)[:, None] * piece + spread[None, :]).reshape(-1)
    segment, _, _ = layout(doc_lengths, bucket, positions)
    all_segment, row_pos, col_pos = layout(doc_lengths, bucket, all_positions)
    all_document = jnp.minimum(all_segment, DOCS - 1)
    document = jnp.minimum(segment, DOCS - 1)
    doc_pick = (document[:, None] == jnp.arange(DOCS, dtype=jnp.int32)[None, :]).astype(jnp.float32)
    is_valid = (segment < DOCS).astype(jnp.float32)
    modulation = jnp.dot(doc_pick, mod_doc, precision=lax.Precision.HIGHEST)
    scale_a, gate_a, scale_f, gate_f = jnp.split(modulation, 4, axis=1)
    tanh_a, tanh_f = jnp.tanh(gate_a), jnp.tanh(gate_f)

    normed1, inverse1 = row_stats(inputs)
    hidden1 = plane_gather((normed1 * gain_attn * (1.0 + scale_a)).astype(jnp.bfloat16))
    projected = matmul(hidden1, full_qkv)
    query_raw, key_raw, value_raw = jnp.split(projected, 3, axis=1)
    query_norm, query_inv = head_stats(query_raw)
    key_norm, key_inv = head_stats(key_raw)
    my_gain_query = pick(gain_query.reshape(tp, local), me_t, 0)
    my_gain_key = pick(gain_key.reshape(tp, local), me_t, 0)
    my_gain_capkey = pick(gain_capkey.reshape(tp, local), me_t, 0)
    query = rotary(query_norm * my_gain_query, row_pos, col_pos, 1.0).astype(jnp.bfloat16)
    keys = rotary(key_norm * my_gain_key, row_pos, col_pos, 1.0).astype(jnp.bfloat16)
    values = value_raw.astype(jnp.bfloat16)

    captions = to_plane(caption[0].transpose(1, 0, 2)).transpose(1, 0, 2)
    capmix = jnp.where(nulls[:, None, None] > 0, null_embed[None, None, :], captions)
    cap_flat = plane_gather(capmix.reshape(DOCS * cap_dev, ctx))
    cap_document = jnp.tile(jnp.repeat(jnp.arange(DOCS, dtype=jnp.int32), cap_dev), tp)
    cap_proj = matmul(cap_flat, full_capkv)
    capkey_raw, capval_raw = jnp.split(cap_proj, 2, axis=1)
    capkey_norm, capkey_inv = head_stats(capkey_raw)
    capkeys = (capkey_norm * my_gain_capkey).astype(jnp.bfloat16)
    capvals = capval_raw.astype(jnp.bfloat16)

    self_allowed = all_segment[:, None] == all_segment[None, :]
    cross_allowed = all_document[:, None] == cap_document[None, :]
    own_out, own_log = attend_forward(query, keys, values, self_allowed)
    cross_out, cross_log = attend_forward(query, capkeys, capvals, cross_allowed)
    gate_tanh = pick(jnp.tanh(gate_head).reshape(tp, local_heads), me_t, 0)
    head_gate = jnp.repeat(gate_tanh, HDIM)[None, :]
    mixed_attn = (own_out + head_gate * cross_out).astype(jnp.bfloat16)
    attn_out = plane_scatter(matmul(mixed_attn, full_out))
    residual = inputs + tanh_a * attn_out
    normed2, inverse2 = row_stats(residual)
    hidden2 = plane_gather((normed2 * gain_ffn * (1.0 + scale_f)).astype(jnp.bfloat16))
    gate_part, up_part = jnp.split(matmul(hidden2, full_gateup), 2, axis=1)
    sig_gate = jax.nn.sigmoid(gate_part)
    silu_gate = gate_part * sig_gate
    hidden_ffn = (silu_gate * up_part).astype(jnp.bfloat16)
    down_out = plane_scatter(matmul(hidden_ffn, full_down))
    result = from_plane((residual + tanh_f * down_out).astype(jnp.bfloat16))

    grad_res0 = to_plane(cotangent).astype(jnp.float32) * (is_valid * scale_loss)[:, None]
    grad_down = plane_gather((tanh_f * grad_res0).astype(jnp.bfloat16))
    grad_gate_f = grad_res0 * down_out * (1.0 - tanh_f * tanh_f)
    grad_ffn = contract_right(grad_down, full_down)
    grad_gate_part = grad_ffn * up_part * sig_gate * (1.0 + gate_part * (1.0 - sig_gate))
    grad_up_part = grad_ffn * silu_gate
    grad_gateup = jnp.concatenate([grad_gate_part, grad_up_part], axis=1).astype(jnp.bfloat16)
    grad_hidden2 = plane_scatter(contract_right(grad_gateup, full_gateup))
    gain_ffn_term = jnp.sum(grad_hidden2 * normed2 * (1.0 + scale_f), axis=0)
    grad_scale_f = grad_hidden2 * normed2 * gain_ffn
    grad_residual = grad_res0 + norm_back(
        grad_hidden2 * gain_ffn * (1.0 + scale_f), normed2, inverse2
    )
    grad_attn = plane_gather((tanh_a * grad_residual).astype(jnp.bfloat16))
    grad_gate_a = grad_residual * attn_out * (1.0 - tanh_a * tanh_a)
    grad_mix = contract_right(grad_attn, full_out)
    grad_own = grad_mix.astype(jnp.bfloat16)
    grad_cross = (head_gate * grad_mix).astype(jnp.bfloat16)
    gate_head_term = jnp.sum(
        (grad_mix * cross_out).reshape(-1, local_heads, HDIM), axis=(0, 2)
    ) * (1.0 - gate_tanh * gate_tanh)
    query_own, grad_keys, grad_values = attend_backward(
        query, keys, values, self_allowed, own_log, grad_own
    )
    query_cross, grad_capkeys, grad_capvals = attend_backward(
        query, capkeys, capvals, cross_allowed, cross_log, grad_cross
    )
    grad_query = rotary(query_own + query_cross, row_pos, col_pos, -1.0)
    gain_query_term = jnp.sum(grad_query * query_norm, axis=0)
    grad_query_raw = head_back(grad_query * my_gain_query, query_norm, query_inv)
    grad_key = rotary(grad_keys, row_pos, col_pos, -1.0)
    gain_key_term = jnp.sum(grad_key * key_norm, axis=0)
    grad_key_raw = head_back(grad_key * my_gain_key, key_norm, key_inv)
    grad_projected = jnp.concatenate([grad_query_raw, grad_key_raw, grad_values], axis=1).astype(
        jnp.bfloat16
    )
    grad_hidden1 = plane_scatter(contract_right(grad_projected, full_qkv))
    gain_attn_term = jnp.sum(grad_hidden1 * normed1 * (1.0 + scale_a), axis=0)
    grad_scale_a = grad_hidden1 * normed1 * gain_attn
    input_grad = from_plane(
        (
            grad_residual + norm_back(grad_hidden1 * gain_attn * (1.0 + scale_a), normed1, inverse1)
        ).astype(jnp.bfloat16)
    )

    grad_mod_tok = jnp.concatenate([grad_scale_a, grad_gate_a, grad_scale_f, grad_gate_f], axis=1)
    grad_mod_doc = lax.dot_general(
        doc_pick,
        grad_mod_tok,
        (((0,), (0,)), ((), ())),
        precision=lax.Precision.HIGHEST,
        preferred_element_type=jnp.float32,
    )
    grad_mod_doc = lax.psum(grad_mod_doc, "tp")
    grad_mod_docs = lax.all_gather(grad_mod_doc, ("seq", "core"), axis=0, tiled=True)
    sum_mod = lax.dot_general(
        cond_mine.astype(jnp.float32),
        grad_mod_docs,
        (((0,), (0,)), ((), ())),
        precision=lax.Precision.HIGHEST,
        preferred_element_type=jnp.float32,
    )
    sum_bias = jnp.sum(grad_mod_docs, axis=0)

    gain_capkey_term = jnp.sum(grad_capkeys * capkey_norm, axis=0)
    grad_capkey_raw = head_back(grad_capkeys * my_gain_capkey, capkey_norm, capkey_inv)
    grad_cap_proj = jnp.concatenate([grad_capkey_raw, grad_capvals], axis=1).astype(jnp.bfloat16)
    null_rows = nulls[cap_document] > 0
    null_sum = jnp.sum(
        jnp.where(null_rows[:, None], grad_cap_proj.astype(jnp.float32), 0.0), axis=0
    )
    null_term = jnp.dot(
        full_capkv.astype(jnp.float32), null_sum, precision=lax.Precision.HIGHEST
    )

    term_down = scatter_rows(contract_rows(hidden_ffn, grad_down))
    sum_down = lax.all_gather(term_down, ("tp", "core"), axis=0, tiled=True)
    term_gateup = scatter_rows(contract_rows(hidden2, grad_gateup))
    term_gateup = lax.all_gather(term_gateup, ("tp", "core"), axis=0, tiled=False)
    sum_gateup = (
        term_gateup.reshape(tp, cores, w_gateup.shape[0] // cores, 2 * planes, -1)
        .transpose(1, 2, 3, 0, 4)
        .reshape(w_gateup.shape)
    )
    term_out = contract_rows(mixed_attn, grad_attn).astype(jnp.bfloat16)
    term_out = term_out.reshape(local, tp, cores, -1).transpose(1, 2, 0, 3)
    term_out = lax.psum_scatter(term_out, "core", scatter_dimension=1, tiled=False)
    term_out = lax.all_to_all(term_out, "tp", 0, 0, tiled=True)
    term_out = lax.psum_scatter(term_out, "seq", scatter_dimension=0, tiled=False)
    sum_out = lax.all_gather(term_out, ("tp", "core"), axis=1, tiled=True)
    term_qkv = scatter_rows(contract_rows(hidden1, grad_projected))
    term_qkv = lax.all_gather(term_qkv, ("tp", "core"), axis=0, tiled=False)
    sum_qkv = (
        term_qkv.reshape(tp, cores, w_qkv.shape[0] // cores, 3, local)
        .transpose(1, 2, 3, 0, 4)
        .reshape(w_qkv.shape)
    )
    term_capkv = scatter_rows(contract_rows(cap_flat, grad_cap_proj))
    term_capkv = lax.all_gather(term_capkv, ("tp", "core"), axis=0, tiled=False)
    sum_capkv = (
        term_capkv.reshape(tp, cores, w_capkv.shape[0] // cores, 2, local)
        .transpose(1, 2, 3, 0, 4)
        .reshape(w_capkv.shape)
    )

    def at_mine(part):
        whole = jnp.zeros((tp,) + part.shape, jnp.float32)
        return lax.dynamic_update_index_in_dim(whole, part, me_t, 0).reshape(-1)

    small = lax.psum(
        jnp.concatenate(
            [
                gain_attn_term,
                gain_ffn_term,
                at_mine(gain_query_term),
                at_mine(gain_key_term),
                at_mine(gain_capkey_term),
                at_mine(gate_head_term),
                null_term,
            ]
        ),
        ("tp", "core", "seq"),
    )
    ends = [width, 2 * width, 3 * width, 4 * width, 5 * width, 5 * width + HEADS]
    small_parts = jnp.split(small, ends)
    f32 = jnp.float32
    return (
        result,
        input_grad,
        sum_qkv.astype(f32),
        sum_out.astype(f32),
        sum_capkv.astype(f32),
        sum_gateup.astype(f32),
        sum_down.astype(f32),
        sum_mod,
        sum_bias,
        *small_parts,
    )


def solution(mesh):
    planes = mesh.shape["seq"]
    cores = mesh.shape["bucket"] // planes
    split = Mesh(mesh.devices.reshape(planes, cores, planes), ("tp", "core", "seq"))
    group = ("tp", "core")
    token = P(("tp", "core", "seq"), None)
    weight = P("seq", None)
    placed = (
        token,
        token,
        P(group, None, None),
        P(group, None, "seq", None),
        P(group, None),
        P(group),
        P(group, None),
        *([weight] * 6),
        *([P()] * 8),
    )
    return jax.shard_map(
        shards,
        mesh=split,
        in_specs=placed,
        out_specs=(token, token, *([weight] * 6), *([P()] * 8)),
        check_vma=False,
    )
```

```python
import functools

import jax
import jax.numpy as jnp
from jax import lax
from jax.experimental import pallas as pl
from jax.experimental.pallas import tpu as pltpu
from jax.sharding import Mesh, PartitionSpec as P

HEADS = 24
HDIM = 64
DOCS = 4
RES = 4


eps = 1e-06

MESH = pl.DeviceIdType.MESH
VMEM_BYTES = 60 * 1024 * 1024


def neighbours():
    me = lax.axis_index("tp")
    return me, me + 1 - 2 * lax.rem(me, 2), lax.rem(me + 2, 4), 3 - me


def greet(places):
    barrier = pltpu.get_barrier_semaphore()
    for place in places:
        pl.semaphore_signal(barrier, inc=1, device_id=place, device_id_type=MESH)
    pl.semaphore_wait(barrier, len(places))


def send(source, target, sems, index, place):
    return pltpu.make_async_remote_copy(
        src_ref=source,
        dst_ref=target,
        send_sem=sems[0].at[index],
        recv_sem=sems[1].at[index],
        device_id=place,
        device_id_type=MESH,
    )


def tile_of(width):
    for tile in (512, 384, 256, 128):
        if width % tile == 0:
            return tile
    return width


def multiply(left, weight_ref, columns, turned):
    if turned:
        return lax.dot_general(
            left, weight_ref[columns, :], (((1,), (1,)), ((), ())),
            preferred_element_type=jnp.float32,
        )
    return jnp.dot(left, weight_ref[:, columns], preferred_element_type=jnp.float32)


def gather_kernel(turned, halved, keep, *refs):
    x_ref, w_ref, all_ref = refs[:3]
    refs = refs[3:]
    if halved:
        full_ref, refs = refs[0], refs[1:]
    y_ref, xbuf, wbuf, ybuf, load, done = refs[:6]
    sems = refs[6:8]
    me, across, along, far = neighbours()
    rows = x_ref.shape[0]
    half = rows // 2
    core = lax.axis_index("core")
    places = [{"tp": across}, {"tp": along}]
    if halved:
        places.append({"core": 1 - core})
    mine = pltpu.make_async_copy(x_ref, xbuf.at[me], load.at[0])
    mine.start()
    if halved:
        planes, part, _ = w_ref.shape
        places_of = [
            pl.ds(pl.multiple_of((z * 2 + core) * part, part), part) for z in range(planes)
        ]
        weights = [
            pltpu.make_async_copy(w_ref.at[z], wbuf.at[places_of[z]], load.at[1 + z])
            for z in range(planes)
        ]
    else:
        weights = [pltpu.make_async_copy(w_ref, wbuf, load.at[1])]
    for copy in weights:
        copy.start()
    greet(places)

    def block(owner, part):
        return xbuf.at[owner, pl.ds(part * half, half)]

    def pass_on(index, owner, part, place):
        return send(block(owner, part), block(owner, part), sems, index, place)

    first = [
        send(x_ref.at[pl.ds(0, half)], block(me, 0), sems, 0, {"tp": across}),
        send(x_ref.at[pl.ds(half, half)], block(me, 1), sems, 1, {"tp": along}),
        send(x_ref.at[pl.ds(half, half)], block(me, 1), sems, 2, {"tp": across}),
        send(x_ref.at[pl.ds(0, half)], block(me, 0), sems, 3, {"tp": along}),
    ]
    for copy in first:
        copy.start()
    swaps = []
    if halved:
        for z in range(planes):
            swaps.append(send(w_ref.at[z], wbuf.at[places_of[z]], sems, 6 + z, {"core": 1 - core}))
        for copy in swaps:
            copy.start()
    mine.wait()
    for copy in weights:
        copy.wait()
    first[0].wait_recv()
    on_a = pass_on(4, across, 0, {"tp": along})
    on_a.start()
    first[1].wait_recv()
    on_b = pass_on(5, along, 1, {"tp": across})
    on_b.start()
    for copy in swaps:
        copy.wait()

    tile = tile_of(ybuf.shape[-1])
    outs = []
    if halved:
        outs.append(pltpu.make_async_copy(wbuf, full_ref, done.at[4]))
        outs[-1].start()

    def compute(owner, index):
        @pl.loop(0, ybuf.shape[-1] // tile)
        def _(step):
            columns = pl.ds(pl.multiple_of(step * tile, tile), tile)
            ybuf[index, :, columns] = multiply(xbuf[owner], wbuf, columns, turned).astype(
                ybuf.dtype
            )

        copy = pltpu.make_async_copy(ybuf.at[index], y_ref.at[owner], done.at[index])
        copy.start()
        outs.append(copy)

    compute(me, 0)
    first[2].wait_recv()
    compute(across, 1)
    first[3].wait_recv()
    compute(along, 2)
    on_a.wait_recv()
    on_b.wait_recv()
    if keep:
        copy = pltpu.make_async_copy(xbuf, all_ref, load.at[0])
        copy.start()
        outs.append(copy)
    compute(far, 3)
    for copy in first + [on_a, on_b]:
        copy.wait_send()
    for copy in outs:
        copy.wait()


def gather_matmul(ident, x, w, turned=False, halved=False, out=jnp.float32):
    rows, depth = x.shape
    if halved:
        planes, part, width = w.shape
        whole = (planes * 2 * part, width)
    else:
        whole = w.shape
    width = whole[0] if turned else whole[1]
    shapes = [jax.ShapeDtypeStruct((4, rows, depth), x.dtype)]
    if halved:
        shapes.append(jax.ShapeDtypeStruct(whole, w.dtype))
    shapes.append(jax.ShapeDtypeStruct((4, rows, width), out))
    hbm = pl.BlockSpec(memory_space=pl.ANY)
    got = pl.pallas_call(
        functools.partial(gather_kernel, turned, halved, True),
        out_shape=shapes,
        in_specs=[hbm, hbm],
        out_specs=[hbm] * len(shapes),
        scratch_shapes=[
            pltpu.VMEM((4, rows, depth), x.dtype),
            pltpu.VMEM(whole, w.dtype),
            pltpu.VMEM((4, rows, width), out),
            pltpu.SemaphoreType.DMA((6,)),
            pltpu.SemaphoreType.DMA((5,)),
            pltpu.SemaphoreType.DMA((10,)),
            pltpu.SemaphoreType.DMA((10,)),
        ],
        compiler_params=pltpu.CompilerParams(
            collective_id=ident, has_side_effects=True, vmem_limit_bytes=VMEM_BYTES
        ),
        cost_estimate=pl.CostEstimate(
            flops=8 * rows * depth * width,
            bytes_accessed=30 * 3_000_000,
            transcendentals=0,
        ),
        name="gather_matmul",
    )(x, w)
    return [got[0].reshape(4 * rows, depth), *got[1:-1], got[-1].reshape(4 * rows, width)]


def scatter_kernel(turned, x_ref, w_ref, out_ref, sums, far_out, near_out, relay, land, s0, s1):
    me, across, along, far = neighbours()
    sems = (s0, s1)
    rows, width = out_ref.shape
    half = rows // 2
    top, low = pl.ds(0, half), pl.ds(half, half)
    tile = tile_of(width)
    to_across, to_along = {"tp": across}, {"tp": along}
    greet([to_across, to_along])

    def tiles(body):
        @pl.loop(0, width // tile)
        def _(step):
            body(pl.ds(pl.multiple_of(step * tile, tile), tile))

    def product(owner, columns):
        return multiply(x_ref[owner], w_ref, columns, turned)

    @tiles
    def _(columns):
        far_out[:, columns] = product(far, columns).astype(far_out.dtype)

    far_a = send(far_out.at[top], relay.at[0], sems, 0, to_across)
    far_b = send(far_out.at[low], relay.at[1], sems, 1, to_along)
    far_a.start()
    far_b.start()

    @tiles
    def _(columns):
        part = product(across, columns)
        near_out[0, top, columns] = part[:half].astype(near_out.dtype)
        sums[0, :, columns] = part[half:]

    across_a = send(near_out.at[0, top], land.at[0, top], sems, 2, to_across)
    across_a.start()

    @tiles
    def _(columns):
        part = product(along, columns)
        near_out[1, low, columns] = part[half:].astype(near_out.dtype)
        sums[1, :, columns] = part[:half]

    along_b = send(near_out.at[1, low], land.at[1, low], sems, 3, to_along)
    along_b.start()
    far_b.wait_recv()

    @tiles
    def _(columns):
        near_out[0, low, columns] = (
            sums[0, :, columns] + relay[1, :, columns].astype(jnp.float32)
        ).astype(near_out.dtype)

    across_b = send(near_out.at[0, low], land.at[0, low], sems, 4, to_across)
    across_b.start()
    far_a.wait_recv()

    @tiles
    def _(columns):
        near_out[1, top, columns] = (
            sums[1, :, columns] + relay[0, :, columns].astype(jnp.float32)
        ).astype(near_out.dtype)

    along_a = send(near_out.at[1, top], land.at[1, top], sems, 5, to_along)
    along_a.start()

    @tiles
    def _(columns):
        out_ref[:, columns] = product(me, columns)

    for copy in (across_a, along_b, across_b, along_a):
        copy.wait_recv()

    @tiles
    def _(columns):
        out_ref[:, columns] += land[0, :, columns].astype(jnp.float32) + land[
            1, :, columns
        ].astype(jnp.float32)

    for copy in (far_a, far_b, across_a, along_b, across_b, along_a):
        copy.wait_send()


def matmul_scatter(ident, x, w, turned=False):
    rows, depth = x.shape[0] // 4, x.shape[1]
    width = w.shape[0] if turned else w.shape[1]
    vmem = pl.BlockSpec(memory_space=pltpu.VMEM)
    return pl.pallas_call(
        functools.partial(scatter_kernel, turned),
        out_shape=jax.ShapeDtypeStruct((rows, width), jnp.float32),
        in_specs=[vmem, vmem],
        out_specs=vmem,
        scratch_shapes=[
            pltpu.VMEM((2, rows // 2, width), jnp.float32),
            pltpu.VMEM((rows, width), jnp.bfloat16),
            pltpu.VMEM((2, rows, width), jnp.bfloat16),
            pltpu.VMEM((2, rows // 2, width), jnp.bfloat16),
            pltpu.VMEM((2, rows, width), jnp.bfloat16),
            pltpu.SemaphoreType.DMA((6,)),
            pltpu.SemaphoreType.DMA((6,)),
        ],
        compiler_params=pltpu.CompilerParams(
            collective_id=ident, has_side_effects=True, vmem_limit_bytes=VMEM_BYTES
        ),
        cost_estimate=pl.CostEstimate(
            flops=8 * rows * depth * width,
            bytes_accessed=30 * 3_000_000,
            transcendentals=0,
        ),
        name="matmul_scatter",
    )(x.reshape(4, rows, depth), w)


def collect_kernel(count, *refs):
    ins, outs = refs[:count], refs[count : 2 * count]
    load, s0, s1 = refs[2 * count :]
    sems = (s0, s1)
    me, across, along, far = neighbours()
    core = lax.axis_index("core")
    to_across, to_along, to_core = {"tp": across}, {"tp": along}, {"core": 1 - core}
    local = [
        pltpu.make_async_copy(ins[i], outs[i].at[me, core], load.at[i]) for i in range(count)
    ]
    for copy in local:
        copy.start()
    greet([to_across, to_along, to_core])

    def half(i, part):
        rows = ins[i].shape[0] // 2
        return pl.ds(part * rows, rows)

    def first(i, part, index, place):
        return send(
            ins[i].at[half(i, part)],
            outs[i].at[me, core, half(i, part)],
            sems,
            10 * i + index,
            place,
        )

    def relay(i, owner, part, index, place):
        block = outs[i].at[owner, core, half(i, part)]
        return send(block, block, sems, 10 * i + index, place)

    def hand(i, owner, index):
        block = outs[i].at[owner, core]
        return send(block, block, sems, 10 * i + index, to_core)

    begun = []
    for i in range(count):
        begun.append(
            [
                first(i, 0, 0, to_across),
                first(i, 1, 1, to_along),
                first(i, 1, 2, to_across),
                first(i, 0, 3, to_along),
                send(ins[i], outs[i].at[me, core], sems, 10 * i + 6, to_core),
            ]
        )
        for copy in begun[i]:
            copy.start()
    for i in range(count):
        begun[i][0].wait_recv()
        on_a = relay(i, across, 0, 4, to_along)
        on_a.start()
        begun[i][1].wait_recv()
        on_b = relay(i, along, 1, 5, to_across)
        on_b.start()
        begun[i] += [on_a, on_b]
    for i in range(count):
        begun[i][2].wait_recv()
        hands = [hand(i, across, 7)]
        hands[0].start()
        begun[i][3].wait_recv()
        hands.append(hand(i, along, 8))
        hands[1].start()
        begun[i][5].wait_recv()
        begun[i][6].wait_recv()
        hands.append(hand(i, far, 9))
        hands[2].start()
        begun[i] += hands
    for i in range(count):
        for copy in begun[i][4:5] + begun[i][7:]:
            copy.wait_recv()
        for copy in begun[i]:
            copy.wait_send()
        local[i].wait()


def collect(ident, pieces):
    hbm = pl.BlockSpec(memory_space=pl.ANY)
    count = len(pieces)
    return pl.pallas_call(
        functools.partial(collect_kernel, count),
        out_shape=[jax.ShapeDtypeStruct((4, 2) + p.shape, p.dtype) for p in pieces],
        in_specs=[hbm] * count,
        out_specs=[hbm] * count,
        scratch_shapes=[
            pltpu.SemaphoreType.DMA((count,)),
            pltpu.SemaphoreType.DMA((10 * count,)),
            pltpu.SemaphoreType.DMA((10 * count,)),
        ],
        compiler_params=pltpu.CompilerParams(
            collective_id=ident, has_side_effects=True, vmem_limit_bytes=4 * 1024 * 1024
        ),
        cost_estimate=pl.CostEstimate(
            flops=0, bytes_accessed=80 * sum(p.size for p in pieces), transcendentals=0
        ),
        name="collect",
    )(*pieces)


def spread_kernel(in_ref, out_ref):
    width = in_ref.shape[-1]
    for t in range(4):
        out_ref[:, pl.ds(t * width, width)] = in_ref[t, 0].astype(jnp.float32)


def spread(blocks, parts):
    _, cores, rows, width = blocks.shape
    width = width // parts
    cut = 1 if rows <= 256 else rows // 256
    return pl.pallas_call(
        spread_kernel,
        grid=(cores, cut, parts),
        out_shape=jax.ShapeDtypeStruct((cores * rows, parts * 4 * width), jnp.float32),
        in_specs=[pl.BlockSpec((4, 1, rows // cut, width), lambda c, k, q: (0, c, k, q))],
        out_specs=pl.BlockSpec((rows // cut, 4 * width), lambda c, k, q: (c * cut + k, q)),
        cost_estimate=pl.CostEstimate(
            flops=0, bytes_accessed=6 * blocks.size, transcendentals=0
        ),
        name="spread",
    )(blocks)


def total_kernel(x_ref, out_ref, land, s0, s1):
    sems = (s0, s1)
    me, across, along, far = neighbours()
    core, plane = lax.axis_index("core"), lax.axis_index("seq")
    peers = [across, along, far]
    others = [lax.rem(plane + k, 4) for k in (1, 2, 3)]
    greet(
        [{"tp": p} for p in peers] + [{"core": 1 - core}] + [{"seq": p} for p in others]
    )
    quarter = x_ref.shape[1] // 4

    def columns(t):
        return pl.ds(pl.multiple_of(t * quarter, quarter), quarter)

    first = [
        send(x_ref.at[:, columns(p)], land.at[k], sems, k, {"tp": p}) for k, p in enumerate(peers)
    ]
    for copy in first:
        copy.start()
    for copy in first:
        copy.wait_recv()
    out_ref[plane, core, :, columns(me)] = (x_ref[:, columns(me)] + land[0]) + (land[1] + land[2])
    here = out_ref.at[plane, core, :, columns(me)]
    swap = send(here, here, sems, 3, {"core": 1 - core})
    swap.start()
    swap.wait_recv()
    here = out_ref.at[plane, :, :, columns(me)]
    second = [send(here, here, sems, 4 + k, {"seq": p}) for k, p in enumerate(others)]
    for copy in second:
        copy.start()
    for copy in second:
        copy.wait_recv()
    here = out_ref.at[:, :, :, columns(me)]
    third = [send(here, here, sems, 7 + k, {"tp": p}) for k, p in enumerate(peers)]
    for copy in third:
        copy.start()
    for copy in third:
        copy.wait_recv()
    for copy in first + [swap] + second + third:
        copy.wait_send()


def total(ident, x):
    vmem = pl.BlockSpec(memory_space=pltpu.VMEM)
    rows, width = x.shape
    return pl.pallas_call(
        total_kernel,
        out_shape=jax.ShapeDtypeStruct((4, 2, rows, width), jnp.float32),
        in_specs=[vmem],
        out_specs=vmem,
        scratch_shapes=[
            pltpu.VMEM((3, rows, width // 4), jnp.float32),
            pltpu.SemaphoreType.DMA((10,)),
            pltpu.SemaphoreType.DMA((10,)),
        ],
        compiler_params=pltpu.CompilerParams(
            collective_id=ident, has_side_effects=True, vmem_limit_bytes=16 * 1024 * 1024
        ),
        cost_estimate=pl.CostEstimate(flops=0, bytes_accessed=60_000_000, transcendentals=0),
        name="total",
    )(x)


def row_stats(values):
    inverse = lax.rsqrt(jnp.mean(values * values, axis=-1, keepdims=True) + eps)
    return (values * inverse, inverse)


def norm_back(grad_normed, normed, inverse):
    inner_mean = jnp.mean(grad_normed * normed, axis=-1, keepdims=True)
    return inverse * (grad_normed - normed * inner_mean)


def head_stats(values):
    shaped = values.reshape(values.shape[0], -1, HDIM)
    normed, inverse = row_stats(shaped)
    return (normed.reshape(values.shape), inverse)


def head_back(grad_normed, normed, inverse):
    shaped_grad = grad_normed.reshape(grad_normed.shape[0], -1, HDIM)
    shaped_norm = normed.reshape(normed.shape[0], -1, HDIM)
    return norm_back(shaped_grad, shaped_norm, inverse).reshape(grad_normed.shape)


def rotary(values, row_pos, col_pos, direction):
    quarter = HDIM // 4
    freqs = 10000.0 ** (-jnp.arange(quarter, dtype=jnp.float32) / quarter)
    angles = jnp.concatenate([row_pos[:, None] * freqs, col_pos[:, None] * freqs], axis=1)
    cosine = jnp.cos(angles)[:, None, :]
    sine = direction * jnp.sin(angles)[:, None, :]
    shaped = values.reshape(values.shape[0], -1, HDIM)
    first_half = shaped[..., : HDIM // 2]
    second_half = shaped[..., HDIM // 2 :]
    turned = jnp.concatenate(
        [first_half * cosine - second_half * sine, second_half * cosine + first_half * sine],
        axis=-1,
    )
    return turned.reshape(values.shape)


def layout(doc_lengths, bucket, positions):
    doc_ends = jnp.cumsum(doc_lengths)
    starts = doc_ends - doc_lengths
    segment = jnp.sum((positions[:, None] >= doc_ends[None, :]).astype(jnp.int32), axis=1)
    matches = segment[:, None] == jnp.arange(DOCS, dtype=jnp.int32)[None, :]
    offset = jnp.sum(jnp.where(matches, starts[None, :], 0), axis=1)
    within = positions - offset
    stride = 32 * (bucket + 1)
    return (segment, (within // stride).astype(jnp.float32), (within % stride).astype(jnp.float32))


def by_head(values):
    return values.reshape(values.shape[0], -1, 1, HDIM).transpose(1, 0, 2, 3)


def from_heads(blocks):
    return blocks.transpose(1, 0, 2, 3).reshape(blocks.shape[1], -1)


def attend_forward(query, keys, values, allowed):
    scale = HDIM ** (-0.5)

    def block(block_args):
        part_q, part_k, part_v = block_args
        scores = (
            jnp.einsum("qhd,khd->hqk", part_q, part_k, preferred_element_type=jnp.float32) * scale
        )
        scores = jnp.where(allowed[None], scores, -1e30)
        row_peak = jnp.max(scores, axis=-1, keepdims=True)
        exp_scores = jnp.exp(scores - row_peak)
        exp_total = jnp.sum(exp_scores, axis=-1, keepdims=True)
        attn_probs = (exp_scores / exp_total).astype(jnp.bfloat16)
        attn_block = jnp.einsum(
            "hqk,khd->qhd", attn_probs, part_v, preferred_element_type=jnp.float32
        )
        return (attn_block, row_peak[..., 0] + jnp.log(exp_total[..., 0]))

    blocks, log_total = lax.map(block, (by_head(query), by_head(keys), by_head(values)))
    return (from_heads(blocks), log_total)


def attend_backward(query, keys, values, allowed, log_total, grad_out):
    scale = HDIM ** (-0.5)

    def block(block_args):
        part_q, part_k, part_v, part_log, part_grad = block_args
        scores = (
            jnp.einsum("qhd,khd->hqk", part_q, part_k, preferred_element_type=jnp.float32) * scale
        )
        scores = jnp.where(allowed[None], scores, -1e30)
        attn_probs = jnp.exp(scores - part_log[..., None])
        grad_probs = jnp.einsum(
            "qhd,khd->hqk", part_grad, part_v, preferred_element_type=jnp.float32
        )
        row_delta = jnp.sum(attn_probs * grad_probs, axis=-1, keepdims=True)
        grad_scores = (attn_probs * (grad_probs - row_delta)).astype(jnp.bfloat16)
        grad_query = (
            jnp.einsum("hqk,khd->qhd", grad_scores, part_k, preferred_element_type=jnp.float32)
            * scale
        )
        grad_keys = (
            jnp.einsum("hqk,qhd->khd", grad_scores, part_q, preferred_element_type=jnp.float32)
            * scale
        )
        grad_values = jnp.einsum(
            "hqk,qhd->khd",
            attn_probs.astype(jnp.bfloat16),
            part_grad,
            preferred_element_type=jnp.float32,
        )
        return (grad_query, grad_keys, grad_values)

    grad_query, grad_keys, grad_values = lax.map(
        block,
        (by_head(query), by_head(keys), by_head(values), log_total, by_head(grad_out)),
    )
    return (from_heads(grad_query), from_heads(grad_keys), from_heads(grad_values))


def matmul(left, right):
    return jnp.dot(left, right, preferred_element_type=jnp.float32)


def contract_right(left, weight):
    return lax.dot_general(
        left, weight, (((1,), (1,)), ((), ())), preferred_element_type=jnp.float32
    )


def contract_rows(left, right):
    return lax.dot_general(
        left, right, (((0,), (0,)), ((), ())), preferred_element_type=jnp.float32
    )


def pick(values, index, axis):
    return lax.dynamic_index_in_dim(values, index, axis, keepdims=False)


def to_plane(values):
    ways = lax.axis_size("tp")
    parts = values.reshape((ways, values.shape[0] // ways) + values.shape[1:])
    parts = lax.all_to_all(parts, "tp", 0, 0, tiled=True)
    parts = lax.all_to_all(parts, "seq", 0, 0, tiled=True)
    return parts.reshape(values.shape)


def from_plane(values):
    ways = lax.axis_size("tp")
    parts = values.reshape((ways, values.shape[0] // ways) + values.shape[1:])
    parts = lax.all_to_all(parts, "seq", 0, 0, tiled=True)
    parts = lax.all_to_all(parts, "tp", 0, 0, tiled=True)
    return parts.reshape(values.shape)


def fast():
    return lax.axis_size("tp") == 4 and lax.axis_size("core") == 2 and lax.axis_size("seq") == 4


def gather_planes(part):
    return lax.all_gather(part, "seq", axis=0, tiled=False)


def join_cores(halves):
    whole = lax.all_gather(halves, "core", axis=1, tiled=False)
    return whole.reshape(-1, halves.shape[-1])


def scatter_rows(term):
    cores, planes = lax.axis_size("core"), lax.axis_size("seq")
    shaped = term.astype(jnp.bfloat16).reshape(planes, cores, -1, term.shape[-1])
    return lax.psum_scatter(swap_halves(shaped), "seq", scatter_dimension=0, tiled=False)


def swap_halves(shaped):
    cores, me_c = lax.axis_size("core"), lax.axis_index("core")
    mine = pick(shaped, me_c, 1)
    for step in range(1, cores):
        ring = [(c, (c + step) % cores) for c in range(cores)]
        other = lax.ppermute(pick(shaped, (me_c + step) % cores, 1), "core", ring)
        mine = (mine.astype(jnp.float32) + other.astype(jnp.float32)).astype(jnp.bfloat16)
    return mine


def plane_gather(values):
    return lax.all_gather(values, "tp", axis=0, tiled=True)


def plane_multiply(ident, x, weight, turned=False, halved=False):
    if fast():
        got = gather_matmul(ident, x, weight, turned, halved)
        return got[0], got[1] if halved else weight, got[-1]
    whole = join_cores(weight) if halved else weight
    x = plane_gather(x)
    return x, whole, contract_right(x, whole) if turned else matmul(x, whole)


def multiply_plane(ident, x, weight, turned=False):
    if fast():
        return matmul_scatter(ident, x, weight, turned)
    term = contract_right(x, weight) if turned else matmul(x, weight)
    return lax.psum_scatter(
        term.astype(jnp.bfloat16), "tp", scatter_dimension=0, tiled=True
    ).astype(jnp.float32)


def collect_plane(ident, pieces):
    if fast():
        return collect(ident, pieces)
    return [
        lax.all_gather(p, ("tp", "core"), axis=0, tiled=False).reshape(
            (lax.axis_size("tp"), lax.axis_size("core")) + p.shape
        )
        for p in pieces
    ]


def spread_parts(blocks, parts):
    if fast():
        return spread(blocks, parts)
    tp, cores, rows, width = blocks.shape
    return (
        blocks.astype(jnp.float32)
        .reshape(tp, cores, rows, parts, width // parts)
        .transpose(1, 2, 3, 0, 4)
        .reshape(cores * rows, tp * width)
    )


def total_plane(ident, x):
    if fast():
        return total(ident, x)
    return lax.all_gather(lax.psum(x, "tp"), ("seq", "core"), axis=0, tiled=False).reshape(
        (lax.axis_size("seq"), lax.axis_size("core")) + x.shape
    )


def shards(
    tokens,
    cotangent,
    step_embed,
    caption,
    lengths,
    group_bucket,
    null_mask,
    w_qkv,
    w_out,
    w_capkv,
    w_gateup,
    w_down,
    w_mod,
    b_mod,
    gain_attn,
    gain_ffn,
    gain_query,
    gain_key,
    gain_capkey,
    gate_head,
    null_embed,
):
    tp, cores, planes = lax.axis_size("tp"), lax.axis_size("core"), lax.axis_size("seq")
    me_t, me_c, me_z = lax.axis_index("tp"), lax.axis_index("core"), lax.axis_index("seq")
    groups = tp * cores
    rows, width = tokens.shape
    piece = rows // tp
    local_heads = HEADS // tp
    local = local_heads * HDIM
    cap_dev = caption.shape[2]
    ctx = caption.shape[3]
    my_group = me_z * cores + me_c

    numbers = jnp.concatenate([lengths[0], group_bucket, null_mask[0]])
    numbers = lax.all_gather(numbers, ("tp", "core"), axis=0, tiled=False).reshape(groups, -1)
    counts = jnp.sum(numbers[:, :DOCS], axis=1).astype(jnp.float32)
    mine = pick(numbers, my_group, 0)
    doc_lengths, bucket, nulls = mine[:DOCS], mine[DOCS], mine[DOCS + 1 :]
    bucket_count = jnp.sum(jnp.where(numbers[:, DOCS] == bucket, counts, 0.0))
    scale_loss = jnp.sum(counts) / (RES * bucket_count)

    steps = lax.all_gather(step_embed[0], ("tp", "core"), axis=0, tiled=True)
    condition = jax.nn.silu(steps.astype(jnp.float32)).astype(jnp.bfloat16)
    mod_rows = w_mod.shape[0]
    cond_mine = lax.dynamic_slice_in_dim(condition, me_z * mod_rows, mod_rows, 1)
    mod_all = matmul(cond_mine, w_mod).reshape(planes, cores * DOCS, -1)
    mod_plane = lax.psum_scatter(mod_all, "seq", scatter_dimension=0, tiled=False)
    mod_doc = pick(mod_plane.reshape(cores, DOCS, -1), me_c, 0) + b_mod

    def columns_of(weight, parts):
        share = weight.shape[0] // cores
        size = weight.shape[1] // (parts * tp)
        return jnp.concatenate(
            [
                lax.dynamic_slice(weight, (me_c * share, (q * tp + me_t) * size), (share, size))
                for q in range(parts)
            ],
            axis=1,
        )

    half_qkv = gather_planes(columns_of(w_qkv, 3))
    half_capkv = gather_planes(columns_of(w_capkv, 2))
    out_part = gather_planes(columns_of(w_out, 1))
    out_part = lax.all_to_all(out_part, "tp", 0, 0, tiled=True)
    out_part = out_part.transpose(1, 0, 2).reshape(local // cores, width)
    full_out = lax.all_gather(out_part, "core", axis=0, tiled=True)
    half_gateup = gather_planes(columns_of(w_gateup, 2 * planes))
    share = w_down.shape[0] // groups
    half_down = gather_planes(
        lax.dynamic_slice_in_dim(w_down, (me_t * cores + me_c) * share, share, 0)
    )
    full_down = join_cores(half_down)

    inputs = to_plane(tokens).astype(jnp.float32)
    row = jnp.arange(rows, dtype=jnp.int32)
    spread = (row // piece) * rows + row % piece
    positions = spread + me_t * piece
    all_positions = (jnp.arange(tp, dtype=jnp.int32)[:, None] * piece + spread[None, :]).reshape(-1)
    segment, _, _ = layout(doc_lengths, bucket, positions)
    all_segment, row_pos, col_pos = layout(doc_lengths, bucket, all_positions)
    all_document = jnp.minimum(all_segment, DOCS - 1)
    document = jnp.minimum(segment, DOCS - 1)
    doc_pick = (document[:, None] == jnp.arange(DOCS, dtype=jnp.int32)[None, :]).astype(jnp.float32)
    is_valid = (segment < DOCS).astype(jnp.float32)
    modulation = jnp.dot(doc_pick, mod_doc, precision=lax.Precision.HIGHEST)
    scale_a, gate_a, scale_f, gate_f = jnp.split(modulation, 4, axis=1)
    tanh_a, tanh_f = jnp.tanh(gate_a), jnp.tanh(gate_f)

    normed1, inverse1 = row_stats(inputs)
    hidden1 = (normed1 * gain_attn * (1.0 + scale_a)).astype(jnp.bfloat16)
    hidden1, full_qkv, projected = plane_multiply(1, hidden1, half_qkv, halved=True)
    query_raw, key_raw, value_raw = jnp.split(projected, 3, axis=1)
    query_norm, query_inv = head_stats(query_raw)
    key_norm, key_inv = head_stats(key_raw)
    my_gain_query = pick(gain_query.reshape(tp, local), me_t, 0)
    my_gain_key = pick(gain_key.reshape(tp, local), me_t, 0)
    my_gain_capkey = pick(gain_capkey.reshape(tp, local), me_t, 0)
    query = rotary(query_norm * my_gain_query, row_pos, col_pos, 1.0).astype(jnp.bfloat16)
    keys = rotary(key_norm * my_gain_key, row_pos, col_pos, 1.0).astype(jnp.bfloat16)
    values = value_raw.astype(jnp.bfloat16)

    captions = to_plane(caption[0].transpose(1, 0, 2)).transpose(1, 0, 2)
    capmix = jnp.where(nulls[:, None, None] > 0, null_embed[None, None, :], captions)
    cap_flat = capmix.reshape(DOCS * cap_dev, ctx)
    cap_flat, full_capkv, cap_proj = plane_multiply(2, cap_flat, half_capkv, halved=True)
    cap_document = jnp.tile(jnp.repeat(jnp.arange(DOCS, dtype=jnp.int32), cap_dev), tp)
    capkey_raw, capval_raw = jnp.split(cap_proj, 2, axis=1)
    capkey_norm, capkey_inv = head_stats(capkey_raw)
    capkeys = (capkey_norm * my_gain_capkey).astype(jnp.bfloat16)
    capvals = capval_raw.astype(jnp.bfloat16)

    self_allowed = all_segment[:, None] == all_segment[None, :]
    cross_allowed = all_document[:, None] == cap_document[None, :]
    own_out, own_log = attend_forward(query, keys, values, self_allowed)
    cross_out, cross_log = attend_forward(query, capkeys, capvals, cross_allowed)
    gate_tanh = pick(jnp.tanh(gate_head).reshape(tp, local_heads), me_t, 0)
    head_gate = jnp.repeat(gate_tanh, HDIM)[None, :]
    mixed_attn = (own_out + head_gate * cross_out).astype(jnp.bfloat16)
    attn_out = multiply_plane(3, mixed_attn, full_out)
    residual = inputs + tanh_a * attn_out
    normed2, inverse2 = row_stats(residual)
    hidden2 = (normed2 * gain_ffn * (1.0 + scale_f)).astype(jnp.bfloat16)
    hidden2, full_gateup, gate_up = plane_multiply(4, hidden2, half_gateup, halved=True)
    gate_part, up_part = jnp.split(gate_up, 2, axis=1)
    sig_gate = jax.nn.sigmoid(gate_part)
    silu_gate = gate_part * sig_gate
    hidden_ffn = (silu_gate * up_part).astype(jnp.bfloat16)
    down_out = multiply_plane(5, hidden_ffn, full_down)
    result = from_plane((residual + tanh_f * down_out).astype(jnp.bfloat16))

    grad_res0 = to_plane(cotangent).astype(jnp.float32) * (is_valid * scale_loss)[:, None]
    grad_down = (tanh_f * grad_res0).astype(jnp.bfloat16)
    grad_down, _, grad_ffn = plane_multiply(6, grad_down, full_down, turned=True)
    grad_gate_f = grad_res0 * down_out * (1.0 - tanh_f * tanh_f)
    grad_gate_part = grad_ffn * up_part * sig_gate * (1.0 + gate_part * (1.0 - sig_gate))
    grad_up_part = grad_ffn * silu_gate
    grad_gateup = jnp.concatenate([grad_gate_part, grad_up_part], axis=1).astype(jnp.bfloat16)
    grad_hidden2 = multiply_plane(7, grad_gateup, full_gateup, turned=True)
    gain_ffn_term = jnp.sum(grad_hidden2 * normed2 * (1.0 + scale_f), axis=0)
    grad_scale_f = grad_hidden2 * normed2 * gain_ffn
    grad_residual = grad_res0 + norm_back(
        grad_hidden2 * gain_ffn * (1.0 + scale_f), normed2, inverse2
    )
    grad_attn = (tanh_a * grad_residual).astype(jnp.bfloat16)
    grad_attn, _, grad_mix = plane_multiply(8, grad_attn, full_out, turned=True)
    grad_gate_a = grad_residual * attn_out * (1.0 - tanh_a * tanh_a)
    grad_own = grad_mix.astype(jnp.bfloat16)
    grad_cross = (head_gate * grad_mix).astype(jnp.bfloat16)
    gate_head_term = jnp.sum(
        (grad_mix * cross_out).reshape(-1, local_heads, HDIM), axis=(0, 2)
    ) * (1.0 - gate_tanh * gate_tanh)
    query_own, grad_keys, grad_values = attend_backward(
        query, keys, values, self_allowed, own_log, grad_own
    )
    query_cross, grad_capkeys, grad_capvals = attend_backward(
        query, capkeys, capvals, cross_allowed, cross_log, grad_cross
    )
    grad_query = rotary(query_own + query_cross, row_pos, col_pos, -1.0)
    gain_query_term = jnp.sum(grad_query * query_norm, axis=0)
    grad_query_raw = head_back(grad_query * my_gain_query, query_norm, query_inv)
    grad_key = rotary(grad_keys, row_pos, col_pos, -1.0)
    gain_key_term = jnp.sum(grad_key * key_norm, axis=0)
    grad_key_raw = head_back(grad_key * my_gain_key, key_norm, key_inv)
    grad_projected = jnp.concatenate([grad_query_raw, grad_key_raw, grad_values], axis=1).astype(
        jnp.bfloat16
    )
    grad_hidden1 = multiply_plane(9, grad_projected, full_qkv, turned=True)
    gain_attn_term = jnp.sum(grad_hidden1 * normed1 * (1.0 + scale_a), axis=0)
    grad_scale_a = grad_hidden1 * normed1 * gain_attn
    input_grad = from_plane(
        (
            grad_residual + norm_back(grad_hidden1 * gain_attn * (1.0 + scale_a), normed1, inverse1)
        ).astype(jnp.bfloat16)
    )

    grad_mod_tok = jnp.concatenate([grad_scale_a, grad_gate_a, grad_scale_f, grad_gate_f], axis=1)
    grad_mod_doc = lax.dot_general(
        doc_pick,
        grad_mod_tok,
        (((0,), (0,)), ((), ())),
        precision=lax.Precision.HIGHEST,
        preferred_element_type=jnp.float32,
    )
    gain_capkey_term = jnp.sum(grad_capkeys * capkey_norm, axis=0)
    grad_capkey_raw = head_back(grad_capkeys * my_gain_capkey, capkey_norm, capkey_inv)
    grad_cap_proj = jnp.concatenate([grad_capkey_raw, grad_capvals], axis=1).astype(jnp.bfloat16)
    null_rows = nulls[cap_document] > 0
    null_sum = jnp.sum(
        jnp.where(null_rows[:, None], grad_cap_proj.astype(jnp.float32), 0.0), axis=0
    )
    null_term = jnp.dot(
        full_capkv.astype(jnp.float32), null_sum, precision=lax.Precision.HIGHEST
    )

    term_down = scatter_rows(contract_rows(hidden_ffn, grad_down))
    term_gateup = scatter_rows(contract_rows(hidden2, grad_gateup))
    term_out = contract_rows(mixed_attn, grad_attn).astype(jnp.bfloat16)
    term_out = swap_halves(term_out.reshape(1, cores, -1, width))[0]
    term_out = term_out.reshape(term_out.shape[0], tp, -1).transpose(1, 0, 2)
    term_out = lax.all_to_all(term_out, "tp", 0, 0, tiled=True)
    term_out = lax.psum_scatter(term_out, "seq", scatter_dimension=0, tiled=False)
    term_capkv = scatter_rows(contract_rows(cap_flat, grad_cap_proj))
    term_qkv = scatter_rows(contract_rows(hidden1, grad_projected))
    all_down, all_gateup, all_out = collect_plane(10, [term_down, term_gateup, term_out])
    all_capkv, all_qkv = collect_plane(11, [term_capkv, term_qkv])
    sum_down = all_down.reshape(w_down.shape).astype(jnp.float32)
    sum_gateup = spread_parts(all_gateup, 2 * planes)
    sum_out = spread_parts(all_out, 1)
    sum_capkv = spread_parts(all_capkv, 2)
    sum_qkv = spread_parts(all_qkv, 3)

    def at_mine(part):
        whole = jnp.zeros((tp,) + part.shape, jnp.float32)
        return lax.dynamic_update_index_in_dim(whole, part, me_t, 0).reshape(-1)

    small = jnp.concatenate(
        [
            gain_attn_term,
            gain_ffn_term,
            at_mine(gain_query_term),
            at_mine(gain_key_term),
            at_mine(gain_capkey_term),
            at_mine(gate_head_term),
            null_term,
        ]
    )
    small_rows = 8 - DOCS
    small_size = small.shape[0]
    small = jnp.pad(small, (0, small_rows * 4 * width - small_size))
    totals = total_plane(
        12, jnp.concatenate([grad_mod_doc, small.reshape(small_rows, 4 * width)], axis=0)
    ).reshape(groups, 8, 4 * width)
    grad_mod_docs = totals[:, :DOCS].reshape(groups * DOCS, 4 * width)
    sum_mod = lax.dot_general(
        cond_mine.astype(jnp.float32),
        grad_mod_docs,
        (((0,), (0,)), ((), ())),
        precision=lax.Precision.HIGHEST,
        preferred_element_type=jnp.float32,
    )
    sum_bias = jnp.sum(grad_mod_docs, axis=0)
    small = jnp.sum(totals[:, DOCS:], axis=0).reshape(-1)[:small_size]
    ends = [width, 2 * width, 3 * width, 4 * width, 5 * width, 5 * width + HEADS]
    small_parts = jnp.split(small, ends)
    return (
        result,
        input_grad,
        sum_qkv,
        sum_out,
        sum_capkv,
        sum_gateup,
        sum_down,
        sum_mod,
        sum_bias,
        *small_parts,
    )


def solution(mesh):
    planes = mesh.shape["seq"]
    cores = mesh.shape["bucket"] // planes
    split = Mesh(mesh.devices.reshape(planes, cores, planes), ("tp", "core", "seq"))
    group = ("tp", "core")
    token = P(("tp", "core", "seq"), None)
    weight = P("seq", None)
    placed = (
        token,
        token,
        P(group, None, None),
        P(group, None, "seq", None),
        P(group, None),
        P(group),
        P(group, None),
        *([weight] * 6),
        *([P()] * 8),
    )
    return jax.shard_map(
        shards,
        mesh=split,
        in_specs=placed,
        out_specs=(token, token, *([weight] * 6), *([P()] * 8)),
        check_vma=False,
    )
```

```python
import functools

import jax
import jax.numpy as jnp
from jax import lax
from jax.experimental import pallas as pl
from jax.experimental.pallas import tpu as pltpu
from jax.sharding import Mesh, PartitionSpec as P

HEADS = 24
HDIM = 64
DOCS = 4
RES = 4


eps = 1e-06

MESH = pl.DeviceIdType.MESH
VMEM_BYTES = 60 * 1024 * 1024


def neighbours():
    me = lax.axis_index("tp")
    return me, me + 1 - 2 * lax.rem(me, 2), lax.rem(me + 2, 4), 3 - me


def greet(places):
    barrier = pltpu.get_barrier_semaphore()
    for place in places:
        pl.semaphore_signal(barrier, inc=1, device_id=place, device_id_type=MESH)
    pl.semaphore_wait(barrier, len(places))


def send(source, target, sems, index, place):
    return pltpu.make_async_remote_copy(
        src_ref=source,
        dst_ref=target,
        send_sem=sems[0].at[index],
        recv_sem=sems[1].at[index],
        device_id=place,
        device_id_type=MESH,
    )


def tile_of(width):
    for tile in (512, 384, 256, 128):
        if width % tile == 0:
            return tile
    return width


def multiply(left, weight_ref, columns, turned):
    if turned:
        return lax.dot_general(
            left, weight_ref[columns, 0 : left.shape[1]], (((1,), (1,)), ((), ())),
            preferred_element_type=jnp.float32,
        )
    return jnp.dot(left, weight_ref[:, columns], preferred_element_type=jnp.float32)


class Aside:
    def __init__(self, operands, outs, scratch, steps):
        self.operands, self.outs, self.scratch, self.steps = operands, outs, scratch, steps

    def in_specs(self):
        return [pl.BlockSpec(memory_space=pl.ANY)] * len(self.operands)

    def out_specs(self):
        return [pl.BlockSpec(memory_space=pltpu.VMEM)] * len(self.outs)

    def scratch_shapes(self):
        return [
            *[pltpu.VMEM(x.shape, x.dtype) for x in self.operands],
            pltpu.SemaphoreType.DMA((len(self.operands),)),
            *self.scratch,
        ]

    def split(self, refs, ins, outs, scratch):
        count, given = len(self.operands), len(self.outs)
        own, refs = list(refs[:ins]), refs[ins:]
        sources, refs = refs[:count], refs[count:]
        own, refs = own + list(refs[:outs]), refs[outs:]
        self.out_refs, refs = refs[:given], refs[given:]
        own, refs = own + list(refs[:scratch]), refs[scratch:]
        self.in_refs, (sem, *self.scratch_refs) = refs[:count], refs[count:]
        self.loads = [
            pltpu.make_async_copy(source, target, sem.at[i])
            for i, (source, target) in enumerate(zip(sources, self.in_refs))
        ]
        return own

    def load(self):
        for copy in self.loads:
            copy.start()

    def step(self, index):
        if index == 0:
            for copy in self.loads:
                copy.wait()
        self.steps(index, self.in_refs, self.out_refs, self.scratch_refs)


class Nothing:
    def __init__(self):
        self.operands, self.outs = [], []

    def in_specs(self):
        return []

    out_specs = scratch_shapes = in_specs

    def split(self, refs, ins, outs, scratch):
        return list(refs)

    def load(self):
        pass

    def step(self, index):
        pass


def gather_kernel(turned, halved, early, aside, *refs):
    refs = aside.split(refs, 2, 3 if halved else 2, 7)
    x_ref, w_ref, all_ref = refs[:3]
    refs = refs[3:]
    if halved:
        full_ref, refs = refs[0], refs[1:]
    y_ref, xbuf, wbuf, ybuf, load, done = refs[:6]
    sems = refs[6:8]
    me, across, along, far = neighbours()
    rows = x_ref.shape[0]
    half = rows // 2
    core = lax.axis_index("core")
    places = [{"tp": across}, {"tp": along}]
    if halved:
        places.append({"core": 1 - core})
    mine = pltpu.make_async_copy(x_ref, xbuf.at[me], load.at[0])
    mine.start()
    if halved:
        planes, part, _ = w_ref.shape
        places_of = [
            pl.ds(pl.multiple_of((z * 2 + core) * part, part), part) for z in range(planes)
        ]
        weights = [
            pltpu.make_async_copy(w_ref.at[z], wbuf.at[places_of[z]], load.at[1 + z])
            for z in range(planes)
        ]
    else:
        weights = [pltpu.make_async_copy(w_ref, wbuf, load.at[1])]
    for copy in weights:
        copy.start()
    greet(places)

    def block(owner, part):
        return xbuf.at[owner, pl.ds(part * half, half)]

    def pass_on(index, owner, part, place):
        return send(block(owner, part), block(owner, part), sems, index, place)

    first = [
        send(x_ref.at[pl.ds(0, half)], block(me, 0), sems, 0, {"tp": across}),
        send(x_ref.at[pl.ds(half, half)], block(me, 1), sems, 1, {"tp": along}),
        send(x_ref.at[pl.ds(half, half)], block(me, 1), sems, 2, {"tp": across}),
        send(x_ref.at[pl.ds(0, half)], block(me, 0), sems, 3, {"tp": along}),
    ]
    for copy in first:
        copy.start()
    swaps = []
    if halved:
        for z in range(planes):
            swaps.append(send(w_ref.at[z], wbuf.at[places_of[z]], sems, 6 + z, {"core": 1 - core}))
        for copy in swaps:
            copy.start()
    aside.load()
    mine.wait()
    for copy in weights:
        copy.wait()
    for step in range(early):
        aside.step(step)
    first[0].wait_recv()
    on_a = pass_on(4, across, 0, {"tp": along})
    on_a.start()
    first[1].wait_recv()
    on_b = pass_on(5, along, 1, {"tp": across})
    on_b.start()
    for copy in swaps:
        copy.wait()
    for step in range(early, 3):
        aside.step(step)

    tile = tile_of(ybuf.shape[-1])
    outs = []
    if halved:
        outs.append(pltpu.make_async_copy(wbuf, full_ref, done.at[4]))
        outs[-1].start()

    def compute(owner, index):
        @pl.loop(0, ybuf.shape[-1] // tile)
        def _(step):
            columns = pl.ds(pl.multiple_of(step * tile, tile), tile)
            ybuf[index, :, columns] = multiply(xbuf[owner], wbuf, columns, turned).astype(
                ybuf.dtype
            )

        copy = pltpu.make_async_copy(ybuf.at[index], y_ref.at[owner], done.at[index])
        copy.start()
        outs.append(copy)

    compute(me, 0)
    first[2].wait_recv()
    compute(across, 1)
    first[3].wait_recv()
    compute(along, 2)
    on_a.wait_recv()
    on_b.wait_recv()
    copy = pltpu.make_async_copy(xbuf, all_ref, load.at[0])
    copy.start()
    outs.append(copy)
    compute(far, 3)
    for copy in first + [on_a, on_b]:
        copy.wait_send()
    for copy in outs:
        copy.wait()


def gather_matmul(
    ident, x, w, turned=False, halved=False, width=None, aside=None, early=3, out=jnp.float32
):
    rows, depth = x.shape
    if halved:
        planes, part, columns = w.shape
        whole = (planes * 2 * part, columns)
    else:
        whole = w.shape
    width = width or (whole[0] if turned else whole[1])
    aside = aside or Nothing()
    shapes = [jax.ShapeDtypeStruct((4, rows, depth), x.dtype)]
    if halved:
        shapes.append(jax.ShapeDtypeStruct(whole, w.dtype))
    shapes.append(jax.ShapeDtypeStruct((4, rows, width), out))
    hbm = pl.BlockSpec(memory_space=pl.ANY)
    got = pl.pallas_call(
        functools.partial(gather_kernel, turned, halved, early, aside),
        out_shape=shapes + aside.outs,
        in_specs=[hbm, hbm] + aside.in_specs(),
        out_specs=[hbm] * len(shapes) + aside.out_specs(),
        scratch_shapes=[
            pltpu.VMEM((4, rows, depth), x.dtype),
            pltpu.VMEM(whole, w.dtype),
            pltpu.VMEM((4, rows, width), out),
            pltpu.SemaphoreType.DMA((6,)),
            pltpu.SemaphoreType.DMA((5,)),
            pltpu.SemaphoreType.DMA((10,)),
            pltpu.SemaphoreType.DMA((10,)),
            *aside.scratch_shapes(),
        ],
        compiler_params=pltpu.CompilerParams(
            collective_id=ident, has_side_effects=True, vmem_limit_bytes=VMEM_BYTES
        ),
        cost_estimate=pl.CostEstimate(
            flops=8 * rows * depth * width,
            bytes_accessed=30 * 3_000_000,
            transcendentals=0,
        ),
        name="gather_matmul",
    )(x, w, *aside.operands)
    last = len(shapes) - 1
    return [
        got[0].reshape(4 * rows, depth),
        got[1] if halved else w,
        got[last].reshape(4 * rows, width),
        *got[last + 1 :],
    ]


def scatter_kernel(turned, aside, *refs):
    refs = aside.split(refs, 2, 1, 7)
    x_ref, w_ref, out_ref, sums, far_out, near_out, relay, land, s0, s1 = refs
    me, across, along, far = neighbours()
    sems = (s0, s1)
    rows, width = out_ref.shape
    half = rows // 2
    top, low = pl.ds(0, half), pl.ds(half, half)
    tile = tile_of(width)
    to_across, to_along = {"tp": across}, {"tp": along}
    aside.load()
    greet([to_across, to_along])

    def tiles(body):
        @pl.loop(0, width // tile)
        def _(step):
            body(pl.ds(pl.multiple_of(step * tile, tile), tile))

    def product(owner, columns):
        return multiply(x_ref[owner], w_ref, columns, turned)

    @tiles
    def _(columns):
        far_out[:, columns] = product(far, columns).astype(far_out.dtype)

    far_a = send(far_out.at[top], relay.at[0], sems, 0, to_across)
    far_b = send(far_out.at[low], relay.at[1], sems, 1, to_along)
    far_a.start()
    far_b.start()

    @tiles
    def _(columns):
        part = product(across, columns)
        near_out[0, top, columns] = part[:half].astype(near_out.dtype)
        sums[0, :, columns] = part[half:]

    across_a = send(near_out.at[0, top], land.at[0, top], sems, 2, to_across)
    across_a.start()

    @tiles
    def _(columns):
        part = product(along, columns)
        near_out[1, low, columns] = part[half:].astype(near_out.dtype)
        sums[1, :, columns] = part[:half]

    along_b = send(near_out.at[1, low], land.at[1, low], sems, 3, to_along)
    along_b.start()
    aside.step(0)
    far_b.wait_recv()

    @tiles
    def _(columns):
        near_out[0, low, columns] = (
            sums[0, :, columns] + relay[1, :, columns].astype(jnp.float32)
        ).astype(near_out.dtype)

    across_b = send(near_out.at[0, low], land.at[0, low], sems, 4, to_across)
    across_b.start()
    far_a.wait_recv()

    @tiles
    def _(columns):
        near_out[1, top, columns] = (
            sums[1, :, columns] + relay[0, :, columns].astype(jnp.float32)
        ).astype(near_out.dtype)

    along_a = send(near_out.at[1, top], land.at[1, top], sems, 5, to_along)
    along_a.start()
    aside.step(1)
    aside.step(2)

    @tiles
    def _(columns):
        out_ref[:, columns] = product(me, columns)

    for copy in (across_a, along_b, across_b, along_a):
        copy.wait_recv()

    @tiles
    def _(columns):
        out_ref[:, columns] += land[0, :, columns].astype(jnp.float32) + land[
            1, :, columns
        ].astype(jnp.float32)

    for copy in (far_a, far_b, across_a, along_b, across_b, along_a):
        copy.wait_send()


def matmul_scatter(ident, x, w, turned=False, aside=None):
    aside = aside or Nothing()
    rows, depth = x.shape[0] // 4, x.shape[1]
    width = w.shape[0] if turned else w.shape[1]
    vmem = pl.BlockSpec(memory_space=pltpu.VMEM)
    return pl.pallas_call(
        functools.partial(scatter_kernel, turned, aside),
        out_shape=[jax.ShapeDtypeStruct((rows, width), jnp.float32)] + aside.outs,
        in_specs=[vmem, vmem] + aside.in_specs(),
        out_specs=[vmem] + aside.out_specs(),
        scratch_shapes=[
            pltpu.VMEM((2, rows // 2, width), jnp.float32),
            pltpu.VMEM((rows, width), jnp.bfloat16),
            pltpu.VMEM((2, rows, width), jnp.bfloat16),
            pltpu.VMEM((2, rows // 2, width), jnp.bfloat16),
            pltpu.VMEM((2, rows, width), jnp.bfloat16),
            pltpu.SemaphoreType.DMA((6,)),
            pltpu.SemaphoreType.DMA((6,)),
            *aside.scratch_shapes(),
        ],
        compiler_params=pltpu.CompilerParams(
            collective_id=ident, has_side_effects=True, vmem_limit_bytes=VMEM_BYTES
        ),
        cost_estimate=pl.CostEstimate(
            flops=8 * rows * depth * width,
            bytes_accessed=30 * 3_000_000,
            transcendentals=0,
        ),
        name="matmul_scatter",
    )(x.reshape(4, rows, depth), w, *aside.operands)


class Gathering:
    def __init__(self, ins, outs, load, sems):
        self.ins, self.outs, self.sems = ins, outs, sems
        self.me, self.across, self.along, self.far = neighbours()
        self.core = lax.axis_index("core")
        self.to_across, self.to_along = {"tp": self.across}, {"tp": self.along}
        self.to_core = {"core": 1 - self.core}
        self.local = [
            pltpu.make_async_copy(x, outs[i].at[self.me, self.core], load.at[i])
            for i, x in enumerate(ins)
        ]
        for copy in self.local:
            copy.start()

    def half(self, i, part):
        rows = self.ins[i].shape[0] // 2
        return pl.ds(part * rows, rows)

    def first(self, i, part, index, place):
        rows = self.half(i, part)
        target = self.outs[i].at[self.me, self.core, rows]
        return send(self.ins[i].at[rows], target, self.sems, 10 * i + index, place)

    def pass_on(self, i, owner, part, index, place):
        block = self.outs[i].at[owner, self.core, self.half(i, part)]
        return send(block, block, self.sems, 10 * i + index, place)

    def to_sibling(self, i, owner, index):
        block = self.outs[i].at[owner, self.core]
        return send(block, block, self.sems, 10 * i + index, self.to_core)

    def begin(self):
        self.begun = []
        for i, x in enumerate(self.ins):
            target = self.outs[i].at[self.me, self.core]
            copies = [
                self.first(i, 0, 0, self.to_across),
                self.first(i, 1, 1, self.to_along),
                self.first(i, 1, 2, self.to_across),
                self.first(i, 0, 3, self.to_along),
                send(x, target, self.sems, 10 * i + 6, self.to_core),
            ]
            for copy in copies:
                copy.start()
            self.begun.append(copies)

    def relay(self):
        for i, copies in enumerate(self.begun):
            copies[0].wait_recv()
            copies.append(self.pass_on(i, self.across, 0, 4, self.to_along))
            copies[5].start()
            copies[1].wait_recv()
            copies.append(self.pass_on(i, self.along, 1, 5, self.to_across))
            copies[6].start()

    def hand(self):
        for i, copies in enumerate(self.begun):
            copies[2].wait_recv()
            copies.append(self.to_sibling(i, self.across, 7))
            copies[7].start()
            copies[3].wait_recv()
            copies.append(self.to_sibling(i, self.along, 8))
            copies[8].start()
            copies[5].wait_recv()
            copies[6].wait_recv()
            copies.append(self.to_sibling(i, self.far, 9))
            copies[9].start()

    def end(self):
        for copies, local in zip(self.begun, self.local):
            for copy in copies[4:5] + copies[7:]:
                copy.wait_recv()
            for copy in copies:
                copy.wait_send()
            local.wait()


class Returning:
    def __init__(self, back, home, stage, load, sems, base):
        self.back, self.home, self.stage, self.load = back, home, stage, load
        self.sems, self.base = sems, base
        self.me, *self.peers = neighbours()
        self.plane, self.others = planes_after()
        self.stay = pltpu.make_async_copy(back.at[self.plane], stage.at[self.plane], load)
        self.keep = pltpu.make_async_copy(stage.at[self.me], home.at[self.me], load)

    def begin(self):
        self.stay.start()
        self.out = [
            send(
                self.back.at[p], self.stage.at[self.plane], self.sems, self.base + k, {"seq": p}
            )
            for k, p in enumerate(self.others)
        ]
        for copy in self.out:
            copy.start()

    def turn(self):
        for copy in self.out:
            copy.wait_recv()
        self.stay.wait()
        self.last = [
            send(
                self.stage.at[p], self.home.at[self.me], self.sems, self.base + 3 + k, {"tp": p}
            )
            for k, p in enumerate(self.peers)
        ]
        for copy in self.last:
            copy.start()
        self.keep.start()

    def end(self):
        for copy in self.last:
            copy.wait_recv()
        self.keep.wait()
        for copy in self.out + self.last:
            copy.wait_send()


def collect_kernel(count, aside, *refs):
    refs = aside.split(refs, count + 1, count + 1, 6)
    ins, outs = refs[:count], refs[count + 1 : 2 * count + 1]
    back, home = refs[count], refs[2 * count + 1]
    stage, load, s0, s1, r0, r1 = refs[2 * count + 2 :]
    gathering = Gathering(ins, outs, load, (s0, s1))
    returning = Returning(back, home, stage, load.at[count], (r0, r1), 0)
    greet_all()
    gathering.begin()
    returning.begin()
    aside.load()
    aside.step(0)
    gathering.relay()
    returning.turn()
    aside.step(1)
    gathering.hand()
    aside.step(2)
    returning.end()
    gathering.end()


def collect(ident, pieces, back, aside=None):
    aside = aside or Nothing()
    hbm = pl.BlockSpec(memory_space=pl.ANY)
    count = len(pieces)
    tall, wide = back.shape
    got = pl.pallas_call(
        functools.partial(collect_kernel, count, aside),
        out_shape=[
            *[jax.ShapeDtypeStruct((4, 2) + p.shape, p.dtype) for p in pieces],
            jax.ShapeDtypeStruct((4, tall // 4, wide), back.dtype),
            *aside.outs,
        ],
        in_specs=[hbm] * (count + 1) + aside.in_specs(),
        out_specs=[hbm] * (count + 1) + aside.out_specs(),
        scratch_shapes=[
            pltpu.VMEM((4, tall // 4, wide), back.dtype),
            pltpu.SemaphoreType.DMA((count + 1,)),
            pltpu.SemaphoreType.DMA((10 * count,)),
            pltpu.SemaphoreType.DMA((10 * count,)),
            pltpu.SemaphoreType.DMA((6,)),
            pltpu.SemaphoreType.DMA((6,)),
            *aside.scratch_shapes(),
        ],
        compiler_params=pltpu.CompilerParams(
            collective_id=ident, has_side_effects=True, vmem_limit_bytes=VMEM_BYTES
        ),
        cost_estimate=pl.CostEstimate(
            flops=0, bytes_accessed=80 * sum(p.size for p in pieces), transcendentals=0
        ),
        name="collect",
    )(*pieces, back.reshape(4, tall // 4, wide), *aside.operands)
    return got[:count], got[count].reshape(tall, wide), got[count + 1 :]


def spread_kernel(in_ref, out_ref):
    width = in_ref.shape[-1]
    for t in range(4):
        out_ref[:, pl.ds(t * width, width)] = in_ref[t, 0].astype(jnp.float32)


def spread(blocks, parts):
    _, cores, rows, width = blocks.shape
    width = width // parts
    cut = 1 if rows <= 256 else rows // 256
    return pl.pallas_call(
        spread_kernel,
        grid=(cores, cut, parts),
        out_shape=jax.ShapeDtypeStruct((cores * rows, parts * 4 * width), jnp.float32),
        in_specs=[pl.BlockSpec((4, 1, rows // cut, width), lambda c, k, q: (0, c, k, q))],
        out_specs=pl.BlockSpec((rows // cut, 4 * width), lambda c, k, q: (c * cut + k, q)),
        cost_estimate=pl.CostEstimate(
            flops=0, bytes_accessed=6 * blocks.size, transcendentals=0
        ),
        name="spread",
    )(blocks)


def planes_after():
    plane = lax.axis_index("seq")
    return plane, [lax.rem(plane + k, 4) for k in (1, 2, 3)]


def greet_all():
    _, across, along, far = neighbours()
    _, others = planes_after()
    greet(
        [{"tp": p} for p in (across, along, far)]
        + [{"core": 1 - lax.axis_index("core")}]
        + [{"seq": p} for p in others]
    )


def arrive_kernel(
    tok_ref, cap_ref, cot_ref, msg_ref, w_ref, in_ref, caps_ref, cots_ref, msgs_ref, mod_ref,
    stage, wbuf, part, land, load, s0, s1,
):
    sems = (s0, s1)
    me, across, along, far = neighbours()
    core = lax.axis_index("core")
    plane, others = planes_after()
    peers = [across, along, far]
    quarter = mod_ref.shape[1] // 4
    depth = msgs_ref.shape[-1]
    columns = pl.ds(pl.multiple_of(me * quarter, quarter), quarter)
    weights = pltpu.make_async_copy(w_ref.at[:, columns], wbuf, load.at[0])
    weights.start()
    mine = pltpu.make_async_copy(tok_ref.at[me], stage.at[me], load.at[1])
    mine.start()
    msgs_ref[me, core] = msg_ref[:, pl.ds(pl.multiple_of(plane * depth, depth), depth)]
    greet_all()
    here = msgs_ref.at[me, core]
    first = [send(here, here, sems, k, {"tp": p}) for k, p in enumerate(peers)]
    for copy in first:
        copy.start()
    spread_out = [
        send(tok_ref.at[p], stage.at[me], sems, 3 + k, {"tp": p}) for k, p in enumerate(peers)
    ]
    for copy in spread_out:
        copy.start()
    captions = [
        send(cap_ref.at[:, p], caps_ref.at[me], sems, 16 + k, {"tp": p})
        for k, p in enumerate(peers)
    ]
    captions += [
        send(cot_ref.at[p], cots_ref.at[me], sems, 19 + k, {"tp": p}) for k, p in enumerate(peers)
    ]
    for copy in captions:
        copy.start()
    own_caps = pltpu.make_async_copy(cap_ref.at[:, me], caps_ref.at[me], load.at[3])
    own_caps.start()
    own_cots = pltpu.make_async_copy(cot_ref.at[me], cots_ref.at[me], load.at[4])
    own_cots.start()
    for copy in first:
        copy.wait_recv()
    here = msgs_ref.at[:, core]
    swap = send(here, here, sems, 6, {"core": 1 - core})
    swap.start()
    weights.wait()
    conditions = msgs_ref[:, core].reshape(4 * 8, depth).astype(wbuf.dtype)
    tile = 512
    for step in range(quarter // tile):
        at = pl.ds(step * tile, tile)
        part[:, :, at] = jnp.dot(
            conditions, wbuf[:, at], preferred_element_type=jnp.float32
        ).reshape(4, 8, tile)
    second = [
        send(part.at[p], land.at[k], sems, 7 + k, {"seq": p}) for k, p in enumerate(others)
    ]
    for copy in second:
        copy.start()
    mine.wait()
    for copy in spread_out:
        copy.wait_recv()
    third = [
        send(stage.at[p], in_ref.at[plane], sems, 10 + k, {"seq": p})
        for k, p in enumerate(others)
    ]
    for copy in third:
        copy.start()
    stay = pltpu.make_async_copy(stage.at[plane], in_ref.at[plane], load.at[2])
    stay.start()
    for copy in second:
        copy.wait_recv()
    mod_ref[:, columns] = (part[plane] + land[0]) + (land[1] + land[2])
    here = mod_ref.at[:, columns]
    fourth = [send(here, here, sems, 13 + k, {"tp": p}) for k, p in enumerate(peers)]
    for copy in fourth:
        copy.start()
    swap.wait_recv()
    for copy in fourth + third + captions:
        copy.wait_recv()
    stay.wait()
    own_caps.wait()
    own_cots.wait()
    for copy in first + spread_out + captions + [swap] + second + third + fourth:
        copy.wait_send()


def arrive(ident, tokens, captions, cotangent, message, w_mod):
    rows, width = tokens.shape
    docs, caps, ctx = captions.shape
    depth, wide = w_mod.shape
    vmem, hbm = pl.BlockSpec(memory_space=pltpu.VMEM), pl.BlockSpec(memory_space=pl.ANY)
    return pl.pallas_call(
        arrive_kernel,
        out_shape=[
            jax.ShapeDtypeStruct((4, rows // 4, width), tokens.dtype),
            jax.ShapeDtypeStruct((4, docs, caps // 4, ctx), captions.dtype),
            jax.ShapeDtypeStruct((4, rows // 4, width), cotangent.dtype),
            jax.ShapeDtypeStruct((4, 2, 8, depth), jnp.float32),
            jax.ShapeDtypeStruct((8, wide), jnp.float32),
        ],
        in_specs=[hbm, hbm, hbm, vmem, hbm],
        out_specs=[hbm, hbm, hbm, vmem, vmem],
        scratch_shapes=[
            pltpu.VMEM((4, rows // 4, width), tokens.dtype),
            pltpu.VMEM((depth, wide // 4), w_mod.dtype),
            pltpu.VMEM((4, 8, wide // 4), jnp.float32),
            pltpu.VMEM((3, 8, wide // 4), jnp.float32),
            pltpu.SemaphoreType.DMA((5,)),
            pltpu.SemaphoreType.DMA((22,)),
            pltpu.SemaphoreType.DMA((22,)),
        ],
        compiler_params=pltpu.CompilerParams(
            collective_id=ident, has_side_effects=True, vmem_limit_bytes=16 * 1024 * 1024
        ),
        cost_estimate=pl.CostEstimate(flops=0, bytes_accessed=90_000_000, transcendentals=0),
        name="arrive",
    )(
        tokens.reshape(4, rows // 4, width),
        captions.reshape(docs, 4, caps // 4, ctx),
        cotangent.reshape(4, rows // 4, width),
        message,
        w_mod,
    )


def finale_kernel(count, *refs):
    ins, (back_ref, x_ref) = refs[:count], refs[count : count + 2]
    outs, (home_ref, out_ref) = refs[count + 2 : 2 * count + 2], refs[2 * count + 2 : 2 * count + 4]
    stage, land, load, c0, c1, s0, s1 = refs[2 * count + 4 :]
    sems = (s0, s1)
    me, across, along, far = neighbours()
    core = lax.axis_index("core")
    plane, others = planes_after()
    peers = [across, along, far]
    quarter = x_ref.shape[1] // 4
    gathering = Gathering(ins, outs, load, (c0, c1))

    def columns(t):
        return pl.ds(pl.multiple_of(t * quarter, quarter), quarter)

    returning = Returning(back_ref, home_ref, stage, load.at[count], sems, 10)
    greet_all()
    first = [
        send(x_ref.at[:, columns(p)], land.at[k], sems, k, {"tp": p}) for k, p in enumerate(peers)
    ]
    for copy in first:
        copy.start()
    returning.begin()
    gathering.begin()
    for copy in first:
        copy.wait_recv()
    out_ref[plane, core, :, columns(me)] = (x_ref[:, columns(me)] + land[0]) + (land[1] + land[2])
    here = out_ref.at[plane, core, :, columns(me)]
    second = [send(here, here, sems, 3 + k, {"seq": p}) for k, p in enumerate(others)]
    for copy in second:
        copy.start()
    for copy in second:
        copy.wait_recv()
    here = out_ref.at[:, core, :, columns(me)]
    third = [send(here, here, sems, 6 + k, {"tp": p}) for k, p in enumerate(peers)]
    for copy in third:
        copy.start()
    returning.turn()
    gathering.relay()
    for copy in third:
        copy.wait_recv()
    here = out_ref.at[:, core]
    swap = send(here, here, sems, 9, {"core": 1 - core})
    swap.start()
    gathering.hand()
    swap.wait_recv()
    returning.end()
    gathering.end()
    for copy in first + second + third + [swap]:
        copy.wait_send()


def finale(ident, pieces, back, x):
    hbm, vmem = pl.BlockSpec(memory_space=pl.ANY), pl.BlockSpec(memory_space=pltpu.VMEM)
    count = len(pieces)
    rows, width = x.shape
    tall, wide = back.shape
    got = pl.pallas_call(
        functools.partial(finale_kernel, count),
        out_shape=[
            *[jax.ShapeDtypeStruct((4, 2) + p.shape, p.dtype) for p in pieces],
            jax.ShapeDtypeStruct((4, tall // 4, wide), back.dtype),
            jax.ShapeDtypeStruct((4, 2, rows, width), jnp.float32),
        ],
        in_specs=[hbm] * (count + 1) + [vmem],
        out_specs=[hbm] * (count + 1) + [vmem],
        scratch_shapes=[
            pltpu.VMEM((4, tall // 4, wide), back.dtype),
            pltpu.VMEM((3, rows, width // 4), jnp.float32),
            pltpu.SemaphoreType.DMA((count + 1,)),
            pltpu.SemaphoreType.DMA((10 * count,)),
            pltpu.SemaphoreType.DMA((10 * count,)),
            pltpu.SemaphoreType.DMA((16,)),
            pltpu.SemaphoreType.DMA((16,)),
        ],
        compiler_params=pltpu.CompilerParams(
            collective_id=ident, has_side_effects=True, vmem_limit_bytes=16 * 1024 * 1024
        ),
        cost_estimate=pl.CostEstimate(flops=0, bytes_accessed=120_000_000, transcendentals=0),
        name="finale",
    )(*pieces, back.reshape(4, tall // 4, wide), x)
    return got[:count], got[count].reshape(tall, wide), got[count + 1]


def lanes_of(rows):
    return lax.broadcasted_iota(jnp.int32, (rows, 128), 1)


def pair_norm(values):
    lane = lanes_of(values.shape[0])
    square = values * values
    low = jnp.sum(jnp.where(lane < HDIM, square, 0.0), axis=-1, keepdims=True)
    high = jnp.sum(jnp.where(lane < HDIM, 0.0, square), axis=-1, keepdims=True)
    inverse = jnp.where(lane < HDIM, lax.rsqrt(low / HDIM + eps), lax.rsqrt(high / HDIM + eps))
    return values * inverse, inverse


def pair_back(grads, normed, inverse):
    lane = lanes_of(grads.shape[0])
    inner = grads * normed
    low = jnp.sum(jnp.where(lane < HDIM, inner, 0.0), axis=-1, keepdims=True)
    high = jnp.sum(jnp.where(lane < HDIM, 0.0, inner), axis=-1, keepdims=True)
    return inverse * (grads - normed * (jnp.where(lane < HDIM, low, high) / HDIM))


def pair_turn(values, cosine, sine):
    lane = lanes_of(values.shape[0])
    partner = jnp.where(
        lane % HDIM < HDIM // 2, pltpu.roll(values, 96, 1), pltpu.roll(values, 32, 1)
    )
    return values * cosine + partner * sine


def store_heads(target, strip, pair, spare):
    lane = lanes_of(pair.shape[0])
    first = jnp.where(lane < HDIM, pair, spare)
    second = jnp.where(lane < HDIM, pltpu.roll(pair, HDIM, 1), spare)
    target[strip, 0:128] = first.astype(target.dtype)
    target[strip, 128:256] = second.astype(target.dtype)


def join_heads(first, second):
    lane = lanes_of(first.shape[0])
    return jnp.where(lane < HDIM, first, pltpu.roll(second, HDIM, 1))


def ones_beside(rows):
    lane = lanes_of(rows)
    return jnp.where((lane == HDIM) | (lane == HDIM + 1), 1.0, 0.0)


def not_turned(left, right):
    return lax.dot_general(
        left, right, (((1,), (1,)), ((), ())), preferred_element_type=jnp.float32
    )


STRIP = 256
SPARE = 128.0


def strips(rows, body):
    @pl.loop(0, rows // STRIP)
    def _(step):
        body(pl.ds(pl.multiple_of(step * STRIP, STRIP), STRIP))


def weigh(qa_ref, ka_ref, va_ref, ov_ref):
    for head in range(2):
        at = pl.ds(head * 128, 128)

        def body(strip):
            scores = not_turned(qa_ref[strip, at], ka_ref[:, at])
            weights = jnp.exp(scores).astype(jnp.bfloat16)
            ov_ref[strip, at] = jnp.dot(
                weights, va_ref[:, at], preferred_element_type=jnp.float32
            )

        strips(qa_ref.shape[0], body)


def own_kernel(
    q_ref, k_ref, v_ref, gq_ref, gk_ref, cos_ref, sin_ref, sq_ref, sk_ref,
    qa_ref, ka_ref, va_ref, ov_ref,
):
    def prepare(strip):
        cosine, sine = cos_ref[strip, :], sin_ref[strip, :]
        query = pair_turn(pair_norm(q_ref[strip, :])[0] * gq_ref[...], cosine, sine)
        store_heads(qa_ref, strip, query * HDIM**-0.5, sq_ref[strip, :])
        keys = pair_turn(pair_norm(k_ref[strip, :])[0] * gk_ref[...], cosine, sine)
        store_heads(ka_ref, strip, keys, sk_ref[strip, :])
        store_heads(va_ref, strip, v_ref[strip, :], ones_beside(STRIP))

    strips(q_ref.shape[0], prepare)
    weigh(qa_ref, ka_ref, va_ref, ov_ref)


def cross_kernel(
    qa_ref, k_ref, v_ref, gk_ref, sq_ref, sk_ref, own_ref, gate_ref,
    ka_ref, va_ref, ov_ref, mix_ref, qx_ref,
):
    def prepare(strip):
        keys = pair_norm(k_ref[strip, :])[0] * gk_ref[...]
        store_heads(ka_ref, strip, keys, sk_ref[strip, :])
        store_heads(va_ref, strip, v_ref[strip, :], ones_beside(STRIP))

    strips(k_ref.shape[0], prepare)

    def requery(strip):
        lane = lanes_of(STRIP)
        for head in range(2):
            at = pl.ds(head * 128, 128)
            qx_ref[strip, at] = jnp.where(
                lane < HDIM, qa_ref[strip, at].astype(jnp.float32), sq_ref[strip, :]
            ).astype(qx_ref.dtype)

    strips(qa_ref.shape[0], requery)
    weigh(qx_ref, ka_ref, va_ref, ov_ref)

    def mix(strip):
        parts = []
        for head in range(2):
            at = pl.ds(head * 128, 128)
            own, cross = own_ref[strip, at], ov_ref[strip, at]
            parts.append((own / own[:, 64:65], cross / cross[:, 64:65]))
        own = join_heads(parts[0][0], parts[1][0])
        cross = join_heads(parts[0][1], parts[1][1])
        mix_ref[strip, :] = (own + gate_ref[...] * cross).astype(mix_ref.dtype)

    strips(qa_ref.shape[0], mix)


def back_kernel(own, *refs):
    g_ref, gate_ref, ov_ref, qa_ref, sq_ref, ka_ref, va_ref, k_ref, gk_ref = refs[:9]
    refs = refs[9:]
    if own:
        q_ref, gq_ref, cos_ref, sin_ref, more_ref = refs[:5]
        refs = refs[5:]
    dq_ref, dk_ref, dv_ref, sum_ref, qx, doa, dqt, dqh, dkh, dvh = refs
    rows, count = qa_ref.shape[0], ka_ref.shape[0]
    sum_ref[...] = jnp.zeros_like(sum_ref)
    for head in range(2):
        at = pl.ds(head * 128, 128)

        def prepare(strip):
            lane = lanes_of(STRIP)
            plain = g_ref[strip, :]
            grads = plain * gate_ref[...]
            if head == 1:
                plain = pltpu.roll(plain, HDIM, 1)
                grads = pltpu.roll(grads, HDIM, 1)
            both = ov_ref[strip, at]
            inverse = 1.0 / both[:, 64:65]
            out = jnp.where(lane < HDIM, both * inverse, 0.0)
            if not own:
                sum_ref[0, head : head + 1, :] += jnp.sum(plain * out, axis=0, keepdims=True)
            scaled = (grads * inverse).astype(jnp.bfloat16).astype(jnp.float32)
            delta = jnp.sum(scaled * out, axis=-1, keepdims=True)
            high = delta.astype(jnp.bfloat16).astype(jnp.float32)
            doa[strip, :] = jnp.where(
                lane < HDIM,
                scaled,
                jnp.where(lane == HDIM, -high, jnp.where(lane == HDIM + 1, high - delta, 0.0)),
            ).astype(doa.dtype)
            qx[strip, :] = jnp.where(
                lane < HDIM, qa_ref[strip, at].astype(jnp.float32), sq_ref[strip, :]
            ).astype(qx.dtype)

        strips(rows, prepare)
        dqt[...] = jnp.zeros_like(dqt)

        def block(strip):
            keys, values = ka_ref[strip, at], va_ref[strip, at]
            weights = jnp.exp(not_turned(keys, qx[...]))
            grads = (weights * not_turned(values, doa[...])).astype(jnp.bfloat16)
            dvh[head, strip, :] = jnp.dot(
                weights.astype(jnp.bfloat16), doa[...], preferred_element_type=jnp.float32
            )
            dkh[head, strip, :] = jnp.dot(grads, qx[...], preferred_element_type=jnp.float32)
            dqt[...] += lax.dot_general(
                keys, grads, (((0,), (0,)), ((), ())), preferred_element_type=jnp.float32
            )

        strips(count, block)
        dqh[head] = dqt[...].T * HDIM**-0.5

    def add_up(row, values):
        sum_ref[0, row : row + 1, :] += jnp.sum(values, axis=0, keepdims=True)

    def finish(strip):
        grads = join_heads(dkh[0, strip, :], dkh[1, strip, :])
        if own:
            grads = pair_turn(grads, cos_ref[strip, :], -sin_ref[strip, :])
        normed, inverse = pair_norm(k_ref[strip, :])
        add_up(2, grads * normed)
        dk_ref[strip, :] = pair_back(grads * gk_ref[...], normed, inverse).astype(dk_ref.dtype)
        dv_ref[strip, :] = join_heads(dvh[0, strip, :], dvh[1, strip, :]).astype(dv_ref.dtype)

    strips(count, finish)

    def finish_query(strip):
        grads = join_heads(dqh[0, strip, :], dqh[1, strip, :])
        if own:
            grads = pair_turn(grads + more_ref[strip, :], cos_ref[strip, :], -sin_ref[strip, :])
            normed, inverse = pair_norm(q_ref[strip, :])
            add_up(3, grads * normed)
            grads = pair_back(grads * gq_ref[...], normed, inverse)
        dq_ref[strip, :] = grads.astype(dq_ref.dtype)

    strips(rows, finish_query)


def view(ref, index, width=128, offset=0):
    return ref.at[:, pl.ds((offset + index) * width, width)]


def attend_own(projected, gain_q, gain_k, cosine, sine, spare_q, spare_k):
    rows, width = projected.shape[0], projected.shape[1] // 3
    count = width // 128
    bf, f32 = jnp.bfloat16, jnp.float32

    def steps(i, ins, outs, scratch):
        raw, gain_q, gain_k, *tables = ins
        own_kernel(
            view(raw, i), view(raw, i, offset=count), view(raw, i, offset=2 * count),
            view(gain_q, i), view(gain_k, i), *tables, *[view(out, i, 256) for out in outs],
        )

    return Aside(
        [projected, gain_q, gain_k, cosine, sine, spare_q, spare_k],
        [jax.ShapeDtypeStruct((rows, 2 * width), d) for d in (bf, bf, bf, f32)],
        [],
        steps,
    )


def attend_cross(qa, cap_proj, gain, spare_q, spare_k, own, gate):
    rows, count = qa.shape[0], qa.shape[1] // 256
    caps, width = cap_proj.shape[0], cap_proj.shape[1] // 2
    bf, f32 = jnp.bfloat16, jnp.float32

    def steps(i, ins, outs, scratch):
        qa, raw, gain, spare_q, spare_k, own, gate = ins
        ka, va, ov, mix = outs
        cross_kernel(
            view(qa, i, 256), view(raw, i), view(raw, i, offset=count), view(gain, i),
            spare_q, spare_k, view(own, i, 256), view(gate, i),
            view(ka, i, 256), view(va, i, 256), view(ov, i, 256), view(mix, i), *scratch,
        )

    return Aside(
        [qa, cap_proj, gain, spare_q, spare_k, own, gate],
        [
            jax.ShapeDtypeStruct((caps, 2 * width), bf),
            jax.ShapeDtypeStruct((caps, 2 * width), bf),
            jax.ShapeDtypeStruct((rows, 2 * width), f32),
            jax.ShapeDtypeStruct((rows, width), bf),
        ],
        [pltpu.VMEM((rows, 256), bf)],
        steps,
    )


def attend_back(grads, gate, ov, qa, spare_q, ka, va, raw, gain_k, rest=None):
    rows, width = grads.shape
    caps, count = ka.shape[0], width // 128
    bf, f32 = jnp.bfloat16, jnp.float32
    own = rest is not None

    def steps(i, ins, outs, scratch):
        grads, gate, ov, qa, spare_q, ka, va, raw, gain_k, *rest = ins
        dq, dk, dv, sums = outs
        operands = [
            view(grads, i), view(gate, i), view(ov, i, 256), view(qa, i, 256), spare_q,
            view(ka, i, 256), view(va, i, 256), view(raw, i, offset=count if own else 0),
            view(gain_k, i),
        ]
        if own:
            gain_q, cosine, sine, more = rest
            operands += [view(raw, i), view(gain_q, i), cosine, sine, view(more, i)]
        back_kernel(
            own, *operands, view(dq, i), view(dk, i), view(dv, i), sums.at[pl.ds(i, 1)], *scratch
        )

    return Aside(
        [grads, gate, ov, qa, spare_q, ka, va, raw, gain_k, *(rest or ())],
        [
            jax.ShapeDtypeStruct((rows, width), bf if own else f32),
            jax.ShapeDtypeStruct((caps, width), bf),
            jax.ShapeDtypeStruct((caps, width), bf),
            jax.ShapeDtypeStruct((count, 8, 128), f32),
        ],
        [
            pltpu.VMEM((rows, 128), bf),
            pltpu.VMEM((rows, 128), bf),
            pltpu.VMEM((128, rows), f32),
            pltpu.VMEM((2, rows, 128), f32),
            pltpu.VMEM((2, caps, 128), f32),
            pltpu.VMEM((2, caps, 128), f32),
        ],
        steps,
    )


def row_stats(values):
    inverse = lax.rsqrt(jnp.mean(values * values, axis=-1, keepdims=True) + eps)
    return (values * inverse, inverse)


def norm_back(grad_normed, normed, inverse):
    inner_mean = jnp.mean(grad_normed * normed, axis=-1, keepdims=True)
    return inverse * (grad_normed - normed * inner_mean)


def head_stats(values):
    shaped = values.reshape(values.shape[0], -1, HDIM)
    normed, inverse = row_stats(shaped)
    return (normed.reshape(values.shape), inverse)


def head_back(grad_normed, normed, inverse):
    shaped_grad = grad_normed.reshape(grad_normed.shape[0], -1, HDIM)
    shaped_norm = normed.reshape(normed.shape[0], -1, HDIM)
    return norm_back(shaped_grad, shaped_norm, inverse).reshape(grad_normed.shape)


def rotary(values, row_pos, col_pos, direction):
    quarter = HDIM // 4
    freqs = 10000.0 ** (-jnp.arange(quarter, dtype=jnp.float32) / quarter)
    angles = jnp.concatenate([row_pos[:, None] * freqs, col_pos[:, None] * freqs], axis=1)
    cosine = jnp.cos(angles)[:, None, :]
    sine = direction * jnp.sin(angles)[:, None, :]
    shaped = values.reshape(values.shape[0], -1, HDIM)
    first_half = shaped[..., : HDIM // 2]
    second_half = shaped[..., HDIM // 2 :]
    turned = jnp.concatenate(
        [first_half * cosine - second_half * sine, second_half * cosine + first_half * sine],
        axis=-1,
    )
    return turned.reshape(values.shape)


def layout(doc_lengths, bucket, positions):
    doc_ends = jnp.cumsum(doc_lengths)
    starts = doc_ends - doc_lengths
    segment = jnp.sum((positions[:, None] >= doc_ends[None, :]).astype(jnp.int32), axis=1)
    matches = segment[:, None] == jnp.arange(DOCS, dtype=jnp.int32)[None, :]
    offset = jnp.sum(jnp.where(matches, starts[None, :], 0), axis=1)
    within = positions - offset
    stride = 32 * (bucket + 1)
    return (segment, (within // stride).astype(jnp.float32), (within % stride).astype(jnp.float32))


def turn_tables(row_pos, col_pos):
    quarter = HDIM // 4
    freqs = 10000.0 ** (-jnp.arange(quarter, dtype=jnp.float32) / quarter)
    angles = jnp.concatenate([row_pos[:, None] * freqs, col_pos[:, None] * freqs], axis=1)
    cosine, sine = jnp.cos(angles), jnp.sin(angles)
    return jnp.tile(cosine, (1, 4)), jnp.concatenate([-sine, sine, -sine, sine], axis=1)


def spare_columns(labels, height):
    lane = jnp.arange(128)[None, :] - HDIM
    at_label = (lane >= 0) & (lane <= DOCS) & (lane == labels[:, None])
    last = lane == DOCS + 1
    if height:
        return jnp.where(at_label, height, jnp.where(last, -height, 0.0)).astype(jnp.float32)
    return (at_label | last).astype(jnp.float32)


def by_head(values):
    return values.reshape(values.shape[0], -1, 1, HDIM).transpose(1, 0, 2, 3)


def from_heads(blocks):
    return blocks.transpose(1, 0, 2, 3).reshape(blocks.shape[1], -1)


def attend_forward(query, keys, values, allowed):
    scale = HDIM ** (-0.5)

    def block(block_args):
        part_q, part_k, part_v = block_args
        scores = (
            jnp.einsum("qhd,khd->hqk", part_q, part_k, preferred_element_type=jnp.float32) * scale
        )
        scores = jnp.where(allowed[None], scores, -1e30)
        row_peak = jnp.max(scores, axis=-1, keepdims=True)
        exp_scores = jnp.exp(scores - row_peak)
        exp_total = jnp.sum(exp_scores, axis=-1, keepdims=True)
        attn_probs = (exp_scores / exp_total).astype(jnp.bfloat16)
        attn_block = jnp.einsum(
            "hqk,khd->qhd", attn_probs, part_v, preferred_element_type=jnp.float32
        )
        return (attn_block, row_peak[..., 0] + jnp.log(exp_total[..., 0]))

    blocks, log_total = lax.map(block, (by_head(query), by_head(keys), by_head(values)))
    return (from_heads(blocks), log_total)


def attend_backward(query, keys, values, allowed, log_total, grad_out):
    scale = HDIM ** (-0.5)

    def block(block_args):
        part_q, part_k, part_v, part_log, part_grad = block_args
        scores = (
            jnp.einsum("qhd,khd->hqk", part_q, part_k, preferred_element_type=jnp.float32) * scale
        )
        scores = jnp.where(allowed[None], scores, -1e30)
        attn_probs = jnp.exp(scores - part_log[..., None])
        grad_probs = jnp.einsum(
            "qhd,khd->hqk", part_grad, part_v, preferred_element_type=jnp.float32
        )
        row_delta = jnp.sum(attn_probs * grad_probs, axis=-1, keepdims=True)
        grad_scores = (attn_probs * (grad_probs - row_delta)).astype(jnp.bfloat16)
        grad_query = (
            jnp.einsum("hqk,khd->qhd", grad_scores, part_k, preferred_element_type=jnp.float32)
            * scale
        )
        grad_keys = (
            jnp.einsum("hqk,qhd->khd", grad_scores, part_q, preferred_element_type=jnp.float32)
            * scale
        )
        grad_values = jnp.einsum(
            "hqk,qhd->khd",
            attn_probs.astype(jnp.bfloat16),
            part_grad,
            preferred_element_type=jnp.float32,
        )
        return (grad_query, grad_keys, grad_values)

    grad_query, grad_keys, grad_values = lax.map(
        block,
        (by_head(query), by_head(keys), by_head(values), log_total, by_head(grad_out)),
    )
    return (from_heads(grad_query), from_heads(grad_keys), from_heads(grad_values))


def matmul(left, right):
    return jnp.dot(left, right, preferred_element_type=jnp.float32)


def contract_right(left, weight):
    return lax.dot_general(
        left, weight, (((1,), (1,)), ((), ())), preferred_element_type=jnp.float32
    )


def contract_rows(left, right):
    return lax.dot_general(
        left, right, (((0,), (0,)), ((), ())), preferred_element_type=jnp.float32
    )


def pick(values, index, axis):
    return lax.dynamic_index_in_dim(values, index, axis, keepdims=False)


def to_plane(values):
    ways = lax.axis_size("tp")
    parts = values.reshape((ways, values.shape[0] // ways) + values.shape[1:])
    parts = lax.all_to_all(parts, "tp", 0, 0, tiled=True)
    parts = lax.all_to_all(parts, "seq", 0, 0, tiled=True)
    return parts.reshape(values.shape)


def from_plane(values):
    ways = lax.axis_size("tp")
    parts = values.reshape((ways, values.shape[0] // ways) + values.shape[1:])
    parts = lax.all_to_all(parts, "seq", 0, 0, tiled=True)
    parts = lax.all_to_all(parts, "tp", 0, 0, tiled=True)
    return parts.reshape(values.shape)


def fast():
    return lax.axis_size("tp") == 4 and lax.axis_size("core") == 2 and lax.axis_size("seq") == 4


def gather_planes(part):
    return lax.all_gather(part, "seq", axis=0, tiled=False)


def join_cores(halves):
    whole = lax.all_gather(halves, "core", axis=1, tiled=False)
    return whole.reshape(-1, halves.shape[-1])


def swap_rows(term):
    cores, planes = lax.axis_size("core"), lax.axis_size("seq")
    return swap_halves(term.astype(jnp.bfloat16).reshape(planes, cores, -1, term.shape[-1]))


def scatter_planes(term):
    return lax.psum_scatter(term, "seq", scatter_dimension=0, tiled=False)


def swap_halves(shaped):
    cores, me_c = lax.axis_size("core"), lax.axis_index("core")
    mine = pick(shaped, me_c, 1)
    for step in range(1, cores):
        ring = [(c, (c + step) % cores) for c in range(cores)]
        other = lax.ppermute(pick(shaped, (me_c + step) % cores, 1), "core", ring)
        mine = (mine.astype(jnp.float32) + other.astype(jnp.float32)).astype(jnp.bfloat16)
    return mine


def plane_gather(values):
    return lax.all_gather(values, "tp", axis=0, tiled=True)


def plane_multiply(ident, x, weight, turned=False, halved=False, width=None, **more):
    if fast():
        return gather_matmul(ident, x, weight, turned, halved, width, **more)
    whole = join_cores(weight) if halved else weight
    x = plane_gather(x)
    return x, whole, contract_right(x, whole) if turned else matmul(x, whole[:, :width])


def multiply_plane(ident, x, weight, turned=False, **more):
    if fast():
        return matmul_scatter(ident, x, weight, turned, **more)
    weight = weight[:, : x.shape[1]] if turned else weight
    term = contract_right(x, weight) if turned else matmul(x, weight)
    return lax.psum_scatter(
        term.astype(jnp.bfloat16), "tp", scatter_dimension=0, tiled=True
    ).astype(jnp.float32), None


def collect_plane(pieces):
    return [
        lax.all_gather(p, ("tp", "core"), axis=0, tiled=False).reshape(
            (lax.axis_size("tp"), lax.axis_size("core")) + p.shape
        )
        for p in pieces
    ]


def spread_parts(blocks, parts):
    if fast():
        return spread(blocks, parts)
    tp, cores, rows, width = blocks.shape
    return (
        blocks.astype(jnp.float32)
        .reshape(tp, cores, rows, parts, width // parts)
        .transpose(1, 2, 3, 0, 4)
        .reshape(cores * rows, tp * width)
    )


def arrive_plane(ident, tokens, captions, cotangent, message, w_mod):
    if fast():
        return arrive(ident, tokens, captions, cotangent, message, w_mod)
    ways = lax.axis_size("tp")
    docs, caps, ctx = captions.shape
    captions = captions.reshape(docs, ways, caps // ways, ctx).transpose(1, 0, 2, 3)
    captions = lax.all_to_all(captions, "tp", 0, 0, tiled=True)
    cotangent = lax.all_to_all(
        cotangent.reshape(ways, -1, cotangent.shape[1]), "tp", 0, 0, tiled=True
    )
    planes, cores = lax.axis_size("seq"), lax.axis_size("core")
    depth = w_mod.shape[0]
    part = lax.dynamic_slice_in_dim(message, lax.axis_index("seq") * depth, depth, 1)
    messages = lax.all_gather(part, ("tp", "core"), axis=0, tiled=False)
    terms = matmul(messages.reshape(-1, depth).astype(w_mod.dtype), w_mod)
    terms = lax.psum_scatter(
        terms.reshape(planes, cores, 8, -1), "seq", scatter_dimension=0, tiled=False
    )
    messages = messages.reshape(lax.axis_size("tp"), cores, 8, depth)
    return to_plane(tokens), captions, cotangent, messages, pick(terms, lax.axis_index("core"), 0)


def finale_plane(ident, pieces, back, x):
    if fast():
        return finale(ident, pieces, back, x)
    totals = lax.all_gather(lax.psum(x, "tp"), ("seq", "core"), axis=0, tiled=False)
    return collect_plane(pieces), from_plane(back), totals


def shards(
    tokens,
    cotangent,
    step_embed,
    caption,
    lengths,
    group_bucket,
    null_mask,
    w_qkv,
    w_out,
    w_capkv,
    w_gateup,
    w_down,
    w_mod,
    b_mod,
    gain_attn,
    gain_ffn,
    gain_query,
    gain_key,
    gain_capkey,
    gate_head,
    null_embed,
):
    tp, cores, planes = lax.axis_size("tp"), lax.axis_size("core"), lax.axis_size("seq")
    me_t, me_c, me_z = lax.axis_index("tp"), lax.axis_index("core"), lax.axis_index("seq")
    groups = tp * cores
    rows, width = tokens.shape
    piece = rows // tp
    local_heads = HEADS // tp
    local = local_heads * HDIM
    cap_dev = caption.shape[2]
    ctx = caption.shape[3]
    my_group = me_z * cores + me_c

    condition = jax.nn.silu(step_embed[0].astype(jnp.float32)).astype(jnp.bfloat16)
    numbers = jnp.concatenate([lengths[0], group_bucket, null_mask[0]]).astype(jnp.float32)
    mod_rows = w_mod.shape[0]
    numbers = jnp.tile(jnp.pad(numbers, (0, mod_rows - numbers.shape[0])), planes)
    message = jnp.concatenate(
        [condition.astype(jnp.float32), numbers[None], jnp.zeros((3, numbers.shape[0]))], axis=0
    )
    arrived, captions, cotangents, messages, mod_doc = arrive_plane(
        13, tokens, caption[0], cotangent, message, w_mod
    )
    captions = lax.all_to_all(captions, "seq", 0, 0, tiled=True)
    messages = messages.reshape(groups, 8, mod_rows)
    cond_mine = messages[:, :DOCS].reshape(groups * DOCS, mod_rows)
    mod_doc = mod_doc[:DOCS] + b_mod

    numbers = messages[:, DOCS, : 2 * DOCS + 1].astype(jnp.int32)
    counts = jnp.sum(numbers[:, :DOCS], axis=1).astype(jnp.float32)
    mine = pick(numbers, my_group, 0)
    doc_lengths, bucket, nulls = mine[:DOCS], mine[DOCS], mine[DOCS + 1 :]
    bucket_count = jnp.sum(jnp.where(numbers[:, DOCS] == bucket, counts, 0.0))
    scale_loss = jnp.sum(counts) / (RES * bucket_count)

    def columns_of(weight, parts):
        share = weight.shape[0] // cores
        size = weight.shape[1] // (parts * tp)
        return jnp.concatenate(
            [
                lax.dynamic_slice(weight, (me_c * share, (q * tp + me_t) * size), (share, size))
                for q in range(parts)
            ],
            axis=1,
        )

    half_qkv = gather_planes(
        jnp.concatenate([columns_of(w_qkv, 3), columns_of(w_out, 1)], axis=1)
    )
    share = w_down.shape[0] // groups
    later = (
        columns_of(w_capkv, 2),
        lax.dynamic_slice_in_dim(w_down, (me_t * cores + me_c) * share, share, 0),
        columns_of(w_gateup, 2 * planes),
    )
    arrived, *later = lax.optimization_barrier((arrived, *later))
    half_capkv, half_down, half_gateup = [gather_planes(part) for part in later]

    inputs = arrived.reshape(tokens.shape).astype(jnp.float32)
    row = jnp.arange(rows, dtype=jnp.int32)
    spread = (row // piece) * rows + row % piece
    positions = spread + me_t * piece
    all_positions = (jnp.arange(tp, dtype=jnp.int32)[:, None] * piece + spread[None, :]).reshape(-1)
    segment, _, _ = layout(doc_lengths, bucket, positions)
    all_segment, row_pos, col_pos = layout(doc_lengths, bucket, all_positions)
    all_document = jnp.minimum(all_segment, DOCS - 1)
    document = jnp.minimum(segment, DOCS - 1)
    doc_pick = (document[:, None] == jnp.arange(DOCS, dtype=jnp.int32)[None, :]).astype(jnp.float32)
    is_valid = (segment < DOCS).astype(jnp.float32)
    modulation = jnp.dot(doc_pick, mod_doc, precision=lax.Precision.HIGHEST)
    scale_a, gate_a, scale_f, gate_f = jnp.split(modulation, 4, axis=1)
    tanh_a, tanh_f = jnp.tanh(gate_a), jnp.tanh(gate_f)

    normed1, inverse1 = row_stats(inputs)
    hidden1 = (normed1 * gain_attn * (1.0 + scale_a)).astype(jnp.bfloat16)
    hidden1, full_qkv, projected = plane_multiply(
        1, hidden1, half_qkv, halved=True, width=3 * local
    )
    cotangents, projected = lax.optimization_barrier((cotangents, projected))
    cotangents = lax.all_to_all(cotangents, "seq", 0, 0, tiled=True).reshape(tokens.shape)
    full_out = full_qkv[:, 3 * local :].reshape(tp, local, local)
    full_out = lax.all_to_all(full_out, "tp", 0, 0, tiled=True)
    full_out = full_out.transpose(1, 0, 2).reshape(local, width)
    my_gain_query = pick(gain_query.reshape(tp, 1, local), me_t, 0)
    my_gain_key = pick(gain_key.reshape(tp, 1, local), me_t, 0)
    my_gain_capkey = pick(gain_capkey.reshape(tp, 1, local), me_t, 0)
    gate_tanh = pick(jnp.tanh(gate_head).reshape(tp, local_heads), me_t, 0)
    head_gate = jnp.repeat(gate_tanh, HDIM)[None, :]
    own_aside = {}
    if fast():
        cosine, sine = turn_tables(row_pos, col_pos)
        own_spare = spare_columns(all_segment, SPARE)
        own_aside["aside"] = attend_own(
            projected, my_gain_query, my_gain_key, cosine, sine,
            own_spare, spare_columns(all_segment, 0),
        )

    captions = captions.transpose(1, 0, 2, 3).reshape(caption.shape[1:])
    capmix = jnp.where(nulls[:, None, None] > 0, null_embed[None, None, :], captions)
    cap_flat = capmix.reshape(DOCS * cap_dev, ctx)
    cap_flat, full_capkv, cap_proj, *own_wides = plane_multiply(
        2, cap_flat, half_capkv, halved=True, **own_aside
    )
    cap_document = jnp.tile(jnp.repeat(jnp.arange(DOCS, dtype=jnp.int32), cap_dev), tp)
    grad_res0 = cotangents.astype(jnp.float32) * (is_valid * scale_loss)[:, None]
    grad_down = (tanh_f * grad_res0).astype(jnp.bfloat16)
    if fast():
        wide_query, wide_keys, wide_values, own_wide = own_wides
        cross_spare = spare_columns(all_document, SPARE)
        cross_aside = attend_cross(
            wide_query, cap_proj, my_gain_capkey, cross_spare,
            spare_columns(cap_document, 0), own_wide, head_gate,
        )
        grad_down, full_down, grad_ffn, wide_capkeys, wide_capvals, cross_wide, mixed_attn = (
            plane_multiply(
                6, grad_down, half_down, turned=True, halved=True, aside=cross_aside, early=1
            )
        )
    else:
        grad_down, full_down, grad_ffn = plane_multiply(
            6, grad_down, half_down, turned=True, halved=True
        )
        query_raw, key_raw, value_raw = jnp.split(projected, 3, axis=1)
        query_norm, query_inv = head_stats(query_raw)
        key_norm, key_inv = head_stats(key_raw)
        capkey_raw, capval_raw = jnp.split(cap_proj, 2, axis=1)
        capkey_norm, capkey_inv = head_stats(capkey_raw)
        query = rotary(query_norm * my_gain_query, row_pos, col_pos, 1.0).astype(jnp.bfloat16)
        keys = rotary(key_norm * my_gain_key, row_pos, col_pos, 1.0).astype(jnp.bfloat16)
        values = value_raw.astype(jnp.bfloat16)
        capkeys = (capkey_norm * my_gain_capkey).astype(jnp.bfloat16)
        capvals = capval_raw.astype(jnp.bfloat16)
        self_allowed = all_segment[:, None] == all_segment[None, :]
        cross_allowed = all_document[:, None] == cap_document[None, :]
        own_out, own_log = attend_forward(query, keys, values, self_allowed)
        cross_out, cross_log = attend_forward(query, capkeys, capvals, cross_allowed)
        mixed_attn = (own_out + head_gate * cross_out).astype(jnp.bfloat16)
    attn_out, *_ = multiply_plane(3, mixed_attn, full_out)
    residual = inputs + tanh_a * attn_out
    normed2, inverse2 = row_stats(residual)
    hidden2 = (normed2 * gain_ffn * (1.0 + scale_f)).astype(jnp.bfloat16)
    hidden2, full_gateup, gate_up = plane_multiply(4, hidden2, half_gateup, halved=True)
    gate_part, up_part = jnp.split(gate_up, 2, axis=1)
    sig_gate = jax.nn.sigmoid(gate_part)
    silu_gate = gate_part * sig_gate
    hidden_ffn = (silu_gate * up_part).astype(jnp.bfloat16)
    grad_gate_part = grad_ffn * up_part * sig_gate * (1.0 + gate_part * (1.0 - sig_gate))
    grad_up_part = grad_ffn * silu_gate
    grad_gateup = jnp.concatenate([grad_gate_part, grad_up_part], axis=1).astype(jnp.bfloat16)
    term_down = swap_rows(contract_rows(hidden_ffn, grad_down))
    term_gateup = swap_rows(contract_rows(hidden2, grad_gateup))
    grad_gateup, term_down, term_gateup = lax.optimization_barrier(
        (grad_gateup, term_down, term_gateup)
    )
    term_down, term_gateup = scatter_planes(term_down), scatter_planes(term_gateup)
    grad_hidden2, *_ = multiply_plane(7, grad_gateup, full_gateup, turned=True)
    gain_ffn_term = jnp.sum(grad_hidden2 * normed2 * (1.0 + scale_f), axis=0)
    grad_scale_f = grad_hidden2 * normed2 * gain_ffn
    grad_residual = grad_res0 + norm_back(
        grad_hidden2 * gain_ffn * (1.0 + scale_f), normed2, inverse2
    )
    grad_attn = (tanh_a * grad_residual).astype(jnp.bfloat16)
    grad_attn, _, grad_mix = plane_multiply(8, grad_attn, full_out, turned=True)
    grad_gate_a = grad_residual * attn_out * (1.0 - tanh_a * tanh_a)
    term_out = contract_rows(mixed_attn, grad_attn).astype(jnp.bfloat16)
    term_out = swap_halves(term_out.reshape(1, cores, -1, width))[0]
    term_out = term_out.reshape(term_out.shape[0], tp, -1).transpose(1, 0, 2)
    term_out = lax.all_to_all(term_out, "tp", 0, 0, tiled=True)
    grad_mix, term_out, term_down, term_gateup = lax.optimization_barrier(
        (grad_mix, term_out, term_down, term_gateup)
    )
    term_out = scatter_planes(term_out)
    if fast():
        cross_aside = attend_back(
            grad_mix, head_gate, cross_wide, wide_query, cross_spare,
            wide_capkeys, wide_capvals, cap_proj, my_gain_capkey,
        )
        down_out, query_cross, grad_capkey_raw, grad_capvals, cross_sums = multiply_plane(
            5, hidden_ffn, full_down, aside=cross_aside
        )
        gate_head_term = jnp.sum(cross_sums[:, :2], axis=-1).reshape(-1)
        gain_capkey_term = cross_sums[:, 2].reshape(-1)
        grad_cap_proj = jnp.concatenate([grad_capkey_raw, grad_capvals], axis=1)
        term_capkv = swap_rows(contract_rows(cap_flat, grad_cap_proj))
        query_cross, term_capkv = lax.optimization_barrier((query_cross, term_capkv))
        term_capkv = scatter_planes(term_capkv)
        own_aside = attend_back(
            grad_mix, jnp.ones_like(head_gate), own_wide, wide_query, own_spare,
            wide_keys, wide_values, projected, my_gain_key,
            (my_gain_query, cosine, sine, query_cross),
        )
        result = (residual + tanh_f * down_out).astype(jnp.bfloat16)
        (all_down, all_gateup, all_out), result, (*grad_projected, own_sums) = collect(
            10, [term_down, term_gateup, term_out], result, own_aside
        )
        gain_key_term, gain_query_term = own_sums[:, 2].reshape(-1), own_sums[:, 3].reshape(-1)
        grad_projected = jnp.concatenate(grad_projected, axis=1)
    else:
        down_out, _ = multiply_plane(5, hidden_ffn, full_down)
        result = from_plane((residual + tanh_f * down_out).astype(jnp.bfloat16))
        all_down, all_gateup, all_out = collect_plane([term_down, term_gateup, term_out])
        grad_own = grad_mix.astype(jnp.bfloat16)
        grad_cross = (head_gate * grad_mix).astype(jnp.bfloat16)
        gate_head_term = jnp.sum(
            (grad_mix * cross_out).reshape(-1, local_heads, HDIM), axis=(0, 2)
        )
        query_own, grad_keys, grad_values = attend_backward(
            query, keys, values, self_allowed, own_log, grad_own
        )
        query_cross, grad_capkeys, grad_capvals = attend_backward(
            query, capkeys, capvals, cross_allowed, cross_log, grad_cross
        )
        grad_query = rotary(query_own + query_cross, row_pos, col_pos, -1.0)
        gain_query_term = jnp.sum(grad_query * query_norm, axis=0)
        grad_query_raw = head_back(grad_query * my_gain_query, query_norm, query_inv)
        grad_key = rotary(grad_keys, row_pos, col_pos, -1.0)
        gain_key_term = jnp.sum(grad_key * key_norm, axis=0)
        grad_key_raw = head_back(grad_key * my_gain_key, key_norm, key_inv)
        grad_projected = jnp.concatenate(
            [grad_query_raw, grad_key_raw, grad_values], axis=1
        ).astype(jnp.bfloat16)
        gain_capkey_term = jnp.sum(grad_capkeys * capkey_norm, axis=0)
        grad_capkey_raw = head_back(grad_capkeys * my_gain_capkey, capkey_norm, capkey_inv)
        grad_cap_proj = jnp.concatenate([grad_capkey_raw, grad_capvals], axis=1).astype(
            jnp.bfloat16
        )
        term_capkv = scatter_planes(swap_rows(contract_rows(cap_flat, grad_cap_proj)))
    grad_gate_f = grad_res0 * down_out * (1.0 - tanh_f * tanh_f)
    gate_head_term = gate_head_term * (1.0 - gate_tanh * gate_tanh)
    term_qkv = swap_rows(contract_rows(hidden1, grad_projected))
    grad_projected, term_qkv = lax.optimization_barrier((grad_projected, term_qkv))
    term_qkv = scatter_planes(term_qkv)
    grad_hidden1, *_ = multiply_plane(9, grad_projected, full_qkv, turned=True)
    gain_attn_term = jnp.sum(grad_hidden1 * normed1 * (1.0 + scale_a), axis=0)
    grad_scale_a = grad_hidden1 * normed1 * gain_attn
    input_grad = (
        grad_residual + norm_back(grad_hidden1 * gain_attn * (1.0 + scale_a), normed1, inverse1)
    ).astype(jnp.bfloat16)

    grad_mod_tok = jnp.concatenate([grad_scale_a, grad_gate_a, grad_scale_f, grad_gate_f], axis=1)
    grad_mod_doc = lax.dot_general(
        doc_pick,
        grad_mod_tok,
        (((0,), (0,)), ((), ())),
        precision=lax.Precision.HIGHEST,
        preferred_element_type=jnp.float32,
    )
    null_rows = nulls[cap_document] > 0
    null_sum = jnp.sum(
        jnp.where(null_rows[:, None], grad_cap_proj.astype(jnp.float32), 0.0), axis=0
    )
    null_term = jnp.dot(
        full_capkv.astype(jnp.float32), null_sum, precision=lax.Precision.HIGHEST
    )

    sum_down = all_down.reshape(w_down.shape).astype(jnp.float32)
    sum_gateup = spread_parts(all_gateup, 2 * planes)
    sum_out = spread_parts(all_out, 1)

    def at_mine(part):
        whole = jnp.zeros((tp,) + part.shape, jnp.float32)
        return lax.dynamic_update_index_in_dim(whole, part, me_t, 0).reshape(-1)

    small = jnp.concatenate(
        [
            gain_attn_term,
            gain_ffn_term,
            at_mine(gain_query_term),
            at_mine(gain_key_term),
            at_mine(gain_capkey_term),
            at_mine(gate_head_term),
            null_term,
        ]
    )
    small_rows = 8 - DOCS
    small_size = small.shape[0]
    small = jnp.pad(small, (0, small_rows * 4 * width - small_size))
    (all_capkv, all_qkv), input_grad, totals = finale_plane(
        12,
        [term_capkv, term_qkv],
        input_grad,
        jnp.concatenate([grad_mod_doc, small.reshape(small_rows, 4 * width)], axis=0),
    )
    totals = totals.reshape(groups, 8, 4 * width)
    sum_capkv = spread_parts(all_capkv, 2)
    sum_qkv = spread_parts(all_qkv, 3)
    grad_mod_docs = totals[:, :DOCS].reshape(groups * DOCS, 4 * width)
    sum_mod = lax.dot_general(
        cond_mine,
        grad_mod_docs,
        (((0,), (0,)), ((), ())),
        precision=lax.Precision.HIGHEST,
        preferred_element_type=jnp.float32,
    )
    sum_bias = jnp.sum(grad_mod_docs, axis=0)
    small = jnp.sum(totals[:, DOCS:], axis=0).reshape(-1)[:small_size]
    ends = [width, 2 * width, 3 * width, 4 * width, 5 * width, 5 * width + HEADS]
    small_parts = jnp.split(small, ends)
    return (
        result,
        input_grad,
        sum_qkv,
        sum_out,
        sum_capkv,
        sum_gateup,
        sum_down,
        sum_mod,
        sum_bias,
        *small_parts,
    )


def solution(mesh):
    planes = mesh.shape["seq"]
    cores = mesh.shape["bucket"] // planes
    split = Mesh(mesh.devices.reshape(planes, cores, planes), ("tp", "core", "seq"))
    group = ("tp", "core")
    token = P(("tp", "core", "seq"), None)
    weight = P("seq", None)
    placed = (
        token,
        token,
        P(group, None, None),
        P(group, None, "seq", None),
        P(group, None),
        P(group),
        P(group, None),
        *([weight] * 6),
        *([P()] * 8),
    )
    return jax.shard_map(
        shards,
        mesh=split,
        in_specs=placed,
        out_specs=(token, token, *([weight] * 6), *([P()] * 8)),
        check_vma=False,
    )
```

```python
import functools

import jax
import jax.numpy as jnp
from jax import lax
from jax.experimental import pallas as pl
from jax.experimental.pallas import tpu as pltpu
from jax.sharding import Mesh, PartitionSpec as P

HEADS = 24
HDIM = 64
DOCS = 4
RES = 4


eps = 1e-06

MESH = pl.DeviceIdType.MESH
VMEM_BYTES = 60 * 1024 * 1024


def neighbours():
    me = lax.axis_index("tp")
    return me, me + 1 - 2 * lax.rem(me, 2), lax.rem(me + 2, 4), 3 - me


def greet(places):
    barrier = pltpu.get_barrier_semaphore()
    for place in places:
        pl.semaphore_signal(barrier, inc=1, device_id=place, device_id_type=MESH)
    pl.semaphore_wait(barrier, len(places))


def send(source, target, sems, index, place):
    return pltpu.make_async_remote_copy(
        src_ref=source,
        dst_ref=target,
        send_sem=sems[0].at[index],
        recv_sem=sems[1].at[index],
        device_id=place,
        device_id_type=MESH,
    )


def tile_of(width):
    for tile in (512, 384, 256, 128):
        if width % tile == 0:
            return tile
    return width


def multiply(left, weight_ref, columns, turned):
    if turned:
        return lax.dot_general(
            left, weight_ref[columns, 0 : left.shape[1]], (((1,), (1,)), ((), ())),
            preferred_element_type=jnp.float32,
        )
    return jnp.dot(left, weight_ref[:, columns], preferred_element_type=jnp.float32)


def bind(refs, counts, *riders):
    refs, own = list(refs), []
    for kind in range(3):
        own += refs[: counts[kind]]
        refs = refs[counts[kind] :]
        for rider in riders:
            count = rider.counts[kind]
            rider.refs[kind] = refs[:count]
            refs = refs[count:]
    return own


class Aside:
    def __init__(self, operands, outs, scratch, steps):
        self.operands, self.outs, self.steps = operands, outs, steps
        self.in_specs = [pl.BlockSpec(memory_space=pl.ANY)] * len(operands)
        self.out_specs = [pl.BlockSpec(memory_space=pltpu.VMEM)] * len(outs)
        self.scratch = [
            *[pltpu.VMEM(x.shape, x.dtype) for x in operands],
            pltpu.SemaphoreType.DMA((max(len(operands), 1),)),
            *scratch,
        ]
        self.counts = (len(operands), len(outs), len(self.scratch))
        self.refs = [None] * 3

    def load(self):
        count = len(self.operands)
        sem = self.refs[2][count]
        self.loads = [
            pltpu.make_async_copy(self.refs[0][i], self.refs[2][i], sem.at[i])
            for i in range(count)
        ]
        for copy in self.loads:
            copy.start()

    def step(self, index):
        count = len(self.operands)
        if index == 0:
            for copy in self.loads:
                copy.wait()
        if self.steps:
            self.steps(index, self.refs[2][:count], self.refs[1], self.refs[2][count + 1 :])


def nothing():
    return Aside([], [], [], None)


class Finish:
    def __init__(self, operands, outs, work):
        self.operands, self.outs, self.work = operands, outs, work
        hbm = pl.BlockSpec(memory_space=pl.ANY)
        self.in_specs, self.out_specs = [hbm] * len(operands), [hbm] * len(outs)
        self.scratch = [
            *[pltpu.VMEM(x.shape, x.dtype) for x in operands],
            *[pltpu.VMEM(x.shape, x.dtype) for x in outs],
            pltpu.SemaphoreType.DMA((max(len(operands), 1),)),
            pltpu.SemaphoreType.DMA((4 * max(len(outs), 1),)),
        ]
        self.counts = (len(operands), len(outs), len(self.scratch))
        self.refs = [None] * 3

    def load(self):
        count = len(self.operands)
        self.ins, self.made = self.refs[2][:count], self.refs[2][count:-2]
        sem = self.refs[2][-2]
        self.loads = [
            pltpu.make_async_copy(self.refs[0][i], self.ins[i], sem.at[i]) for i in range(count)
        ]
        for copy in self.loads:
            copy.start()
        self.copies = []

    def run(self, index, owner, product):
        if not self.work:
            return
        if index == 0:
            for copy in self.loads:
                copy.wait()
        made = [ref.at[owner] for ref in self.made]
        self.work(product, [ref.at[owner] for ref in self.ins], made)
        for i, ref in enumerate(made):
            copy = pltpu.make_async_copy(
                ref, self.refs[1][i].at[owner], self.refs[2][-1].at[4 * i + index]
            )
            copy.start()
            self.copies.append(copy)

    def end(self):
        for copy in self.copies:
            copy.wait()


class Trade:
    def __init__(self, *items):
        self.items = items
        hbm = pl.BlockSpec(memory_space=pl.ANY)
        self.operands = [item[0] for item in items]
        self.outs = [jax.ShapeDtypeStruct(item[2], item[0].dtype) for item in items]
        self.in_specs = self.out_specs = [hbm] * len(items)
        count = max(len(items), 1)
        self.scratch = [pltpu.SemaphoreType.DMA((n,)) for n in (count, 3 * count, 3 * count)]
        self.counts = (len(items), len(items), 3)
        self.refs = [None] * 3

    def begin(self):
        local, *sems = self.refs[2]
        self.copies, self.local = [], []
        for i, (_, axis, _, source, target) in enumerate(self.items):
            from_ref, to_ref = self.refs[0][i], self.refs[1][i]
            if axis == "tp":
                here, *others = neighbours()
            else:
                here, others = planes_after()
            self.local.append(
                pltpu.make_async_copy(source(from_ref, here), target(to_ref, here), local.at[i])
            )
            self.copies += [
                send(source(from_ref, p), target(to_ref, here), sems, 3 * i + k, {axis: p})
                for k, p in enumerate(others)
            ]
        for copy in self.local + self.copies:
            copy.start()

    def end(self):
        for copy in self.local + self.copies:
            copy.wait()


def block_of(ref, place):
    return ref.at[place]


def swap_blocks(x, axis):
    return (x, axis, x.shape, block_of, block_of)


def gather_kernel(turned, halved, early, aside, trade, finish, keep, *refs):
    refs = bind(refs, (2, 1 + halved + keep, 7), aside, trade, finish)
    x_ref, w_ref, all_ref, *refs = refs
    if halved:
        full_ref, *refs = refs
    if keep:
        y_ref, *refs = refs
    xbuf, wbuf, ybuf, load, done, *sems = refs
    me, across, along, far = neighbours()
    rows = x_ref.shape[0]
    half = rows // 2
    core = lax.axis_index("core")
    places = [{"tp": across}, {"tp": along}]
    if halved:
        places.append({"core": 1 - core})
    mine = pltpu.make_async_copy(x_ref, xbuf.at[me], load.at[0])
    mine.start()
    if halved:
        planes, part, _ = w_ref.shape
        places_of = [
            pl.ds(pl.multiple_of((z * 2 + core) * part, part), part) for z in range(planes)
        ]
        weights = [
            pltpu.make_async_copy(w_ref.at[z], wbuf.at[places_of[z]], load.at[1 + z])
            for z in range(planes)
        ]
    else:
        weights = [pltpu.make_async_copy(w_ref, wbuf, load.at[1])]
    for copy in weights:
        copy.start()
    if trade.items:
        greet_all()
    else:
        greet(places)

    def block(owner, part):
        return xbuf.at[owner, pl.ds(part * half, half)]

    def pass_on(index, owner, part, place):
        return send(block(owner, part), block(owner, part), sems, index, place)

    first = [
        send(x_ref.at[pl.ds(0, half)], block(me, 0), sems, 0, {"tp": across}),
        send(x_ref.at[pl.ds(half, half)], block(me, 1), sems, 1, {"tp": along}),
        send(x_ref.at[pl.ds(half, half)], block(me, 1), sems, 2, {"tp": across}),
        send(x_ref.at[pl.ds(0, half)], block(me, 0), sems, 3, {"tp": along}),
    ]
    for copy in first:
        copy.start()
    swaps = []
    if halved:
        for z in range(planes):
            swaps.append(send(w_ref.at[z], wbuf.at[places_of[z]], sems, 6 + z, {"core": 1 - core}))
        for copy in swaps:
            copy.start()
    trade.begin()
    aside.load()
    finish.load()
    mine.wait()
    for copy in weights:
        copy.wait()
    for step in range(early):
        aside.step(step)
    first[0].wait_recv()
    on_a = pass_on(4, across, 0, {"tp": along})
    on_a.start()
    first[1].wait_recv()
    on_b = pass_on(5, along, 1, {"tp": across})
    on_b.start()
    for copy in swaps:
        copy.wait()
    for step in range(early, 3):
        aside.step(step)

    tile = tile_of(ybuf.shape[-1])
    outs = []
    if halved:
        outs.append(pltpu.make_async_copy(wbuf, full_ref, done.at[4]))
        outs[-1].start()

    def compute(owner, index):
        @pl.loop(0, ybuf.shape[-1] // tile)
        def _(step):
            columns = pl.ds(pl.multiple_of(step * tile, tile), tile)
            ybuf[index, :, columns] = multiply(xbuf[owner], wbuf, columns, turned).astype(
                ybuf.dtype
            )

        if keep:
            copy = pltpu.make_async_copy(ybuf.at[index], y_ref.at[owner], done.at[index])
            copy.start()
            outs.append(copy)
        finish.run(index, owner, ybuf.at[index])

    compute(me, 0)
    first[2].wait_recv()
    compute(across, 1)
    first[3].wait_recv()
    compute(along, 2)
    on_a.wait_recv()
    on_b.wait_recv()
    copy = pltpu.make_async_copy(xbuf, all_ref, load.at[0])
    copy.start()
    outs.append(copy)
    compute(far, 3)
    for copy in first + [on_a, on_b]:
        copy.wait_send()
    for copy in outs:
        copy.wait()
    finish.end()
    trade.end()


def gather_matmul(
    ident, x, w, turned=False, halved=False, width=None, aside=None, early=3, trade=(),
    finish=None, keep=True,
):
    rows, depth = x.shape
    if halved:
        planes, part, columns = w.shape
        whole = (planes * 2 * part, columns)
    else:
        whole = w.shape
    width = width or (whole[0] if turned else whole[1])
    riders = [aside or nothing(), Trade(*trade), finish or Finish([], [], None)]
    shapes = [jax.ShapeDtypeStruct((4, rows, depth), x.dtype)]
    if halved:
        shapes.append(jax.ShapeDtypeStruct(whole, w.dtype))
    if keep:
        shapes.append(jax.ShapeDtypeStruct((4, rows, width), jnp.float32))
    hbm = pl.BlockSpec(memory_space=pl.ANY)
    got = pl.pallas_call(
        functools.partial(gather_kernel, turned, halved, early, *riders, keep),
        out_shape=shapes + [y for rider in riders for y in rider.outs],
        in_specs=[hbm, hbm] + [y for rider in riders for y in rider.in_specs],
        out_specs=[hbm] * len(shapes) + [y for rider in riders for y in rider.out_specs],
        scratch_shapes=[
            pltpu.VMEM((4, rows, depth), x.dtype),
            pltpu.VMEM(whole, w.dtype),
            pltpu.VMEM((4, rows, width), jnp.float32),
            pltpu.SemaphoreType.DMA((6,)),
            pltpu.SemaphoreType.DMA((5,)),
            pltpu.SemaphoreType.DMA((10,)),
            pltpu.SemaphoreType.DMA((10,)),
            *[y for rider in riders for y in rider.scratch],
        ],
        compiler_params=pltpu.CompilerParams(
            collective_id=ident, has_side_effects=True, vmem_limit_bytes=VMEM_BYTES
        ),
        cost_estimate=pl.CostEstimate(
            flops=8 * rows * depth * width,
            bytes_accessed=30 * 3_000_000,
            transcendentals=0,
        ),
        name="gather_matmul",
    )(x, w, *[y for rider in riders for y in rider.operands])
    return [
        got[0].reshape(4 * rows, depth),
        got[1] if halved else w,
        *[part.reshape(4 * rows, width) for part in got[1 + halved : len(shapes)]],
        *got[len(shapes) :],
    ]


def head_finish(rows, width, gain):
    def work(product, ins, outs):
        (gain_ref,), (out_ref,) = ins, outs
        size = width // 2
        for at in range(0, size, 128):
            keys = pair_norm(product[:, at : at + 128])[0] * gain_ref[:, at : at + 128]
            out_ref[:, at : at + 128] = keys.astype(out_ref.dtype)
        out_ref[:, size:] = product[:, size:].astype(out_ref.dtype)

    gains = jnp.broadcast_to(gain[None], (4, 1, width // 2))
    return Finish([gains], [jax.ShapeDtypeStruct((4, rows, width), jnp.bfloat16)], work)


def swiglu_finish(grads):
    rows, size = grads.shape[0] // 4, grads.shape[1]

    def work(product, ins, outs):
        (grad_ref,), (ffn_ref, back_ref) = ins, outs

        @pl.loop(0, rows // 32)
        def _(step):
            strip = pl.ds(pl.multiple_of(step * 32, 32), 32)
            for at in range(0, size, 256):
                lanes, ups = pl.ds(at, 256), pl.ds(size + at, 256)
                gate, up, grad = product[strip, lanes], product[strip, ups], grad_ref[strip, lanes]
                sig = 1.0 / (1.0 + jnp.exp(-gate))
                silu = gate * sig
                ffn_ref[strip, lanes] = (silu * up).astype(ffn_ref.dtype)
                back = grad * up * sig * (1.0 + gate * (1.0 - sig))
                back_ref[strip, lanes] = back.astype(back_ref.dtype)
                back_ref[strip, ups] = (grad * silu).astype(back_ref.dtype)

    return Finish(
        [grads.reshape(4, rows, size)],
        [jax.ShapeDtypeStruct((4, rows, n), jnp.bfloat16) for n in (size, 2 * size)],
        work,
    )


def scatter_kernel(turned, aside, trade, *refs):
    refs = bind(refs, (2, 1, 10), aside, trade)
    x_hbm, w_hbm, out_ref, sums, far_out, near_out, relay, land, s0, s1, x_ref, w_ref, load = refs
    me, across, along, far = neighbours()
    sems = (s0, s1)
    rows, width = out_ref.shape
    half = rows // 2
    top, low = pl.ds(0, half), pl.ds(half, half)
    tile = tile_of(width)
    to_across, to_along = {"tp": across}, {"tp": along}
    weights = pltpu.make_async_copy(w_hbm, w_ref, load.at[4])
    weights.start()
    blocks = {}
    for k, owner in enumerate((far, across, along, me)):
        blocks[k] = pltpu.make_async_copy(x_hbm.at[owner], x_ref.at[owner], load.at[k])
        blocks[k].start()
    aside.load()
    if trade.items:
        greet_all()
    else:
        greet([to_across, to_along])

    def tiles(body):
        @pl.loop(0, width // tile)
        def _(step):
            body(pl.ds(pl.multiple_of(step * tile, tile), tile))

    def product(owner, columns, part=slice(None)):
        return multiply(x_ref[owner, part], w_ref, columns, turned)

    weights.wait()
    blocks[0].wait()

    @tiles
    def _(columns):
        far_out[top, columns] = product(far, columns, top).astype(far_out.dtype)

    far_a = send(far_out.at[top], relay.at[0], sems, 0, to_across)
    far_a.start()

    @tiles
    def _(columns):
        far_out[low, columns] = product(far, columns, low).astype(far_out.dtype)

    far_b = send(far_out.at[low], relay.at[1], sems, 1, to_along)
    far_b.start()
    blocks[1].wait()

    @tiles
    def _(columns):
        part = product(across, columns)
        near_out[0, top, columns] = part[:half].astype(near_out.dtype)
        sums[0, :, columns] = part[half:]

    across_a = send(near_out.at[0, top], land.at[0, top], sems, 2, to_across)
    across_a.start()
    blocks[2].wait()

    @tiles
    def _(columns):
        part = product(along, columns)
        near_out[1, low, columns] = part[half:].astype(near_out.dtype)
        sums[1, :, columns] = part[:half]

    along_b = send(near_out.at[1, low], land.at[1, low], sems, 3, to_along)
    along_b.start()
    trade.begin()
    aside.step(0)
    far_b.wait_recv()

    @tiles
    def _(columns):
        near_out[0, low, columns] = (
            sums[0, :, columns] + relay[1, :, columns].astype(jnp.float32)
        ).astype(near_out.dtype)

    across_b = send(near_out.at[0, low], land.at[0, low], sems, 4, to_across)
    across_b.start()
    far_a.wait_recv()

    @tiles
    def _(columns):
        near_out[1, top, columns] = (
            sums[1, :, columns] + relay[0, :, columns].astype(jnp.float32)
        ).astype(near_out.dtype)

    along_a = send(near_out.at[1, top], land.at[1, top], sems, 5, to_along)
    along_a.start()
    aside.step(1)
    aside.step(2)
    blocks[3].wait()

    @tiles
    def _(columns):
        out_ref[:, columns] = product(me, columns)

    for copy in (across_a, along_b, across_b, along_a):
        copy.wait_recv()

    @tiles
    def _(columns):
        out_ref[:, columns] += land[0, :, columns].astype(jnp.float32) + land[
            1, :, columns
        ].astype(jnp.float32)

    for copy in (far_a, far_b, across_a, along_b, across_b, along_a):
        copy.wait_send()
    trade.end()


def matmul_scatter(ident, x, w, turned=False, aside=None, trade=()):
    aside, trade = aside or nothing(), Trade(*trade)
    rows, depth = x.shape[0] // 4, x.shape[1]
    width = w.shape[0] if turned else w.shape[1]
    vmem = pl.BlockSpec(memory_space=pltpu.VMEM)
    return pl.pallas_call(
        functools.partial(scatter_kernel, turned, aside, trade),
        out_shape=[jax.ShapeDtypeStruct((rows, width), jnp.float32)] + aside.outs + trade.outs,
        in_specs=[pl.BlockSpec(memory_space=pl.ANY)] * 2 + aside.in_specs + trade.in_specs,
        out_specs=[vmem] + aside.out_specs + trade.out_specs,
        scratch_shapes=[
            pltpu.VMEM((2, rows // 2, width), jnp.float32),
            pltpu.VMEM((rows, width), jnp.bfloat16),
            pltpu.VMEM((2, rows, width), jnp.bfloat16),
            pltpu.VMEM((2, rows // 2, width), jnp.bfloat16),
            pltpu.VMEM((2, rows, width), jnp.bfloat16),
            pltpu.SemaphoreType.DMA((6,)),
            pltpu.SemaphoreType.DMA((6,)),
            pltpu.VMEM((4, rows, depth), x.dtype),
            pltpu.VMEM(w.shape, w.dtype),
            pltpu.SemaphoreType.DMA((5,)),
            *aside.scratch,
            *trade.scratch,
        ],
        compiler_params=pltpu.CompilerParams(
            collective_id=ident, has_side_effects=True, vmem_limit_bytes=VMEM_BYTES
        ),
        cost_estimate=pl.CostEstimate(
            flops=8 * rows * depth * width,
            bytes_accessed=30 * 3_000_000,
            transcendentals=0,
        ),
        name="matmul_scatter",
    )(x.reshape(4, rows, depth), w, *aside.operands, *trade.operands)


class Gathering:
    def __init__(self, ins, outs, load, sems):
        self.ins, self.outs, self.sems = ins, outs, sems
        self.me, self.across, self.along, self.far = neighbours()
        self.core = lax.axis_index("core")
        self.to_across, self.to_along = {"tp": self.across}, {"tp": self.along}
        self.to_core = {"core": 1 - self.core}
        self.local = [
            pltpu.make_async_copy(x, outs[i].at[self.me, self.core], load.at[i])
            for i, x in enumerate(ins)
        ]
        for copy in self.local:
            copy.start()

    def half(self, i, part):
        rows = self.ins[i].shape[0] // 2
        return pl.ds(part * rows, rows)

    def first(self, i, part, index, place):
        rows = self.half(i, part)
        target = self.outs[i].at[self.me, self.core, rows]
        return send(self.ins[i].at[rows], target, self.sems, 10 * i + index, place)

    def pass_on(self, i, owner, part, index, place):
        block = self.outs[i].at[owner, self.core, self.half(i, part)]
        return send(block, block, self.sems, 10 * i + index, place)

    def to_sibling(self, i, owner, index):
        block = self.outs[i].at[owner, self.core]
        return send(block, block, self.sems, 10 * i + index, self.to_core)

    def begin(self):
        self.begun = []
        for i, x in enumerate(self.ins):
            target = self.outs[i].at[self.me, self.core]
            copies = [
                self.first(i, 0, 0, self.to_across),
                self.first(i, 1, 1, self.to_along),
                self.first(i, 1, 2, self.to_across),
                self.first(i, 0, 3, self.to_along),
                send(x, target, self.sems, 10 * i + 6, self.to_core),
            ]
            for copy in copies:
                copy.start()
            self.begun.append(copies)

    def relay(self):
        for i, copies in enumerate(self.begun):
            copies[0].wait_recv()
            copies.append(self.pass_on(i, self.across, 0, 4, self.to_along))
            copies[5].start()
            copies[1].wait_recv()
            copies.append(self.pass_on(i, self.along, 1, 5, self.to_across))
            copies[6].start()

    def hand(self):
        for i, copies in enumerate(self.begun):
            copies[2].wait_recv()
            copies.append(self.to_sibling(i, self.across, 7))
            copies[7].start()
            copies[3].wait_recv()
            copies.append(self.to_sibling(i, self.along, 8))
            copies[8].start()
            copies[5].wait_recv()
            copies[6].wait_recv()
            copies.append(self.to_sibling(i, self.far, 9))
            copies[9].start()

    def end(self):
        for copies, local in zip(self.begun, self.local):
            for copy in copies[4:5] + copies[7:]:
                copy.wait_recv()
            for copy in copies:
                copy.wait_send()
            local.wait()


class Returning:
    def __init__(self, back, home, stage, load, sems, base):
        self.back, self.home, self.stage, self.load = back, home, stage, load
        self.sems, self.base = sems, base
        self.me, *self.peers = neighbours()
        self.plane, self.others = planes_after()
        self.stay = pltpu.make_async_copy(back.at[self.plane], stage.at[self.plane], load)
        self.keep = pltpu.make_async_copy(stage.at[self.me], home.at[self.me], load)

    def begin(self):
        self.stay.start()
        self.out = [
            send(
                self.back.at[p], self.stage.at[self.plane], self.sems, self.base + k, {"seq": p}
            )
            for k, p in enumerate(self.others)
        ]
        for copy in self.out:
            copy.start()

    def turn(self):
        for copy in self.out:
            copy.wait_recv()
        self.stay.wait()
        self.last = [
            send(
                self.stage.at[p], self.home.at[self.me], self.sems, self.base + 3 + k, {"tp": p}
            )
            for k, p in enumerate(self.peers)
        ]
        for copy in self.last:
            copy.start()
        self.keep.start()

    def end(self):
        for copy in self.last:
            copy.wait_recv()
        self.keep.wait()
        for copy in self.out + self.last:
            copy.wait_send()


class Home:
    def __init__(self, backs):
        self.outs, self.operands, self.scratch = [], [], []
        for back in backs:
            tall, wide = back.shape
            blocks = (4, tall // 4, wide)
            self.operands.append(back.reshape(blocks))
            self.outs.append(jax.ShapeDtypeStruct(blocks, back.dtype))
            self.scratch += [
                pltpu.VMEM(blocks, back.dtype),
                *[pltpu.SemaphoreType.DMA((n,)) for n in (1, 6, 6)],
            ]
        self.in_specs = self.out_specs = [pl.BlockSpec(memory_space=pl.ANY)] * len(self.outs)
        self.counts = (len(self.operands), len(self.outs), len(self.scratch))
        self.refs = [None] * 3

    def begin(self):
        self.ways = []
        for i, (back, home) in enumerate(zip(*self.refs[:2])):
            stage, load, *sems = self.refs[2][4 * i : 4 * i + 4]
            self.ways.append(Returning(back, home, stage, load.at[0], sems, 0))
        for way in self.ways:
            way.begin()

    def turn(self):
        for way in self.ways:
            way.turn()

    def end(self):
        for way in self.ways:
            way.end()


class Total:
    def __init__(self, x):
        vmem = pl.BlockSpec(memory_space=pltpu.VMEM)
        self.outs, self.operands, self.scratch = [], [], []
        if x is not None:
            rows, width = x.shape
            self.operands = [x]
            self.outs = [jax.ShapeDtypeStruct((4, 2, rows, width), jnp.float32)]
            self.scratch = [
                pltpu.VMEM((3, rows, width // 4), jnp.float32),
                *[pltpu.SemaphoreType.DMA((10,))] * 2,
            ]
        self.in_specs = self.out_specs = [vmem] * len(self.outs)
        self.counts = (len(self.operands), len(self.outs), len(self.scratch))
        self.refs = [None] * 3

    def begin(self):
        if not self.operands:
            return
        (x_ref,), (out_ref,), (land, *sems) = self.refs
        me, *peers = neighbours()
        core = lax.axis_index("core")
        plane, others = planes_after()
        quarter = x_ref.shape[1] // 4

        def columns(t):
            return pl.ds(pl.multiple_of(t * quarter, quarter), quarter)

        self.first = [
            send(x_ref.at[:, columns(p)], land.at[k], sems, k, {"tp": p})
            for k, p in enumerate(peers)
        ]
        for copy in self.first:
            copy.start()

    def go_on(self):
        if not self.operands:
            return
        (x_ref,), (out_ref,), (land, *sems) = self.refs
        me, *peers = neighbours()
        core = lax.axis_index("core")
        plane, others = planes_after()
        quarter = x_ref.shape[1] // 4

        def columns(t):
            return pl.ds(pl.multiple_of(t * quarter, quarter), quarter)

        for copy in self.first:
            copy.wait_recv()
        mine = (x_ref[:, columns(me)] + land[0]) + (land[1] + land[2])
        out_ref[plane, core, :, columns(me)] = mine
        here = out_ref.at[plane, core, :, columns(me)]
        second = [send(here, here, sems, 3 + k, {"seq": p}) for k, p in enumerate(others)]
        for copy in second:
            copy.start()
        for copy in second:
            copy.wait_recv()
        here = out_ref.at[:, core, :, columns(me)]
        self.third = [send(here, here, sems, 6 + k, {"tp": p}) for k, p in enumerate(peers)]
        for copy in self.third:
            copy.start()
        self.copies = self.first + second + self.third

    def end(self):
        if not self.operands:
            return
        (_,), (out_ref,), (_, *sems) = self.refs
        core = lax.axis_index("core")
        for copy in self.third:
            copy.wait_recv()
        here = out_ref.at[:, core]
        swap = send(here, here, sems, 9, {"core": 1 - core})
        swap.start()
        swap.wait_recv()
        for copy in self.copies + [swap]:
            copy.wait_send()


def collect_kernel(count, aside, trade, home, total, *refs):
    refs = bind(refs, (count, count, 3), aside, trade, home, total)
    load, *sems = refs[2 * count :]
    gathering = Gathering(refs[:count], refs[count : 2 * count], load, sems)
    if trade.items or home.operands or total.operands:
        greet_all()
    else:
        greet([gathering.to_across, gathering.to_along, gathering.to_core])
    total.begin()
    gathering.begin()
    total.go_on()
    trade.begin()
    home.begin()
    aside.load()
    aside.step(0)
    gathering.relay()
    aside.step(1)
    home.turn()
    gathering.hand()
    aside.step(2)
    trade.end()
    total.end()
    home.end()
    gathering.end()


def collect(ident, pieces, aside=None, trade=(), backs=(), sums=None):
    riders = [aside or nothing(), Trade(*trade), Home(backs), Total(sums)]
    hbm = pl.BlockSpec(memory_space=pl.ANY)
    count = len(pieces)
    got = pl.pallas_call(
        functools.partial(collect_kernel, count, *riders),
        out_shape=[
            *[jax.ShapeDtypeStruct((4, 2) + p.shape, p.dtype) for p in pieces],
            *[x for rider in riders for x in rider.outs],
        ],
        in_specs=[hbm] * count + [x for rider in riders for x in rider.in_specs],
        out_specs=[hbm] * count + [x for rider in riders for x in rider.out_specs],
        scratch_shapes=[
            pltpu.SemaphoreType.DMA((count,)),
            pltpu.SemaphoreType.DMA((10 * count,)),
            pltpu.SemaphoreType.DMA((10 * count,)),
            *[x for rider in riders for x in rider.scratch],
        ],
        compiler_params=pltpu.CompilerParams(
            collective_id=ident, has_side_effects=True, vmem_limit_bytes=VMEM_BYTES
        ),
        cost_estimate=pl.CostEstimate(
            flops=0, bytes_accessed=80 * sum(p.size for p in pieces), transcendentals=0
        ),
        name="collect",
    )(*pieces, *[x for rider in riders for x in rider.operands])
    return got[:count], got[count:]


def spread_kernel(parts, in_ref, out_ref):
    size = in_ref.shape[-1] // parts
    for q in range(parts):
        for t in range(4):
            out_ref[:, pl.ds((q * 4 + t) * size, size)] = in_ref[
                t, 0, :, pl.ds(q * size, size)
            ].astype(jnp.float32)


def spread(blocks, parts):
    _, cores, rows, width = blocks.shape
    cut = 2
    tall = rows // cut
    return pl.pallas_call(
        functools.partial(spread_kernel, parts),
        grid=(cores, cut),
        out_shape=jax.ShapeDtypeStruct((cores * rows, 4 * width), jnp.float32),
        in_specs=[pl.BlockSpec((4, 1, tall, width), lambda c, k: (0, c, k, 0))],
        out_specs=pl.BlockSpec((tall, 4 * width), lambda c, k: (c * cut + k, 0)),
        compiler_params=pltpu.CompilerParams(vmem_limit_bytes=32 * 1024 * 1024),
        cost_estimate=pl.CostEstimate(
            flops=0, bytes_accessed=6 * blocks.size, transcendentals=0
        ),
        name="spread",
    )(blocks)


def planes_after():
    plane = lax.axis_index("seq")
    return plane, [lax.rem(plane + k, 4) for k in (1, 2, 3)]


def greet_all():
    _, across, along, far = neighbours()
    _, others = planes_after()
    greet(
        [{"tp": p} for p in (across, along, far)]
        + [{"core": 1 - lax.axis_index("core")}]
        + [{"seq": p} for p in others]
    )


def arrive_kernel(
    tok_ref, cot_ref, msg_ref, w_ref, qkv_ref, wout_ref, down_ref, gateup_ref,
    in_ref, cots_ref, msgs_ref, mod_ref, qkv_cut, down_cut, gateup_cut,
    stage, wbuf, part, land, qkv_buf, down_buf, gateup_buf, load, cuts, s0, s1,
):
    sems = (s0, s1)
    me, across, along, far = neighbours()
    core = lax.axis_index("core")
    plane, others = planes_after()
    peers = [across, along, far]
    quarter = mod_ref.shape[1] // 4
    depth = msgs_ref.shape[-1]
    columns = pl.ds(pl.multiple_of(me * quarter, quarter), quarter)
    weights = pltpu.make_async_copy(w_ref.at[:, columns], wbuf, load.at[0])
    weights.start()
    cutting = []

    def cut(source, target, parts, at):
        rows, size = target.shape[0], source.shape[1] // (parts * 4)
        for q in range(parts):
            lanes = pl.ds(pl.multiple_of((q * 4 + me) * size, size), size)
            cutting.append(
                pltpu.make_async_copy(
                    source.at[pl.ds(pl.multiple_of(core * rows, rows), rows), lanes],
                    target.at[:, pl.ds(at + q * size, size)],
                    cuts.at[len(cutting)],
                )
            )

    cut(qkv_ref, qkv_buf, 3, 0)
    cut(wout_ref, qkv_buf, 1, qkv_ref.shape[1] // 4)
    cut(gateup_ref, gateup_buf, 8, 0)
    share = down_cut.shape[0]
    rows = pl.ds(pl.multiple_of((me * 2 + core) * share, share), share)
    cutting.append(pltpu.make_async_copy(down_ref.at[rows], down_buf, cuts.at[len(cutting)]))
    for copy in cutting:
        copy.start()
    keeping = [
        pltpu.make_async_copy(source, target, cuts.at[13 + k])
        for k, (source, target) in enumerate(
            zip((qkv_buf, down_buf, gateup_buf), (qkv_cut, down_cut, gateup_cut))
        )
    ]
    mine = pltpu.make_async_copy(tok_ref.at[me], stage.at[me], load.at[1])
    mine.start()
    msgs_ref[me, core] = msg_ref[:, pl.ds(pl.multiple_of(plane * depth, depth), depth)]
    greet_all()
    here = msgs_ref.at[me, core]
    first = [send(here, here, sems, k, {"tp": p}) for k, p in enumerate(peers)]
    for copy in first:
        copy.start()
    spread_out = [
        send(tok_ref.at[p], stage.at[me], sems, 3 + k, {"tp": p}) for k, p in enumerate(peers)
    ]
    for copy in spread_out:
        copy.start()
    cotangents = [
        send(cot_ref.at[p], cots_ref.at[me], sems, 16 + k, {"tp": p}) for k, p in enumerate(peers)
    ]
    for copy in cotangents:
        copy.start()
    own_cots = pltpu.make_async_copy(cot_ref.at[me], cots_ref.at[me], load.at[3])
    own_cots.start()
    for copy in first:
        copy.wait_recv()
    here = msgs_ref.at[:, core]
    swap = send(here, here, sems, 6, {"core": 1 - core})
    swap.start()
    weights.wait()
    conditions = msgs_ref[:, core].reshape(4 * 8, depth).astype(wbuf.dtype)
    tile = 512
    for copy in cutting:
        copy.wait()
    for copy in keeping:
        copy.start()
    for step in range(quarter // tile):
        at = pl.ds(step * tile, tile)
        part[:, :, at] = jnp.dot(
            conditions, wbuf[:, at], preferred_element_type=jnp.float32
        ).reshape(4, 8, tile)
    second = [
        send(part.at[p], land.at[k], sems, 7 + k, {"seq": p}) for k, p in enumerate(others)
    ]
    for copy in second:
        copy.start()
    mine.wait()
    for copy in spread_out:
        copy.wait_recv()
    third = [
        send(stage.at[p], in_ref.at[plane], sems, 10 + k, {"seq": p})
        for k, p in enumerate(others)
    ]
    for copy in third:
        copy.start()
    stay = pltpu.make_async_copy(stage.at[plane], in_ref.at[plane], load.at[2])
    stay.start()
    for copy in second:
        copy.wait_recv()
    mod_ref[:, columns] = (part[plane] + land[0]) + (land[1] + land[2])
    here = mod_ref.at[:, columns]
    fourth = [send(here, here, sems, 13 + k, {"tp": p}) for k, p in enumerate(peers)]
    for copy in fourth:
        copy.start()
    swap.wait_recv()
    for copy in fourth + third + cotangents:
        copy.wait_recv()
    stay.wait()
    own_cots.wait()
    for copy in keeping:
        copy.wait()
    for copy in first + spread_out + cotangents + [swap] + second + third + fourth:
        copy.wait_send()


def arrive(ident, tokens, cotangent, message, w_mod, w_qkv, w_out, w_down, w_gateup):
    rows, width = tokens.shape
    share, kind = w_qkv.shape[0] // 2, w_qkv.dtype
    depth, wide = w_mod.shape
    vmem, hbm = pl.BlockSpec(memory_space=pltpu.VMEM), pl.BlockSpec(memory_space=pl.ANY)
    return pl.pallas_call(
        arrive_kernel,
        out_shape=[
            jax.ShapeDtypeStruct((4, rows // 4, width), tokens.dtype),
            jax.ShapeDtypeStruct((4, rows // 4, width), cotangent.dtype),
            jax.ShapeDtypeStruct((4, 2, 8, depth), jnp.float32),
            jax.ShapeDtypeStruct((8, wide), jnp.float32),
            jax.ShapeDtypeStruct((share, (w_qkv.shape[1] + w_out.shape[1]) // 4), kind),
            jax.ShapeDtypeStruct((w_down.shape[0] // 8, w_down.shape[1]), kind),
            jax.ShapeDtypeStruct((share, w_gateup.shape[1] // 4), kind),
        ],
        in_specs=[hbm, hbm, vmem] + [hbm] * 5,
        out_specs=[hbm, hbm, vmem, vmem, hbm, hbm, hbm],
        scratch_shapes=[
            pltpu.VMEM((4, rows // 4, width), tokens.dtype),
            pltpu.VMEM((depth, wide // 4), w_mod.dtype),
            pltpu.VMEM((4, 8, wide // 4), jnp.float32),
            pltpu.VMEM((3, 8, wide // 4), jnp.float32),
            pltpu.VMEM((share, (w_qkv.shape[1] + w_out.shape[1]) // 4), kind),
            pltpu.VMEM((w_down.shape[0] // 8, w_down.shape[1]), kind),
            pltpu.VMEM((share, w_gateup.shape[1] // 4), kind),
            pltpu.SemaphoreType.DMA((4,)),
            pltpu.SemaphoreType.DMA((16,)),
            pltpu.SemaphoreType.DMA((19,)),
            pltpu.SemaphoreType.DMA((19,)),
        ],
        compiler_params=pltpu.CompilerParams(
            collective_id=ident, has_side_effects=True, vmem_limit_bytes=VMEM_BYTES
        ),
        cost_estimate=pl.CostEstimate(flops=0, bytes_accessed=90_000_000, transcendentals=0),
        name="arrive",
    )(
        tokens.reshape(4, rows // 4, width),
        cotangent.reshape(4, rows // 4, width),
        message,
        w_mod,
        w_qkv,
        w_out,
        w_down,
        w_gateup,
    )


def lanes_of(rows):
    return lax.broadcasted_iota(jnp.int32, (rows, 128), 1)


def pair_norm(values):
    lane = lanes_of(values.shape[0])
    square = values * values
    low = jnp.sum(jnp.where(lane < HDIM, square, 0.0), axis=-1, keepdims=True)
    high = jnp.sum(jnp.where(lane < HDIM, 0.0, square), axis=-1, keepdims=True)
    inverse = jnp.where(lane < HDIM, lax.rsqrt(low / HDIM + eps), lax.rsqrt(high / HDIM + eps))
    return values * inverse, inverse


def pair_back(grads, normed, inverse):
    lane = lanes_of(grads.shape[0])
    inner = grads * normed
    low = jnp.sum(jnp.where(lane < HDIM, inner, 0.0), axis=-1, keepdims=True)
    high = jnp.sum(jnp.where(lane < HDIM, 0.0, inner), axis=-1, keepdims=True)
    return inverse * (grads - normed * (jnp.where(lane < HDIM, low, high) / HDIM))


def pair_turn(values, cosine, sine):
    lane = lanes_of(values.shape[0])
    partner = jnp.where(
        lane % HDIM < HDIM // 2, pltpu.roll(values, 96, 1), pltpu.roll(values, 32, 1)
    )
    return values * cosine + partner * sine


def store_heads(target, strip, pair, spare):
    lane = lanes_of(pair.shape[0])
    first = jnp.where(lane < HDIM, pair, spare)
    second = jnp.where(lane < HDIM, pltpu.roll(pair, HDIM, 1), spare)
    target[strip, 0:128] = first.astype(target.dtype)
    target[strip, 128:256] = second.astype(target.dtype)


def join_heads(first, second):
    lane = lanes_of(first.shape[0])
    return jnp.where(lane < HDIM, first, pltpu.roll(second, HDIM, 1))


def ones_beside(rows):
    lane = lanes_of(rows)
    return jnp.where((lane == HDIM) | (lane == HDIM + 1), 1.0, 0.0)


def not_turned(left, right):
    return lax.dot_general(
        left, right, (((1,), (1,)), ((), ())), preferred_element_type=jnp.float32
    )


STRIP = 256
SPARE = 128.0


def strips(rows, body):
    @pl.loop(0, rows // STRIP)
    def _(step):
        body(pl.ds(pl.multiple_of(step * STRIP, STRIP), STRIP))


def weigh(qa_ref, ka_ref, va_ref, ov_ref):
    for head in range(2):
        at = pl.ds(head * 128, 128)

        def body(strip):
            scores = not_turned(qa_ref[strip, at], ka_ref[:, at])
            weights = jnp.exp(scores).astype(jnp.bfloat16)
            ov_ref[strip, at] = jnp.dot(
                weights, va_ref[:, at], preferred_element_type=jnp.float32
            )

        strips(qa_ref.shape[0], body)


def own_kernel(
    q_ref, k_ref, v_ref, gq_ref, gk_ref, cos_ref, sin_ref, sq_ref, sk_ref,
    qa_ref, ka_ref, va_ref, ov_ref,
):
    def prepare(strip):
        cosine, sine = cos_ref[strip, :], sin_ref[strip, :]
        query = pair_turn(pair_norm(q_ref[strip, :])[0] * gq_ref[...], cosine, sine)
        store_heads(qa_ref, strip, query * HDIM**-0.5, sq_ref[strip, :])
        keys = pair_turn(pair_norm(k_ref[strip, :])[0] * gk_ref[...], cosine, sine)
        store_heads(ka_ref, strip, keys, sk_ref[strip, :])
        store_heads(va_ref, strip, v_ref[strip, :], ones_beside(STRIP))

    strips(q_ref.shape[0], prepare)
    weigh(qa_ref, ka_ref, va_ref, ov_ref)


def cross_kernel(
    qa_ref, k_ref, v_ref, sq_ref, sk_ref, own_ref, gate_ref,
    ka_ref, va_ref, ov_ref, mix_ref, qx_ref,
):
    def prepare(strip):
        store_heads(ka_ref, strip, k_ref[strip, :].astype(jnp.float32), sk_ref[strip, :])
        store_heads(va_ref, strip, v_ref[strip, :].astype(jnp.float32), ones_beside(STRIP))

    strips(k_ref.shape[0], prepare)

    def requery(strip):
        lane = lanes_of(STRIP)
        for head in range(2):
            at = pl.ds(head * 128, 128)
            qx_ref[strip, at] = jnp.where(
                lane < HDIM, qa_ref[strip, at].astype(jnp.float32), sq_ref[strip, :]
            ).astype(qx_ref.dtype)

    strips(qa_ref.shape[0], requery)
    weigh(qx_ref, ka_ref, va_ref, ov_ref)

    def mix(strip):
        parts = []
        for head in range(2):
            at = pl.ds(head * 128, 128)
            own, cross = own_ref[strip, at], ov_ref[strip, at]
            parts.append((own / own[:, 64:65], cross / cross[:, 64:65]))
        own = join_heads(parts[0][0], parts[1][0])
        cross = join_heads(parts[0][1], parts[1][1])
        mix_ref[strip, :] = (own + gate_ref[...] * cross).astype(mix_ref.dtype)

    strips(qa_ref.shape[0], mix)


def back_kernel(own, *refs):
    g_ref, gate_ref, ov_ref, qa_ref, sq_ref, ka_ref, va_ref = refs[:7]
    refs = refs[7:]
    if own:
        k_ref, gk_ref, q_ref, gq_ref, cos_ref, sin_ref, more_ref = refs[:7]
        refs = refs[7:]
    dq_ref, dk_ref, dv_ref, sum_ref, qx, doa, dqt, dqh, dkh, dvh = refs
    rows, count = qa_ref.shape[0], ka_ref.shape[0]
    sum_ref[...] = jnp.zeros_like(sum_ref)
    for head in range(2):
        at = pl.ds(head * 128, 128)

        def prepare(strip):
            lane = lanes_of(STRIP)
            plain = g_ref[strip, :]
            grads = plain * gate_ref[...]
            if head == 1:
                plain = pltpu.roll(plain, HDIM, 1)
                grads = pltpu.roll(grads, HDIM, 1)
            both = ov_ref[strip, at]
            inverse = 1.0 / both[:, 64:65]
            out = jnp.where(lane < HDIM, both * inverse, 0.0)
            if not own:
                sum_ref[0, head : head + 1, :] += jnp.sum(plain * out, axis=0, keepdims=True)
            scaled = (grads * inverse).astype(jnp.bfloat16).astype(jnp.float32)
            delta = jnp.sum(scaled * out, axis=-1, keepdims=True)
            high = delta.astype(jnp.bfloat16).astype(jnp.float32)
            doa[strip, :] = jnp.where(
                lane < HDIM,
                scaled,
                jnp.where(lane == HDIM, -high, jnp.where(lane == HDIM + 1, high - delta, 0.0)),
            ).astype(doa.dtype)
            qx[strip, :] = jnp.where(
                lane < HDIM, qa_ref[strip, at].astype(jnp.float32), sq_ref[strip, :]
            ).astype(qx.dtype)

        strips(rows, prepare)
        dqt[...] = jnp.zeros_like(dqt)

        def block(strip):
            keys, values = ka_ref[strip, at], va_ref[strip, at]
            weights = jnp.exp(not_turned(keys, qx[...]))
            grads = (weights * not_turned(values, doa[...])).astype(jnp.bfloat16)
            dvh[head, strip, :] = jnp.dot(
                weights.astype(jnp.bfloat16), doa[...], preferred_element_type=jnp.float32
            )
            dkh[head, strip, :] = jnp.dot(grads, qx[...], preferred_element_type=jnp.float32)
            dqt[...] += lax.dot_general(
                keys, grads, (((0,), (0,)), ((), ())), preferred_element_type=jnp.float32
            )

        strips(count, block)
        dqh[head] = dqt[...].T * HDIM**-0.5

    def add_up(row, values):
        sum_ref[0, row : row + 1, :] += jnp.sum(values, axis=0, keepdims=True)

    def finish(strip):
        grads = join_heads(dkh[0, strip, :], dkh[1, strip, :])
        if own:
            grads = pair_turn(grads, cos_ref[strip, :], -sin_ref[strip, :])
            normed, inverse = pair_norm(k_ref[strip, :])
            add_up(2, grads * normed)
            grads = pair_back(grads * gk_ref[...], normed, inverse)
        dk_ref[strip, :] = grads.astype(dk_ref.dtype)
        dv_ref[strip, :] = join_heads(dvh[0, strip, :], dvh[1, strip, :]).astype(dv_ref.dtype)

    strips(count, finish)

    def finish_query(strip):
        grads = join_heads(dqh[0, strip, :], dqh[1, strip, :])
        if own:
            grads = pair_turn(grads + more_ref[strip, :], cos_ref[strip, :], -sin_ref[strip, :])
            normed, inverse = pair_norm(q_ref[strip, :])
            add_up(3, grads * normed)
            grads = pair_back(grads * gq_ref[...], normed, inverse)
        dq_ref[strip, :] = grads.astype(dq_ref.dtype)

    strips(rows, finish_query)


def view(ref, index, width=128, offset=0):
    return ref.at[:, pl.ds((offset + index) * width, width)]


def attend(
    projected, heads, gain_q, gain_k, gate, cosine, sine, own_q, own_k, cross_q, cross_k
):
    rows, width = projected.shape[0], projected.shape[1] // 3
    caps, count = heads.shape[0], width // 128
    bf, f32 = jnp.bfloat16, jnp.float32

    def steps(i, ins, outs, scratch):
        raw, heads, gain_q, gain_k, gate, cosine, sine, own_q, own_k, cross_q, cross_k = ins
        qa, ka, va, own, cka, cva, cross, mix = outs
        own_kernel(
            view(raw, i), view(raw, i, offset=count), view(raw, i, offset=2 * count),
            view(gain_q, i), view(gain_k, i), cosine, sine, own_q, own_k,
            view(qa, i, 256), view(ka, i, 256), view(va, i, 256), view(own, i, 256),
        )
        cross_kernel(
            view(qa, i, 256), view(heads, i), view(heads, i, offset=count), cross_q, cross_k,
            view(own, i, 256), view(gate, i), view(cka, i, 256), view(cva, i, 256),
            view(cross, i, 256), view(mix, i), *scratch,
        )

    return Aside(
        [projected, heads, gain_q, gain_k, gate, cosine, sine, own_q, own_k, cross_q, cross_k],
        [
            *[jax.ShapeDtypeStruct((rows, 2 * width), d) for d in (bf, bf, bf, f32)],
            *[jax.ShapeDtypeStruct((caps, 2 * width), bf)] * 2,
            jax.ShapeDtypeStruct((rows, 2 * width), f32),
            jax.ShapeDtypeStruct((rows, width), bf),
        ],
        [pltpu.VMEM((rows, 256), bf)],
        steps,
    )


def cap_back_kernel(g_ref, k_ref, gain_ref, out_ref, sum_ref):
    sum_ref[...] = jnp.zeros_like(sum_ref)

    def body(strip):
        for at in range(0, k_ref.shape[1], 128):
            lanes = pl.ds(at, 128)
            grads = g_ref[strip, lanes].astype(jnp.float32)
            normed, inverse = pair_norm(k_ref[strip, lanes])
            sum_ref[0:1, lanes] += jnp.sum(grads * normed, axis=0, keepdims=True)
            out_ref[strip, lanes] = pair_back(
                grads * gain_ref[:, lanes], normed, inverse
            ).astype(out_ref.dtype)
        values = pl.ds(k_ref.shape[1], k_ref.shape[1])
        out_ref[strip, values] = g_ref[strip, values]

    strips(g_ref.shape[0], body)


def cap_back(grads, cap_proj, gain):
    rows, width = grads.shape
    whole = pl.BlockSpec((rows, width), lambda i: (0, 0))
    part = pl.BlockSpec((rows, width // 2), lambda i: (0, 0))
    return pl.pallas_call(
        cap_back_kernel,
        grid=(1,),
        out_shape=[
            jax.ShapeDtypeStruct((rows, width), jnp.bfloat16),
            jax.ShapeDtypeStruct((8, width // 2), jnp.float32),
        ],
        in_specs=[whole, part, pl.BlockSpec((1, width // 2), lambda i: (0, 0))],
        out_specs=[whole, pl.BlockSpec((8, width // 2), lambda i: (0, 0))],
        compiler_params=pltpu.CompilerParams(vmem_limit_bytes=32 * 1024 * 1024),
        cost_estimate=pl.CostEstimate(
            flops=0, bytes_accessed=6 * grads.size, transcendentals=0
        ),
        name="cap_back",
    )(grads, cap_proj, gain)


def attend_back(grads, gate, ov, qa, spare_q, ka, va, rest=None):
    rows, width = grads.shape
    caps, count = ka.shape[0], width // 128
    bf, f32 = jnp.bfloat16, jnp.float32
    own = rest is not None

    def steps(i, ins, outs, scratch):
        grads, gate, ov, qa, spare_q, ka, va, *rest = ins
        dq, dk, dv, sums = outs
        operands = [
            view(grads, i), view(gate, i), view(ov, i, 256), view(qa, i, 256), spare_q,
            view(ka, i, 256), view(va, i, 256),
        ]
        if own:
            raw, gain_k, gain_q, cosine, sine, more = rest
            operands += [view(raw, i, offset=count), view(gain_k, i)]
            operands += [view(raw, i), view(gain_q, i), cosine, sine, view(more, i)]
        back_kernel(
            own, *operands, view(dq, i), view(dk, i), view(dv, i), sums.at[pl.ds(i, 1)], *scratch
        )

    return Aside(
        [grads, gate, ov, qa, spare_q, ka, va, *(rest or ())],
        [
            jax.ShapeDtypeStruct((rows, width), bf if own else f32),
            jax.ShapeDtypeStruct((caps, width), bf),
            jax.ShapeDtypeStruct((caps, width), bf),
            jax.ShapeDtypeStruct((count, 8, 128), f32),
        ],
        [
            pltpu.VMEM((rows, 128), bf),
            pltpu.VMEM((rows, 128), bf),
            pltpu.VMEM((128, rows), f32),
            pltpu.VMEM((2, rows, 128), f32),
            pltpu.VMEM((2, caps, 128), f32),
            pltpu.VMEM((2, caps, 128), f32),
        ],
        steps,
    )


def row_stats(values):
    inverse = lax.rsqrt(jnp.mean(values * values, axis=-1, keepdims=True) + eps)
    return (values * inverse, inverse)


def norm_back(grad_normed, normed, inverse):
    inner_mean = jnp.mean(grad_normed * normed, axis=-1, keepdims=True)
    return inverse * (grad_normed - normed * inner_mean)


def head_stats(values):
    shaped = values.reshape(values.shape[0], -1, HDIM)
    normed, inverse = row_stats(shaped)
    return (normed.reshape(values.shape), inverse)


def head_back(grad_normed, normed, inverse):
    shaped_grad = grad_normed.reshape(grad_normed.shape[0], -1, HDIM)
    shaped_norm = normed.reshape(normed.shape[0], -1, HDIM)
    return norm_back(shaped_grad, shaped_norm, inverse).reshape(grad_normed.shape)


def rotary(values, row_pos, col_pos, direction):
    quarter = HDIM // 4
    freqs = 10000.0 ** (-jnp.arange(quarter, dtype=jnp.float32) / quarter)
    angles = jnp.concatenate([row_pos[:, None] * freqs, col_pos[:, None] * freqs], axis=1)
    cosine = jnp.cos(angles)[:, None, :]
    sine = direction * jnp.sin(angles)[:, None, :]
    shaped = values.reshape(values.shape[0], -1, HDIM)
    first_half = shaped[..., : HDIM // 2]
    second_half = shaped[..., HDIM // 2 :]
    turned = jnp.concatenate(
        [first_half * cosine - second_half * sine, second_half * cosine + first_half * sine],
        axis=-1,
    )
    return turned.reshape(values.shape)


def layout(doc_lengths, bucket, positions):
    doc_ends = jnp.cumsum(doc_lengths)
    starts = doc_ends - doc_lengths
    segment = jnp.sum((positions[:, None] >= doc_ends[None, :]).astype(jnp.int32), axis=1)
    matches = segment[:, None] == jnp.arange(DOCS, dtype=jnp.int32)[None, :]
    offset = jnp.sum(jnp.where(matches, starts[None, :], 0), axis=1)
    within = positions - offset
    stride = 32 * (bucket + 1)
    return (segment, (within // stride).astype(jnp.float32), (within % stride).astype(jnp.float32))


def turn_tables(row_pos, col_pos):
    quarter = HDIM // 4
    freqs = 10000.0 ** (-jnp.arange(quarter, dtype=jnp.float32) / quarter)
    angles = jnp.concatenate([row_pos[:, None] * freqs, col_pos[:, None] * freqs], axis=1)
    cosine, sine = jnp.cos(angles), jnp.sin(angles)
    return jnp.tile(cosine, (1, 4)), jnp.concatenate([-sine, sine, -sine, sine], axis=1)


def spare_columns(labels, height):
    lane = jnp.arange(128)[None, :] - HDIM
    at_label = (lane >= 0) & (lane <= DOCS) & (lane == labels[:, None])
    last = lane == DOCS + 1
    if height:
        return jnp.where(at_label, height, jnp.where(last, -height, 0.0)).astype(jnp.float32)
    return (at_label | last).astype(jnp.float32)


def by_head(values):
    return values.reshape(values.shape[0], -1, 1, HDIM).transpose(1, 0, 2, 3)


def from_heads(blocks):
    return blocks.transpose(1, 0, 2, 3).reshape(blocks.shape[1], -1)


def attend_forward(query, keys, values, allowed):
    scale = HDIM ** (-0.5)

    def block(block_args):
        part_q, part_k, part_v = block_args
        scores = (
            jnp.einsum("qhd,khd->hqk", part_q, part_k, preferred_element_type=jnp.float32) * scale
        )
        scores = jnp.where(allowed[None], scores, -1e30)
        row_peak = jnp.max(scores, axis=-1, keepdims=True)
        exp_scores = jnp.exp(scores - row_peak)
        exp_total = jnp.sum(exp_scores, axis=-1, keepdims=True)
        attn_probs = (exp_scores / exp_total).astype(jnp.bfloat16)
        attn_block = jnp.einsum(
            "hqk,khd->qhd", attn_probs, part_v, preferred_element_type=jnp.float32
        )
        return (attn_block, row_peak[..., 0] + jnp.log(exp_total[..., 0]))

    blocks, log_total = lax.map(block, (by_head(query), by_head(keys), by_head(values)))
    return (from_heads(blocks), log_total)


def attend_backward(query, keys, values, allowed, log_total, grad_out):
    scale = HDIM ** (-0.5)

    def block(block_args):
        part_q, part_k, part_v, part_log, part_grad = block_args
        scores = (
            jnp.einsum("qhd,khd->hqk", part_q, part_k, preferred_element_type=jnp.float32) * scale
        )
        scores = jnp.where(allowed[None], scores, -1e30)
        attn_probs = jnp.exp(scores - part_log[..., None])
        grad_probs = jnp.einsum(
            "qhd,khd->hqk", part_grad, part_v, preferred_element_type=jnp.float32
        )
        row_delta = jnp.sum(attn_probs * grad_probs, axis=-1, keepdims=True)
        grad_scores = (attn_probs * (grad_probs - row_delta)).astype(jnp.bfloat16)
        grad_query = (
            jnp.einsum("hqk,khd->qhd", grad_scores, part_k, preferred_element_type=jnp.float32)
            * scale
        )
        grad_keys = (
            jnp.einsum("hqk,qhd->khd", grad_scores, part_q, preferred_element_type=jnp.float32)
            * scale
        )
        grad_values = jnp.einsum(
            "hqk,qhd->khd",
            attn_probs.astype(jnp.bfloat16),
            part_grad,
            preferred_element_type=jnp.float32,
        )
        return (grad_query, grad_keys, grad_values)

    grad_query, grad_keys, grad_values = lax.map(
        block,
        (by_head(query), by_head(keys), by_head(values), log_total, by_head(grad_out)),
    )
    return (from_heads(grad_query), from_heads(grad_keys), from_heads(grad_values))


def matmul(left, right):
    return jnp.dot(left, right, preferred_element_type=jnp.float32)


def contract_right(left, weight):
    return lax.dot_general(
        left, weight, (((1,), (1,)), ((), ())), preferred_element_type=jnp.float32
    )


def contract_rows(left, right):
    return lax.dot_general(
        left, right, (((0,), (0,)), ((), ())), preferred_element_type=jnp.float32
    )


def pick(values, index, axis):
    return lax.dynamic_index_in_dim(values, index, axis, keepdims=False)


def to_plane(values):
    ways = lax.axis_size("tp")
    parts = values.reshape((ways, values.shape[0] // ways) + values.shape[1:])
    parts = lax.all_to_all(parts, "tp", 0, 0, tiled=True)
    parts = lax.all_to_all(parts, "seq", 0, 0, tiled=True)
    return parts.reshape(values.shape)


def from_plane(values):
    ways = lax.axis_size("tp")
    parts = values.reshape((ways, values.shape[0] // ways) + values.shape[1:])
    parts = lax.all_to_all(parts, "seq", 0, 0, tiled=True)
    parts = lax.all_to_all(parts, "tp", 0, 0, tiled=True)
    return parts.reshape(values.shape)


def fast():
    return lax.axis_size("tp") == 4 and lax.axis_size("core") == 2 and lax.axis_size("seq") == 4


def gather_planes(part):
    return lax.all_gather(part, "seq", axis=0, tiled=False)


def join_cores(halves):
    whole = lax.all_gather(halves, "core", axis=1, tiled=False)
    return whole.reshape(-1, halves.shape[-1])


def swap_rows(term):
    cores, planes = lax.axis_size("core"), lax.axis_size("seq")
    return swap_halves(term.astype(jnp.bfloat16).reshape(planes, cores, -1, term.shape[-1]))


def scatter_planes(term):
    return lax.psum_scatter(term, "seq", scatter_dimension=0, tiled=False)


def swap_halves(shaped):
    cores, me_c = lax.axis_size("core"), lax.axis_index("core")
    mine = pick(shaped, me_c, 1)
    for step in range(1, cores):
        ring = [(c, (c + step) % cores) for c in range(cores)]
        other = lax.ppermute(pick(shaped, (me_c + step) % cores, 1), "core", ring)
        mine = (mine.astype(jnp.float32) + other.astype(jnp.float32)).astype(jnp.bfloat16)
    return mine


def plane_gather(values):
    return lax.all_gather(values, "tp", axis=0, tiled=True)


def plane_multiply(ident, x, weight, turned=False, halved=False, width=None, **more):
    if fast():
        return gather_matmul(ident, x, weight, turned, halved, width, **more)
    whole = join_cores(weight) if halved else weight
    x = plane_gather(x)
    return x, whole, contract_right(x, whole) if turned else matmul(x, whole[:, :width])


def multiply_plane(ident, x, weight, turned=False, **more):
    if fast():
        return matmul_scatter(ident, x, weight, turned, **more)
    weight = weight[:, : x.shape[1]] if turned else weight
    term = contract_right(x, weight) if turned else matmul(x, weight)
    return lax.psum_scatter(
        term.astype(jnp.bfloat16), "tp", scatter_dimension=0, tiled=True
    ).astype(jnp.float32), None


def collect_plane(pieces):
    return [
        lax.all_gather(p, ("tp", "core"), axis=0, tiled=False).reshape(
            (lax.axis_size("tp"), lax.axis_size("core")) + p.shape
        )
        for p in pieces
    ]


def spread_parts(blocks, parts):
    if fast():
        return spread(blocks, parts)
    tp, cores, rows, width = blocks.shape
    return (
        blocks.astype(jnp.float32)
        .reshape(tp, cores, rows, parts, width // parts)
        .transpose(1, 2, 3, 0, 4)
        .reshape(cores * rows, tp * width)
    )


def arrive_plane(ident, tokens, cotangent, message, w_mod, *weights):
    if fast():
        return arrive(ident, tokens, cotangent, message, w_mod, *weights)
    ways = lax.axis_size("tp")
    cotangent = lax.all_to_all(
        cotangent.reshape(ways, -1, cotangent.shape[1]), "tp", 0, 0, tiled=True
    )
    planes, cores = lax.axis_size("seq"), lax.axis_size("core")
    depth = w_mod.shape[0]
    part = lax.dynamic_slice_in_dim(message, lax.axis_index("seq") * depth, depth, 1)
    messages = lax.all_gather(part, ("tp", "core"), axis=0, tiled=False)
    terms = matmul(messages.reshape(-1, depth).astype(w_mod.dtype), w_mod)
    terms = lax.psum_scatter(
        terms.reshape(planes, cores, 8, -1), "seq", scatter_dimension=0, tiled=False
    )
    messages = messages.reshape(lax.axis_size("tp"), cores, 8, depth)
    w_qkv, w_out, w_down, w_gateup = weights
    share = w_down.shape[0] // (ways * cores)
    block = lax.axis_index("tp") * cores + lax.axis_index("core")
    return (
        to_plane(tokens),
        cotangent,
        messages,
        pick(terms, lax.axis_index("core"), 0),
        jnp.concatenate([columns_of(w_qkv, 3), columns_of(w_out, 1)], axis=1),
        lax.dynamic_slice_in_dim(w_down, block * share, share, 0),
        columns_of(w_gateup, 2 * planes),
    )


def columns_of(weight, parts):
    tp, cores = lax.axis_size("tp"), lax.axis_size("core")
    me_t, me_c = lax.axis_index("tp"), lax.axis_index("core")
    share = weight.shape[0] // cores
    size = weight.shape[1] // (parts * tp)
    return jnp.concatenate(
        [
            lax.dynamic_slice(weight, (me_c * share, (q * tp + me_t) * size), (share, size))
            for q in range(parts)
        ],
        axis=1,
    )


def shards(
    tokens,
    cotangent,
    step_embed,
    caption,
    lengths,
    group_bucket,
    null_mask,
    w_qkv,
    w_out,
    w_capkv,
    w_gateup,
    w_down,
    w_mod,
    b_mod,
    gain_attn,
    gain_ffn,
    gain_query,
    gain_key,
    gain_capkey,
    gate_head,
    null_embed,
):
    tp, cores, planes = lax.axis_size("tp"), lax.axis_size("core"), lax.axis_size("seq")
    me_t, me_c, me_z = lax.axis_index("tp"), lax.axis_index("core"), lax.axis_index("seq")
    groups = tp * cores
    rows, width = tokens.shape
    piece = rows // tp
    local_heads = HEADS // tp
    local = local_heads * HDIM
    cap_dev = caption.shape[2]
    ctx = caption.shape[3]
    my_group = me_z * cores + me_c

    condition = jax.nn.silu(step_embed[0].astype(jnp.float32)).astype(jnp.bfloat16)
    numbers = jnp.concatenate([lengths[0], group_bucket, null_mask[0]]).astype(jnp.float32)
    mod_rows = w_mod.shape[0]
    numbers = jnp.tile(jnp.pad(numbers, (0, mod_rows - numbers.shape[0])), planes)
    message = jnp.concatenate(
        [condition.astype(jnp.float32), numbers[None], jnp.zeros((3, numbers.shape[0]))], axis=0
    )
    arrived, cotangents, messages, mod_doc, *cuts = arrive_plane(
        13, tokens, cotangent, message, w_mod, w_qkv, w_out, w_down, w_gateup
    )
    messages = messages.reshape(groups, 8, mod_rows)
    cond_mine = messages[:, :DOCS].reshape(groups * DOCS, mod_rows)
    mod_doc = mod_doc[:DOCS] + b_mod

    numbers = messages[:, DOCS, : 2 * DOCS + 1].astype(jnp.int32)
    counts = jnp.sum(numbers[:, :DOCS], axis=1).astype(jnp.float32)
    mine = pick(numbers, my_group, 0)
    doc_lengths, bucket = mine[:DOCS], mine[DOCS]
    bucket_count = jnp.sum(jnp.where(numbers[:, DOCS] == bucket, counts, 0.0))
    scale_loss = jnp.sum(counts) / (RES * bucket_count)

    half_capkv = gather_planes(columns_of(w_capkv, 2))
    half_qkv, half_down, half_gateup = [gather_planes(part) for part in cuts]

    capmix = jnp.where(null_mask[0][:, None, None] > 0, null_embed[None, None, :], caption[0])
    my_gain_capkey = pick(gain_capkey.reshape(tp, 1, local), me_t, 0)
    cap_flat = capmix.reshape(DOCS * cap_dev, ctx)
    if fast():
        cap_flat, full_capkv, cap_proj, cotangents, heads = gather_matmul(
            2, cap_flat, half_capkv, halved=True, trade=[swap_blocks(cotangents, "seq")],
            finish=head_finish(DOCS * cap_dev, 2 * local, my_gain_capkey),
        )
    else:
        cap_flat, full_capkv, cap_proj = plane_multiply(2, cap_flat, half_capkv, halved=True)
        capkey_raw, capval_raw = jnp.split(cap_proj, 2, axis=1)
        capkey_norm, capkey_inv = head_stats(capkey_raw)
        heads = jnp.concatenate([capkey_norm * my_gain_capkey, capval_raw], axis=1)
        heads = heads.astype(jnp.bfloat16)
        cotangents = lax.all_to_all(cotangents, "seq", 0, 0, tiled=True)
    cotangents = cotangents.reshape(tokens.shape)
    cap_document = jnp.tile(jnp.repeat(jnp.arange(DOCS, dtype=jnp.int32), cap_dev), planes)

    inputs = arrived.reshape(tokens.shape).astype(jnp.float32)
    row = jnp.arange(rows, dtype=jnp.int32)
    spread = (row // piece) * rows + row % piece
    positions = spread + me_t * piece
    all_positions = (jnp.arange(tp, dtype=jnp.int32)[:, None] * piece + spread[None, :]).reshape(-1)
    segment, _, _ = layout(doc_lengths, bucket, positions)
    all_segment, row_pos, col_pos = layout(doc_lengths, bucket, all_positions)
    all_document = jnp.minimum(all_segment, DOCS - 1)
    document = jnp.minimum(segment, DOCS - 1)
    doc_pick = (document[:, None] == jnp.arange(DOCS, dtype=jnp.int32)[None, :]).astype(jnp.float32)
    is_valid = (segment < DOCS).astype(jnp.float32)
    modulation = jnp.dot(doc_pick, mod_doc, precision=lax.Precision.HIGHEST)
    scale_a, gate_a, scale_f, gate_f = jnp.split(modulation, 4, axis=1)
    tanh_a, tanh_f = jnp.tanh(gate_a), jnp.tanh(gate_f)

    normed1, inverse1 = row_stats(inputs)
    hidden1 = (normed1 * gain_attn * (1.0 + scale_a)).astype(jnp.bfloat16)
    hidden1, heads = lax.optimization_barrier((hidden1, heads))
    heads = heads.reshape(planes, DOCS * cap_dev, 2 * local)
    if fast():
        hidden1, full_qkv, projected, heads = gather_matmul(
            1, hidden1, half_qkv, halved=True, width=3 * local,
            trade=[swap_blocks(heads, "seq")],
        )
    else:
        hidden1, full_qkv, projected = plane_multiply(
            1, hidden1, half_qkv, halved=True, width=3 * local
        )
        heads = lax.all_to_all(heads, "seq", 0, 0, tiled=True)
        full_out = full_qkv[:, 3 * local :].reshape(tp, local, local)
        full_out = lax.all_to_all(full_out, "tp", 0, 0, tiled=True)
        full_out = full_out.transpose(1, 0, 2).reshape(local, width)
    heads = heads.reshape(-1, 2 * local)
    my_gain_query = pick(gain_query.reshape(tp, 1, local), me_t, 0)
    my_gain_key = pick(gain_key.reshape(tp, 1, local), me_t, 0)
    gate_tanh = pick(jnp.tanh(gate_head).reshape(tp, local_heads), me_t, 0)
    head_gate = jnp.repeat(gate_tanh, HDIM)[None, :]
    grad_res0 = cotangents.astype(jnp.float32) * (is_valid * scale_loss)[:, None]
    grad_down = (tanh_f * grad_res0).astype(jnp.bfloat16)
    if fast():
        cosine, sine = turn_tables(row_pos, col_pos)
        own_spare = spare_columns(all_segment, SPARE)
        cross_spare = spare_columns(all_document, SPARE)
        aside = attend(
            projected, heads, my_gain_query, my_gain_key, head_gate, cosine, sine,
            own_spare, spare_columns(all_segment, 0),
            cross_spare, spare_columns(cap_document, 0),
        )
        out_rows = (
            full_qkv,
            "tp",
            (local, width),
            lambda ref, p: ref.at[pl.ds(p * local, local), pl.ds(3 * local, local)],
            lambda ref, p: ref.at[:, pl.ds(pl.multiple_of(p * local, local), local)],
        )
        grad_down, full_down, grad_ffn, *wides, full_out = gather_matmul(
            6, grad_down, half_down, turned=True, halved=True, aside=aside, early=1,
            trade=[out_rows],
        )
        wide_query, wide_keys, wide_values, own_wide = wides[:4]
        wide_capkeys, wide_capvals, cross_wide, mixed_attn = wides[4:]
    else:
        grad_down, full_down, grad_ffn = plane_multiply(
            6, grad_down, half_down, turned=True, halved=True
        )
        query_raw, key_raw, value_raw = jnp.split(projected, 3, axis=1)
        query_norm, query_inv = head_stats(query_raw)
        key_norm, key_inv = head_stats(key_raw)
        query = rotary(query_norm * my_gain_query, row_pos, col_pos, 1.0).astype(jnp.bfloat16)
        keys = rotary(key_norm * my_gain_key, row_pos, col_pos, 1.0).astype(jnp.bfloat16)
        values = value_raw.astype(jnp.bfloat16)
        capkeys, capvals = jnp.split(heads, 2, axis=1)
        self_allowed = all_segment[:, None] == all_segment[None, :]
        cross_allowed = all_document[:, None] == cap_document[None, :]
        own_out, own_log = attend_forward(query, keys, values, self_allowed)
        cross_out, cross_log = attend_forward(query, capkeys, capvals, cross_allowed)
        mixed_attn = (own_out + head_gate * cross_out).astype(jnp.bfloat16)
    attn_out, *_ = multiply_plane(3, mixed_attn, full_out)
    residual = inputs + tanh_a * attn_out
    normed2, inverse2 = row_stats(residual)
    hidden2 = (normed2 * gain_ffn * (1.0 + scale_f)).astype(jnp.bfloat16)
    if fast():
        hidden2, full_gateup, hidden_ffn, grad_gateup = gather_matmul(
            4, hidden2, half_gateup, halved=True, finish=swiglu_finish(grad_ffn), keep=False
        )
        hidden_ffn = hidden_ffn.reshape(grad_ffn.shape)
        grad_gateup = grad_gateup.reshape(grad_ffn.shape[0], -1)
    else:
        hidden2, full_gateup, gate_up = plane_multiply(4, hidden2, half_gateup, halved=True)
        gate_part, up_part = jnp.split(gate_up, 2, axis=1)
        sig_gate = jax.nn.sigmoid(gate_part)
        silu_gate = gate_part * sig_gate
        hidden_ffn = (silu_gate * up_part).astype(jnp.bfloat16)
        grad_gate_part = grad_ffn * up_part * sig_gate * (1.0 + gate_part * (1.0 - sig_gate))
        grad_gateup = jnp.concatenate([grad_gate_part, grad_ffn * silu_gate], axis=1)
        grad_gateup = grad_gateup.astype(jnp.bfloat16)
    term_down = swap_rows(contract_rows(hidden_ffn, grad_down))
    term_gateup = swap_rows(contract_rows(hidden2, grad_gateup))
    grad_gateup, term_down, term_gateup = lax.optimization_barrier(
        (grad_gateup, term_down, term_gateup)
    )
    term_down, term_gateup = scatter_planes(term_down), scatter_planes(term_gateup)
    grad_hidden2, *_ = multiply_plane(7, grad_gateup, full_gateup, turned=True)
    gain_ffn_term = jnp.sum(grad_hidden2 * normed2 * (1.0 + scale_f), axis=0)
    grad_scale_f = grad_hidden2 * normed2 * gain_ffn
    grad_residual = grad_res0 + norm_back(
        grad_hidden2 * gain_ffn * (1.0 + scale_f), normed2, inverse2
    )
    grad_attn = (tanh_a * grad_residual).astype(jnp.bfloat16)
    grad_attn, _, grad_mix = plane_multiply(8, grad_attn, full_out, turned=True)
    grad_gate_a = grad_residual * attn_out * (1.0 - tanh_a * tanh_a)
    term_out = contract_rows(mixed_attn, grad_attn).astype(jnp.bfloat16)
    term_out = swap_halves(term_out.reshape(1, cores, -1, width))[0]
    term_out = term_out.reshape(term_out.shape[0], tp, -1).transpose(1, 0, 2)
    if fast():
        cross_aside = attend_back(
            grad_mix, head_gate, cross_wide, wide_query, cross_spare,
            wide_capkeys, wide_capvals,
        )
        down_out, query_cross, grad_capkeys, grad_capvals, cross_sums, term_out = matmul_scatter(
            5, hidden_ffn, full_down, aside=cross_aside, trade=[swap_blocks(term_out, "tp")]
        )
        grad_heads = jnp.concatenate([grad_capkeys, grad_capvals], axis=1)
        grad_heads = grad_heads.reshape(planes, DOCS * cap_dev, 2 * local)
        gate_head_term = jnp.sum(cross_sums[:, :2], axis=-1).reshape(-1)
        own_aside = attend_back(
            grad_mix, jnp.ones_like(head_gate), own_wide, wide_query, own_spare,
            wide_keys, wide_values,
            (projected, my_gain_key, my_gain_query, cosine, sine, query_cross),
        )
        result = (residual + tanh_f * down_out).astype(jnp.bfloat16)
        (all_down, all_gateup), riders = collect(
            10,
            [term_down, term_gateup],
            own_aside,
            [swap_blocks(grad_heads, "seq"), swap_blocks(term_out, "seq")],
        )
        *grad_projected, own_sums, grad_heads, term_out = riders
        term_out = jnp.sum(term_out.astype(jnp.float32), axis=0).astype(jnp.bfloat16)
        gain_key_term, gain_query_term = own_sums[:, 2].reshape(-1), own_sums[:, 3].reshape(-1)
        grad_projected = jnp.concatenate(grad_projected, axis=1)
    else:
        down_out, _ = multiply_plane(5, hidden_ffn, full_down)
        result = from_plane((residual + tanh_f * down_out).astype(jnp.bfloat16))
        all_down, all_gateup = collect_plane([term_down, term_gateup])
        term_out = scatter_planes(lax.all_to_all(term_out, "tp", 0, 0, tiled=True))
        grad_own = grad_mix.astype(jnp.bfloat16)
        grad_cross = (head_gate * grad_mix).astype(jnp.bfloat16)
        gate_head_term = jnp.sum(
            (grad_mix * cross_out).reshape(-1, local_heads, HDIM), axis=(0, 2)
        )
        query_own, grad_keys, grad_values = attend_backward(
            query, keys, values, self_allowed, own_log, grad_own
        )
        query_cross, grad_capkeys, grad_capvals = attend_backward(
            query, capkeys, capvals, cross_allowed, cross_log, grad_cross
        )
        grad_query = rotary(query_own + query_cross, row_pos, col_pos, -1.0)
        gain_query_term = jnp.sum(grad_query * query_norm, axis=0)
        grad_query_raw = head_back(grad_query * my_gain_query, query_norm, query_inv)
        grad_key = rotary(grad_keys, row_pos, col_pos, -1.0)
        gain_key_term = jnp.sum(grad_key * key_norm, axis=0)
        grad_key_raw = head_back(grad_key * my_gain_key, key_norm, key_inv)
        grad_projected = jnp.concatenate(
            [grad_query_raw, grad_key_raw, grad_values], axis=1
        ).astype(jnp.bfloat16)
        grad_heads = jnp.concatenate([grad_capkeys, grad_capvals], axis=1).astype(jnp.bfloat16)
        grad_heads = grad_heads.reshape(planes, DOCS * cap_dev, 2 * local)
        grad_heads = lax.all_to_all(grad_heads, "seq", 0, 0, tiled=True)
    grad_gate_f = grad_res0 * down_out * (1.0 - tanh_f * tanh_f)
    gate_head_term = gate_head_term * (1.0 - gate_tanh * gate_tanh)
    grad_heads = grad_heads.reshape(-1, 2 * local)
    if fast():
        grad_cap_proj, capkey_sums = cap_back(grad_heads, cap_proj, my_gain_capkey)
        gain_capkey_term = capkey_sums[0]
    else:
        grad_capkeys, grad_capvals = jnp.split(grad_heads.astype(jnp.float32), 2, axis=1)
        gain_capkey_term = jnp.sum(grad_capkeys * capkey_norm, axis=0)
        grad_capkey_raw = head_back(grad_capkeys * my_gain_capkey, capkey_norm, capkey_inv)
        grad_cap_proj = jnp.concatenate([grad_capkey_raw, grad_capvals], axis=1).astype(
            jnp.bfloat16
        )
    term_qkv = swap_rows(contract_rows(hidden1, grad_projected))
    cap_side, _ = lax.optimization_barrier((grad_cap_proj, term_qkv))
    term_qkv = scatter_planes(term_qkv)
    term_capkv = swap_rows(contract_rows(cap_flat, cap_side))
    grad_projected, _ = lax.optimization_barrier((grad_projected, term_capkv))
    term_capkv = scatter_planes(term_capkv)
    grad_hidden1, *_ = multiply_plane(9, grad_projected, full_qkv, turned=True)
    gain_attn_term = jnp.sum(grad_hidden1 * normed1 * (1.0 + scale_a), axis=0)
    grad_scale_a = grad_hidden1 * normed1 * gain_attn
    input_grad = (
        grad_residual + norm_back(grad_hidden1 * gain_attn * (1.0 + scale_a), normed1, inverse1)
    ).astype(jnp.bfloat16)

    grad_mod_tok = jnp.concatenate([grad_scale_a, grad_gate_a, grad_scale_f, grad_gate_f], axis=1)
    grad_mod_doc = lax.dot_general(
        doc_pick,
        grad_mod_tok,
        (((0,), (0,)), ((), ())),
        precision=lax.Precision.HIGHEST,
        preferred_element_type=jnp.float32,
    )
    plane_nulls = pick(numbers[:, DOCS + 1 :].reshape(tp, cores, DOCS), me_c, 1)
    null_rows = jnp.repeat(plane_nulls.reshape(-1), cap_dev) > 0
    grad_hidden1, null_rows, all_down, all_gateup = lax.optimization_barrier(
        (grad_hidden1, null_rows, all_down, all_gateup)
    )
    null_sum = jnp.sum(
        jnp.where(null_rows[:, None], grad_cap_proj.astype(jnp.float32), 0.0), axis=0
    )
    null_term = jnp.dot(
        full_capkv.astype(jnp.float32), null_sum, precision=lax.Precision.HIGHEST
    )

    def at_mine(part):
        whole = jnp.zeros((tp,) + part.shape, jnp.float32)
        return lax.dynamic_update_index_in_dim(whole, part, me_t, 0).reshape(-1)

    small = jnp.concatenate(
        [
            gain_attn_term,
            gain_ffn_term,
            at_mine(gain_query_term),
            at_mine(gain_key_term),
            at_mine(gain_capkey_term),
            at_mine(gate_head_term),
            null_term,
        ]
    )
    small_rows = 8 - DOCS
    small_size = small.shape[0]
    small = jnp.pad(small, (0, small_rows * 4 * width - small_size))
    sums = jnp.concatenate([grad_mod_doc, small.reshape(small_rows, 4 * width)], axis=0)
    if fast():
        (all_qkv, all_out), _ = collect(12, [term_qkv, term_out])
    else:
        all_qkv, all_out = collect_plane([term_qkv, term_out])
    all_qkv, all_down, all_gateup = lax.optimization_barrier((all_qkv, all_down, all_gateup))
    sum_down = all_down.reshape(w_down.shape).astype(jnp.float32)
    sum_gateup = spread_parts(all_gateup, 2 * planes)
    sum_out = spread_parts(all_out, 1)
    sum_qkv = spread_parts(all_qkv, 3)
    sum_qkv, sum_gateup, sum_down, sum_out, term_capkv = lax.optimization_barrier(
        (sum_qkv, sum_gateup, sum_down, sum_out, term_capkv)
    )
    if fast():
        (all_capkv,), (result, input_grad, totals) = collect(
            14, [term_capkv], backs=[result, input_grad], sums=sums
        )
        result, input_grad = result.reshape(tokens.shape), input_grad.reshape(tokens.shape)
    else:
        (all_capkv,) = collect_plane([term_capkv])
        input_grad = from_plane(input_grad)
        totals = lax.all_gather(lax.psum(sums, "tp"), ("seq", "core"), axis=0, tiled=False)
    totals = totals.reshape(groups, 8, 4 * width)
    sum_capkv = spread_parts(all_capkv, 2)
    grad_mod_docs = totals[:, :DOCS].reshape(groups * DOCS, 4 * width)
    sum_mod = lax.dot_general(
        cond_mine,
        grad_mod_docs,
        (((0,), (0,)), ((), ())),
        precision=lax.Precision.HIGHEST,
        preferred_element_type=jnp.float32,
    )
    sum_bias = jnp.sum(grad_mod_docs, axis=0)
    small = jnp.sum(totals[:, DOCS:], axis=0).reshape(-1)[:small_size]
    ends = [width, 2 * width, 3 * width, 4 * width, 5 * width, 5 * width + HEADS]
    small_parts = jnp.split(small, ends)
    return (
        result,
        input_grad,
        sum_qkv,
        sum_out,
        sum_capkv,
        sum_gateup,
        sum_down,
        sum_mod,
        sum_bias,
        *small_parts,
    )


def solution(mesh):
    planes = mesh.shape["seq"]
    cores = mesh.shape["bucket"] // planes
    split = Mesh(mesh.devices.reshape(planes, cores, planes), ("tp", "core", "seq"))
    group = ("tp", "core")
    token = P(("tp", "core", "seq"), None)
    weight = P("seq", None)
    placed = (
        token,
        token,
        P(group, None, None),
        P(group, None, "seq", None),
        P(group, None),
        P(group),
        P(group, None),
        *([weight] * 6),
        *([P()] * 8),
    )
    return jax.shard_map(
        shards,
        mesh=split,
        in_specs=placed,
        out_specs=(token, token, *([weight] * 6), *([P()] * 8)),
        check_vma=False,
    )
```

```python
import functools

import jax
import jax.numpy as jnp
from jax import lax
from jax.experimental import pallas as pl
from jax.experimental.pallas import tpu as pltpu
from jax.sharding import Mesh, PartitionSpec as P

HEADS = 24
HDIM = 64
DOCS = 4
RES = 4


eps = 1e-06

MESH = pl.DeviceIdType.MESH
VMEM_BYTES = 60 * 1024 * 1024


def neighbours():
    me = lax.axis_index("tp")
    return me, me + 1 - 2 * lax.rem(me, 2), lax.rem(me + 2, 4), 3 - me


def greet(places):
    barrier = pltpu.get_barrier_semaphore()
    for place in places:
        pl.semaphore_signal(barrier, inc=1, device_id=place, device_id_type=MESH)
    pl.semaphore_wait(barrier, len(places))


def send(source, target, sems, index, place):
    return pltpu.make_async_remote_copy(
        src_ref=source,
        dst_ref=target,
        send_sem=sems[0].at[index],
        recv_sem=sems[1].at[index],
        device_id=place,
        device_id_type=MESH,
    )


def tile_of(width):
    for tile in (512, 384, 256, 128):
        if width % tile == 0:
            return tile
    return width


def multiply(left, weight_ref, columns, turned):
    if turned:
        return lax.dot_general(
            left, weight_ref[columns, 0 : left.shape[1]], (((1,), (1,)), ((), ())),
            preferred_element_type=jnp.float32,
        )
    return jnp.dot(left, weight_ref[:, columns], preferred_element_type=jnp.float32)


def bind(refs, counts, *riders):
    refs, own = list(refs), []
    for kind in range(3):
        own += refs[: counts[kind]]
        refs = refs[counts[kind] :]
        for rider in riders:
            count = rider.counts[kind]
            rider.refs[kind] = refs[:count]
            refs = refs[count:]
    return own


class Aside:
    def __init__(self, operands, outs, scratch, steps):
        self.operands, self.outs, self.steps = operands, outs, steps
        self.in_specs = [pl.BlockSpec(memory_space=pl.ANY)] * len(operands)
        self.out_specs = [pl.BlockSpec(memory_space=pltpu.VMEM)] * len(outs)
        self.scratch = [
            *[pltpu.VMEM(x.shape, x.dtype) for x in operands],
            pltpu.SemaphoreType.DMA((max(len(operands), 1),)),
            *scratch,
        ]
        self.counts = (len(operands), len(outs), len(self.scratch))
        self.refs = [None] * 3

    def load(self):
        count = len(self.operands)
        sem = self.refs[2][count]
        self.loads = [
            pltpu.make_async_copy(self.refs[0][i], self.refs[2][i], sem.at[i])
            for i in range(count)
        ]
        for copy in self.loads:
            copy.start()

    def step(self, index):
        count = len(self.operands)
        if index == 0:
            for copy in self.loads:
                copy.wait()
        if self.steps:
            self.steps(index, self.refs[2][:count], self.refs[1], self.refs[2][count + 1 :])


def nothing():
    return Aside([], [], [], None)


class Finish:
    def __init__(self, operands, outs, work):
        self.operands, self.outs, self.work = operands, outs, work
        hbm = pl.BlockSpec(memory_space=pl.ANY)
        self.in_specs, self.out_specs = [hbm] * len(operands), [hbm] * len(outs)
        self.scratch = [
            *[pltpu.VMEM(x.shape, x.dtype) for x in operands],
            *[pltpu.VMEM(x.shape, x.dtype) for x in outs],
            pltpu.SemaphoreType.DMA((max(len(operands), 1),)),
            pltpu.SemaphoreType.DMA((4 * max(len(outs), 1),)),
        ]
        self.counts = (len(operands), len(outs), len(self.scratch))
        self.refs = [None] * 3

    def load(self):
        count = len(self.operands)
        self.ins, self.made = self.refs[2][:count], self.refs[2][count:-2]
        sem = self.refs[2][-2]
        self.loads = [
            pltpu.make_async_copy(self.refs[0][i], self.ins[i], sem.at[i]) for i in range(count)
        ]
        for copy in self.loads:
            copy.start()
        self.copies = []

    def run(self, index, owner, product):
        if not self.work:
            return
        if index == 0:
            for copy in self.loads:
                copy.wait()
        made = [ref.at[owner] for ref in self.made]
        self.work(product, [ref.at[owner] for ref in self.ins], made)
        for i, ref in enumerate(made):
            copy = pltpu.make_async_copy(
                ref, self.refs[1][i].at[owner], self.refs[2][-1].at[4 * i + index]
            )
            copy.start()
            self.copies.append(copy)

    def end(self):
        for copy in self.copies:
            copy.wait()


class Trade:
    def __init__(self, *items):
        self.items = items
        hbm = pl.BlockSpec(memory_space=pl.ANY)
        self.operands = [item[0] for item in items]
        self.outs = [jax.ShapeDtypeStruct(item[2], item[0].dtype) for item in items]
        self.in_specs = self.out_specs = [hbm] * len(items)
        count = max(len(items), 1)
        self.scratch = [pltpu.SemaphoreType.DMA((n,)) for n in (count, 3 * count, 3 * count)]
        self.counts = (len(items), len(items), 3)
        self.refs = [None] * 3

    def begin(self):
        local, *sems = self.refs[2]
        self.copies, self.local = [], []
        for i, (_, axis, _, source, target) in enumerate(self.items):
            from_ref, to_ref = self.refs[0][i], self.refs[1][i]
            if axis == "tp":
                here, *others = neighbours()
            else:
                here, others = planes_after()
            self.local.append(
                pltpu.make_async_copy(source(from_ref, here), target(to_ref, here), local.at[i])
            )
            self.copies += [
                send(source(from_ref, p), target(to_ref, here), sems, 3 * i + k, {axis: p})
                for k, p in enumerate(others)
            ]
        for copy in self.local + self.copies:
            copy.start()

    def end(self):
        for copy in self.local + self.copies:
            copy.wait()


def block_of(ref, place):
    return ref.at[place]


def swap_blocks(x, axis):
    return (x, axis, x.shape, block_of, block_of)


def gather_kernel(turned, halved, early, aside, trade, finish, keep, *refs):
    refs = bind(refs, (2, 1 + halved + keep, 7), aside, trade, finish)
    x_ref, w_ref, all_ref, *refs = refs
    if halved:
        full_ref, *refs = refs
    if keep:
        y_ref, *refs = refs
    xbuf, wbuf, ybuf, load, done, *sems = refs
    me, across, along, far = neighbours()
    rows = x_ref.shape[0]
    half = rows // 2
    core = lax.axis_index("core")
    places = [{"tp": across}, {"tp": along}]
    if halved:
        places.append({"core": 1 - core})
    mine = pltpu.make_async_copy(x_ref, xbuf.at[me], load.at[0])
    mine.start()
    if halved:
        planes, part, _ = w_ref.shape
        places_of = [
            pl.ds(pl.multiple_of((z * 2 + core) * part, part), part) for z in range(planes)
        ]
        weights = [
            pltpu.make_async_copy(w_ref.at[z], wbuf.at[places_of[z]], load.at[1 + z])
            for z in range(planes)
        ]
    else:
        weights = [pltpu.make_async_copy(w_ref, wbuf, load.at[1])]
    for copy in weights:
        copy.start()
    if trade.items:
        greet_all()
    else:
        greet(places)

    def block(owner, part):
        return xbuf.at[owner, pl.ds(part * half, half)]

    def pass_on(index, owner, part, place):
        return send(block(owner, part), block(owner, part), sems, index, place)

    first = [
        send(x_ref.at[pl.ds(0, half)], block(me, 0), sems, 0, {"tp": across}),
        send(x_ref.at[pl.ds(half, half)], block(me, 1), sems, 1, {"tp": along}),
        send(x_ref.at[pl.ds(half, half)], block(me, 1), sems, 2, {"tp": across}),
        send(x_ref.at[pl.ds(0, half)], block(me, 0), sems, 3, {"tp": along}),
    ]
    for copy in first:
        copy.start()
    swaps = []
    if halved:
        for z in range(planes):
            swaps.append(send(w_ref.at[z], wbuf.at[places_of[z]], sems, 6 + z, {"core": 1 - core}))
        for copy in swaps:
            copy.start()
    trade.begin()
    aside.load()
    finish.load()
    mine.wait()
    for copy in weights:
        copy.wait()
    for step in range(early):
        aside.step(step)
    first[0].wait_recv()
    on_a = pass_on(4, across, 0, {"tp": along})
    on_a.start()
    first[1].wait_recv()
    on_b = pass_on(5, along, 1, {"tp": across})
    on_b.start()
    for copy in swaps:
        copy.wait()
    for step in range(early, 3):
        aside.step(step)

    tile = tile_of(ybuf.shape[-1])
    outs = []
    if halved:
        outs.append(pltpu.make_async_copy(wbuf, full_ref, done.at[4]))
        outs[-1].start()

    def compute(owner, index):
        @pl.loop(0, ybuf.shape[-1] // tile)
        def _(step):
            columns = pl.ds(pl.multiple_of(step * tile, tile), tile)
            ybuf[index, :, columns] = multiply(xbuf[owner], wbuf, columns, turned).astype(
                ybuf.dtype
            )

        if keep:
            copy = pltpu.make_async_copy(ybuf.at[index], y_ref.at[owner], done.at[index])
            copy.start()
            outs.append(copy)
        finish.run(index, owner, ybuf.at[index])

    compute(me, 0)
    first[2].wait_recv()
    compute(across, 1)
    first[3].wait_recv()
    compute(along, 2)
    on_a.wait_recv()
    on_b.wait_recv()
    copy = pltpu.make_async_copy(xbuf, all_ref, load.at[0])
    copy.start()
    outs.append(copy)
    compute(far, 3)
    for copy in first + [on_a, on_b]:
        copy.wait_send()
    for copy in outs:
        copy.wait()
    finish.end()
    trade.end()


def gather_matmul(
    ident, x, w, turned=False, halved=False, width=None, aside=None, early=3, trade=(),
    finish=None, keep=True,
):
    rows, depth = x.shape
    if halved:
        planes, part, columns = w.shape
        whole = (planes * 2 * part, columns)
    else:
        whole = w.shape
    width = width or (whole[0] if turned else whole[1])
    riders = [aside or nothing(), Trade(*trade), finish or Finish([], [], None)]
    shapes = [jax.ShapeDtypeStruct((4, rows, depth), x.dtype)]
    if halved:
        shapes.append(jax.ShapeDtypeStruct(whole, w.dtype))
    if keep:
        shapes.append(jax.ShapeDtypeStruct((4, rows, width), jnp.float32))
    hbm = pl.BlockSpec(memory_space=pl.ANY)
    got = pl.pallas_call(
        functools.partial(gather_kernel, turned, halved, early, *riders, keep),
        out_shape=shapes + [y for rider in riders for y in rider.outs],
        in_specs=[hbm, hbm] + [y for rider in riders for y in rider.in_specs],
        out_specs=[hbm] * len(shapes) + [y for rider in riders for y in rider.out_specs],
        scratch_shapes=[
            pltpu.VMEM((4, rows, depth), x.dtype),
            pltpu.VMEM(whole, w.dtype),
            pltpu.VMEM((4, rows, width), jnp.float32),
            pltpu.SemaphoreType.DMA((6,)),
            pltpu.SemaphoreType.DMA((5,)),
            pltpu.SemaphoreType.DMA((10,)),
            pltpu.SemaphoreType.DMA((10,)),
            *[y for rider in riders for y in rider.scratch],
        ],
        compiler_params=pltpu.CompilerParams(
            collective_id=ident, has_side_effects=True, vmem_limit_bytes=VMEM_BYTES
        ),
        cost_estimate=pl.CostEstimate(
            flops=8 * rows * depth * width,
            bytes_accessed=30 * 3_000_000,
            transcendentals=0,
        ),
        name="gather_matmul",
    )(x, w, *[y for rider in riders for y in rider.operands])
    return [
        got[0].reshape(4 * rows, depth),
        got[1] if halved else w,
        *[part.reshape(4 * rows, width) for part in got[1 + halved : len(shapes)]],
        *got[len(shapes) :],
    ]


def head_finish(rows, width, gain):
    def work(product, ins, outs):
        (gain_ref,), (out_ref,) = ins, outs
        size = width // 2
        for at in range(0, size, 128):
            keys = pair_norm(product[:, at : at + 128])[0] * gain_ref[:, at : at + 128]
            out_ref[:, at : at + 128] = keys.astype(out_ref.dtype)
        out_ref[:, size:] = product[:, size:].astype(out_ref.dtype)

    gains = jnp.broadcast_to(gain[None], (4, 1, width // 2))
    return Finish([gains], [jax.ShapeDtypeStruct((4, rows, width), jnp.bfloat16)], work)


def swiglu_finish(grads):
    rows, size = grads.shape[0] // 4, grads.shape[1]

    def work(product, ins, outs):
        (grad_ref,), (ffn_ref, back_ref) = ins, outs

        @pl.loop(0, rows // 32)
        def _(step):
            strip = pl.ds(pl.multiple_of(step * 32, 32), 32)
            for at in range(0, size, 256):
                lanes, ups = pl.ds(at, 256), pl.ds(size + at, 256)
                gate, up, grad = product[strip, lanes], product[strip, ups], grad_ref[strip, lanes]
                sig = 1.0 / (1.0 + jnp.exp(-gate))
                silu = gate * sig
                ffn_ref[strip, lanes] = (silu * up).astype(ffn_ref.dtype)
                back = grad * up * sig * (1.0 + gate * (1.0 - sig))
                back_ref[strip, lanes] = back.astype(back_ref.dtype)
                back_ref[strip, ups] = (grad * silu).astype(back_ref.dtype)

    return Finish(
        [grads.reshape(4, rows, size)],
        [jax.ShapeDtypeStruct((4, rows, n), jnp.bfloat16) for n in (size, 2 * size)],
        work,
    )


def finished(aside, out_ref):
    count = len(aside.operands)
    for copy in aside.loads:
        copy.wait()
    if aside.steps:
        aside.steps(out_ref, aside.refs[2][:count], aside.refs[1], aside.refs[2][count + 1 :])


def scatter_kernel(turned, aside, trade, after, *refs):
    refs = bind(refs, (2, 1, 10), aside, trade, after)
    x_hbm, w_hbm, out_ref, sums, far_out, near_out, relay, land, s0, s1, x_ref, w_ref, load = refs
    me, across, along, far = neighbours()
    sems = (s0, s1)
    rows, width = out_ref.shape
    half = rows // 2
    top, low = pl.ds(0, half), pl.ds(half, half)
    tile = tile_of(width)
    to_across, to_along = {"tp": across}, {"tp": along}
    weights = pltpu.make_async_copy(w_hbm, w_ref, load.at[4])
    weights.start()
    blocks = {}
    for k, owner in enumerate((far, across, along, me)):
        blocks[k] = pltpu.make_async_copy(x_hbm.at[owner], x_ref.at[owner], load.at[k])
        blocks[k].start()
    aside.load()
    after.load()
    if trade.items:
        greet_all()
    else:
        greet([to_across, to_along])

    def tiles(body):
        @pl.loop(0, width // tile)
        def _(step):
            body(pl.ds(pl.multiple_of(step * tile, tile), tile))

    def product(owner, columns, part=slice(None)):
        return multiply(x_ref[owner, part], w_ref, columns, turned)

    weights.wait()
    blocks[0].wait()

    @tiles
    def _(columns):
        far_out[top, columns] = product(far, columns, top).astype(far_out.dtype)

    far_a = send(far_out.at[top], relay.at[0], sems, 0, to_across)
    far_a.start()

    @tiles
    def _(columns):
        far_out[low, columns] = product(far, columns, low).astype(far_out.dtype)

    far_b = send(far_out.at[low], relay.at[1], sems, 1, to_along)
    far_b.start()
    blocks[1].wait()

    @tiles
    def _(columns):
        part = product(across, columns)
        near_out[0, top, columns] = part[:half].astype(near_out.dtype)
        sums[0, :, columns] = part[half:]

    across_a = send(near_out.at[0, top], land.at[0, top], sems, 2, to_across)
    across_a.start()
    blocks[2].wait()

    @tiles
    def _(columns):
        part = product(along, columns)
        near_out[1, low, columns] = part[half:].astype(near_out.dtype)
        sums[1, :, columns] = part[:half]

    along_b = send(near_out.at[1, low], land.at[1, low], sems, 3, to_along)
    along_b.start()
    trade.begin()
    aside.step(0)
    far_b.wait_recv()

    @tiles
    def _(columns):
        near_out[0, low, columns] = (
            sums[0, :, columns] + relay[1, :, columns].astype(jnp.float32)
        ).astype(near_out.dtype)

    across_b = send(near_out.at[0, low], land.at[0, low], sems, 4, to_across)
    across_b.start()
    far_a.wait_recv()

    @tiles
    def _(columns):
        near_out[1, top, columns] = (
            sums[1, :, columns] + relay[0, :, columns].astype(jnp.float32)
        ).astype(near_out.dtype)

    along_a = send(near_out.at[1, top], land.at[1, top], sems, 5, to_along)
    along_a.start()
    aside.step(1)
    aside.step(2)
    blocks[3].wait()

    @tiles
    def _(columns):
        out_ref[:, columns] = product(me, columns)

    for copy in (across_a, along_b, across_b, along_a):
        copy.wait_recv()

    @tiles
    def _(columns):
        out_ref[:, columns] += land[0, :, columns].astype(jnp.float32) + land[
            1, :, columns
        ].astype(jnp.float32)

    finished(after, out_ref)
    for copy in (far_a, far_b, across_a, along_b, across_b, along_a):
        copy.wait_send()
    trade.end()


def matmul_scatter(ident, x, w, turned=False, aside=None, trade=(), after=None):
    riders = [aside or nothing(), Trade(*trade), after or nothing()]
    rows, depth = x.shape[0] // 4, x.shape[1]
    width = w.shape[0] if turned else w.shape[1]
    vmem = pl.BlockSpec(memory_space=pltpu.VMEM)
    return pl.pallas_call(
        functools.partial(scatter_kernel, turned, *riders),
        out_shape=[jax.ShapeDtypeStruct((rows, width), jnp.float32)]
        + [y for rider in riders for y in rider.outs],
        in_specs=[pl.BlockSpec(memory_space=pl.ANY)] * 2
        + [y for rider in riders for y in rider.in_specs],
        out_specs=[vmem] + [y for rider in riders for y in rider.out_specs],
        scratch_shapes=[
            pltpu.VMEM((2, rows // 2, width), jnp.float32),
            pltpu.VMEM((rows, width), jnp.bfloat16),
            pltpu.VMEM((2, rows, width), jnp.bfloat16),
            pltpu.VMEM((2, rows // 2, width), jnp.bfloat16),
            pltpu.VMEM((2, rows, width), jnp.bfloat16),
            pltpu.SemaphoreType.DMA((6,)),
            pltpu.SemaphoreType.DMA((6,)),
            pltpu.VMEM((4, rows, depth), x.dtype),
            pltpu.VMEM(w.shape, w.dtype),
            pltpu.SemaphoreType.DMA((5,)),
            *[y for rider in riders for y in rider.scratch],
        ],
        compiler_params=pltpu.CompilerParams(
            collective_id=ident, has_side_effects=True, vmem_limit_bytes=VMEM_BYTES
        ),
        cost_estimate=pl.CostEstimate(
            flops=8 * rows * depth * width,
            bytes_accessed=30 * 3_000_000,
            transcendentals=0,
        ),
        name="matmul_scatter",
    )(x.reshape(4, rows, depth), w, *[y for rider in riders for y in rider.operands])


def outer_kernel(count, *refs):
    pairs, outs = refs[: 2 * count], refs[2 * count : 3 * count]
    lefts, rights, owns, aways, lands = [
        refs[(3 + k) * count : (4 + k) * count] for k in range(5)
    ]
    load, s0, s1 = refs[8 * count :]
    core = lax.axis_index("core")
    to_core = {"core": 1 - core}
    loads = []
    for i in range(count):
        left, right = pairs[2 * i : 2 * i + 2]
        blocks = outs[i].shape[0]
        size = left.shape[1] // blocks
        copies = [pltpu.make_async_copy(right, rights[i], load.at[5 * i])]
        for z in range(blocks):
            at = pl.ds(z * size, size)
            copies.append(
                pltpu.make_async_copy(left.at[:, at], lefts[i].at[:, at], load.at[5 * i + 1 + z])
            )
        for copy in copies:
            copy.start()
        loads.append(copies)
    greet([to_core])
    sent = []
    for i in range(count):
        blocks, rows, width = outs[i].shape
        tile = tile_of(width)
        loads[i][0].wait()
        for z in range(blocks):
            loads[i][1 + z].wait()
            left = lefts[i][:, z * 2 * rows : (z + 1) * 2 * rows]

            @pl.loop(0, width // tile)
            def _(step):
                columns = pl.ds(pl.multiple_of(step * tile, tile), tile)
                product = lax.dot_general(
                    left, rights[i][:, columns], (((0,), (0,)), ((), ())),
                    preferred_element_type=jnp.float32,
                )
                first, second = product[:rows], product[rows:]
                mine = jnp.where(core == 0, first, second)
                away = jnp.where(core == 0, second, first)
                owns[i][z, :, columns] = mine
                aways[i][z, :, columns] = away.astype(aways[i].dtype)

            copy = send(aways[i].at[z], lands[i].at[z], (s0, s1), 4 * i + z, to_core)
            copy.start()
            sent.append((i, z, copy))
    for i, z, copy in sent:
        copy.wait_recv()
        tile = tile_of(outs[i].shape[-1])

        @pl.loop(0, outs[i].shape[-1] // tile)
        def _(step):
            columns = pl.ds(pl.multiple_of(step * tile, tile), tile)
            outs[i][z, :, columns] = (
                owns[i][z, :, columns] + lands[i][z, :, columns].astype(jnp.float32)
            ).astype(outs[i].dtype)

    for _, _, copy in sent:
        copy.wait_send()


def outer(ident, *items):
    bf, f32 = jnp.bfloat16, jnp.float32
    shapes = [
        (blocks, left.shape[1] // (2 * blocks), right.shape[1]) for left, right, blocks in items
    ]
    count = len(items)
    hbm, vmem = pl.BlockSpec(memory_space=pl.ANY), pl.BlockSpec(memory_space=pltpu.VMEM)
    return pl.pallas_call(
        functools.partial(outer_kernel, count),
        out_shape=[jax.ShapeDtypeStruct(shape, bf) for shape in shapes],
        in_specs=[hbm] * (2 * count),
        out_specs=[vmem] * count,
        scratch_shapes=[
            *[pltpu.VMEM(left.shape, bf) for left, _, _ in items],
            *[pltpu.VMEM(right.shape, bf) for _, right, _ in items],
            *[pltpu.VMEM(shape, f32) for shape in shapes],
            *[pltpu.VMEM(shape, bf) for shape in shapes],
            *[pltpu.VMEM(shape, bf) for shape in shapes],
            pltpu.SemaphoreType.DMA((5 * count,)),
            pltpu.SemaphoreType.DMA((4 * count,)),
            pltpu.SemaphoreType.DMA((4 * count,)),
        ],
        compiler_params=pltpu.CompilerParams(
            collective_id=ident, has_side_effects=True, vmem_limit_bytes=VMEM_BYTES
        ),
        cost_estimate=pl.CostEstimate(
            flops=sum(2 * left.size * right.shape[1] for left, right, _ in items),
            bytes_accessed=20_000_000,
            transcendentals=0,
        ),
        name="outer",
    )(*[x for left, right, _ in items for x in (left, right)])


class Gathering:
    def __init__(self, ins, outs, load, sems):
        self.ins, self.outs, self.sems = ins, outs, sems
        self.me, self.across, self.along, self.far = neighbours()
        self.core = lax.axis_index("core")
        self.to_across, self.to_along = {"tp": self.across}, {"tp": self.along}
        self.to_core = {"core": 1 - self.core}
        self.local = [
            pltpu.make_async_copy(x, outs[i].at[self.me, self.core], load.at[i])
            for i, x in enumerate(ins)
        ]
        for copy in self.local:
            copy.start()

    def half(self, i, part):
        rows = self.ins[i].shape[0] // 2
        return pl.ds(part * rows, rows)

    def first(self, i, part, index, place):
        rows = self.half(i, part)
        target = self.outs[i].at[self.me, self.core, rows]
        return send(self.ins[i].at[rows], target, self.sems, 10 * i + index, place)

    def pass_on(self, i, owner, part, index, place):
        block = self.outs[i].at[owner, self.core, self.half(i, part)]
        return send(block, block, self.sems, 10 * i + index, place)

    def to_sibling(self, i, owner, index):
        block = self.outs[i].at[owner, self.core]
        return send(block, block, self.sems, 10 * i + index, self.to_core)

    def begin(self):
        self.begun = []
        for i, x in enumerate(self.ins):
            target = self.outs[i].at[self.me, self.core]
            copies = [
                self.first(i, 0, 0, self.to_across),
                self.first(i, 1, 1, self.to_along),
                self.first(i, 1, 2, self.to_across),
                self.first(i, 0, 3, self.to_along),
                send(x, target, self.sems, 10 * i + 6, self.to_core),
            ]
            for copy in copies:
                copy.start()
            self.begun.append(copies)

    def relay(self):
        for i, copies in enumerate(self.begun):
            copies[0].wait_recv()
            copies.append(self.pass_on(i, self.across, 0, 4, self.to_along))
            copies[5].start()
            copies[1].wait_recv()
            copies.append(self.pass_on(i, self.along, 1, 5, self.to_across))
            copies[6].start()

    def hand(self):
        for i, copies in enumerate(self.begun):
            copies[2].wait_recv()
            copies.append(self.to_sibling(i, self.across, 7))
            copies[7].start()
            copies[3].wait_recv()
            copies.append(self.to_sibling(i, self.along, 8))
            copies[8].start()
            copies[5].wait_recv()
            copies[6].wait_recv()
            copies.append(self.to_sibling(i, self.far, 9))
            copies[9].start()

    def end(self):
        for copies, local in zip(self.begun, self.local):
            for copy in copies[4:5] + copies[7:]:
                copy.wait_recv()
            for copy in copies:
                copy.wait_send()
            local.wait()


class Returning:
    def __init__(self, back, home, stage, load, sems, base):
        self.back, self.home, self.stage, self.load = back, home, stage, load
        self.sems, self.base = sems, base
        self.me, *self.peers = neighbours()
        self.plane, self.others = planes_after()
        self.stay = pltpu.make_async_copy(back.at[self.plane], stage.at[self.plane], load)
        self.keep = pltpu.make_async_copy(stage.at[self.me], home.at[self.me], load)

    def begin(self):
        self.stay.start()
        self.out = [
            send(
                self.back.at[p], self.stage.at[self.plane], self.sems, self.base + k, {"seq": p}
            )
            for k, p in enumerate(self.others)
        ]
        for copy in self.out:
            copy.start()

    def turn(self):
        for copy in self.out:
            copy.wait_recv()
        self.stay.wait()
        self.last = [
            send(
                self.stage.at[p], self.home.at[self.me], self.sems, self.base + 3 + k, {"tp": p}
            )
            for k, p in enumerate(self.peers)
        ]
        for copy in self.last:
            copy.start()
        self.keep.start()

    def end(self):
        for copy in self.last:
            copy.wait_recv()
        self.keep.wait()
        for copy in self.out + self.last:
            copy.wait_send()


class Home:
    def __init__(self, backs):
        self.outs, self.operands, self.scratch = [], [], []
        for back in backs:
            tall, wide = back.shape
            blocks = (4, tall // 4, wide)
            self.operands.append(back.reshape(blocks))
            self.outs.append(jax.ShapeDtypeStruct(blocks, back.dtype))
            self.scratch += [
                pltpu.VMEM(blocks, back.dtype),
                *[pltpu.SemaphoreType.DMA((n,)) for n in (1, 6, 6)],
            ]
        self.in_specs = self.out_specs = [pl.BlockSpec(memory_space=pl.ANY)] * len(self.outs)
        self.counts = (len(self.operands), len(self.outs), len(self.scratch))
        self.refs = [None] * 3

    def begin(self):
        self.ways = []
        for i, (back, home) in enumerate(zip(*self.refs[:2])):
            stage, load, *sems = self.refs[2][4 * i : 4 * i + 4]
            self.ways.append(Returning(back, home, stage, load.at[0], sems, 0))
        for way in self.ways:
            way.begin()

    def turn(self):
        for way in self.ways:
            way.turn()

    def end(self):
        for way in self.ways:
            way.end()


class Total:
    def __init__(self, x):
        vmem = pl.BlockSpec(memory_space=pltpu.VMEM)
        self.outs, self.operands, self.scratch = [], [], []
        if x is not None:
            rows, width = x.shape
            self.operands = [x]
            self.outs = [jax.ShapeDtypeStruct((4, 2, rows, width), jnp.float32)]
            self.scratch = [
                pltpu.VMEM((3, rows, width // 4), jnp.float32),
                *[pltpu.SemaphoreType.DMA((10,))] * 2,
            ]
        self.in_specs = self.out_specs = [vmem] * len(self.outs)
        self.counts = (len(self.operands), len(self.outs), len(self.scratch))
        self.refs = [None] * 3

    def begin(self):
        if not self.operands:
            return
        (x_ref,), (out_ref,), (land, *sems) = self.refs
        me, *peers = neighbours()
        core = lax.axis_index("core")
        plane, others = planes_after()
        quarter = x_ref.shape[1] // 4

        def columns(t):
            return pl.ds(pl.multiple_of(t * quarter, quarter), quarter)

        self.first = [
            send(x_ref.at[:, columns(p)], land.at[k], sems, k, {"tp": p})
            for k, p in enumerate(peers)
        ]
        for copy in self.first:
            copy.start()

    def go_on(self):
        if not self.operands:
            return
        (x_ref,), (out_ref,), (land, *sems) = self.refs
        me, *peers = neighbours()
        core = lax.axis_index("core")
        plane, others = planes_after()
        quarter = x_ref.shape[1] // 4

        def columns(t):
            return pl.ds(pl.multiple_of(t * quarter, quarter), quarter)

        for copy in self.first:
            copy.wait_recv()
        mine = (x_ref[:, columns(me)] + land[0]) + (land[1] + land[2])
        out_ref[plane, core, :, columns(me)] = mine
        here = out_ref.at[plane, core, :, columns(me)]
        second = [send(here, here, sems, 3 + k, {"seq": p}) for k, p in enumerate(others)]
        for copy in second:
            copy.start()
        for copy in second:
            copy.wait_recv()
        here = out_ref.at[:, core, :, columns(me)]
        self.third = [send(here, here, sems, 6 + k, {"tp": p}) for k, p in enumerate(peers)]
        for copy in self.third:
            copy.start()
        self.copies = self.first + second + self.third

    def end(self):
        if not self.operands:
            return
        (_,), (out_ref,), (_, *sems) = self.refs
        core = lax.axis_index("core")
        for copy in self.third:
            copy.wait_recv()
        here = out_ref.at[:, core]
        swap = send(here, here, sems, 9, {"core": 1 - core})
        swap.start()
        swap.wait_recv()
        for copy in self.copies + [swap]:
            copy.wait_send()


def collect_kernel(count, aside, trade, home, total, *refs):
    refs = bind(refs, (count, count, 3), aside, trade, home, total)
    load, *sems = refs[2 * count :]
    gathering = Gathering(refs[:count], refs[count : 2 * count], load, sems)
    if trade.items or home.operands or total.operands:
        greet_all()
    else:
        greet([gathering.to_across, gathering.to_along, gathering.to_core])
    total.begin()
    gathering.begin()
    total.go_on()
    trade.begin()
    home.begin()
    aside.load()
    aside.step(0)
    gathering.relay()
    aside.step(1)
    home.turn()
    gathering.hand()
    aside.step(2)
    trade.end()
    total.end()
    home.end()
    gathering.end()


def collect(ident, pieces, aside=None, trade=(), backs=(), sums=None):
    riders = [aside or nothing(), Trade(*trade), Home(backs), Total(sums)]
    hbm = pl.BlockSpec(memory_space=pl.ANY)
    count = len(pieces)
    got = pl.pallas_call(
        functools.partial(collect_kernel, count, *riders),
        out_shape=[
            *[jax.ShapeDtypeStruct((4, 2) + p.shape, p.dtype) for p in pieces],
            *[x for rider in riders for x in rider.outs],
        ],
        in_specs=[hbm] * count + [x for rider in riders for x in rider.in_specs],
        out_specs=[hbm] * count + [x for rider in riders for x in rider.out_specs],
        scratch_shapes=[
            pltpu.SemaphoreType.DMA((count,)),
            pltpu.SemaphoreType.DMA((10 * count,)),
            pltpu.SemaphoreType.DMA((10 * count,)),
            *[x for rider in riders for x in rider.scratch],
        ],
        compiler_params=pltpu.CompilerParams(
            collective_id=ident, has_side_effects=True, vmem_limit_bytes=VMEM_BYTES
        ),
        cost_estimate=pl.CostEstimate(
            flops=0, bytes_accessed=80 * sum(p.size for p in pieces), transcendentals=0
        ),
        name="collect",
    )(*pieces, *[x for rider in riders for x in rider.operands])
    return got[:count], got[count:]


def spread_kernel(parts, in_ref, out_ref):
    size = in_ref.shape[-1] // parts
    for q in range(parts):
        for t in range(4):
            out_ref[:, pl.ds((q * 4 + t) * size, size)] = in_ref[
                t, 0, :, pl.ds(q * size, size)
            ].astype(jnp.float32)


def spread(blocks, parts):
    _, cores, rows, width = blocks.shape
    cut = 2
    tall = rows // cut
    return pl.pallas_call(
        functools.partial(spread_kernel, parts),
        grid=(cores, cut),
        out_shape=jax.ShapeDtypeStruct((cores * rows, 4 * width), jnp.float32),
        in_specs=[pl.BlockSpec((4, 1, tall, width), lambda c, k: (0, c, k, 0))],
        out_specs=pl.BlockSpec((tall, 4 * width), lambda c, k: (c * cut + k, 0)),
        compiler_params=pltpu.CompilerParams(vmem_limit_bytes=32 * 1024 * 1024),
        cost_estimate=pl.CostEstimate(
            flops=0, bytes_accessed=6 * blocks.size, transcendentals=0
        ),
        name="spread",
    )(blocks)


def planes_after():
    plane = lax.axis_index("seq")
    return plane, [lax.rem(plane + k, 4) for k in (1, 2, 3)]


def greet_all():
    _, across, along, far = neighbours()
    _, others = planes_after()
    greet(
        [{"tp": p} for p in (across, along, far)]
        + [{"core": 1 - lax.axis_index("core")}]
        + [{"seq": p} for p in others]
    )


def arrive_kernel(
    tok_ref, cot_ref, msg_ref, w_ref, qkv_ref, wout_ref, down_ref, gateup_ref,
    in_ref, cots_ref, msgs_ref, mod_ref, qkv_cut, down_cut, gateup_cut,
    stage, wbuf, part, land, qkv_buf, down_buf, gateup_buf, load, cuts, s0, s1,
):
    sems = (s0, s1)
    me, across, along, far = neighbours()
    core = lax.axis_index("core")
    plane, others = planes_after()
    peers = [across, along, far]
    quarter = mod_ref.shape[1] // 4
    depth = msgs_ref.shape[-1]
    columns = pl.ds(pl.multiple_of(me * quarter, quarter), quarter)
    weights = pltpu.make_async_copy(w_ref.at[:, columns], wbuf, load.at[0])
    weights.start()
    cutting = []

    def cut(source, target, parts, at):
        rows, size = target.shape[0], source.shape[1] // (parts * 4)
        for q in range(parts):
            lanes = pl.ds(pl.multiple_of((q * 4 + me) * size, size), size)
            cutting.append(
                pltpu.make_async_copy(
                    source.at[pl.ds(pl.multiple_of(core * rows, rows), rows), lanes],
                    target.at[:, pl.ds(at + q * size, size)],
                    cuts.at[len(cutting)],
                )
            )

    cut(qkv_ref, qkv_buf, 3, 0)
    cut(wout_ref, qkv_buf, 1, qkv_ref.shape[1] // 4)
    cut(gateup_ref, gateup_buf, 8, 0)
    share = down_cut.shape[0]
    rows = pl.ds(pl.multiple_of((me * 2 + core) * share, share), share)
    cutting.append(pltpu.make_async_copy(down_ref.at[rows], down_buf, cuts.at[len(cutting)]))
    for copy in cutting:
        copy.start()
    keeping = [
        pltpu.make_async_copy(source, target, cuts.at[13 + k])
        for k, (source, target) in enumerate(
            zip((qkv_buf, down_buf, gateup_buf), (qkv_cut, down_cut, gateup_cut))
        )
    ]
    mine = pltpu.make_async_copy(tok_ref.at[me], stage.at[me], load.at[1])
    mine.start()
    msgs_ref[me, core] = msg_ref[:, pl.ds(pl.multiple_of(plane * depth, depth), depth)]
    greet_all()
    here = msgs_ref.at[me, core]
    first = [send(here, here, sems, k, {"tp": p}) for k, p in enumerate(peers)]
    for copy in first:
        copy.start()
    spread_out = [
        send(tok_ref.at[p], stage.at[me], sems, 3 + k, {"tp": p}) for k, p in enumerate(peers)
    ]
    for copy in spread_out:
        copy.start()
    cotangents = [
        send(cot_ref.at[p], cots_ref.at[me], sems, 16 + k, {"tp": p}) for k, p in enumerate(peers)
    ]
    for copy in cotangents:
        copy.start()
    own_cots = pltpu.make_async_copy(cot_ref.at[me], cots_ref.at[me], load.at[3])
    own_cots.start()
    for copy in first:
        copy.wait_recv()
    here = msgs_ref.at[:, core]
    swap = send(here, here, sems, 6, {"core": 1 - core})
    swap.start()
    weights.wait()
    conditions = msgs_ref[:, core].reshape(4 * 8, depth).astype(wbuf.dtype)
    tile = 512
    for copy in cutting:
        copy.wait()
    for copy in keeping:
        copy.start()
    for step in range(quarter // tile):
        at = pl.ds(step * tile, tile)
        part[:, :, at] = jnp.dot(
            conditions, wbuf[:, at], preferred_element_type=jnp.float32
        ).reshape(4, 8, tile)
    second = [
        send(part.at[p], land.at[k], sems, 7 + k, {"seq": p}) for k, p in enumerate(others)
    ]
    for copy in second:
        copy.start()
    mine.wait()
    for copy in spread_out:
        copy.wait_recv()
    third = [
        send(stage.at[p], in_ref.at[plane], sems, 10 + k, {"seq": p})
        for k, p in enumerate(others)
    ]
    for copy in third:
        copy.start()
    stay = pltpu.make_async_copy(stage.at[plane], in_ref.at[plane], load.at[2])
    stay.start()
    for copy in second:
        copy.wait_recv()
    mod_ref[:, columns] = (part[plane] + land[0]) + (land[1] + land[2])
    here = mod_ref.at[:, columns]
    fourth = [send(here, here, sems, 13 + k, {"tp": p}) for k, p in enumerate(peers)]
    for copy in fourth:
        copy.start()
    swap.wait_recv()
    for copy in fourth + third + cotangents:
        copy.wait_recv()
    stay.wait()
    own_cots.wait()
    for copy in keeping:
        copy.wait()
    for copy in first + spread_out + cotangents + [swap] + second + third + fourth:
        copy.wait_send()


def arrive(ident, tokens, cotangent, message, w_mod, w_qkv, w_out, w_down, w_gateup):
    rows, width = tokens.shape
    share, kind = w_qkv.shape[0] // 2, w_qkv.dtype
    depth, wide = w_mod.shape
    vmem, hbm = pl.BlockSpec(memory_space=pltpu.VMEM), pl.BlockSpec(memory_space=pl.ANY)
    return pl.pallas_call(
        arrive_kernel,
        out_shape=[
            jax.ShapeDtypeStruct((4, rows // 4, width), tokens.dtype),
            jax.ShapeDtypeStruct((4, rows // 4, width), cotangent.dtype),
            jax.ShapeDtypeStruct((4, 2, 8, depth), jnp.float32),
            jax.ShapeDtypeStruct((8, wide), jnp.float32),
            jax.ShapeDtypeStruct((share, (w_qkv.shape[1] + w_out.shape[1]) // 4), kind),
            jax.ShapeDtypeStruct((w_down.shape[0] // 8, w_down.shape[1]), kind),
            jax.ShapeDtypeStruct((share, w_gateup.shape[1] // 4), kind),
        ],
        in_specs=[hbm, hbm, vmem] + [hbm] * 5,
        out_specs=[hbm, hbm, vmem, vmem, hbm, hbm, hbm],
        scratch_shapes=[
            pltpu.VMEM((4, rows // 4, width), tokens.dtype),
            pltpu.VMEM((depth, wide // 4), w_mod.dtype),
            pltpu.VMEM((4, 8, wide // 4), jnp.float32),
            pltpu.VMEM((3, 8, wide // 4), jnp.float32),
            pltpu.VMEM((share, (w_qkv.shape[1] + w_out.shape[1]) // 4), kind),
            pltpu.VMEM((w_down.shape[0] // 8, w_down.shape[1]), kind),
            pltpu.VMEM((share, w_gateup.shape[1] // 4), kind),
            pltpu.SemaphoreType.DMA((4,)),
            pltpu.SemaphoreType.DMA((16,)),
            pltpu.SemaphoreType.DMA((19,)),
            pltpu.SemaphoreType.DMA((19,)),
        ],
        compiler_params=pltpu.CompilerParams(
            collective_id=ident, has_side_effects=True, vmem_limit_bytes=VMEM_BYTES
        ),
        cost_estimate=pl.CostEstimate(flops=0, bytes_accessed=90_000_000, transcendentals=0),
        name="arrive",
    )(
        tokens.reshape(4, rows // 4, width),
        cotangent.reshape(4, rows // 4, width),
        message,
        w_mod,
        w_qkv,
        w_out,
        w_down,
        w_gateup,
    )


def by_rows(rows, sums, body):
    for ref in sums:
        ref[...] = jnp.zeros_like(ref)

    @pl.loop(0, rows // 32)
    def _(step):
        body(pl.ds(pl.multiple_of(step * 32, 32), 32))


def chosen(mod_ref, document, part, width):
    at = pl.ds(part * width, width)
    found = mod_ref[DOCS - 1 : DOCS, at]
    for d in range(DOCS - 1):
        found = jnp.where(document == d, mod_ref[d : d + 1, at], found)
    return found


def tally(ref, row, values):
    ref[row] += (values[:8] + values[8:16]) + (values[16:24] + values[24:])


def tally_docs(ref, row, document, values):
    for d in range(DOCS):
        tally(ref, row + d, jnp.where(document == d, values, 0.0))


def norm_of(values):
    inverse = lax.rsqrt(jnp.mean(values * values, axis=-1, keepdims=True) + eps)
    return values * inverse, inverse


def settle(out_ref, sums):
    out_ref[...] = jnp.sum(sums[...], axis=1)


def after_attention(inputs, mod_doc, document, gain):
    rows, width = inputs.shape

    def work(attn_ref, ins, outs, scratch):
        (x_ref, mod_ref, doc_ref, gain_ref), (residual_ref, hidden_ref) = ins, outs

        def body(strip):
            document = doc_ref[strip, 0:1]
            gate = jnp.tanh(chosen(mod_ref, document, 1, width))
            residual = x_ref[strip, :].astype(jnp.float32) + gate * attn_ref[strip, :]
            residual_ref[strip, :] = residual
            normed, _ = norm_of(residual)
            scale = chosen(mod_ref, document, 2, width)
            hidden_ref[strip, :] = (normed * gain_ref[...] * (1.0 + scale)).astype(
                hidden_ref.dtype
            )

        by_rows(rows, [], body)

    return Aside(
        [inputs, mod_doc, document, gain],
        [
            jax.ShapeDtypeStruct((rows, width), jnp.float32),
            jax.ShapeDtypeStruct((rows, width), jnp.bfloat16),
        ],
        [],
        work,
    )


def after_ffn_back(residual, attn_out, cotangent, weight, mod_doc, document, gain):
    rows, width = residual.shape

    def work(back_ref, ins, outs, scratch):
        res_ref, attn_ref, cot_ref, weight_ref, mod_ref, doc_ref, gain_ref = ins
        grad_ref, attn_back_ref, sum_ref = outs
        (sums,) = scratch

        def body(strip):
            document = doc_ref[strip, 0:1]
            normed, inverse = norm_of(res_ref[strip, :])
            scale = 1.0 + chosen(mod_ref, document, 2, width)
            gain = gain_ref[...]
            back = back_ref[strip, :]
            both = back * normed
            tally(sums, 8, both * scale)
            tally_docs(sums, 0, document, both * gain)
            inner = back * gain * scale
            inner = inner - normed * jnp.mean(inner * normed, axis=-1, keepdims=True)
            grads = cot_ref[strip, :].astype(jnp.float32) * weight_ref[strip, 0:1]
            grads = grads + inverse * inner
            grad_ref[strip, :] = grads
            gate = jnp.tanh(chosen(mod_ref, document, 1, width))
            attn_back_ref[strip, :] = (gate * grads).astype(attn_back_ref.dtype)
            tally_docs(sums, 4, document, grads * attn_ref[strip, :] * (1.0 - gate * gate))

        by_rows(rows, [sums], body)
        settle(sum_ref, sums)

    return Aside(
        [residual, attn_out, cotangent, weight, mod_doc, document, gain],
        [
            jax.ShapeDtypeStruct((rows, width), jnp.float32),
            jax.ShapeDtypeStruct((rows, width), jnp.bfloat16),
            jax.ShapeDtypeStruct((16, width), jnp.float32),
        ],
        [pltpu.VMEM((16, 8, width), jnp.float32)],
        work,
    )


def after_ffn(residual, cotangent, weight, mod_doc, document):
    rows, width = residual.shape

    def work(down_ref, ins, outs, scratch):
        res_ref, cot_ref, weight_ref, mod_ref, doc_ref = ins
        result_ref, sum_ref = outs
        (sums,) = scratch

        def body(strip):
            document = doc_ref[strip, 0:1]
            gate = jnp.tanh(chosen(mod_ref, document, 3, width))
            down = down_ref[strip, :]
            result_ref[strip, :] = (res_ref[strip, :] + gate * down).astype(result_ref.dtype)
            grads = cot_ref[strip, :].astype(jnp.float32) * weight_ref[strip, 0:1]
            tally_docs(sums, 0, document, grads * down * (1.0 - gate * gate))

        by_rows(rows, [sums], body)
        settle(sum_ref, sums)

    return Aside(
        [residual, cotangent, weight, mod_doc, document],
        [
            jax.ShapeDtypeStruct((rows, width), jnp.bfloat16),
            jax.ShapeDtypeStruct((8, width), jnp.float32),
        ],
        [pltpu.VMEM((8, 8, width), jnp.float32)],
        work,
    )


def after_input_back(inputs, grads, mod_doc, document, gain):
    rows, width = inputs.shape

    def work(back_ref, ins, outs, scratch):
        x_ref, grad_ref, mod_ref, doc_ref, gain_ref = ins
        out_ref, sum_ref = outs
        (sums,) = scratch

        def body(strip):
            document = doc_ref[strip, 0:1]
            normed, inverse = norm_of(x_ref[strip, :].astype(jnp.float32))
            scale = 1.0 + chosen(mod_ref, document, 0, width)
            gain = gain_ref[...]
            back = back_ref[strip, :]
            both = back * normed
            tally(sums, 4, both * scale)
            tally_docs(sums, 0, document, both * gain)
            inner = back * gain * scale
            inner = inner - normed * jnp.mean(inner * normed, axis=-1, keepdims=True)
            out_ref[strip, :] = (grad_ref[strip, :] + inverse * inner).astype(out_ref.dtype)

        by_rows(rows, [sums], body)
        settle(sum_ref, sums)

    return Aside(
        [inputs, grads, mod_doc, document, gain],
        [
            jax.ShapeDtypeStruct((rows, width), jnp.bfloat16),
            jax.ShapeDtypeStruct((8, width), jnp.float32),
        ],
        [pltpu.VMEM((8, 8, width), jnp.float32)],
        work,
    )


def lanes_of(rows):
    return lax.broadcasted_iota(jnp.int32, (rows, 128), 1)


def pair_norm(values):
    lane = lanes_of(values.shape[0])
    square = values * values
    low = jnp.sum(jnp.where(lane < HDIM, square, 0.0), axis=-1, keepdims=True)
    high = jnp.sum(jnp.where(lane < HDIM, 0.0, square), axis=-1, keepdims=True)
    inverse = jnp.where(lane < HDIM, lax.rsqrt(low / HDIM + eps), lax.rsqrt(high / HDIM + eps))
    return values * inverse, inverse


def pair_back(grads, normed, inverse):
    lane = lanes_of(grads.shape[0])
    inner = grads * normed
    low = jnp.sum(jnp.where(lane < HDIM, inner, 0.0), axis=-1, keepdims=True)
    high = jnp.sum(jnp.where(lane < HDIM, 0.0, inner), axis=-1, keepdims=True)
    return inverse * (grads - normed * (jnp.where(lane < HDIM, low, high) / HDIM))


def pair_turn(values, cosine, sine):
    lane = lanes_of(values.shape[0])
    partner = jnp.where(
        lane % HDIM < HDIM // 2, pltpu.roll(values, 96, 1), pltpu.roll(values, 32, 1)
    )
    return values * cosine + partner * sine


def store_heads(target, strip, pair, spare):
    lane = lanes_of(pair.shape[0])
    first = jnp.where(lane < HDIM, pair, spare)
    second = jnp.where(lane < HDIM, pltpu.roll(pair, HDIM, 1), spare)
    target[strip, 0:128] = first.astype(target.dtype)
    target[strip, 128:256] = second.astype(target.dtype)


def join_heads(first, second):
    lane = lanes_of(first.shape[0])
    return jnp.where(lane < HDIM, first, pltpu.roll(second, HDIM, 1))


def ones_beside(rows):
    lane = lanes_of(rows)
    return jnp.where((lane == HDIM) | (lane == HDIM + 1), 1.0, 0.0)


def not_turned(left, right):
    return lax.dot_general(
        left, right, (((1,), (1,)), ((), ())), preferred_element_type=jnp.float32
    )


STRIP = 256
SPARE = 128.0


def strips(rows, body):
    @pl.loop(0, rows // STRIP)
    def _(step):
        body(pl.ds(pl.multiple_of(step * STRIP, STRIP), STRIP))


def weigh(qa_ref, ka_ref, va_ref, ov_ref):
    for head in range(2):
        at = pl.ds(head * 128, 128)

        def body(strip):
            scores = not_turned(qa_ref[strip, at], ka_ref[:, at])
            weights = jnp.exp(scores).astype(jnp.bfloat16)
            ov_ref[strip, at] = jnp.dot(
                weights, va_ref[:, at], preferred_element_type=jnp.float32
            )

        strips(qa_ref.shape[0], body)


def own_kernel(
    q_ref, k_ref, v_ref, gq_ref, gk_ref, cos_ref, sin_ref, sq_ref, sk_ref,
    qa_ref, ka_ref, va_ref, ov_ref,
):
    def prepare(strip):
        cosine, sine = cos_ref[strip, :], sin_ref[strip, :]
        query = pair_turn(pair_norm(q_ref[strip, :])[0] * gq_ref[...], cosine, sine)
        store_heads(qa_ref, strip, query * HDIM**-0.5, sq_ref[strip, :])
        keys = pair_turn(pair_norm(k_ref[strip, :])[0] * gk_ref[...], cosine, sine)
        store_heads(ka_ref, strip, keys, sk_ref[strip, :])
        store_heads(va_ref, strip, v_ref[strip, :], ones_beside(STRIP))

    strips(q_ref.shape[0], prepare)
    weigh(qa_ref, ka_ref, va_ref, ov_ref)


def cross_kernel(
    qa_ref, k_ref, v_ref, sq_ref, sk_ref, own_ref, gate_ref,
    ka_ref, va_ref, ov_ref, mix_ref, qx_ref,
):
    def prepare(strip):
        store_heads(ka_ref, strip, k_ref[strip, :].astype(jnp.float32), sk_ref[strip, :])
        store_heads(va_ref, strip, v_ref[strip, :].astype(jnp.float32), ones_beside(STRIP))

    strips(k_ref.shape[0], prepare)

    def requery(strip):
        lane = lanes_of(STRIP)
        for head in range(2):
            at = pl.ds(head * 128, 128)
            qx_ref[strip, at] = jnp.where(
                lane < HDIM, qa_ref[strip, at].astype(jnp.float32), sq_ref[strip, :]
            ).astype(qx_ref.dtype)

    strips(qa_ref.shape[0], requery)
    weigh(qx_ref, ka_ref, va_ref, ov_ref)

    def mix(strip):
        parts = []
        for head in range(2):
            at = pl.ds(head * 128, 128)
            own, cross = own_ref[strip, at], ov_ref[strip, at]
            parts.append((own / own[:, 64:65], cross / cross[:, 64:65]))
        own = join_heads(parts[0][0], parts[1][0])
        cross = join_heads(parts[0][1], parts[1][1])
        mix_ref[strip, :] = (own + gate_ref[...] * cross).astype(mix_ref.dtype)

    strips(qa_ref.shape[0], mix)


def back_kernel(own, *refs):
    g_ref, gate_ref, ov_ref, qa_ref, sq_ref, ka_ref, va_ref = refs[:7]
    refs = refs[7:]
    if own:
        k_ref, gk_ref, q_ref, gq_ref, cos_ref, sin_ref, more_ref = refs[:7]
        refs = refs[7:]
    dq_ref, dk_ref, dv_ref, sum_ref, qx, doa, dqt, dqh, dkh, dvh = refs
    rows, count = qa_ref.shape[0], ka_ref.shape[0]
    sum_ref[...] = jnp.zeros_like(sum_ref)
    for head in range(2):
        at = pl.ds(head * 128, 128)

        def prepare(strip):
            lane = lanes_of(STRIP)
            plain = g_ref[strip, :]
            grads = plain * gate_ref[...]
            if head == 1:
                plain = pltpu.roll(plain, HDIM, 1)
                grads = pltpu.roll(grads, HDIM, 1)
            both = ov_ref[strip, at]
            inverse = 1.0 / both[:, 64:65]
            out = jnp.where(lane < HDIM, both * inverse, 0.0)
            if not own:
                sum_ref[0, head : head + 1, :] += jnp.sum(plain * out, axis=0, keepdims=True)
            scaled = (grads * inverse).astype(jnp.bfloat16).astype(jnp.float32)
            delta = jnp.sum(scaled * out, axis=-1, keepdims=True)
            high = delta.astype(jnp.bfloat16).astype(jnp.float32)
            doa[strip, :] = jnp.where(
                lane < HDIM,
                scaled,
                jnp.where(lane == HDIM, -high, jnp.where(lane == HDIM + 1, high - delta, 0.0)),
            ).astype(doa.dtype)
            qx[strip, :] = jnp.where(
                lane < HDIM, qa_ref[strip, at].astype(jnp.float32), sq_ref[strip, :]
            ).astype(qx.dtype)

        strips(rows, prepare)
        dqt[...] = jnp.zeros_like(dqt)

        def block(strip):
            keys, values = ka_ref[strip, at], va_ref[strip, at]
            weights = jnp.exp(not_turned(keys, qx[...]))
            grads = (weights * not_turned(values, doa[...])).astype(jnp.bfloat16)
            dvh[head, strip, :] = jnp.dot(
                weights.astype(jnp.bfloat16), doa[...], preferred_element_type=jnp.float32
            )
            dkh[head, strip, :] = jnp.dot(grads, qx[...], preferred_element_type=jnp.float32)
            dqt[...] += lax.dot_general(
                keys, grads, (((0,), (0,)), ((), ())), preferred_element_type=jnp.float32
            )

        strips(count, block)
        dqh[head] = dqt[...].T * HDIM**-0.5

    def add_up(row, values):
        sum_ref[0, row : row + 1, :] += jnp.sum(values, axis=0, keepdims=True)

    def finish(strip):
        grads = join_heads(dkh[0, strip, :], dkh[1, strip, :])
        if own:
            grads = pair_turn(grads, cos_ref[strip, :], -sin_ref[strip, :])
            normed, inverse = pair_norm(k_ref[strip, :])
            add_up(2, grads * normed)
            grads = pair_back(grads * gk_ref[...], normed, inverse)
        dk_ref[strip, :] = grads.astype(dk_ref.dtype)
        dv_ref[strip, :] = join_heads(dvh[0, strip, :], dvh[1, strip, :]).astype(dv_ref.dtype)

    strips(count, finish)

    def finish_query(strip):
        grads = join_heads(dqh[0, strip, :], dqh[1, strip, :])
        if own:
            grads = pair_turn(grads + more_ref[strip, :], cos_ref[strip, :], -sin_ref[strip, :])
            normed, inverse = pair_norm(q_ref[strip, :])
            add_up(3, grads * normed)
            grads = pair_back(grads * gq_ref[...], normed, inverse)
        dq_ref[strip, :] = grads.astype(dq_ref.dtype)

    strips(rows, finish_query)


def view(ref, index, width=128, offset=0):
    return ref.at[:, pl.ds((offset + index) * width, width)]


def attend(
    projected, heads, gain_q, gain_k, gate, cosine, sine, own_q, own_k, cross_q, cross_k
):
    rows, width = projected.shape[0], projected.shape[1] // 3
    caps, count = heads.shape[0], width // 128
    bf, f32 = jnp.bfloat16, jnp.float32

    def steps(i, ins, outs, scratch):
        raw, heads, gain_q, gain_k, gate, cosine, sine, own_q, own_k, cross_q, cross_k = ins
        qa, ka, va, own, cka, cva, cross, mix = outs
        own_kernel(
            view(raw, i), view(raw, i, offset=count), view(raw, i, offset=2 * count),
            view(gain_q, i), view(gain_k, i), cosine, sine, own_q, own_k,
            view(qa, i, 256), view(ka, i, 256), view(va, i, 256), view(own, i, 256),
        )
        cross_kernel(
            view(qa, i, 256), view(heads, i), view(heads, i, offset=count), cross_q, cross_k,
            view(own, i, 256), view(gate, i), view(cka, i, 256), view(cva, i, 256),
            view(cross, i, 256), view(mix, i), *scratch,
        )

    return Aside(
        [projected, heads, gain_q, gain_k, gate, cosine, sine, own_q, own_k, cross_q, cross_k],
        [
            *[jax.ShapeDtypeStruct((rows, 2 * width), d) for d in (bf, bf, bf, f32)],
            *[jax.ShapeDtypeStruct((caps, 2 * width), bf)] * 2,
            jax.ShapeDtypeStruct((rows, 2 * width), f32),
            jax.ShapeDtypeStruct((rows, width), bf),
        ],
        [pltpu.VMEM((rows, 256), bf)],
        steps,
    )


def cap_back_kernel(g_ref, k_ref, gain_ref, out_ref, sum_ref):
    sum_ref[...] = jnp.zeros_like(sum_ref)

    def body(strip):
        for at in range(0, k_ref.shape[1], 128):
            lanes = pl.ds(at, 128)
            grads = g_ref[strip, lanes].astype(jnp.float32)
            normed, inverse = pair_norm(k_ref[strip, lanes])
            sum_ref[0:1, lanes] += jnp.sum(grads * normed, axis=0, keepdims=True)
            out_ref[strip, lanes] = pair_back(
                grads * gain_ref[:, lanes], normed, inverse
            ).astype(out_ref.dtype)
        values = pl.ds(k_ref.shape[1], k_ref.shape[1])
        out_ref[strip, values] = g_ref[strip, values]

    strips(g_ref.shape[0], body)


def cap_back(grads, cap_proj, gain):
    rows, width = grads.shape
    whole = pl.BlockSpec((rows, width), lambda i: (0, 0))
    part = pl.BlockSpec((rows, width // 2), lambda i: (0, 0))
    return pl.pallas_call(
        cap_back_kernel,
        grid=(1,),
        out_shape=[
            jax.ShapeDtypeStruct((rows, width), jnp.bfloat16),
            jax.ShapeDtypeStruct((8, width // 2), jnp.float32),
        ],
        in_specs=[whole, part, pl.BlockSpec((1, width // 2), lambda i: (0, 0))],
        out_specs=[whole, pl.BlockSpec((8, width // 2), lambda i: (0, 0))],
        compiler_params=pltpu.CompilerParams(vmem_limit_bytes=32 * 1024 * 1024),
        cost_estimate=pl.CostEstimate(
            flops=0, bytes_accessed=6 * grads.size, transcendentals=0
        ),
        name="cap_back",
    )(grads, cap_proj, gain)


def attend_back(grads, gate, ov, qa, spare_q, ka, va, rest=None):
    rows, width = grads.shape
    caps, count = ka.shape[0], width // 128
    bf, f32 = jnp.bfloat16, jnp.float32
    own = rest is not None

    def steps(i, ins, outs, scratch):
        grads, gate, ov, qa, spare_q, ka, va, *rest = ins
        if own:
            all_out, sums = outs
            dq, dk, dv = [view(all_out, i, offset=k * count) for k in range(3)]
        else:
            dq, all_out, sums = outs
            dq, dk, dv = view(dq, i), view(all_out, i), view(all_out, i, offset=count)
        operands = [
            view(grads, i), view(gate, i), view(ov, i, 256), view(qa, i, 256), spare_q,
            view(ka, i, 256), view(va, i, 256),
        ]
        if own:
            raw, gain_k, gain_q, cosine, sine, more = rest
            operands += [view(raw, i, offset=count), view(gain_k, i)]
            operands += [view(raw, i), view(gain_q, i), cosine, sine, view(more, i)]
        back_kernel(own, *operands, dq, dk, dv, sums.at[pl.ds(i, 1)], *scratch)

    return Aside(
        [grads, gate, ov, qa, spare_q, ka, va, *(rest or ())],
        [
            *(
                [jax.ShapeDtypeStruct((rows, 3 * width), bf)]
                if own
                else [
                    jax.ShapeDtypeStruct((rows, width), f32),
                    jax.ShapeDtypeStruct((caps, 2 * width), bf),
                ]
            ),
            jax.ShapeDtypeStruct((count, 8, 128), f32),
        ],
        [
            pltpu.VMEM((rows, 128), bf),
            pltpu.VMEM((rows, 128), bf),
            pltpu.VMEM((128, rows), f32),
            pltpu.VMEM((2, rows, 128), f32),
            pltpu.VMEM((2, caps, 128), f32),
            pltpu.VMEM((2, caps, 128), f32),
        ],
        steps,
    )


def row_stats(values):
    inverse = lax.rsqrt(jnp.mean(values * values, axis=-1, keepdims=True) + eps)
    return (values * inverse, inverse)


def norm_back(grad_normed, normed, inverse):
    inner_mean = jnp.mean(grad_normed * normed, axis=-1, keepdims=True)
    return inverse * (grad_normed - normed * inner_mean)


def head_stats(values):
    shaped = values.reshape(values.shape[0], -1, HDIM)
    normed, inverse = row_stats(shaped)
    return (normed.reshape(values.shape), inverse)


def head_back(grad_normed, normed, inverse):
    shaped_grad = grad_normed.reshape(grad_normed.shape[0], -1, HDIM)
    shaped_norm = normed.reshape(normed.shape[0], -1, HDIM)
    return norm_back(shaped_grad, shaped_norm, inverse).reshape(grad_normed.shape)


def rotary(values, row_pos, col_pos, direction):
    quarter = HDIM // 4
    freqs = 10000.0 ** (-jnp.arange(quarter, dtype=jnp.float32) / quarter)
    angles = jnp.concatenate([row_pos[:, None] * freqs, col_pos[:, None] * freqs], axis=1)
    cosine = jnp.cos(angles)[:, None, :]
    sine = direction * jnp.sin(angles)[:, None, :]
    shaped = values.reshape(values.shape[0], -1, HDIM)
    first_half = shaped[..., : HDIM // 2]
    second_half = shaped[..., HDIM // 2 :]
    turned = jnp.concatenate(
        [first_half * cosine - second_half * sine, second_half * cosine + first_half * sine],
        axis=-1,
    )
    return turned.reshape(values.shape)


def layout(doc_lengths, bucket, positions):
    doc_ends = jnp.cumsum(doc_lengths)
    starts = doc_ends - doc_lengths
    segment = jnp.sum((positions[:, None] >= doc_ends[None, :]).astype(jnp.int32), axis=1)
    matches = segment[:, None] == jnp.arange(DOCS, dtype=jnp.int32)[None, :]
    offset = jnp.sum(jnp.where(matches, starts[None, :], 0), axis=1)
    within = positions - offset
    stride = 32 * (bucket + 1)
    return (segment, (within // stride).astype(jnp.float32), (within % stride).astype(jnp.float32))


def turn_tables(row_pos, col_pos):
    quarter = HDIM // 4
    freqs = 10000.0 ** (-jnp.arange(quarter, dtype=jnp.float32) / quarter)
    angles = jnp.concatenate([row_pos[:, None] * freqs, col_pos[:, None] * freqs], axis=1)
    cosine, sine = jnp.cos(angles), jnp.sin(angles)
    return jnp.tile(cosine, (1, 4)), jnp.concatenate([-sine, sine, -sine, sine], axis=1)


def spare_columns(labels, height):
    lane = jnp.arange(128)[None, :] - HDIM
    at_label = (lane >= 0) & (lane <= DOCS) & (lane == labels[:, None])
    last = lane == DOCS + 1
    if height:
        return jnp.where(at_label, height, jnp.where(last, -height, 0.0)).astype(jnp.float32)
    return (at_label | last).astype(jnp.float32)


def by_head(values):
    return values.reshape(values.shape[0], -1, 1, HDIM).transpose(1, 0, 2, 3)


def from_heads(blocks):
    return blocks.transpose(1, 0, 2, 3).reshape(blocks.shape[1], -1)


def attend_forward(query, keys, values, allowed):
    scale = HDIM ** (-0.5)

    def block(block_args):
        part_q, part_k, part_v = block_args
        scores = (
            jnp.einsum("qhd,khd->hqk", part_q, part_k, preferred_element_type=jnp.float32) * scale
        )
        scores = jnp.where(allowed[None], scores, -1e30)
        row_peak = jnp.max(scores, axis=-1, keepdims=True)
        exp_scores = jnp.exp(scores - row_peak)
        exp_total = jnp.sum(exp_scores, axis=-1, keepdims=True)
        attn_probs = (exp_scores / exp_total).astype(jnp.bfloat16)
        attn_block = jnp.einsum(
            "hqk,khd->qhd", attn_probs, part_v, preferred_element_type=jnp.float32
        )
        return (attn_block, row_peak[..., 0] + jnp.log(exp_total[..., 0]))

    blocks, log_total = lax.map(block, (by_head(query), by_head(keys), by_head(values)))
    return (from_heads(blocks), log_total)


def attend_backward(query, keys, values, allowed, log_total, grad_out):
    scale = HDIM ** (-0.5)

    def block(block_args):
        part_q, part_k, part_v, part_log, part_grad = block_args
        scores = (
            jnp.einsum("qhd,khd->hqk", part_q, part_k, preferred_element_type=jnp.float32) * scale
        )
        scores = jnp.where(allowed[None], scores, -1e30)
        attn_probs = jnp.exp(scores - part_log[..., None])
        grad_probs = jnp.einsum(
            "qhd,khd->hqk", part_grad, part_v, preferred_element_type=jnp.float32
        )
        row_delta = jnp.sum(attn_probs * grad_probs, axis=-1, keepdims=True)
        grad_scores = (attn_probs * (grad_probs - row_delta)).astype(jnp.bfloat16)
        grad_query = (
            jnp.einsum("hqk,khd->qhd", grad_scores, part_k, preferred_element_type=jnp.float32)
            * scale
        )
        grad_keys = (
            jnp.einsum("hqk,qhd->khd", grad_scores, part_q, preferred_element_type=jnp.float32)
            * scale
        )
        grad_values = jnp.einsum(
            "hqk,qhd->khd",
            attn_probs.astype(jnp.bfloat16),
            part_grad,
            preferred_element_type=jnp.float32,
        )
        return (grad_query, grad_keys, grad_values)

    grad_query, grad_keys, grad_values = lax.map(
        block,
        (by_head(query), by_head(keys), by_head(values), log_total, by_head(grad_out)),
    )
    return (from_heads(grad_query), from_heads(grad_keys), from_heads(grad_values))


def matmul(left, right):
    return jnp.dot(left, right, preferred_element_type=jnp.float32)


def contract_right(left, weight):
    return lax.dot_general(
        left, weight, (((1,), (1,)), ((), ())), preferred_element_type=jnp.float32
    )


def contract_rows(left, right):
    return lax.dot_general(
        left, right, (((0,), (0,)), ((), ())), preferred_element_type=jnp.float32
    )


def pick(values, index, axis):
    return lax.dynamic_index_in_dim(values, index, axis, keepdims=False)


def to_plane(values):
    ways = lax.axis_size("tp")
    parts = values.reshape((ways, values.shape[0] // ways) + values.shape[1:])
    parts = lax.all_to_all(parts, "tp", 0, 0, tiled=True)
    parts = lax.all_to_all(parts, "seq", 0, 0, tiled=True)
    return parts.reshape(values.shape)


def from_plane(values):
    ways = lax.axis_size("tp")
    parts = values.reshape((ways, values.shape[0] // ways) + values.shape[1:])
    parts = lax.all_to_all(parts, "seq", 0, 0, tiled=True)
    parts = lax.all_to_all(parts, "tp", 0, 0, tiled=True)
    return parts.reshape(values.shape)


def fast():
    return lax.axis_size("tp") == 4 and lax.axis_size("core") == 2 and lax.axis_size("seq") == 4


def gather_planes(part):
    return lax.all_gather(part, "seq", axis=0, tiled=False)


def join_cores(halves):
    whole = lax.all_gather(halves, "core", axis=1, tiled=False)
    return whole.reshape(-1, halves.shape[-1])


def outer_plane(ident, *items):
    if fast():
        return outer(ident, *items)
    cores = lax.axis_size("core")
    terms = [contract_rows(left, right).astype(jnp.bfloat16) for left, right, _ in items]
    return [
        swap_halves(term.reshape(item[2], cores, -1, term.shape[-1]))
        for term, item in zip(terms, items)
    ]


def scatter_planes(term):
    return lax.psum_scatter(term, "seq", scatter_dimension=0, tiled=False)


def swap_halves(shaped):
    cores, me_c = lax.axis_size("core"), lax.axis_index("core")
    mine = pick(shaped, me_c, 1)
    for step in range(1, cores):
        ring = [(c, (c + step) % cores) for c in range(cores)]
        other = lax.ppermute(pick(shaped, (me_c + step) % cores, 1), "core", ring)
        mine = (mine.astype(jnp.float32) + other.astype(jnp.float32)).astype(jnp.bfloat16)
    return mine


def plane_gather(values):
    return lax.all_gather(values, "tp", axis=0, tiled=True)


def plane_multiply(ident, x, weight, turned=False, halved=False, width=None, **more):
    if fast():
        return gather_matmul(ident, x, weight, turned, halved, width, **more)
    whole = join_cores(weight) if halved else weight
    x = plane_gather(x)
    return x, whole, contract_right(x, whole) if turned else matmul(x, whole[:, :width])


def multiply_plane(ident, x, weight, turned=False, **more):
    if fast():
        return matmul_scatter(ident, x, weight, turned, **more)
    weight = weight[:, : x.shape[1]] if turned else weight
    term = contract_right(x, weight) if turned else matmul(x, weight)
    return lax.psum_scatter(
        term.astype(jnp.bfloat16), "tp", scatter_dimension=0, tiled=True
    ).astype(jnp.float32), None


def collect_plane(pieces):
    return [
        lax.all_gather(p, ("tp", "core"), axis=0, tiled=False).reshape(
            (lax.axis_size("tp"), lax.axis_size("core")) + p.shape
        )
        for p in pieces
    ]


def spread_parts(blocks, parts):
    if fast():
        return spread(blocks, parts)
    tp, cores, rows, width = blocks.shape
    return (
        blocks.astype(jnp.float32)
        .reshape(tp, cores, rows, parts, width // parts)
        .transpose(1, 2, 3, 0, 4)
        .reshape(cores * rows, tp * width)
    )


def arrive_plane(ident, tokens, cotangent, message, w_mod, *weights):
    if fast():
        return arrive(ident, tokens, cotangent, message, w_mod, *weights)
    ways = lax.axis_size("tp")
    cotangent = lax.all_to_all(
        cotangent.reshape(ways, -1, cotangent.shape[1]), "tp", 0, 0, tiled=True
    )
    planes, cores = lax.axis_size("seq"), lax.axis_size("core")
    depth = w_mod.shape[0]
    part = lax.dynamic_slice_in_dim(message, lax.axis_index("seq") * depth, depth, 1)
    messages = lax.all_gather(part, ("tp", "core"), axis=0, tiled=False)
    terms = matmul(messages.reshape(-1, depth).astype(w_mod.dtype), w_mod)
    terms = lax.psum_scatter(
        terms.reshape(planes, cores, 8, -1), "seq", scatter_dimension=0, tiled=False
    )
    messages = messages.reshape(lax.axis_size("tp"), cores, 8, depth)
    w_qkv, w_out, w_down, w_gateup = weights
    share = w_down.shape[0] // (ways * cores)
    block = lax.axis_index("tp") * cores + lax.axis_index("core")
    return (
        to_plane(tokens),
        cotangent,
        messages,
        pick(terms, lax.axis_index("core"), 0),
        jnp.concatenate([columns_of(w_qkv, 3), columns_of(w_out, 1)], axis=1),
        lax.dynamic_slice_in_dim(w_down, block * share, share, 0),
        columns_of(w_gateup, 2 * planes),
    )


def three_parts(values):
    parts = []
    for _ in range(3):
        part = lax.reduce_precision(values, 8, 7)
        parts.append(part.astype(jnp.bfloat16))
        values = values - part
    return parts


def by_document(doc_pick, values):
    return lax.dot_general(
        doc_pick,
        values,
        (((0,), (0,)), ((), ())),
        precision=lax.Precision.HIGHEST,
        preferred_element_type=jnp.float32,
    )


def columns_of(weight, parts):
    tp, cores = lax.axis_size("tp"), lax.axis_size("core")
    me_t, me_c = lax.axis_index("tp"), lax.axis_index("core")
    share = weight.shape[0] // cores
    size = weight.shape[1] // (parts * tp)
    return jnp.concatenate(
        [
            lax.dynamic_slice(weight, (me_c * share, (q * tp + me_t) * size), (share, size))
            for q in range(parts)
        ],
        axis=1,
    )


def shards(
    tokens,
    cotangent,
    step_embed,
    caption,
    lengths,
    group_bucket,
    null_mask,
    w_qkv,
    w_out,
    w_capkv,
    w_gateup,
    w_down,
    w_mod,
    b_mod,
    gain_attn,
    gain_ffn,
    gain_query,
    gain_key,
    gain_capkey,
    gate_head,
    null_embed,
):
    tp, cores, planes = lax.axis_size("tp"), lax.axis_size("core"), lax.axis_size("seq")
    me_t, me_c, me_z = lax.axis_index("tp"), lax.axis_index("core"), lax.axis_index("seq")
    groups = tp * cores
    rows, width = tokens.shape
    piece = rows // tp
    local_heads = HEADS // tp
    local = local_heads * HDIM
    cap_dev = caption.shape[2]
    ctx = caption.shape[3]
    my_group = me_z * cores + me_c

    condition = jax.nn.silu(step_embed[0].astype(jnp.float32)).astype(jnp.bfloat16)
    numbers = jnp.concatenate([lengths[0], group_bucket, null_mask[0]]).astype(jnp.float32)
    mod_rows = w_mod.shape[0]
    numbers = jnp.tile(jnp.pad(numbers, (0, mod_rows - numbers.shape[0])), planes)
    message = jnp.concatenate(
        [condition.astype(jnp.float32), numbers[None], jnp.zeros((3, numbers.shape[0]))], axis=0
    )
    arrived, cotangents, messages, mod_doc, *cuts = arrive_plane(
        13, tokens, cotangent, message, w_mod, w_qkv, w_out, w_down, w_gateup
    )
    messages = messages.reshape(groups, 8, mod_rows)
    cond_mine = messages[:, :DOCS].reshape(groups * DOCS, mod_rows)
    mod_rows_doc = mod_doc + b_mod
    mod_doc = mod_rows_doc[:DOCS]

    numbers = messages[:, DOCS, : 2 * DOCS + 1].astype(jnp.int32)
    counts = jnp.sum(numbers[:, :DOCS], axis=1).astype(jnp.float32)
    mine = pick(numbers, my_group, 0)
    doc_lengths, bucket = mine[:DOCS], mine[DOCS]
    bucket_count = jnp.sum(jnp.where(numbers[:, DOCS] == bucket, counts, 0.0))
    scale_loss = jnp.sum(counts) / (RES * bucket_count)

    half_capkv = gather_planes(columns_of(w_capkv, 2))
    half_qkv, half_down, half_gateup = [gather_planes(part) for part in cuts]

    capmix = jnp.where(null_mask[0][:, None, None] > 0, null_embed[None, None, :], caption[0])
    my_gain_capkey = pick(gain_capkey.reshape(tp, 1, local), me_t, 0)
    cap_flat = capmix.reshape(DOCS * cap_dev, ctx)
    if fast():
        cap_flat, full_capkv, cap_proj, cotangents, heads = gather_matmul(
            2, cap_flat, half_capkv, halved=True, trade=[swap_blocks(cotangents, "seq")],
            finish=head_finish(DOCS * cap_dev, 2 * local, my_gain_capkey),
        )
    else:
        cap_flat, full_capkv, cap_proj = plane_multiply(2, cap_flat, half_capkv, halved=True)
        capkey_raw, capval_raw = jnp.split(cap_proj, 2, axis=1)
        capkey_norm, capkey_inv = head_stats(capkey_raw)
        heads = jnp.concatenate([capkey_norm * my_gain_capkey, capval_raw], axis=1)
        heads = heads.astype(jnp.bfloat16)
        cotangents = lax.all_to_all(cotangents, "seq", 0, 0, tiled=True)
    cotangents = cotangents.reshape(tokens.shape)
    cap_document = jnp.tile(jnp.repeat(jnp.arange(DOCS, dtype=jnp.int32), cap_dev), planes)

    inputs = arrived.reshape(tokens.shape).astype(jnp.float32)
    row = jnp.arange(rows, dtype=jnp.int32)
    spread = (row // piece) * rows + row % piece
    positions = spread + me_t * piece
    all_positions = (jnp.arange(tp, dtype=jnp.int32)[:, None] * piece + spread[None, :]).reshape(-1)
    segment, _, _ = layout(doc_lengths, bucket, positions)
    all_segment, row_pos, col_pos = layout(doc_lengths, bucket, all_positions)
    all_document = jnp.minimum(all_segment, DOCS - 1)
    document = jnp.minimum(segment, DOCS - 1)
    doc_pick = (document[:, None] == jnp.arange(DOCS, dtype=jnp.int32)[None, :]).astype(jnp.float32)
    is_valid = (segment < DOCS).astype(jnp.float32)
    modulation = jnp.dot(doc_pick, mod_doc, precision=lax.Precision.HIGHEST)
    scale_a, gate_a, scale_f, gate_f = jnp.split(modulation, 4, axis=1)
    tanh_a, tanh_f = jnp.tanh(gate_a), jnp.tanh(gate_f)

    normed1, inverse1 = row_stats(inputs)
    hidden1 = (normed1 * gain_attn * (1.0 + scale_a)).astype(jnp.bfloat16)
    hidden1, heads = lax.optimization_barrier((hidden1, heads))
    heads = heads.reshape(planes, DOCS * cap_dev, 2 * local)
    if fast():
        hidden1, full_qkv, projected, heads = gather_matmul(
            1, hidden1, half_qkv, halved=True, width=3 * local,
            trade=[swap_blocks(heads, "seq")],
        )
    else:
        hidden1, full_qkv, projected = plane_multiply(
            1, hidden1, half_qkv, halved=True, width=3 * local
        )
        heads = lax.all_to_all(heads, "seq", 0, 0, tiled=True)
        full_out = full_qkv[:, 3 * local :].reshape(tp, local, local)
        full_out = lax.all_to_all(full_out, "tp", 0, 0, tiled=True)
        full_out = full_out.transpose(1, 0, 2).reshape(local, width)
    heads = heads.reshape(-1, 2 * local)
    my_gain_query = pick(gain_query.reshape(tp, 1, local), me_t, 0)
    my_gain_key = pick(gain_key.reshape(tp, 1, local), me_t, 0)
    gate_tanh = pick(jnp.tanh(gate_head).reshape(tp, local_heads), me_t, 0)
    head_gate = jnp.repeat(gate_tanh, HDIM)[None, :]
    grad_res0 = cotangents.astype(jnp.float32) * (is_valid * scale_loss)[:, None]
    grad_down = (tanh_f * grad_res0).astype(jnp.bfloat16)
    if fast():
        cosine, sine = turn_tables(row_pos, col_pos)
        own_spare = spare_columns(all_segment, SPARE)
        cross_spare = spare_columns(all_document, SPARE)
        aside = attend(
            projected, heads, my_gain_query, my_gain_key, head_gate, cosine, sine,
            own_spare, spare_columns(all_segment, 0),
            cross_spare, spare_columns(cap_document, 0),
        )
        out_rows = (
            full_qkv,
            "tp",
            (local, width),
            lambda ref, p: ref.at[pl.ds(p * local, local), pl.ds(3 * local, local)],
            lambda ref, p: ref.at[:, pl.ds(pl.multiple_of(p * local, local), local)],
        )
        grad_down, full_down, grad_ffn, *wides, full_out = gather_matmul(
            6, grad_down, half_down, turned=True, halved=True, aside=aside, early=1,
            trade=[out_rows],
        )
        wide_query, wide_keys, wide_values, own_wide = wides[:4]
        wide_capkeys, wide_capvals, cross_wide, mixed_attn = wides[4:]
    else:
        grad_down, full_down, grad_ffn = plane_multiply(
            6, grad_down, half_down, turned=True, halved=True
        )
        query_raw, key_raw, value_raw = jnp.split(projected, 3, axis=1)
        query_norm, query_inv = head_stats(query_raw)
        key_norm, key_inv = head_stats(key_raw)
        query = rotary(query_norm * my_gain_query, row_pos, col_pos, 1.0).astype(jnp.bfloat16)
        keys = rotary(key_norm * my_gain_key, row_pos, col_pos, 1.0).astype(jnp.bfloat16)
        values = value_raw.astype(jnp.bfloat16)
        capkeys, capvals = jnp.split(heads, 2, axis=1)
        self_allowed = all_segment[:, None] == all_segment[None, :]
        cross_allowed = all_document[:, None] == cap_document[None, :]
        own_out, own_log = attend_forward(query, keys, values, self_allowed)
        cross_out, cross_log = attend_forward(query, capkeys, capvals, cross_allowed)
        mixed_attn = (own_out + head_gate * cross_out).astype(jnp.bfloat16)
    token_rows = arrived.reshape(tokens.shape)
    doc_column = jnp.broadcast_to(document.astype(jnp.float32)[:, None], (rows, 128))
    weight_column = jnp.broadcast_to((is_valid * scale_loss)[:, None], (rows, 128))
    if fast():
        attn_out, residual, hidden2 = matmul_scatter(
            3, mixed_attn, full_out,
            after=after_attention(token_rows, mod_rows_doc, doc_column, gain_ffn[None]),
        )
    else:
        attn_out, *_ = multiply_plane(3, mixed_attn, full_out)
        residual = inputs + tanh_a * attn_out
        normed2, inverse2 = row_stats(residual)
        hidden2 = (normed2 * gain_ffn * (1.0 + scale_f)).astype(jnp.bfloat16)
    if fast():
        hidden2, full_gateup, hidden_ffn, grad_gateup = gather_matmul(
            4, hidden2, half_gateup, halved=True, finish=swiglu_finish(grad_ffn), keep=False
        )
        hidden_ffn = hidden_ffn.reshape(grad_ffn.shape)
        grad_gateup = grad_gateup.reshape(grad_ffn.shape[0], -1)
    else:
        hidden2, full_gateup, gate_up = plane_multiply(4, hidden2, half_gateup, halved=True)
        gate_part, up_part = jnp.split(gate_up, 2, axis=1)
        sig_gate = jax.nn.sigmoid(gate_part)
        silu_gate = gate_part * sig_gate
        hidden_ffn = (silu_gate * up_part).astype(jnp.bfloat16)
        grad_gate_part = grad_ffn * up_part * sig_gate * (1.0 + gate_part * (1.0 - sig_gate))
        grad_gateup = jnp.concatenate([grad_gate_part, grad_ffn * silu_gate], axis=1)
        grad_gateup = grad_gateup.astype(jnp.bfloat16)
    term_gateup, term_down = outer_plane(
        15, (hidden2, grad_gateup, planes), (hidden_ffn, grad_down, planes)
    )
    grad_gateup, term_down, term_gateup = lax.optimization_barrier(
        (grad_gateup, term_down, term_gateup)
    )
    term_down, term_gateup = scatter_planes(term_down), scatter_planes(term_gateup)
    if fast():
        _, grad_residual, grad_attn, ffn_sums = matmul_scatter(
            7, grad_gateup, full_gateup, turned=True,
            after=after_ffn_back(
                residual, attn_out, cotangents, weight_column, mod_rows_doc, doc_column,
                gain_ffn[None],
            ),
        )
        doc_scale_f, doc_gate_a, gain_ffn_term = ffn_sums[:4], ffn_sums[4:8], ffn_sums[8]
    else:
        grad_hidden2, *_ = multiply_plane(7, grad_gateup, full_gateup, turned=True)
        gain_ffn_term = jnp.sum(grad_hidden2 * normed2 * (1.0 + scale_f), axis=0)
        doc_scale_f = by_document(doc_pick, grad_hidden2 * normed2 * gain_ffn)
        grad_residual = grad_res0 + norm_back(
            grad_hidden2 * gain_ffn * (1.0 + scale_f), normed2, inverse2
        )
        grad_attn = (tanh_a * grad_residual).astype(jnp.bfloat16)
        doc_gate_a = by_document(doc_pick, grad_residual * attn_out * (1.0 - tanh_a * tanh_a))
    grad_attn, _, grad_mix = plane_multiply(8, grad_attn, full_out, turned=True)
    term_out = outer_plane(16, (mixed_attn, grad_attn, 1))[0][0]
    if fast():
        cross_aside = attend_back(
            grad_mix, head_gate, cross_wide, wide_query, cross_spare,
            wide_capkeys, wide_capvals,
        )
        out_columns = (
            term_out,
            "tp",
            (tp, term_out.shape[0], local),
            lambda ref, p: ref.at[:, pl.ds(pl.multiple_of(p * local, local), local)],
            block_of,
        )
        _, query_cross, grad_heads, cross_sums, term_out, result, gate_sums = matmul_scatter(
            5, hidden_ffn, full_down, aside=cross_aside, trade=[out_columns],
            after=after_ffn(residual, cotangents, weight_column, mod_rows_doc, doc_column),
        )
        doc_gate_f = gate_sums[:DOCS]
        grad_heads = grad_heads.reshape(planes, DOCS * cap_dev, 2 * local)
        gate_head_term = jnp.sum(cross_sums[:, :2], axis=-1).reshape(-1)
        own_aside = attend_back(
            grad_mix, jnp.ones_like(head_gate), own_wide, wide_query, own_spare,
            wide_keys, wide_values,
            (projected, my_gain_key, my_gain_query, cosine, sine, query_cross),
        )
        (all_down, all_gateup), riders = collect(
            10,
            [term_down, term_gateup],
            own_aside,
            [swap_blocks(grad_heads, "seq"), swap_blocks(term_out, "seq")],
        )
        grad_projected, own_sums, grad_heads, term_out = riders
        term_out = jnp.sum(term_out.astype(jnp.float32), axis=0).astype(jnp.bfloat16)
        gain_key_term, gain_query_term = own_sums[:, 2].reshape(-1), own_sums[:, 3].reshape(-1)
    else:
        down_out, _ = multiply_plane(5, hidden_ffn, full_down)
        result = from_plane((residual + tanh_f * down_out).astype(jnp.bfloat16))
        all_down, all_gateup = collect_plane([term_down, term_gateup])
        term_out = term_out.reshape(term_out.shape[0], tp, -1).transpose(1, 0, 2)
        term_out = scatter_planes(lax.all_to_all(term_out, "tp", 0, 0, tiled=True))
        grad_own = grad_mix.astype(jnp.bfloat16)
        grad_cross = (head_gate * grad_mix).astype(jnp.bfloat16)
        gate_head_term = jnp.sum(
            (grad_mix * cross_out).reshape(-1, local_heads, HDIM), axis=(0, 2)
        )
        query_own, grad_keys, grad_values = attend_backward(
            query, keys, values, self_allowed, own_log, grad_own
        )
        query_cross, grad_capkeys, grad_capvals = attend_backward(
            query, capkeys, capvals, cross_allowed, cross_log, grad_cross
        )
        grad_query = rotary(query_own + query_cross, row_pos, col_pos, -1.0)
        gain_query_term = jnp.sum(grad_query * query_norm, axis=0)
        grad_query_raw = head_back(grad_query * my_gain_query, query_norm, query_inv)
        grad_key = rotary(grad_keys, row_pos, col_pos, -1.0)
        gain_key_term = jnp.sum(grad_key * key_norm, axis=0)
        grad_key_raw = head_back(grad_key * my_gain_key, key_norm, key_inv)
        grad_projected = jnp.concatenate(
            [grad_query_raw, grad_key_raw, grad_values], axis=1
        ).astype(jnp.bfloat16)
        grad_heads = jnp.concatenate([grad_capkeys, grad_capvals], axis=1).astype(jnp.bfloat16)
        grad_heads = grad_heads.reshape(planes, DOCS * cap_dev, 2 * local)
        grad_heads = lax.all_to_all(grad_heads, "seq", 0, 0, tiled=True)
        doc_gate_f = by_document(doc_pick, grad_res0 * down_out * (1.0 - tanh_f * tanh_f))
    gate_head_term = gate_head_term * (1.0 - gate_tanh * gate_tanh)
    grad_heads = grad_heads.reshape(-1, 2 * local)
    if fast():
        grad_cap_proj, capkey_sums = cap_back(grad_heads, cap_proj, my_gain_capkey)
        gain_capkey_term = capkey_sums[0]
    else:
        grad_capkeys, grad_capvals = jnp.split(grad_heads.astype(jnp.float32), 2, axis=1)
        gain_capkey_term = jnp.sum(grad_capkeys * capkey_norm, axis=0)
        grad_capkey_raw = head_back(grad_capkeys * my_gain_capkey, capkey_norm, capkey_inv)
        grad_cap_proj = jnp.concatenate([grad_capkey_raw, grad_capvals], axis=1).astype(
            jnp.bfloat16
        )
    (term_qkv,) = outer_plane(17, (hidden1, grad_projected, planes))
    cap_side, _ = lax.optimization_barrier((grad_cap_proj, term_qkv))
    term_qkv = scatter_planes(term_qkv)
    (term_capkv,) = outer_plane(18, (cap_flat, cap_side, planes))
    grad_projected, _ = lax.optimization_barrier((grad_projected, term_capkv))
    term_capkv = scatter_planes(term_capkv)
    if fast():
        _, input_grad, input_sums = matmul_scatter(
            9, grad_projected, full_qkv, turned=True,
            after=after_input_back(
                token_rows, grad_residual, mod_rows_doc, doc_column, gain_attn[None]
            ),
        )
        doc_scale_a, gain_attn_term = input_sums[:4], input_sums[4]
    else:
        grad_hidden1, *_ = multiply_plane(9, grad_projected, full_qkv, turned=True)
        gain_attn_term = jnp.sum(grad_hidden1 * normed1 * (1.0 + scale_a), axis=0)
        doc_scale_a = by_document(doc_pick, grad_hidden1 * normed1 * gain_attn)
        input_grad = (
            grad_residual + norm_back(grad_hidden1 * gain_attn * (1.0 + scale_a), normed1, inverse1)
        ).astype(jnp.bfloat16)
    grad_mod_doc = jnp.concatenate([doc_scale_a, doc_gate_a, doc_scale_f, doc_gate_f], axis=1)

    plane_nulls = pick(numbers[:, DOCS + 1 :].reshape(tp, cores, DOCS), me_c, 1)
    null_rows = jnp.repeat(plane_nulls.reshape(-1), cap_dev) > 0
    grad_mod_doc, null_rows, all_down, all_gateup = lax.optimization_barrier(
        (grad_mod_doc, null_rows, all_down, all_gateup)
    )
    null_sum = jnp.sum(
        jnp.where(null_rows[:, None], grad_cap_proj.astype(jnp.float32), 0.0), axis=0
    )
    null_parts = jnp.stack(three_parts(null_sum), axis=1)
    null_term = jnp.sum(matmul(full_capkv, null_parts), axis=1)

    def at_mine(part):
        whole = jnp.zeros((tp,) + part.shape, jnp.float32)
        return lax.dynamic_update_index_in_dim(whole, part, me_t, 0).reshape(-1)

    small = jnp.concatenate(
        [
            gain_attn_term,
            gain_ffn_term,
            at_mine(gain_query_term),
            at_mine(gain_key_term),
            at_mine(gain_capkey_term),
            at_mine(gate_head_term),
            null_term,
        ]
    )
    small_rows = 8 - DOCS
    small_size = small.shape[0]
    small = jnp.pad(small, (0, small_rows * 4 * width - small_size))
    sums = jnp.concatenate([grad_mod_doc, small.reshape(small_rows, 4 * width)], axis=0)
    if fast():
        (all_qkv, all_out), _ = collect(12, [term_qkv, term_out])
    else:
        all_qkv, all_out = collect_plane([term_qkv, term_out])
    all_qkv, all_down, all_gateup = lax.optimization_barrier((all_qkv, all_down, all_gateup))
    sum_down = all_down.reshape(w_down.shape).astype(jnp.float32)
    sum_gateup = spread_parts(all_gateup, 2 * planes)
    sum_out = spread_parts(all_out, 1)
    sum_qkv = spread_parts(all_qkv, 3)
    sum_qkv, sum_gateup, sum_down, sum_out, term_capkv = lax.optimization_barrier(
        (sum_qkv, sum_gateup, sum_down, sum_out, term_capkv)
    )
    if fast():
        (all_capkv,), (result, input_grad, totals) = collect(
            14, [term_capkv], backs=[result, input_grad], sums=sums
        )
        result, input_grad = result.reshape(tokens.shape), input_grad.reshape(tokens.shape)
    else:
        (all_capkv,) = collect_plane([term_capkv])
        input_grad = from_plane(input_grad)
        totals = lax.all_gather(lax.psum(sums, "tp"), ("seq", "core"), axis=0, tiled=False)
    totals = totals.reshape(groups, 8, 4 * width)
    sum_capkv = spread_parts(all_capkv, 2)
    grad_mod_docs = totals[:, :DOCS].reshape(groups * DOCS, 4 * width)
    sum_mod = contract_rows(
        jnp.concatenate([cond_mine.astype(jnp.bfloat16)] * 3, axis=0),
        jnp.concatenate(three_parts(grad_mod_docs), axis=0),
    )
    sum_bias = jnp.sum(grad_mod_docs, axis=0)
    small = jnp.sum(totals[:, DOCS:], axis=0).reshape(-1)[:small_size]
    ends = [width, 2 * width, 3 * width, 4 * width, 5 * width, 5 * width + HEADS]
    small_parts = jnp.split(small, ends)
    return (
        result,
        input_grad,
        sum_qkv,
        sum_out,
        sum_capkv,
        sum_gateup,
        sum_down,
        sum_mod,
        sum_bias,
        *small_parts,
    )


def solution(mesh):
    planes = mesh.shape["seq"]
    cores = mesh.shape["bucket"] // planes
    split = Mesh(mesh.devices.reshape(planes, cores, planes), ("tp", "core", "seq"))
    group = ("tp", "core")
    token = P(("tp", "core", "seq"), None)
    weight = P("seq", None)
    placed = (
        token,
        token,
        P(group, None, None),
        P(group, None, "seq", None),
        P(group, None),
        P(group),
        P(group, None),
        *([weight] * 6),
        *([P()] * 8),
    )
    return jax.shard_map(
        shards,
        mesh=split,
        in_specs=placed,
        out_specs=(token, token, *([weight] * 6), *([P()] * 8)),
        check_vma=False,
    )
```

```python
import functools

import jax
import jax.numpy as jnp
from jax import lax
from jax.experimental import pallas as pl
from jax.experimental.pallas import tpu as pltpu
from jax.sharding import Mesh, PartitionSpec as P

HEADS = 24
HDIM = 64
DOCS = 4
RES = 4


eps = 1e-06

MESH = pl.DeviceIdType.MESH
VMEM_BYTES = 60 * 1024 * 1024


def neighbours():
    me = lax.axis_index("tp")
    return me, me + 1 - 2 * lax.rem(me, 2), lax.rem(me + 2, 4), 3 - me


def greet(places):
    barrier = pltpu.get_barrier_semaphore()
    for place in places:
        pl.semaphore_signal(barrier, inc=1, device_id=place, device_id_type=MESH)
    pl.semaphore_wait(barrier, len(places))


def send(source, target, sems, index, place):
    return pltpu.make_async_remote_copy(
        src_ref=source,
        dst_ref=target,
        send_sem=sems[0].at[index],
        recv_sem=sems[1].at[index],
        device_id=place,
        device_id_type=MESH,
    )


def tile_of(width):
    for tile in (512, 384, 256, 128):
        if width % tile == 0:
            return tile
    return width


def multiply(left, weight_ref, columns, turned):
    if turned:
        return lax.dot_general(
            left, weight_ref[columns, 0 : left.shape[1]], (((1,), (1,)), ((), ())),
            preferred_element_type=jnp.float32,
        )
    return jnp.dot(left, weight_ref[:, columns], preferred_element_type=jnp.float32)


def bind(refs, counts, *riders):
    refs, own = list(refs), []
    for kind in range(3):
        own += refs[: counts[kind]]
        refs = refs[counts[kind] :]
        for rider in riders:
            count = rider.counts[kind]
            rider.refs[kind] = refs[:count]
            refs = refs[count:]
    return own


class Aside:
    def __init__(self, operands, outs, scratch, steps):
        self.operands, self.outs, self.steps = operands, outs, steps
        self.in_specs = [pl.BlockSpec(memory_space=pl.ANY)] * len(operands)
        self.out_specs = [pl.BlockSpec(memory_space=pltpu.VMEM)] * len(outs)
        self.scratch = [
            *[pltpu.VMEM(x.shape, x.dtype) for x in operands],
            pltpu.SemaphoreType.DMA((max(len(operands), 1),)),
            *scratch,
        ]
        self.counts = (len(operands), len(outs), len(self.scratch))
        self.refs = [None] * 3

    def load(self):
        count = len(self.operands)
        sem = self.refs[2][count]
        self.loads = [
            pltpu.make_async_copy(self.refs[0][i], self.refs[2][i], sem.at[i])
            for i in range(count)
        ]
        for copy in self.loads:
            copy.start()

    def step(self, index):
        count = len(self.operands)
        if index == 0:
            for copy in self.loads:
                copy.wait()
        if self.steps:
            self.steps(index, self.refs[2][:count], self.refs[1], self.refs[2][count + 1 :])


def nothing():
    return Aside([], [], [], None)


class Finish:
    def __init__(self, operands, outs, work):
        self.operands, self.outs, self.work = operands, outs, work
        hbm = pl.BlockSpec(memory_space=pl.ANY)
        self.in_specs, self.out_specs = [hbm] * len(operands), [hbm] * len(outs)
        self.scratch = [
            *[pltpu.VMEM(x.shape, x.dtype) for x in operands],
            *[pltpu.VMEM(x.shape, x.dtype) for x in outs],
            pltpu.SemaphoreType.DMA((max(len(operands), 1),)),
            pltpu.SemaphoreType.DMA((4 * max(len(outs), 1),)),
        ]
        self.counts = (len(operands), len(outs), len(self.scratch))
        self.refs = [None] * 3

    def load(self):
        count = len(self.operands)
        self.ins, self.made = self.refs[2][:count], self.refs[2][count:-2]
        sem = self.refs[2][-2]
        self.loads = [
            pltpu.make_async_copy(self.refs[0][i], self.ins[i], sem.at[i]) for i in range(count)
        ]
        for copy in self.loads:
            copy.start()
        self.copies = []

    def run(self, index, owner, product):
        if not self.work:
            return
        if index == 0:
            for copy in self.loads:
                copy.wait()
        made = [ref.at[owner] for ref in self.made]
        self.work(product, [ref.at[owner] for ref in self.ins], made)
        for i, ref in enumerate(made):
            copy = pltpu.make_async_copy(
                ref, self.refs[1][i].at[owner], self.refs[2][-1].at[4 * i + index]
            )
            copy.start()
            self.copies.append(copy)

    def end(self):
        for copy in self.copies:
            copy.wait()


class Trade:
    def __init__(self, *items):
        self.items = items
        hbm = pl.BlockSpec(memory_space=pl.ANY)
        self.operands = [item[0] for item in items]
        self.outs = [jax.ShapeDtypeStruct(item[2], item[0].dtype) for item in items]
        self.in_specs = self.out_specs = [hbm] * len(items)
        count = max(len(items), 1)
        self.scratch = [pltpu.SemaphoreType.DMA((n,)) for n in (count, 3 * count, 3 * count)]
        self.counts = (len(items), len(items), 3)
        self.refs = [None] * 3

    def begin(self):
        local, *sems = self.refs[2]
        self.copies, self.local = [], []
        for i, (_, axis, _, source, target) in enumerate(self.items):
            from_ref, to_ref = self.refs[0][i], self.refs[1][i]
            if axis == "tp":
                here, *others = neighbours()
            else:
                here, others = planes_after()
            self.local.append(
                pltpu.make_async_copy(source(from_ref, here), target(to_ref, here), local.at[i])
            )
            self.copies += [
                send(source(from_ref, p), target(to_ref, here), sems, 3 * i + k, {axis: p})
                for k, p in enumerate(others)
            ]
        for copy in self.local + self.copies:
            copy.start()

    def end(self):
        for copy in self.local + self.copies:
            copy.wait()


def block_of(ref, place):
    return ref.at[place]


def swap_blocks(x, axis):
    return (x, axis, x.shape, block_of, block_of)


def gather_kernel(turned, halved, early, aside, trade, finish, keep, *refs):
    refs = bind(refs, (2, 1 + halved + keep, 7), aside, trade, finish)
    x_ref, w_ref, all_ref, *refs = refs
    if halved:
        full_ref, *refs = refs
    if keep:
        y_ref, *refs = refs
    xbuf, wbuf, ybuf, load, done, *sems = refs
    me, across, along, far = neighbours()
    rows = x_ref.shape[0]
    half = rows // 2
    core = lax.axis_index("core")
    places = [{"tp": across}, {"tp": along}]
    if halved:
        places.append({"core": 1 - core})
    mine = pltpu.make_async_copy(x_ref, xbuf.at[me], load.at[0])
    mine.start()
    if halved:
        planes, part, _ = w_ref.shape
        places_of = [
            pl.ds(pl.multiple_of((z * 2 + core) * part, part), part) for z in range(planes)
        ]
        weights = [
            pltpu.make_async_copy(w_ref.at[z], wbuf.at[places_of[z]], load.at[1 + z])
            for z in range(planes)
        ]
    else:
        weights = [pltpu.make_async_copy(w_ref, wbuf, load.at[1])]
    for copy in weights:
        copy.start()
    if trade.items:
        greet_all()
    else:
        greet(places)

    def block(owner, part):
        return xbuf.at[owner, pl.ds(part * half, half)]

    def pass_on(index, owner, part, place):
        return send(block(owner, part), block(owner, part), sems, index, place)

    first = [
        send(x_ref.at[pl.ds(0, half)], block(me, 0), sems, 0, {"tp": across}),
        send(x_ref.at[pl.ds(half, half)], block(me, 1), sems, 1, {"tp": along}),
        send(x_ref.at[pl.ds(half, half)], block(me, 1), sems, 2, {"tp": across}),
        send(x_ref.at[pl.ds(0, half)], block(me, 0), sems, 3, {"tp": along}),
    ]
    for copy in first:
        copy.start()
    swaps = []
    if halved:
        for z in range(planes):
            swaps.append(send(w_ref.at[z], wbuf.at[places_of[z]], sems, 6 + z, {"core": 1 - core}))
        for copy in swaps:
            copy.start()
    trade.begin()
    aside.load()
    finish.load()
    mine.wait()
    for copy in weights:
        copy.wait()
    for step in range(early):
        aside.step(step)
    first[0].wait_recv()
    on_a = pass_on(4, across, 0, {"tp": along})
    on_a.start()
    first[1].wait_recv()
    on_b = pass_on(5, along, 1, {"tp": across})
    on_b.start()
    for copy in swaps:
        copy.wait()
    for step in range(early, 3):
        aside.step(step)

    tile = tile_of(ybuf.shape[-1])
    outs = []
    if halved:
        outs.append(pltpu.make_async_copy(wbuf, full_ref, done.at[4]))
        outs[-1].start()

    def compute(owner, index):
        @pl.loop(0, ybuf.shape[-1] // tile)
        def _(step):
            columns = pl.ds(pl.multiple_of(step * tile, tile), tile)
            ybuf[index, :, columns] = multiply(xbuf[owner], wbuf, columns, turned).astype(
                ybuf.dtype
            )

        if keep:
            copy = pltpu.make_async_copy(ybuf.at[index], y_ref.at[owner], done.at[index])
            copy.start()
            outs.append(copy)
        finish.run(index, owner, ybuf.at[index])

    compute(me, 0)
    first[2].wait_recv()
    compute(across, 1)
    first[3].wait_recv()
    compute(along, 2)
    on_a.wait_recv()
    on_b.wait_recv()
    copy = pltpu.make_async_copy(xbuf, all_ref, load.at[0])
    copy.start()
    outs.append(copy)
    compute(far, 3)
    for copy in first + [on_a, on_b]:
        copy.wait_send()
    for copy in outs:
        copy.wait()
    finish.end()
    trade.end()


def gather_matmul(
    ident, x, w, turned=False, halved=False, width=None, aside=None, early=3, trade=(),
    finish=None, keep=True,
):
    rows, depth = x.shape
    if halved:
        planes, part, columns = w.shape
        whole = (planes * 2 * part, columns)
    else:
        whole = w.shape
    width = width or (whole[0] if turned else whole[1])
    riders = [aside or nothing(), Trade(*trade), finish or Finish([], [], None)]
    shapes = [jax.ShapeDtypeStruct((4, rows, depth), x.dtype)]
    if halved:
        shapes.append(jax.ShapeDtypeStruct(whole, w.dtype))
    if keep:
        shapes.append(jax.ShapeDtypeStruct((4, rows, width), jnp.float32))
    hbm = pl.BlockSpec(memory_space=pl.ANY)
    got = pl.pallas_call(
        functools.partial(gather_kernel, turned, halved, early, *riders, keep),
        out_shape=shapes + [y for rider in riders for y in rider.outs],
        in_specs=[hbm, hbm] + [y for rider in riders for y in rider.in_specs],
        out_specs=[hbm] * len(shapes) + [y for rider in riders for y in rider.out_specs],
        scratch_shapes=[
            pltpu.VMEM((4, rows, depth), x.dtype),
            pltpu.VMEM(whole, w.dtype),
            pltpu.VMEM((4, rows, width), jnp.float32),
            pltpu.SemaphoreType.DMA((6,)),
            pltpu.SemaphoreType.DMA((5,)),
            pltpu.SemaphoreType.DMA((10,)),
            pltpu.SemaphoreType.DMA((10,)),
            *[y for rider in riders for y in rider.scratch],
        ],
        compiler_params=pltpu.CompilerParams(
            collective_id=ident, has_side_effects=True, vmem_limit_bytes=VMEM_BYTES
        ),
        cost_estimate=pl.CostEstimate(
            flops=8 * rows * depth * width,
            bytes_accessed=30 * 3_000_000,
            transcendentals=0,
        ),
        name="gather_matmul",
    )(x, w, *[y for rider in riders for y in rider.operands])
    return [
        got[0].reshape(4 * rows, depth),
        got[1] if halved else w,
        *[part.reshape(4 * rows, width) for part in got[1 + halved : len(shapes)]],
        *got[len(shapes) :],
    ]


def head_finish(rows, width, gain):
    def work(product, ins, outs):
        (gain_ref,), (out_ref,) = ins, outs
        size = width // 2
        for at in range(0, size, 128):
            keys = pair_norm(product[:, at : at + 128])[0] * gain_ref[:, at : at + 128]
            out_ref[:, at : at + 128] = keys.astype(out_ref.dtype)
        out_ref[:, size:] = product[:, size:].astype(out_ref.dtype)

    gains = jnp.broadcast_to(gain[None], (4, 1, width // 2))
    return Finish([gains], [jax.ShapeDtypeStruct((4, rows, width), jnp.bfloat16)], work)


def swiglu_finish(grads):
    rows, size = grads.shape[0] // 4, grads.shape[1]

    def work(product, ins, outs):
        (grad_ref,), (ffn_ref, back_ref) = ins, outs

        @pl.loop(0, rows // 32)
        def _(step):
            strip = pl.ds(pl.multiple_of(step * 32, 32), 32)
            for at in range(0, size, 256):
                lanes, ups = pl.ds(at, 256), pl.ds(size + at, 256)
                gate, up, grad = product[strip, lanes], product[strip, ups], grad_ref[strip, lanes]
                sig = 1.0 / (1.0 + jnp.exp(-gate))
                silu = gate * sig
                ffn_ref[strip, lanes] = (silu * up).astype(ffn_ref.dtype)
                back = grad * up * sig * (1.0 + gate * (1.0 - sig))
                back_ref[strip, lanes] = back.astype(back_ref.dtype)
                back_ref[strip, ups] = (grad * silu).astype(back_ref.dtype)

    return Finish(
        [grads.reshape(4, rows, size)],
        [jax.ShapeDtypeStruct((4, rows, n), jnp.bfloat16) for n in (size, 2 * size)],
        work,
    )


def finished(aside, out_ref):
    count = len(aside.operands)
    for copy in aside.loads:
        copy.wait()
    if aside.steps:
        aside.steps(out_ref, aside.refs[2][:count], aside.refs[1], aside.refs[2][count + 1 :])


def scatter_kernel(turned, aside, after, trade, *refs):
    refs = bind(refs, (2, 1, 10), aside, after, trade)
    x_hbm, w_hbm, out_ref, sums, far_out, near_out, relay, land, s0, s1, x_ref, w_ref, load = refs
    me, across, along, far = neighbours()
    sems = (s0, s1)
    rows, width = out_ref.shape
    half = rows // 2
    top, low = pl.ds(0, half), pl.ds(half, half)
    tile = tile_of(width)
    to_across, to_along = {"tp": across}, {"tp": along}
    weights = pltpu.make_async_copy(w_hbm, w_ref, load.at[4])
    weights.start()
    blocks = {}
    for k, owner in enumerate((far, across, along, me)):
        blocks[k] = pltpu.make_async_copy(x_hbm.at[owner], x_ref.at[owner], load.at[k])
        blocks[k].start()
    aside.load()
    after.load()
    if trade.items:
        greet_all()
    else:
        greet([to_across, to_along])

    def tiles(body):
        @pl.loop(0, width // tile)
        def _(step):
            body(pl.ds(pl.multiple_of(step * tile, tile), tile))

    def product(owner, columns, part=slice(None)):
        return multiply(x_ref[owner, part], w_ref, columns, turned)

    weights.wait()
    blocks[0].wait()

    @tiles
    def _(columns):
        far_out[top, columns] = product(far, columns, top).astype(far_out.dtype)

    far_a = send(far_out.at[top], relay.at[0], sems, 0, to_across)
    far_a.start()

    @tiles
    def _(columns):
        far_out[low, columns] = product(far, columns, low).astype(far_out.dtype)

    far_b = send(far_out.at[low], relay.at[1], sems, 1, to_along)
    far_b.start()
    blocks[1].wait()

    @tiles
    def _(columns):
        part = product(across, columns)
        near_out[0, top, columns] = part[:half].astype(near_out.dtype)
        sums[0, :, columns] = part[half:]

    across_a = send(near_out.at[0, top], land.at[0, top], sems, 2, to_across)
    across_a.start()
    blocks[2].wait()

    @tiles
    def _(columns):
        part = product(along, columns)
        near_out[1, low, columns] = part[half:].astype(near_out.dtype)
        sums[1, :, columns] = part[:half]

    along_b = send(near_out.at[1, low], land.at[1, low], sems, 3, to_along)
    along_b.start()
    trade.begin()
    aside.step(0)
    far_b.wait_recv()

    @tiles
    def _(columns):
        near_out[0, low, columns] = (
            sums[0, :, columns] + relay[1, :, columns].astype(jnp.float32)
        ).astype(near_out.dtype)

    across_b = send(near_out.at[0, low], land.at[0, low], sems, 4, to_across)
    across_b.start()
    far_a.wait_recv()

    @tiles
    def _(columns):
        near_out[1, top, columns] = (
            sums[1, :, columns] + relay[0, :, columns].astype(jnp.float32)
        ).astype(near_out.dtype)

    along_a = send(near_out.at[1, top], land.at[1, top], sems, 5, to_along)
    along_a.start()
    aside.step(1)
    aside.step(2)
    blocks[3].wait()

    @tiles
    def _(columns):
        out_ref[:, columns] = product(me, columns)

    for copy in (across_a, along_b, across_b, along_a):
        copy.wait_recv()

    @tiles
    def _(columns):
        out_ref[:, columns] += land[0, :, columns].astype(jnp.float32) + land[
            1, :, columns
        ].astype(jnp.float32)

    finished(after, out_ref)
    for copy in (far_a, far_b, across_a, along_b, across_b, along_a):
        copy.wait_send()
    trade.end()


def matmul_scatter(ident, x, w, turned=False, aside=None, trade=(), after=None):
    riders = [aside or nothing(), after or nothing(), Trade(*trade)]
    rows, depth = x.shape[0] // 4, x.shape[1]
    width = w.shape[0] if turned else w.shape[1]
    vmem = pl.BlockSpec(memory_space=pltpu.VMEM)
    return pl.pallas_call(
        functools.partial(scatter_kernel, turned, *riders),
        out_shape=[jax.ShapeDtypeStruct((rows, width), jnp.float32)]
        + [y for rider in riders for y in rider.outs],
        in_specs=[pl.BlockSpec(memory_space=pl.ANY)] * 2
        + [y for rider in riders for y in rider.in_specs],
        out_specs=[vmem] + [y for rider in riders for y in rider.out_specs],
        scratch_shapes=[
            pltpu.VMEM((2, rows // 2, width), jnp.float32),
            pltpu.VMEM((rows, width), jnp.bfloat16),
            pltpu.VMEM((2, rows, width), jnp.bfloat16),
            pltpu.VMEM((2, rows // 2, width), jnp.bfloat16),
            pltpu.VMEM((2, rows, width), jnp.bfloat16),
            pltpu.SemaphoreType.DMA((6,)),
            pltpu.SemaphoreType.DMA((6,)),
            pltpu.VMEM((4, rows, depth), x.dtype),
            pltpu.VMEM(w.shape, w.dtype),
            pltpu.SemaphoreType.DMA((5,)),
            *[y for rider in riders for y in rider.scratch],
        ],
        compiler_params=pltpu.CompilerParams(
            collective_id=ident, has_side_effects=True, vmem_limit_bytes=VMEM_BYTES
        ),
        cost_estimate=pl.CostEstimate(
            flops=8 * rows * depth * width,
            bytes_accessed=30 * 3_000_000,
            transcendentals=0,
        ),
        name="matmul_scatter",
    )(x.reshape(4, rows, depth), w, *[y for rider in riders for y in rider.operands])


def outer_kernel(count, *refs):
    pairs, outs = refs[: 2 * count], refs[2 * count : 3 * count]
    lefts, rights, owns, aways, lands = [
        refs[(3 + k) * count : (4 + k) * count] for k in range(5)
    ]
    load, s0, s1 = refs[8 * count :]
    core = lax.axis_index("core")
    to_core = {"core": 1 - core}
    loads = []
    for i in range(count):
        left, right = pairs[2 * i : 2 * i + 2]
        blocks = outs[i].shape[0]
        size = left.shape[1] // blocks
        copies = [pltpu.make_async_copy(right, rights[i], load.at[5 * i])]
        for z in range(blocks):
            at = pl.ds(z * size, size)
            copies.append(
                pltpu.make_async_copy(left.at[:, at], lefts[i].at[:, at], load.at[5 * i + 1 + z])
            )
        for copy in copies:
            copy.start()
        loads.append(copies)
    greet([to_core])
    sent = []
    for i in range(count):
        blocks, rows, width = outs[i].shape
        tile = width
        loads[i][0].wait()
        for z in range(blocks):
            loads[i][1 + z].wait()
            left = lefts[i][:, z * 2 * rows : (z + 1) * 2 * rows]

            @pl.loop(0, width // tile)
            def _(step):
                columns = pl.ds(pl.multiple_of(step * tile, tile), tile)
                product = lax.dot_general(
                    left, rights[i][:, columns], (((0,), (0,)), ((), ())),
                    preferred_element_type=jnp.float32,
                )
                first, second = product[:rows], product[rows:]
                mine = jnp.where(core == 0, first, second)
                away = jnp.where(core == 0, second, first)
                owns[i][z, :, columns] = mine
                aways[i][z, :, columns] = away.astype(aways[i].dtype)

            copy = send(aways[i].at[z], lands[i].at[z], (s0, s1), 4 * i + z, to_core)
            copy.start()
            sent.append((i, z, copy))
    for i, z, copy in sent:
        copy.wait_recv()
        tile = tile_of(outs[i].shape[-1])

        @pl.loop(0, outs[i].shape[-1] // tile)
        def _(step):
            columns = pl.ds(pl.multiple_of(step * tile, tile), tile)
            outs[i][z, :, columns] = (
                owns[i][z, :, columns] + lands[i][z, :, columns].astype(jnp.float32)
            ).astype(outs[i].dtype)

    for _, _, copy in sent:
        copy.wait_send()


def outer(ident, *items):
    bf, f32 = jnp.bfloat16, jnp.float32
    shapes = [
        (blocks, left.shape[1] // (2 * blocks), right.shape[1]) for left, right, blocks in items
    ]
    count = len(items)
    hbm, vmem = pl.BlockSpec(memory_space=pl.ANY), pl.BlockSpec(memory_space=pltpu.VMEM)
    return pl.pallas_call(
        functools.partial(outer_kernel, count),
        out_shape=[jax.ShapeDtypeStruct(shape, bf) for shape in shapes],
        in_specs=[hbm] * (2 * count),
        out_specs=[vmem] * count,
        scratch_shapes=[
            *[pltpu.VMEM(left.shape, bf) for left, _, _ in items],
            *[pltpu.VMEM(right.shape, bf) for _, right, _ in items],
            *[pltpu.VMEM(shape, f32) for shape in shapes],
            *[pltpu.VMEM(shape, bf) for shape in shapes],
            *[pltpu.VMEM(shape, bf) for shape in shapes],
            pltpu.SemaphoreType.DMA((5 * count,)),
            pltpu.SemaphoreType.DMA((4 * count,)),
            pltpu.SemaphoreType.DMA((4 * count,)),
        ],
        compiler_params=pltpu.CompilerParams(
            collective_id=ident, has_side_effects=True, vmem_limit_bytes=VMEM_BYTES
        ),
        cost_estimate=pl.CostEstimate(
            flops=sum(2 * left.size * right.shape[1] for left, right, _ in items),
            bytes_accessed=20_000_000,
            transcendentals=0,
        ),
        name="outer",
    )(*[x for left, right, _ in items for x in (left, right)])


class Gathering:
    def __init__(self, ins, outs, load, sems):
        self.ins, self.outs, self.sems = ins, outs, sems
        self.me, self.across, self.along, self.far = neighbours()
        self.core = lax.axis_index("core")
        self.to_across, self.to_along = {"tp": self.across}, {"tp": self.along}
        self.to_core = {"core": 1 - self.core}
        self.local = [
            pltpu.make_async_copy(x, outs[i].at[self.me, self.core], load.at[i])
            for i, x in enumerate(ins)
        ]
        for copy in self.local:
            copy.start()

    def half(self, i, part):
        rows = self.ins[i].shape[0] // 2
        return pl.ds(part * rows, rows)

    def first(self, i, part, index, place):
        rows = self.half(i, part)
        target = self.outs[i].at[self.me, self.core, rows]
        return send(self.ins[i].at[rows], target, self.sems, 10 * i + index, place)

    def pass_on(self, i, owner, part, index, place):
        block = self.outs[i].at[owner, self.core, self.half(i, part)]
        return send(block, block, self.sems, 10 * i + index, place)

    def to_sibling(self, i, owner, index):
        block = self.outs[i].at[owner, self.core]
        return send(block, block, self.sems, 10 * i + index, self.to_core)

    def begin(self):
        self.begun = []
        for i, x in enumerate(self.ins):
            target = self.outs[i].at[self.me, self.core]
            copies = [
                self.first(i, 0, 0, self.to_across),
                self.first(i, 1, 1, self.to_along),
                self.first(i, 1, 2, self.to_across),
                self.first(i, 0, 3, self.to_along),
                send(x, target, self.sems, 10 * i + 6, self.to_core),
            ]
            for copy in copies:
                copy.start()
            self.begun.append(copies)

    def relay(self):
        for i, copies in enumerate(self.begun):
            copies[0].wait_recv()
            copies.append(self.pass_on(i, self.across, 0, 4, self.to_along))
            copies[5].start()
            copies[1].wait_recv()
            copies.append(self.pass_on(i, self.along, 1, 5, self.to_across))
            copies[6].start()

    def hand(self):
        for i, copies in enumerate(self.begun):
            copies[2].wait_recv()
            copies.append(self.to_sibling(i, self.across, 7))
            copies[7].start()
            copies[3].wait_recv()
            copies.append(self.to_sibling(i, self.along, 8))
            copies[8].start()
            copies[5].wait_recv()
            copies[6].wait_recv()
            copies.append(self.to_sibling(i, self.far, 9))
            copies[9].start()

    def end(self):
        for copies, local in zip(self.begun, self.local):
            for copy in copies[4:5] + copies[7:]:
                copy.wait_recv()
            for copy in copies:
                copy.wait_send()
            local.wait()


class Returning:
    def __init__(self, back, home, stage, load, sems, base):
        self.back, self.home, self.stage, self.load = back, home, stage, load
        self.sems, self.base = sems, base
        self.me, *self.peers = neighbours()
        self.plane, self.others = planes_after()
        self.stay = pltpu.make_async_copy(back.at[self.plane], stage.at[self.plane], load)
        self.keep = pltpu.make_async_copy(stage.at[self.me], home.at[self.me], load)

    def begin(self):
        self.stay.start()
        self.out = [
            send(
                self.back.at[p], self.stage.at[self.plane], self.sems, self.base + k, {"seq": p}
            )
            for k, p in enumerate(self.others)
        ]
        for copy in self.out:
            copy.start()

    def turn(self):
        for copy in self.out:
            copy.wait_recv()
        self.stay.wait()
        self.last = [
            send(
                self.stage.at[p], self.home.at[self.me], self.sems, self.base + 3 + k, {"tp": p}
            )
            for k, p in enumerate(self.peers)
        ]
        for copy in self.last:
            copy.start()
        self.keep.start()

    def end(self):
        for copy in self.last:
            copy.wait_recv()
        self.keep.wait()
        for copy in self.out + self.last:
            copy.wait_send()


class Home:
    def __init__(self, backs):
        self.outs, self.operands, self.scratch = [], [], []
        for back in backs:
            tall, wide = back.shape
            blocks = (4, tall // 4, wide)
            self.operands.append(back.reshape(blocks))
            self.outs.append(jax.ShapeDtypeStruct(blocks, back.dtype))
            self.scratch += [
                pltpu.VMEM(blocks, back.dtype),
                *[pltpu.SemaphoreType.DMA((n,)) for n in (1, 6, 6)],
            ]
        self.in_specs = self.out_specs = [pl.BlockSpec(memory_space=pl.ANY)] * len(self.outs)
        self.counts = (len(self.operands), len(self.outs), len(self.scratch))
        self.refs = [None] * 3

    def begin(self):
        self.ways = []
        for i, (back, home) in enumerate(zip(*self.refs[:2])):
            stage, load, *sems = self.refs[2][4 * i : 4 * i + 4]
            self.ways.append(Returning(back, home, stage, load.at[0], sems, 0))
        for way in self.ways:
            way.begin()

    def turn(self):
        for way in self.ways:
            way.turn()

    def end(self):
        for way in self.ways:
            way.end()


class Total:
    def __init__(self, x):
        vmem = pl.BlockSpec(memory_space=pltpu.VMEM)
        self.outs, self.operands, self.scratch = [], [], []
        if x is not None:
            rows, width = x.shape
            self.operands = [x]
            self.outs = [jax.ShapeDtypeStruct((4, 2, rows, width), jnp.float32)]
            self.scratch = [
                pltpu.VMEM((3, rows, width // 4), jnp.float32),
                *[pltpu.SemaphoreType.DMA((10,))] * 2,
            ]
        self.in_specs = self.out_specs = [vmem] * len(self.outs)
        self.counts = (len(self.operands), len(self.outs), len(self.scratch))
        self.refs = [None] * 3

    def begin(self):
        if not self.operands:
            return
        (x_ref,), (out_ref,), (land, *sems) = self.refs
        me, *peers = neighbours()
        core = lax.axis_index("core")
        plane, others = planes_after()
        quarter = x_ref.shape[1] // 4

        def columns(t):
            return pl.ds(pl.multiple_of(t * quarter, quarter), quarter)

        self.first = [
            send(x_ref.at[:, columns(p)], land.at[k], sems, k, {"tp": p})
            for k, p in enumerate(peers)
        ]
        for copy in self.first:
            copy.start()

    def go_on(self):
        if not self.operands:
            return
        (x_ref,), (out_ref,), (land, *sems) = self.refs
        me, *peers = neighbours()
        core = lax.axis_index("core")
        plane, others = planes_after()
        quarter = x_ref.shape[1] // 4

        def columns(t):
            return pl.ds(pl.multiple_of(t * quarter, quarter), quarter)

        for copy in self.first:
            copy.wait_recv()
        mine = (x_ref[:, columns(me)] + land[0]) + (land[1] + land[2])
        out_ref[plane, core, :, columns(me)] = mine
        here = out_ref.at[plane, core, :, columns(me)]
        second = [send(here, here, sems, 3 + k, {"seq": p}) for k, p in enumerate(others)]
        for copy in second:
            copy.start()
        for copy in second:
            copy.wait_recv()
        here = out_ref.at[:, core, :, columns(me)]
        self.third = [send(here, here, sems, 6 + k, {"tp": p}) for k, p in enumerate(peers)]
        for copy in self.third:
            copy.start()
        self.copies = self.first + second + self.third

    def end(self):
        if not self.operands:
            return
        (_,), (out_ref,), (_, *sems) = self.refs
        core = lax.axis_index("core")
        for copy in self.third:
            copy.wait_recv()
        here = out_ref.at[:, core]
        swap = send(here, here, sems, 9, {"core": 1 - core})
        swap.start()
        swap.wait_recv()
        for copy in self.copies + [swap]:
            copy.wait_send()


def collect_kernel(count, aside, trade, home, total, *refs):
    refs = bind(refs, (count, count, 3), aside, trade, home, total)
    load, *sems = refs[2 * count :]
    gathering = Gathering(refs[:count], refs[count : 2 * count], load, sems)
    if trade.items or home.operands or total.operands:
        greet_all()
    else:
        greet([gathering.to_across, gathering.to_along, gathering.to_core])
    total.begin()
    gathering.begin()
    total.go_on()
    trade.begin()
    home.begin()
    aside.load()
    aside.step(0)
    gathering.relay()
    aside.step(1)
    home.turn()
    gathering.hand()
    aside.step(2)
    trade.end()
    total.end()
    home.end()
    gathering.end()


def collect(ident, pieces, aside=None, trade=(), backs=(), sums=None):
    riders = [aside or nothing(), Trade(*trade), Home(backs), Total(sums)]
    hbm = pl.BlockSpec(memory_space=pl.ANY)
    count = len(pieces)
    got = pl.pallas_call(
        functools.partial(collect_kernel, count, *riders),
        out_shape=[
            *[jax.ShapeDtypeStruct((4, 2) + p.shape, p.dtype) for p in pieces],
            *[x for rider in riders for x in rider.outs],
        ],
        in_specs=[hbm] * count + [x for rider in riders for x in rider.in_specs],
        out_specs=[hbm] * count + [x for rider in riders for x in rider.out_specs],
        scratch_shapes=[
            pltpu.SemaphoreType.DMA((count,)),
            pltpu.SemaphoreType.DMA((10 * count,)),
            pltpu.SemaphoreType.DMA((10 * count,)),
            *[x for rider in riders for x in rider.scratch],
        ],
        compiler_params=pltpu.CompilerParams(
            collective_id=ident, has_side_effects=True, vmem_limit_bytes=VMEM_BYTES
        ),
        cost_estimate=pl.CostEstimate(
            flops=0, bytes_accessed=80 * sum(p.size for p in pieces), transcendentals=0
        ),
        name="collect",
    )(*pieces, *[x for rider in riders for x in rider.operands])
    return got[:count], got[count:]


def spread_kernel(parts, in_ref, out_ref):
    size = in_ref.shape[-1] // parts
    for q in range(parts):
        for t in range(4):
            out_ref[:, pl.ds((q * 4 + t) * size, size)] = in_ref[
                t, 0, :, pl.ds(q * size, size)
            ].astype(jnp.float32)


def spread(blocks, parts):
    _, cores, rows, width = blocks.shape
    cut = 2
    tall = rows // cut
    return pl.pallas_call(
        functools.partial(spread_kernel, parts),
        grid=(cores, cut),
        out_shape=jax.ShapeDtypeStruct((cores * rows, 4 * width), jnp.float32),
        in_specs=[pl.BlockSpec((4, 1, tall, width), lambda c, k: (0, c, k, 0))],
        out_specs=pl.BlockSpec((tall, 4 * width), lambda c, k: (c * cut + k, 0)),
        compiler_params=pltpu.CompilerParams(vmem_limit_bytes=32 * 1024 * 1024),
        cost_estimate=pl.CostEstimate(
            flops=0, bytes_accessed=6 * blocks.size, transcendentals=0
        ),
        name="spread",
    )(blocks)


def planes_after():
    plane = lax.axis_index("seq")
    return plane, [lax.rem(plane + k, 4) for k in (1, 2, 3)]


def greet_all():
    _, across, along, far = neighbours()
    _, others = planes_after()
    greet(
        [{"tp": p} for p in (across, along, far)]
        + [{"core": 1 - lax.axis_index("core")}]
        + [{"seq": p} for p in others]
    )


def arrive_kernel(
    tok_ref, cot_ref, msg_ref, w_ref, qkv_ref, wout_ref, down_ref, gateup_ref,
    in_ref, cots_ref, msgs_ref, mod_ref, qkv_cut, down_cut, gateup_cut,
    stage, wbuf, part, land, qkv_buf, down_buf, gateup_buf, load, cuts, s0, s1,
):
    sems = (s0, s1)
    me, across, along, far = neighbours()
    core = lax.axis_index("core")
    plane, others = planes_after()
    peers = [across, along, far]
    quarter = mod_ref.shape[1] // 4
    depth = msgs_ref.shape[-1]
    columns = pl.ds(pl.multiple_of(me * quarter, quarter), quarter)
    weights = pltpu.make_async_copy(w_ref.at[:, columns], wbuf, load.at[0])
    weights.start()
    cutting = []

    def cut(source, target, parts, at):
        rows, size = target.shape[0], source.shape[1] // (parts * 4)
        for q in range(parts):
            lanes = pl.ds(pl.multiple_of((q * 4 + me) * size, size), size)
            cutting.append(
                pltpu.make_async_copy(
                    source.at[pl.ds(pl.multiple_of(core * rows, rows), rows), lanes],
                    target.at[:, pl.ds(at + q * size, size)],
                    cuts.at[len(cutting)],
                )
            )

    cut(qkv_ref, qkv_buf, 3, 0)
    cut(wout_ref, qkv_buf, 1, qkv_ref.shape[1] // 4)
    cut(gateup_ref, gateup_buf, 8, 0)
    share = down_cut.shape[0]
    rows = pl.ds(pl.multiple_of((me * 2 + core) * share, share), share)
    cutting.append(pltpu.make_async_copy(down_ref.at[rows], down_buf, cuts.at[len(cutting)]))
    for copy in cutting:
        copy.start()
    keeping = [
        pltpu.make_async_copy(source, target, cuts.at[13 + k])
        for k, (source, target) in enumerate(
            zip((qkv_buf, down_buf, gateup_buf), (qkv_cut, down_cut, gateup_cut))
        )
    ]
    mine = pltpu.make_async_copy(tok_ref.at[me], stage.at[me], load.at[1])
    mine.start()
    msgs_ref[me, core] = msg_ref[:, pl.ds(pl.multiple_of(plane * depth, depth), depth)]
    greet_all()
    here = msgs_ref.at[me, core]
    first = [send(here, here, sems, k, {"tp": p}) for k, p in enumerate(peers)]
    for copy in first:
        copy.start()
    spread_out = [
        send(tok_ref.at[p], stage.at[me], sems, 3 + k, {"tp": p}) for k, p in enumerate(peers)
    ]
    for copy in spread_out:
        copy.start()
    cotangents = [
        send(cot_ref.at[p], cots_ref.at[me], sems, 16 + k, {"tp": p}) for k, p in enumerate(peers)
    ]
    for copy in cotangents:
        copy.start()
    own_cots = pltpu.make_async_copy(cot_ref.at[me], cots_ref.at[me], load.at[3])
    own_cots.start()
    for copy in first:
        copy.wait_recv()
    here = msgs_ref.at[:, core]
    swap = send(here, here, sems, 6, {"core": 1 - core})
    swap.start()
    weights.wait()
    conditions = msgs_ref[:, core].reshape(4 * 8, depth).astype(wbuf.dtype)
    tile = 512
    for copy in cutting:
        copy.wait()
    for copy in keeping:
        copy.start()
    for step in range(quarter // tile):
        at = pl.ds(step * tile, tile)
        part[:, :, at] = jnp.dot(
            conditions, wbuf[:, at], preferred_element_type=jnp.float32
        ).reshape(4, 8, tile)
    second = [
        send(part.at[p], land.at[k], sems, 7 + k, {"seq": p}) for k, p in enumerate(others)
    ]
    for copy in second:
        copy.start()
    mine.wait()
    for copy in spread_out:
        copy.wait_recv()
    third = [
        send(stage.at[p], in_ref.at[plane], sems, 10 + k, {"seq": p})
        for k, p in enumerate(others)
    ]
    for copy in third:
        copy.start()
    stay = pltpu.make_async_copy(stage.at[plane], in_ref.at[plane], load.at[2])
    stay.start()
    for copy in second:
        copy.wait_recv()
    mod_ref[:, columns] = (part[plane] + land[0]) + (land[1] + land[2])
    here = mod_ref.at[:, columns]
    fourth = [send(here, here, sems, 13 + k, {"tp": p}) for k, p in enumerate(peers)]
    for copy in fourth:
        copy.start()
    swap.wait_recv()
    for copy in fourth + third + cotangents:
        copy.wait_recv()
    stay.wait()
    own_cots.wait()
    for copy in keeping:
        copy.wait()
    for copy in first + spread_out + cotangents + [swap] + second + third + fourth:
        copy.wait_send()


def arrive(ident, tokens, cotangent, message, w_mod, w_qkv, w_out, w_down, w_gateup):
    rows, width = tokens.shape
    share, kind = w_qkv.shape[0] // 2, w_qkv.dtype
    depth, wide = w_mod.shape
    vmem, hbm = pl.BlockSpec(memory_space=pltpu.VMEM), pl.BlockSpec(memory_space=pl.ANY)
    return pl.pallas_call(
        arrive_kernel,
        out_shape=[
            jax.ShapeDtypeStruct((4, rows // 4, width), tokens.dtype),
            jax.ShapeDtypeStruct((4, rows // 4, width), cotangent.dtype),
            jax.ShapeDtypeStruct((4, 2, 8, depth), jnp.float32),
            jax.ShapeDtypeStruct((8, wide), jnp.float32),
            jax.ShapeDtypeStruct((share, (w_qkv.shape[1] + w_out.shape[1]) // 4), kind),
            jax.ShapeDtypeStruct((w_down.shape[0] // 8, w_down.shape[1]), kind),
            jax.ShapeDtypeStruct((share, w_gateup.shape[1] // 4), kind),
        ],
        in_specs=[hbm, hbm, vmem] + [hbm] * 5,
        out_specs=[hbm, hbm, vmem, vmem, hbm, hbm, hbm],
        scratch_shapes=[
            pltpu.VMEM((4, rows // 4, width), tokens.dtype),
            pltpu.VMEM((depth, wide // 4), w_mod.dtype),
            pltpu.VMEM((4, 8, wide // 4), jnp.float32),
            pltpu.VMEM((3, 8, wide // 4), jnp.float32),
            pltpu.VMEM((share, (w_qkv.shape[1] + w_out.shape[1]) // 4), kind),
            pltpu.VMEM((w_down.shape[0] // 8, w_down.shape[1]), kind),
            pltpu.VMEM((share, w_gateup.shape[1] // 4), kind),
            pltpu.SemaphoreType.DMA((4,)),
            pltpu.SemaphoreType.DMA((16,)),
            pltpu.SemaphoreType.DMA((19,)),
            pltpu.SemaphoreType.DMA((19,)),
        ],
        compiler_params=pltpu.CompilerParams(
            collective_id=ident, has_side_effects=True, vmem_limit_bytes=VMEM_BYTES
        ),
        cost_estimate=pl.CostEstimate(flops=0, bytes_accessed=90_000_000, transcendentals=0),
        name="arrive",
    )(
        tokens.reshape(4, rows // 4, width),
        cotangent.reshape(4, rows // 4, width),
        message,
        w_mod,
        w_qkv,
        w_out,
        w_down,
        w_gateup,
    )


def by_rows(rows, sums, body):
    for ref in sums:
        ref[...] = jnp.zeros_like(ref)

    @pl.loop(0, rows // 32)
    def _(step):
        body(pl.ds(pl.multiple_of(step * 32, 32), 32))


def chosen(mod_ref, document, part, width):
    at = pl.ds(part * width, width)
    found = mod_ref[DOCS - 1 : DOCS, at]
    for d in range(DOCS - 1):
        found = jnp.where(document == d, mod_ref[d : d + 1, at], found)
    return found


def tally(ref, row, values):
    ref[row] += (values[:8] + values[8:16]) + (values[16:24] + values[24:])


def tally_docs(ref, row, document, values):
    for d in range(DOCS):
        tally(ref, row + d, jnp.where(document == d, values, 0.0))


def norm_of(values):
    inverse = lax.rsqrt(jnp.mean(values * values, axis=-1, keepdims=True) + eps)
    return values * inverse, inverse


def settle(out_ref, sums):
    out_ref[...] = jnp.sum(sums[...], axis=1)


def after_attention(inputs, mod_doc, document, gain):
    rows, width = inputs.shape

    def work(attn_ref, ins, outs, scratch):
        (x_ref, mod_ref, doc_ref, gain_ref), (residual_ref, hidden_ref) = ins, outs

        def body(strip):
            document = doc_ref[strip, 0:1]
            gate = jnp.tanh(chosen(mod_ref, document, 1, width))
            residual = x_ref[strip, :].astype(jnp.float32) + gate * attn_ref[strip, :]
            residual_ref[strip, :] = residual
            normed, _ = norm_of(residual)
            scale = chosen(mod_ref, document, 2, width)
            hidden_ref[strip, :] = (normed * gain_ref[...] * (1.0 + scale)).astype(
                hidden_ref.dtype
            )

        by_rows(rows, [], body)

    return Aside(
        [inputs, mod_doc, document, gain],
        [
            jax.ShapeDtypeStruct((rows, width), jnp.float32),
            jax.ShapeDtypeStruct((rows, width), jnp.bfloat16),
        ],
        [],
        work,
    )


def after_ffn_back(residual, attn_out, cotangent, weight, mod_doc, document, gain):
    rows, width = residual.shape

    def work(back_ref, ins, outs, scratch):
        res_ref, attn_ref, cot_ref, weight_ref, mod_ref, doc_ref, gain_ref = ins
        grad_ref, attn_back_ref, sum_ref = outs
        (sums,) = scratch

        def body(strip):
            document = doc_ref[strip, 0:1]
            normed, inverse = norm_of(res_ref[strip, :])
            scale = 1.0 + chosen(mod_ref, document, 2, width)
            gain = gain_ref[...]
            back = back_ref[strip, :]
            both = back * normed
            tally(sums, 8, both * scale)
            tally_docs(sums, 0, document, both * gain)
            inner = back * gain * scale
            inner = inner - normed * jnp.mean(inner * normed, axis=-1, keepdims=True)
            grads = cot_ref[strip, :].astype(jnp.float32) * weight_ref[strip, 0:1]
            grads = grads + inverse * inner
            grad_ref[strip, :] = grads
            gate = jnp.tanh(chosen(mod_ref, document, 1, width))
            attn_back_ref[strip, :] = (gate * grads).astype(attn_back_ref.dtype)
            tally_docs(sums, 4, document, grads * attn_ref[strip, :] * (1.0 - gate * gate))

        by_rows(rows, [sums], body)
        settle(sum_ref, sums)

    return Aside(
        [residual, attn_out, cotangent, weight, mod_doc, document, gain],
        [
            jax.ShapeDtypeStruct((rows, width), jnp.float32),
            jax.ShapeDtypeStruct((rows, width), jnp.bfloat16),
            jax.ShapeDtypeStruct((16, width), jnp.float32),
        ],
        [pltpu.VMEM((16, 8, width), jnp.float32)],
        work,
    )


def after_ffn(residual, cotangent, weight, mod_doc, document):
    rows, width = residual.shape

    def work(down_ref, ins, outs, scratch):
        res_ref, cot_ref, weight_ref, mod_ref, doc_ref = ins
        result_ref, sum_ref = outs
        (sums,) = scratch

        def body(strip):
            document = doc_ref[strip, 0:1]
            gate = jnp.tanh(chosen(mod_ref, document, 3, width))
            down = down_ref[strip, :]
            result_ref[strip, :] = (res_ref[strip, :] + gate * down).astype(result_ref.dtype)
            grads = cot_ref[strip, :].astype(jnp.float32) * weight_ref[strip, 0:1]
            tally_docs(sums, 0, document, grads * down * (1.0 - gate * gate))

        by_rows(rows, [sums], body)
        settle(sum_ref, sums)

    return Aside(
        [residual, cotangent, weight, mod_doc, document],
        [
            jax.ShapeDtypeStruct((rows, width), jnp.bfloat16),
            jax.ShapeDtypeStruct((8, width), jnp.float32),
        ],
        [pltpu.VMEM((8, 8, width), jnp.float32)],
        work,
    )


def after_input_back(inputs, grads, mod_doc, document, gain):
    rows, width = inputs.shape

    def work(back_ref, ins, outs, scratch):
        x_ref, grad_ref, mod_ref, doc_ref, gain_ref = ins
        out_ref, sum_ref = outs
        (sums,) = scratch

        def body(strip):
            document = doc_ref[strip, 0:1]
            normed, inverse = norm_of(x_ref[strip, :].astype(jnp.float32))
            scale = 1.0 + chosen(mod_ref, document, 0, width)
            gain = gain_ref[...]
            back = back_ref[strip, :]
            both = back * normed
            tally(sums, 4, both * scale)
            tally_docs(sums, 0, document, both * gain)
            inner = back * gain * scale
            inner = inner - normed * jnp.mean(inner * normed, axis=-1, keepdims=True)
            out_ref[strip, :] = (grad_ref[strip, :] + inverse * inner).astype(out_ref.dtype)

        by_rows(rows, [sums], body)
        settle(sum_ref, sums)

    return Aside(
        [inputs, grads, mod_doc, document, gain],
        [
            jax.ShapeDtypeStruct((rows, width), jnp.bfloat16),
            jax.ShapeDtypeStruct((8, width), jnp.float32),
        ],
        [pltpu.VMEM((8, 8, width), jnp.float32)],
        work,
    )


def lanes_of(rows):
    return lax.broadcasted_iota(jnp.int32, (rows, 128), 1)


def pair_norm(values):
    lane = lanes_of(values.shape[0])
    square = values * values
    low = jnp.sum(jnp.where(lane < HDIM, square, 0.0), axis=-1, keepdims=True)
    high = jnp.sum(jnp.where(lane < HDIM, 0.0, square), axis=-1, keepdims=True)
    inverse = jnp.where(lane < HDIM, lax.rsqrt(low / HDIM + eps), lax.rsqrt(high / HDIM + eps))
    return values * inverse, inverse


def pair_back(grads, normed, inverse):
    lane = lanes_of(grads.shape[0])
    inner = grads * normed
    low = jnp.sum(jnp.where(lane < HDIM, inner, 0.0), axis=-1, keepdims=True)
    high = jnp.sum(jnp.where(lane < HDIM, 0.0, inner), axis=-1, keepdims=True)
    return inverse * (grads - normed * (jnp.where(lane < HDIM, low, high) / HDIM))


def pair_turn(values, cosine, sine):
    lane = lanes_of(values.shape[0])
    partner = jnp.where(
        lane % HDIM < HDIM // 2, pltpu.roll(values, 96, 1), pltpu.roll(values, 32, 1)
    )
    return values * cosine + partner * sine


def store_heads(target, strip, pair, spare):
    lane = lanes_of(pair.shape[0])
    first = jnp.where(lane < HDIM, pair, spare)
    second = jnp.where(lane < HDIM, pltpu.roll(pair, HDIM, 1), spare)
    target[strip, 0:128] = first.astype(target.dtype)
    target[strip, 128:256] = second.astype(target.dtype)


def join_heads(first, second):
    lane = lanes_of(first.shape[0])
    return jnp.where(lane < HDIM, first, pltpu.roll(second, HDIM, 1))


def ones_beside(rows):
    lane = lanes_of(rows)
    return jnp.where((lane == HDIM) | (lane == HDIM + 1), 1.0, 0.0)


def not_turned(left, right):
    return lax.dot_general(
        left, right, (((1,), (1,)), ((), ())), preferred_element_type=jnp.float32
    )


STRIP = 256
SPARE = 128.0


def strips(rows, body):
    @pl.loop(0, rows // STRIP)
    def _(step):
        body(pl.ds(pl.multiple_of(step * STRIP, STRIP), STRIP))


def weigh(qa_ref, ka_ref, va_ref, ov_ref):
    for head in range(2):
        at = pl.ds(head * 128, 128)

        def body(strip):
            scores = not_turned(qa_ref[strip, at], ka_ref[:, at])
            weights = jnp.exp(scores).astype(jnp.bfloat16)
            ov_ref[strip, at] = jnp.dot(
                weights, va_ref[:, at], preferred_element_type=jnp.float32
            )

        strips(qa_ref.shape[0], body)


def own_kernel(
    q_ref, k_ref, v_ref, gq_ref, gk_ref, cos_ref, sin_ref, sq_ref, sk_ref,
    qa_ref, ka_ref, va_ref, ov_ref,
):
    def prepare(strip):
        cosine, sine = cos_ref[strip, :], sin_ref[strip, :]
        query = pair_turn(pair_norm(q_ref[strip, :])[0] * gq_ref[...], cosine, sine)
        store_heads(qa_ref, strip, query * HDIM**-0.5, sq_ref[strip, :])
        keys = pair_turn(pair_norm(k_ref[strip, :])[0] * gk_ref[...], cosine, sine)
        store_heads(ka_ref, strip, keys, sk_ref[strip, :])
        store_heads(va_ref, strip, v_ref[strip, :], ones_beside(STRIP))

    strips(q_ref.shape[0], prepare)
    weigh(qa_ref, ka_ref, va_ref, ov_ref)


def cross_kernel(
    qa_ref, k_ref, v_ref, sq_ref, sk_ref, own_ref, gate_ref,
    ka_ref, va_ref, ov_ref, mix_ref, qx_ref,
):
    def prepare(strip):
        store_heads(ka_ref, strip, k_ref[strip, :].astype(jnp.float32), sk_ref[strip, :])
        store_heads(va_ref, strip, v_ref[strip, :].astype(jnp.float32), ones_beside(STRIP))

    strips(k_ref.shape[0], prepare)

    def requery(strip):
        lane = lanes_of(STRIP)
        for head in range(2):
            at = pl.ds(head * 128, 128)
            qx_ref[strip, at] = jnp.where(
                lane < HDIM, qa_ref[strip, at].astype(jnp.float32), sq_ref[strip, :]
            ).astype(qx_ref.dtype)

    strips(qa_ref.shape[0], requery)
    weigh(qx_ref, ka_ref, va_ref, ov_ref)

    def mix(strip):
        parts = []
        for head in range(2):
            at = pl.ds(head * 128, 128)
            own, cross = own_ref[strip, at], ov_ref[strip, at]
            parts.append((own / own[:, 64:65], cross / cross[:, 64:65]))
        own = join_heads(parts[0][0], parts[1][0])
        cross = join_heads(parts[0][1], parts[1][1])
        mix_ref[strip, :] = (own + gate_ref[...] * cross).astype(mix_ref.dtype)

    strips(qa_ref.shape[0], mix)


def back_kernel(own, *refs):
    g_ref, gate_ref, ov_ref, qa_ref, sq_ref, ka_ref, va_ref = refs[:7]
    refs = refs[7:]
    if own:
        k_ref, gk_ref, q_ref, gq_ref, cos_ref, sin_ref, more_ref = refs[:7]
        refs = refs[7:]
    dq_ref, dk_ref, dv_ref, sum_ref, qx, doa, dqt, dqh, dkh, dvh = refs
    rows, count = qa_ref.shape[0], ka_ref.shape[0]
    sum_ref[...] = jnp.zeros_like(sum_ref)
    for head in range(2):
        at = pl.ds(head * 128, 128)

        def prepare(strip):
            lane = lanes_of(STRIP)
            plain = g_ref[strip, :]
            grads = plain * gate_ref[...]
            if head == 1:
                plain = pltpu.roll(plain, HDIM, 1)
                grads = pltpu.roll(grads, HDIM, 1)
            both = ov_ref[strip, at]
            inverse = 1.0 / both[:, 64:65]
            out = jnp.where(lane < HDIM, both * inverse, 0.0)
            if not own:
                sum_ref[0, head : head + 1, :] += jnp.sum(plain * out, axis=0, keepdims=True)
            scaled = (grads * inverse).astype(jnp.bfloat16).astype(jnp.float32)
            delta = jnp.sum(scaled * out, axis=-1, keepdims=True)
            high = delta.astype(jnp.bfloat16).astype(jnp.float32)
            doa[strip, :] = jnp.where(
                lane < HDIM,
                scaled,
                jnp.where(lane == HDIM, -high, jnp.where(lane == HDIM + 1, high - delta, 0.0)),
            ).astype(doa.dtype)
            qx[strip, :] = jnp.where(
                lane < HDIM, qa_ref[strip, at].astype(jnp.float32), sq_ref[strip, :]
            ).astype(qx.dtype)

        strips(rows, prepare)
        dqt[...] = jnp.zeros_like(dqt)

        def block(strip):
            keys, values = ka_ref[strip, at], va_ref[strip, at]
            weights = jnp.exp(not_turned(keys, qx[...]))
            grads = (weights * not_turned(values, doa[...])).astype(jnp.bfloat16)
            dvh[head, strip, :] = jnp.dot(
                weights.astype(jnp.bfloat16), doa[...], preferred_element_type=jnp.float32
            )
            dkh[head, strip, :] = jnp.dot(grads, qx[...], preferred_element_type=jnp.float32)
            dqt[...] += lax.dot_general(
                keys, grads, (((0,), (0,)), ((), ())), preferred_element_type=jnp.float32
            )

        strips(count, block)
        dqh[head] = dqt[...].T * HDIM**-0.5

    def add_up(row, values):
        sum_ref[0, row : row + 1, :] += jnp.sum(values, axis=0, keepdims=True)

    def finish(strip):
        grads = join_heads(dkh[0, strip, :], dkh[1, strip, :])
        if own:
            grads = pair_turn(grads, cos_ref[strip, :], -sin_ref[strip, :])
            normed, inverse = pair_norm(k_ref[strip, :])
            add_up(2, grads * normed)
            grads = pair_back(grads * gk_ref[...], normed, inverse)
        dk_ref[strip, :] = grads.astype(dk_ref.dtype)
        dv_ref[strip, :] = join_heads(dvh[0, strip, :], dvh[1, strip, :]).astype(dv_ref.dtype)

    strips(count, finish)

    def finish_query(strip):
        grads = join_heads(dqh[0, strip, :], dqh[1, strip, :])
        if own:
            grads = pair_turn(grads + more_ref[strip, :], cos_ref[strip, :], -sin_ref[strip, :])
            normed, inverse = pair_norm(q_ref[strip, :])
            add_up(3, grads * normed)
            grads = pair_back(grads * gq_ref[...], normed, inverse)
        dq_ref[strip, :] = grads.astype(dq_ref.dtype)

    strips(rows, finish_query)


def view(ref, index, width=128, offset=0):
    return ref.at[:, pl.ds((offset + index) * width, width)]


def attend(
    projected, heads, gain_q, gain_k, gate, cosine, sine, own_q, own_k, cross_q, cross_k
):
    rows, width = projected.shape[0], projected.shape[1] // 3
    caps, count = heads.shape[0], width // 128
    bf, f32 = jnp.bfloat16, jnp.float32

    def steps(i, ins, outs, scratch):
        raw, heads, gain_q, gain_k, gate, cosine, sine, own_q, own_k, cross_q, cross_k = ins
        qa, ka, va, own, cka, cva, cross, mix = outs
        own_kernel(
            view(raw, i), view(raw, i, offset=count), view(raw, i, offset=2 * count),
            view(gain_q, i), view(gain_k, i), cosine, sine, own_q, own_k,
            view(qa, i, 256), view(ka, i, 256), view(va, i, 256), view(own, i, 256),
        )
        cross_kernel(
            view(qa, i, 256), view(heads, i), view(heads, i, offset=count), cross_q, cross_k,
            view(own, i, 256), view(gate, i), view(cka, i, 256), view(cva, i, 256),
            view(cross, i, 256), view(mix, i), *scratch,
        )

    return Aside(
        [projected, heads, gain_q, gain_k, gate, cosine, sine, own_q, own_k, cross_q, cross_k],
        [
            *[jax.ShapeDtypeStruct((rows, 2 * width), d) for d in (bf, bf, bf, f32)],
            *[jax.ShapeDtypeStruct((caps, 2 * width), bf)] * 2,
            jax.ShapeDtypeStruct((rows, 2 * width), f32),
            jax.ShapeDtypeStruct((rows, width), bf),
        ],
        [pltpu.VMEM((rows, 256), bf)],
        steps,
    )


def cap_back_kernel(g_ref, k_ref, gain_ref, out_ref, sum_ref):
    sum_ref[...] = jnp.zeros_like(sum_ref)

    def body(strip):
        for at in range(0, k_ref.shape[1], 128):
            lanes = pl.ds(at, 128)
            grads = g_ref[strip, lanes].astype(jnp.float32)
            normed, inverse = pair_norm(k_ref[strip, lanes])
            sum_ref[0:1, lanes] += jnp.sum(grads * normed, axis=0, keepdims=True)
            out_ref[strip, lanes] = pair_back(
                grads * gain_ref[:, lanes], normed, inverse
            ).astype(out_ref.dtype)
        values = pl.ds(k_ref.shape[1], k_ref.shape[1])
        out_ref[strip, values] = g_ref[strip, values]

    strips(g_ref.shape[0], body)


def cap_back(grads, cap_proj, gain):
    rows, width = grads.shape
    whole = pl.BlockSpec((rows, width), lambda i: (0, 0))
    part = pl.BlockSpec((rows, width // 2), lambda i: (0, 0))
    return pl.pallas_call(
        cap_back_kernel,
        grid=(1,),
        out_shape=[
            jax.ShapeDtypeStruct((rows, width), jnp.bfloat16),
            jax.ShapeDtypeStruct((8, width // 2), jnp.float32),
        ],
        in_specs=[whole, part, pl.BlockSpec((1, width // 2), lambda i: (0, 0))],
        out_specs=[whole, pl.BlockSpec((8, width // 2), lambda i: (0, 0))],
        compiler_params=pltpu.CompilerParams(vmem_limit_bytes=32 * 1024 * 1024),
        cost_estimate=pl.CostEstimate(
            flops=0, bytes_accessed=6 * grads.size, transcendentals=0
        ),
        name="cap_back",
    )(grads, cap_proj, gain)


def attend_back(grads, gate, ov, qa, spare_q, ka, va, rest=None):
    rows, width = grads.shape
    caps, count = ka.shape[0], width // 128
    bf, f32 = jnp.bfloat16, jnp.float32
    own = rest is not None

    def steps(i, ins, outs, scratch):
        grads, gate, ov, qa, spare_q, ka, va, *rest = ins
        if own:
            all_out, sums = outs
            dq, dk, dv = [view(all_out, i, offset=k * count) for k in range(3)]
        else:
            dq, all_out, sums = outs
            dq, dk, dv = view(dq, i), view(all_out, i), view(all_out, i, offset=count)
        operands = [
            view(grads, i), view(gate, i), view(ov, i, 256), view(qa, i, 256), spare_q,
            view(ka, i, 256), view(va, i, 256),
        ]
        if own:
            raw, gain_k, gain_q, cosine, sine, more = rest
            operands += [view(raw, i, offset=count), view(gain_k, i)]
            operands += [view(raw, i), view(gain_q, i), cosine, sine, view(more, i)]
        back_kernel(own, *operands, dq, dk, dv, sums.at[pl.ds(i, 1)], *scratch)

    return Aside(
        [grads, gate, ov, qa, spare_q, ka, va, *(rest or ())],
        [
            *(
                [jax.ShapeDtypeStruct((rows, 3 * width), bf)]
                if own
                else [
                    jax.ShapeDtypeStruct((rows, width), f32),
                    jax.ShapeDtypeStruct((caps, 2 * width), bf),
                ]
            ),
            jax.ShapeDtypeStruct((count, 8, 128), f32),
        ],
        [
            pltpu.VMEM((rows, 128), bf),
            pltpu.VMEM((rows, 128), bf),
            pltpu.VMEM((128, rows), f32),
            pltpu.VMEM((2, rows, 128), f32),
            pltpu.VMEM((2, caps, 128), f32),
            pltpu.VMEM((2, caps, 128), f32),
        ],
        steps,
    )


def row_stats(values):
    inverse = lax.rsqrt(jnp.mean(values * values, axis=-1, keepdims=True) + eps)
    return (values * inverse, inverse)


def norm_back(grad_normed, normed, inverse):
    inner_mean = jnp.mean(grad_normed * normed, axis=-1, keepdims=True)
    return inverse * (grad_normed - normed * inner_mean)


def head_stats(values):
    shaped = values.reshape(values.shape[0], -1, HDIM)
    normed, inverse = row_stats(shaped)
    return (normed.reshape(values.shape), inverse)


def head_back(grad_normed, normed, inverse):
    shaped_grad = grad_normed.reshape(grad_normed.shape[0], -1, HDIM)
    shaped_norm = normed.reshape(normed.shape[0], -1, HDIM)
    return norm_back(shaped_grad, shaped_norm, inverse).reshape(grad_normed.shape)


def rotary(values, row_pos, col_pos, direction):
    quarter = HDIM // 4
    freqs = 10000.0 ** (-jnp.arange(quarter, dtype=jnp.float32) / quarter)
    angles = jnp.concatenate([row_pos[:, None] * freqs, col_pos[:, None] * freqs], axis=1)
    cosine = jnp.cos(angles)[:, None, :]
    sine = direction * jnp.sin(angles)[:, None, :]
    shaped = values.reshape(values.shape[0], -1, HDIM)
    first_half = shaped[..., : HDIM // 2]
    second_half = shaped[..., HDIM // 2 :]
    turned = jnp.concatenate(
        [first_half * cosine - second_half * sine, second_half * cosine + first_half * sine],
        axis=-1,
    )
    return turned.reshape(values.shape)


def layout(doc_lengths, bucket, positions):
    doc_ends = jnp.cumsum(doc_lengths)
    starts = doc_ends - doc_lengths
    segment = jnp.sum((positions[:, None] >= doc_ends[None, :]).astype(jnp.int32), axis=1)
    matches = segment[:, None] == jnp.arange(DOCS, dtype=jnp.int32)[None, :]
    offset = jnp.sum(jnp.where(matches, starts[None, :], 0), axis=1)
    within = positions - offset
    stride = 32 * (bucket + 1)
    return (segment, (within // stride).astype(jnp.float32), (within % stride).astype(jnp.float32))


def turn_tables(row_pos, col_pos):
    quarter = HDIM // 4
    freqs = 10000.0 ** (-jnp.arange(quarter, dtype=jnp.float32) / quarter)
    angles = jnp.concatenate([row_pos[:, None] * freqs, col_pos[:, None] * freqs], axis=1)
    cosine, sine = jnp.cos(angles), jnp.sin(angles)
    return jnp.tile(cosine, (1, 4)), jnp.concatenate([-sine, sine, -sine, sine], axis=1)


def spare_columns(labels, height):
    lane = jnp.arange(128)[None, :] - HDIM
    at_label = (lane >= 0) & (lane <= DOCS) & (lane == labels[:, None])
    last = lane == DOCS + 1
    if height:
        return jnp.where(at_label, height, jnp.where(last, -height, 0.0)).astype(jnp.float32)
    return (at_label | last).astype(jnp.float32)


def by_head(values):
    return values.reshape(values.shape[0], -1, 1, HDIM).transpose(1, 0, 2, 3)


def from_heads(blocks):
    return blocks.transpose(1, 0, 2, 3).reshape(blocks.shape[1], -1)


def attend_forward(query, keys, values, allowed):
    scale = HDIM ** (-0.5)

    def block(block_args):
        part_q, part_k, part_v = block_args
        scores = (
            jnp.einsum("qhd,khd->hqk", part_q, part_k, preferred_element_type=jnp.float32) * scale
        )
        scores = jnp.where(allowed[None], scores, -1e30)
        row_peak = jnp.max(scores, axis=-1, keepdims=True)
        exp_scores = jnp.exp(scores - row_peak)
        exp_total = jnp.sum(exp_scores, axis=-1, keepdims=True)
        attn_probs = (exp_scores / exp_total).astype(jnp.bfloat16)
        attn_block = jnp.einsum(
            "hqk,khd->qhd", attn_probs, part_v, preferred_element_type=jnp.float32
        )
        return (attn_block, row_peak[..., 0] + jnp.log(exp_total[..., 0]))

    blocks, log_total = lax.map(block, (by_head(query), by_head(keys), by_head(values)))
    return (from_heads(blocks), log_total)


def attend_backward(query, keys, values, allowed, log_total, grad_out):
    scale = HDIM ** (-0.5)

    def block(block_args):
        part_q, part_k, part_v, part_log, part_grad = block_args
        scores = (
            jnp.einsum("qhd,khd->hqk", part_q, part_k, preferred_element_type=jnp.float32) * scale
        )
        scores = jnp.where(allowed[None], scores, -1e30)
        attn_probs = jnp.exp(scores - part_log[..., None])
        grad_probs = jnp.einsum(
            "qhd,khd->hqk", part_grad, part_v, preferred_element_type=jnp.float32
        )
        row_delta = jnp.sum(attn_probs * grad_probs, axis=-1, keepdims=True)
        grad_scores = (attn_probs * (grad_probs - row_delta)).astype(jnp.bfloat16)
        grad_query = (
            jnp.einsum("hqk,khd->qhd", grad_scores, part_k, preferred_element_type=jnp.float32)
            * scale
        )
        grad_keys = (
            jnp.einsum("hqk,qhd->khd", grad_scores, part_q, preferred_element_type=jnp.float32)
            * scale
        )
        grad_values = jnp.einsum(
            "hqk,qhd->khd",
            attn_probs.astype(jnp.bfloat16),
            part_grad,
            preferred_element_type=jnp.float32,
        )
        return (grad_query, grad_keys, grad_values)

    grad_query, grad_keys, grad_values = lax.map(
        block,
        (by_head(query), by_head(keys), by_head(values), log_total, by_head(grad_out)),
    )
    return (from_heads(grad_query), from_heads(grad_keys), from_heads(grad_values))


def matmul(left, right):
    return jnp.dot(left, right, preferred_element_type=jnp.float32)


def contract_right(left, weight):
    return lax.dot_general(
        left, weight, (((1,), (1,)), ((), ())), preferred_element_type=jnp.float32
    )


def contract_rows(left, right):
    return lax.dot_general(
        left, right, (((0,), (0,)), ((), ())), preferred_element_type=jnp.float32
    )


def pick(values, index, axis):
    return lax.dynamic_index_in_dim(values, index, axis, keepdims=False)


def to_plane(values):
    ways = lax.axis_size("tp")
    parts = values.reshape((ways, values.shape[0] // ways) + values.shape[1:])
    parts = lax.all_to_all(parts, "tp", 0, 0, tiled=True)
    parts = lax.all_to_all(parts, "seq", 0, 0, tiled=True)
    return parts.reshape(values.shape)


def from_plane(values):
    ways = lax.axis_size("tp")
    parts = values.reshape((ways, values.shape[0] // ways) + values.shape[1:])
    parts = lax.all_to_all(parts, "seq", 0, 0, tiled=True)
    parts = lax.all_to_all(parts, "tp", 0, 0, tiled=True)
    return parts.reshape(values.shape)


def fast():
    return lax.axis_size("tp") == 4 and lax.axis_size("core") == 2 and lax.axis_size("seq") == 4


def gather_planes(part):
    return lax.all_gather(part, "seq", axis=0, tiled=False)


def join_cores(halves):
    whole = lax.all_gather(halves, "core", axis=1, tiled=False)
    return whole.reshape(-1, halves.shape[-1])


def outer_plane(ident, *items):
    if fast():
        return outer(ident, *items)
    cores = lax.axis_size("core")
    terms = [contract_rows(left, right).astype(jnp.bfloat16) for left, right, _ in items]
    return [
        swap_halves(term.reshape(item[2], cores, -1, term.shape[-1]))
        for term, item in zip(terms, items)
    ]


def scatter_planes(term):
    return lax.psum_scatter(term, "seq", scatter_dimension=0, tiled=False)


def swap_halves(shaped):
    cores, me_c = lax.axis_size("core"), lax.axis_index("core")
    mine = pick(shaped, me_c, 1)
    for step in range(1, cores):
        ring = [(c, (c + step) % cores) for c in range(cores)]
        other = lax.ppermute(pick(shaped, (me_c + step) % cores, 1), "core", ring)
        mine = (mine.astype(jnp.float32) + other.astype(jnp.float32)).astype(jnp.bfloat16)
    return mine


def plane_gather(values):
    return lax.all_gather(values, "tp", axis=0, tiled=True)


def plane_multiply(ident, x, weight, turned=False, halved=False, width=None, **more):
    if fast():
        return gather_matmul(ident, x, weight, turned, halved, width, **more)
    whole = join_cores(weight) if halved else weight
    x = plane_gather(x)
    return x, whole, contract_right(x, whole) if turned else matmul(x, whole[:, :width])


def multiply_plane(ident, x, weight, turned=False, **more):
    if fast():
        return matmul_scatter(ident, x, weight, turned, **more)
    weight = weight[:, : x.shape[1]] if turned else weight
    term = contract_right(x, weight) if turned else matmul(x, weight)
    return lax.psum_scatter(
        term.astype(jnp.bfloat16), "tp", scatter_dimension=0, tiled=True
    ).astype(jnp.float32), None


def collect_plane(pieces):
    return [
        lax.all_gather(p, ("tp", "core"), axis=0, tiled=False).reshape(
            (lax.axis_size("tp"), lax.axis_size("core")) + p.shape
        )
        for p in pieces
    ]


def spread_parts(blocks, parts):
    if fast():
        return spread(blocks, parts)
    tp, cores, rows, width = blocks.shape
    return (
        blocks.astype(jnp.float32)
        .reshape(tp, cores, rows, parts, width // parts)
        .transpose(1, 2, 3, 0, 4)
        .reshape(cores * rows, tp * width)
    )


def arrive_plane(ident, tokens, cotangent, message, w_mod, *weights):
    if fast():
        return arrive(ident, tokens, cotangent, message, w_mod, *weights)
    ways = lax.axis_size("tp")
    cotangent = lax.all_to_all(
        cotangent.reshape(ways, -1, cotangent.shape[1]), "tp", 0, 0, tiled=True
    )
    planes, cores = lax.axis_size("seq"), lax.axis_size("core")
    depth = w_mod.shape[0]
    part = lax.dynamic_slice_in_dim(message, lax.axis_index("seq") * depth, depth, 1)
    messages = lax.all_gather(part, ("tp", "core"), axis=0, tiled=False)
    terms = matmul(messages.reshape(-1, depth).astype(w_mod.dtype), w_mod)
    terms = lax.psum_scatter(
        terms.reshape(planes, cores, 8, -1), "seq", scatter_dimension=0, tiled=False
    )
    messages = messages.reshape(lax.axis_size("tp"), cores, 8, depth)
    w_qkv, w_out, w_down, w_gateup = weights
    share = w_down.shape[0] // (ways * cores)
    block = lax.axis_index("tp") * cores + lax.axis_index("core")
    return (
        to_plane(tokens),
        cotangent,
        messages,
        pick(terms, lax.axis_index("core"), 0),
        jnp.concatenate([columns_of(w_qkv, 3), columns_of(w_out, 1)], axis=1),
        lax.dynamic_slice_in_dim(w_down, block * share, share, 0),
        columns_of(w_gateup, 2 * planes),
    )


def three_parts(values):
    parts = []
    for _ in range(3):
        part = lax.reduce_precision(values, 8, 7)
        parts.append(part.astype(jnp.bfloat16))
        values = values - part
    return parts


def by_document(doc_pick, values):
    return lax.dot_general(
        doc_pick,
        values,
        (((0,), (0,)), ((), ())),
        precision=lax.Precision.HIGHEST,
        preferred_element_type=jnp.float32,
    )


def columns_of(weight, parts):
    tp, cores = lax.axis_size("tp"), lax.axis_size("core")
    me_t, me_c = lax.axis_index("tp"), lax.axis_index("core")
    share = weight.shape[0] // cores
    size = weight.shape[1] // (parts * tp)
    return jnp.concatenate(
        [
            lax.dynamic_slice(weight, (me_c * share, (q * tp + me_t) * size), (share, size))
            for q in range(parts)
        ],
        axis=1,
    )


def shards(
    tokens,
    cotangent,
    step_embed,
    caption,
    lengths,
    group_bucket,
    null_mask,
    w_qkv,
    w_out,
    w_capkv,
    w_gateup,
    w_down,
    w_mod,
    b_mod,
    gain_attn,
    gain_ffn,
    gain_query,
    gain_key,
    gain_capkey,
    gate_head,
    null_embed,
):
    tp, cores, planes = lax.axis_size("tp"), lax.axis_size("core"), lax.axis_size("seq")
    me_t, me_c, me_z = lax.axis_index("tp"), lax.axis_index("core"), lax.axis_index("seq")
    groups = tp * cores
    rows, width = tokens.shape
    piece = rows // tp
    local_heads = HEADS // tp
    local = local_heads * HDIM
    cap_dev = caption.shape[2]
    ctx = caption.shape[3]
    my_group = me_z * cores + me_c

    condition = jax.nn.silu(step_embed[0].astype(jnp.float32)).astype(jnp.bfloat16)
    numbers = jnp.concatenate([lengths[0], group_bucket, null_mask[0]]).astype(jnp.float32)
    mod_rows = w_mod.shape[0]
    numbers = jnp.tile(jnp.pad(numbers, (0, mod_rows - numbers.shape[0])), planes)
    message = jnp.concatenate(
        [condition.astype(jnp.float32), numbers[None], jnp.zeros((3, numbers.shape[0]))], axis=0
    )
    arrived, cotangents, messages, mod_doc, *cuts = arrive_plane(
        13, tokens, cotangent, message, w_mod, w_qkv, w_out, w_down, w_gateup
    )
    messages = messages.reshape(groups, 8, mod_rows)
    cond_mine = messages[:, :DOCS].reshape(groups * DOCS, mod_rows)
    mod_rows_doc = mod_doc + b_mod
    mod_doc = mod_rows_doc[:DOCS]

    numbers = messages[:, DOCS, : 2 * DOCS + 1].astype(jnp.int32)
    counts = jnp.sum(numbers[:, :DOCS], axis=1).astype(jnp.float32)
    mine = pick(numbers, my_group, 0)
    doc_lengths, bucket = mine[:DOCS], mine[DOCS]
    bucket_count = jnp.sum(jnp.where(numbers[:, DOCS] == bucket, counts, 0.0))
    scale_loss = jnp.sum(counts) / (RES * bucket_count)

    half_capkv = gather_planes(columns_of(w_capkv, 2))
    half_qkv, half_down, half_gateup = [gather_planes(part) for part in cuts]

    capmix = jnp.where(null_mask[0][:, None, None] > 0, null_embed[None, None, :], caption[0])
    my_gain_capkey = pick(gain_capkey.reshape(tp, 1, local), me_t, 0)
    cap_flat = capmix.reshape(DOCS * cap_dev, ctx)
    if fast():
        cap_flat, full_capkv, cap_proj, cotangents, heads = gather_matmul(
            2, cap_flat, half_capkv, halved=True, trade=[swap_blocks(cotangents, "seq")],
            finish=head_finish(DOCS * cap_dev, 2 * local, my_gain_capkey),
        )
    else:
        cap_flat, full_capkv, cap_proj = plane_multiply(2, cap_flat, half_capkv, halved=True)
        capkey_raw, capval_raw = jnp.split(cap_proj, 2, axis=1)
        capkey_norm, capkey_inv = head_stats(capkey_raw)
        heads = jnp.concatenate([capkey_norm * my_gain_capkey, capval_raw], axis=1)
        heads = heads.astype(jnp.bfloat16)
        cotangents = lax.all_to_all(cotangents, "seq", 0, 0, tiled=True)
    cotangents = cotangents.reshape(tokens.shape)
    cap_document = jnp.tile(jnp.repeat(jnp.arange(DOCS, dtype=jnp.int32), cap_dev), planes)

    inputs = arrived.reshape(tokens.shape).astype(jnp.float32)
    row = jnp.arange(rows, dtype=jnp.int32)
    spread = (row // piece) * rows + row % piece
    positions = spread + me_t * piece
    all_positions = (jnp.arange(tp, dtype=jnp.int32)[:, None] * piece + spread[None, :]).reshape(-1)
    segment, _, _ = layout(doc_lengths, bucket, positions)
    all_segment, row_pos, col_pos = layout(doc_lengths, bucket, all_positions)
    all_document = jnp.minimum(all_segment, DOCS - 1)
    document = jnp.minimum(segment, DOCS - 1)
    doc_pick = (document[:, None] == jnp.arange(DOCS, dtype=jnp.int32)[None, :]).astype(jnp.float32)
    is_valid = (segment < DOCS).astype(jnp.float32)
    modulation = jnp.dot(doc_pick, mod_doc, precision=lax.Precision.HIGHEST)
    scale_a, gate_a, scale_f, gate_f = jnp.split(modulation, 4, axis=1)
    tanh_a, tanh_f = jnp.tanh(gate_a), jnp.tanh(gate_f)

    normed1, inverse1 = row_stats(inputs)
    hidden1 = (normed1 * gain_attn * (1.0 + scale_a)).astype(jnp.bfloat16)
    hidden1, heads = lax.optimization_barrier((hidden1, heads))
    heads = heads.reshape(planes, DOCS * cap_dev, 2 * local)
    if fast():
        hidden1, full_qkv, projected, heads = gather_matmul(
            1, hidden1, half_qkv, halved=True, width=3 * local,
            trade=[swap_blocks(heads, "seq")],
        )
    else:
        hidden1, full_qkv, projected = plane_multiply(
            1, hidden1, half_qkv, halved=True, width=3 * local
        )
        heads = lax.all_to_all(heads, "seq", 0, 0, tiled=True)
        full_out = full_qkv[:, 3 * local :].reshape(tp, local, local)
        full_out = lax.all_to_all(full_out, "tp", 0, 0, tiled=True)
        full_out = full_out.transpose(1, 0, 2).reshape(local, width)
    heads = heads.reshape(-1, 2 * local)
    my_gain_query = pick(gain_query.reshape(tp, 1, local), me_t, 0)
    my_gain_key = pick(gain_key.reshape(tp, 1, local), me_t, 0)
    gate_tanh = pick(jnp.tanh(gate_head).reshape(tp, local_heads), me_t, 0)
    head_gate = jnp.repeat(gate_tanh, HDIM)[None, :]
    grad_res0 = cotangents.astype(jnp.float32) * (is_valid * scale_loss)[:, None]
    grad_down = (tanh_f * grad_res0).astype(jnp.bfloat16)
    if fast():
        cosine, sine = turn_tables(row_pos, col_pos)
        own_spare = spare_columns(all_segment, SPARE)
        cross_spare = spare_columns(all_document, SPARE)
        aside = attend(
            projected, heads, my_gain_query, my_gain_key, head_gate, cosine, sine,
            own_spare, spare_columns(all_segment, 0),
            cross_spare, spare_columns(cap_document, 0),
        )
        out_rows = (
            full_qkv,
            "tp",
            (local, width),
            lambda ref, p: ref.at[pl.ds(p * local, local), pl.ds(3 * local, local)],
            lambda ref, p: ref.at[:, pl.ds(pl.multiple_of(p * local, local), local)],
        )
        grad_down, full_down, grad_ffn, *wides, full_out = gather_matmul(
            6, grad_down, half_down, turned=True, halved=True, aside=aside, early=1,
            trade=[out_rows],
        )
        wide_query, wide_keys, wide_values, own_wide = wides[:4]
        wide_capkeys, wide_capvals, cross_wide, mixed_attn = wides[4:]
    else:
        grad_down, full_down, grad_ffn = plane_multiply(
            6, grad_down, half_down, turned=True, halved=True
        )
        query_raw, key_raw, value_raw = jnp.split(projected, 3, axis=1)
        query_norm, query_inv = head_stats(query_raw)
        key_norm, key_inv = head_stats(key_raw)
        query = rotary(query_norm * my_gain_query, row_pos, col_pos, 1.0).astype(jnp.bfloat16)
        keys = rotary(key_norm * my_gain_key, row_pos, col_pos, 1.0).astype(jnp.bfloat16)
        values = value_raw.astype(jnp.bfloat16)
        capkeys, capvals = jnp.split(heads, 2, axis=1)
        self_allowed = all_segment[:, None] == all_segment[None, :]
        cross_allowed = all_document[:, None] == cap_document[None, :]
        own_out, own_log = attend_forward(query, keys, values, self_allowed)
        cross_out, cross_log = attend_forward(query, capkeys, capvals, cross_allowed)
        mixed_attn = (own_out + head_gate * cross_out).astype(jnp.bfloat16)
    token_rows = arrived.reshape(tokens.shape)
    doc_column = jnp.broadcast_to(document.astype(jnp.float32)[:, None], (rows, 128))
    weight_column = jnp.broadcast_to((is_valid * scale_loss)[:, None], (rows, 128))
    if fast():
        attn_out, residual, hidden2 = matmul_scatter(
            3, mixed_attn, full_out,
            after=after_attention(token_rows, mod_rows_doc, doc_column, gain_ffn[None]),
        )
    else:
        attn_out, *_ = multiply_plane(3, mixed_attn, full_out)
        residual = inputs + tanh_a * attn_out
        normed2, inverse2 = row_stats(residual)
        hidden2 = (normed2 * gain_ffn * (1.0 + scale_f)).astype(jnp.bfloat16)
    if fast():
        hidden2, full_gateup, hidden_ffn, grad_gateup = gather_matmul(
            4, hidden2, half_gateup, halved=True, finish=swiglu_finish(grad_ffn), keep=False
        )
        hidden_ffn = hidden_ffn.reshape(grad_ffn.shape)
        grad_gateup = grad_gateup.reshape(grad_ffn.shape[0], -1)
    else:
        hidden2, full_gateup, gate_up = plane_multiply(4, hidden2, half_gateup, halved=True)
        gate_part, up_part = jnp.split(gate_up, 2, axis=1)
        sig_gate = jax.nn.sigmoid(gate_part)
        silu_gate = gate_part * sig_gate
        hidden_ffn = (silu_gate * up_part).astype(jnp.bfloat16)
        grad_gate_part = grad_ffn * up_part * sig_gate * (1.0 + gate_part * (1.0 - sig_gate))
        grad_gateup = jnp.concatenate([grad_gate_part, grad_ffn * silu_gate], axis=1)
        grad_gateup = grad_gateup.astype(jnp.bfloat16)
    term_gateup, term_down = outer_plane(
        15, (hidden2, grad_gateup, planes), (hidden_ffn, grad_down, planes)
    )
    grad_gateup, term_down, term_gateup = lax.optimization_barrier(
        (grad_gateup, term_down, term_gateup)
    )
    term_down, term_gateup = scatter_planes(term_down), scatter_planes(term_gateup)
    if fast():
        _, grad_residual, grad_attn, ffn_sums = matmul_scatter(
            7, grad_gateup, full_gateup, turned=True,
            after=after_ffn_back(
                residual, attn_out, cotangents, weight_column, mod_rows_doc, doc_column,
                gain_ffn[None],
            ),
        )
        doc_scale_f, doc_gate_a, gain_ffn_term = ffn_sums[:4], ffn_sums[4:8], ffn_sums[8]
    else:
        grad_hidden2, *_ = multiply_plane(7, grad_gateup, full_gateup, turned=True)
        gain_ffn_term = jnp.sum(grad_hidden2 * normed2 * (1.0 + scale_f), axis=0)
        doc_scale_f = by_document(doc_pick, grad_hidden2 * normed2 * gain_ffn)
        grad_residual = grad_res0 + norm_back(
            grad_hidden2 * gain_ffn * (1.0 + scale_f), normed2, inverse2
        )
        grad_attn = (tanh_a * grad_residual).astype(jnp.bfloat16)
        doc_gate_a = by_document(doc_pick, grad_residual * attn_out * (1.0 - tanh_a * tanh_a))
    grad_attn, _, grad_mix = plane_multiply(8, grad_attn, full_out, turned=True)
    term_out = outer_plane(16, (mixed_attn, grad_attn, 1))[0][0]
    if fast():
        cross_aside = attend_back(
            grad_mix, head_gate, cross_wide, wide_query, cross_spare,
            wide_capkeys, wide_capvals,
        )
        out_columns = (
            term_out,
            "tp",
            (tp, term_out.shape[0], local),
            lambda ref, p: ref.at[:, pl.ds(pl.multiple_of(p * local, local), local)],
            block_of,
        )
        _, query_cross, grad_heads, cross_sums, result, gate_sums, term_out = matmul_scatter(
            5, hidden_ffn, full_down, aside=cross_aside, trade=[out_columns],
            after=after_ffn(residual, cotangents, weight_column, mod_rows_doc, doc_column),
        )
        doc_gate_f = gate_sums[:DOCS]
        grad_heads = grad_heads.reshape(planes, DOCS * cap_dev, 2 * local)
        gate_head_term = jnp.sum(cross_sums[:, :2], axis=-1).reshape(-1)
        own_aside = attend_back(
            grad_mix, jnp.ones_like(head_gate), own_wide, wide_query, own_spare,
            wide_keys, wide_values,
            (projected, my_gain_key, my_gain_query, cosine, sine, query_cross),
        )
        (all_down, all_gateup), riders = collect(
            10,
            [term_down, term_gateup],
            own_aside,
            [swap_blocks(grad_heads, "seq")],
        )
        grad_projected, own_sums, grad_heads = riders
        gain_key_term, gain_query_term = own_sums[:, 2].reshape(-1), own_sums[:, 3].reshape(-1)
    else:
        down_out, _ = multiply_plane(5, hidden_ffn, full_down)
        result = from_plane((residual + tanh_f * down_out).astype(jnp.bfloat16))
        all_down, all_gateup = collect_plane([term_down, term_gateup])
        term_out = term_out.reshape(term_out.shape[0], tp, -1).transpose(1, 0, 2)
        term_out = scatter_planes(lax.all_to_all(term_out, "tp", 0, 0, tiled=True))
        grad_own = grad_mix.astype(jnp.bfloat16)
        grad_cross = (head_gate * grad_mix).astype(jnp.bfloat16)
        gate_head_term = jnp.sum(
            (grad_mix * cross_out).reshape(-1, local_heads, HDIM), axis=(0, 2)
        )
        query_own, grad_keys, grad_values = attend_backward(
            query, keys, values, self_allowed, own_log, grad_own
        )
        query_cross, grad_capkeys, grad_capvals = attend_backward(
            query, capkeys, capvals, cross_allowed, cross_log, grad_cross
        )
        grad_query = rotary(query_own + query_cross, row_pos, col_pos, -1.0)
        gain_query_term = jnp.sum(grad_query * query_norm, axis=0)
        grad_query_raw = head_back(grad_query * my_gain_query, query_norm, query_inv)
        grad_key = rotary(grad_keys, row_pos, col_pos, -1.0)
        gain_key_term = jnp.sum(grad_key * key_norm, axis=0)
        grad_key_raw = head_back(grad_key * my_gain_key, key_norm, key_inv)
        grad_projected = jnp.concatenate(
            [grad_query_raw, grad_key_raw, grad_values], axis=1
        ).astype(jnp.bfloat16)
        grad_heads = jnp.concatenate([grad_capkeys, grad_capvals], axis=1).astype(jnp.bfloat16)
        grad_heads = grad_heads.reshape(planes, DOCS * cap_dev, 2 * local)
        grad_heads = lax.all_to_all(grad_heads, "seq", 0, 0, tiled=True)
        doc_gate_f = by_document(doc_pick, grad_res0 * down_out * (1.0 - tanh_f * tanh_f))
    gate_head_term = gate_head_term * (1.0 - gate_tanh * gate_tanh)
    grad_heads = grad_heads.reshape(-1, 2 * local)
    if fast():
        grad_cap_proj, capkey_sums = cap_back(grad_heads, cap_proj, my_gain_capkey)
        gain_capkey_term = capkey_sums[0]
    else:
        grad_capkeys, grad_capvals = jnp.split(grad_heads.astype(jnp.float32), 2, axis=1)
        gain_capkey_term = jnp.sum(grad_capkeys * capkey_norm, axis=0)
        grad_capkey_raw = head_back(grad_capkeys * my_gain_capkey, capkey_norm, capkey_inv)
        grad_cap_proj = jnp.concatenate([grad_capkey_raw, grad_capvals], axis=1).astype(
            jnp.bfloat16
        )
    (term_qkv,) = outer_plane(17, (hidden1, grad_projected, planes))
    cap_side, _ = lax.optimization_barrier((grad_cap_proj, term_qkv))
    term_qkv = scatter_planes(term_qkv)
    (term_capkv,) = outer_plane(18, (cap_flat, cap_side, planes))
    grad_projected, _ = lax.optimization_barrier((grad_projected, term_capkv))
    term_capkv = scatter_planes(term_capkv)
    if fast():
        _, input_grad, input_sums, term_out = matmul_scatter(
            9, grad_projected, full_qkv, turned=True, trade=[swap_blocks(term_out, "seq")],
            after=after_input_back(
                token_rows, grad_residual, mod_rows_doc, doc_column, gain_attn[None]
            ),
        )
        doc_scale_a, gain_attn_term = input_sums[:4], input_sums[4]
        term_out = jnp.sum(term_out.astype(jnp.float32), axis=0).astype(jnp.bfloat16)
    else:
        grad_hidden1, *_ = multiply_plane(9, grad_projected, full_qkv, turned=True)
        gain_attn_term = jnp.sum(grad_hidden1 * normed1 * (1.0 + scale_a), axis=0)
        doc_scale_a = by_document(doc_pick, grad_hidden1 * normed1 * gain_attn)
        input_grad = (
            grad_residual + norm_back(grad_hidden1 * gain_attn * (1.0 + scale_a), normed1, inverse1)
        ).astype(jnp.bfloat16)
    grad_mod_doc = jnp.concatenate([doc_scale_a, doc_gate_a, doc_scale_f, doc_gate_f], axis=1)

    plane_nulls = pick(numbers[:, DOCS + 1 :].reshape(tp, cores, DOCS), me_c, 1)
    null_rows = jnp.repeat(plane_nulls.reshape(-1), cap_dev) > 0
    grad_mod_doc, null_rows, all_down, all_gateup = lax.optimization_barrier(
        (grad_mod_doc, null_rows, all_down, all_gateup)
    )
    null_sum = jnp.sum(
        jnp.where(null_rows[:, None], grad_cap_proj.astype(jnp.float32), 0.0), axis=0
    )
    null_parts = jnp.stack(three_parts(null_sum), axis=1)
    null_term = jnp.sum(matmul(full_capkv, null_parts), axis=1)

    def at_mine(part):
        whole = jnp.zeros((tp,) + part.shape, jnp.float32)
        return lax.dynamic_update_index_in_dim(whole, part, me_t, 0).reshape(-1)

    small = jnp.concatenate(
        [
            gain_attn_term,
            gain_ffn_term,
            at_mine(gain_query_term),
            at_mine(gain_key_term),
            at_mine(gain_capkey_term),
            at_mine(gate_head_term),
            null_term,
        ]
    )
    small_rows = 8 - DOCS
    small_size = small.shape[0]
    small = jnp.pad(small, (0, small_rows * 4 * width - small_size))
    sums = jnp.concatenate([grad_mod_doc, small.reshape(small_rows, 4 * width)], axis=0)
    if fast():
        (all_qkv, all_out), _ = collect(12, [term_qkv, term_out])
    else:
        all_qkv, all_out = collect_plane([term_qkv, term_out])
    all_qkv, all_down, all_gateup = lax.optimization_barrier((all_qkv, all_down, all_gateup))
    sum_down = all_down.reshape(w_down.shape).astype(jnp.float32)
    sum_gateup = spread_parts(all_gateup, 2 * planes)
    sum_out = spread_parts(all_out, 1)
    sum_qkv = spread_parts(all_qkv, 3)
    sum_qkv, sum_gateup, sum_down, sum_out, term_capkv = lax.optimization_barrier(
        (sum_qkv, sum_gateup, sum_down, sum_out, term_capkv)
    )
    if fast():
        (all_capkv,), (result, input_grad, totals) = collect(
            14, [term_capkv], backs=[result, input_grad], sums=sums
        )
        result, input_grad = result.reshape(tokens.shape), input_grad.reshape(tokens.shape)
    else:
        (all_capkv,) = collect_plane([term_capkv])
        input_grad = from_plane(input_grad)
        totals = lax.all_gather(lax.psum(sums, "tp"), ("seq", "core"), axis=0, tiled=False)
    totals = totals.reshape(groups, 8, 4 * width)
    sum_capkv = spread_parts(all_capkv, 2)
    grad_mod_docs = totals[:, :DOCS].reshape(groups * DOCS, 4 * width)
    sum_mod = contract_rows(
        jnp.concatenate([cond_mine.astype(jnp.bfloat16)] * 3, axis=0),
        jnp.concatenate(three_parts(grad_mod_docs), axis=0),
    )
    sum_bias = jnp.sum(grad_mod_docs, axis=0)
    small = jnp.sum(totals[:, DOCS:], axis=0).reshape(-1)[:small_size]
    ends = [width, 2 * width, 3 * width, 4 * width, 5 * width, 5 * width + HEADS]
    small_parts = jnp.split(small, ends)
    return (
        result,
        input_grad,
        sum_qkv,
        sum_out,
        sum_capkv,
        sum_gateup,
        sum_down,
        sum_mod,
        sum_bias,
        *small_parts,
    )


def solution(mesh):
    planes = mesh.shape["seq"]
    cores = mesh.shape["bucket"] // planes
    split = Mesh(mesh.devices.reshape(planes, cores, planes), ("tp", "core", "seq"))
    group = ("tp", "core")
    token = P(("tp", "core", "seq"), None)
    weight = P("seq", None)
    placed = (
        token,
        token,
        P(group, None, None),
        P(group, None, "seq", None),
        P(group, None),
        P(group),
        P(group, None),
        *([weight] * 6),
        *([P()] * 8),
    )
    return jax.shard_map(
        shards,
        mesh=split,
        in_specs=placed,
        out_specs=(token, token, *([weight] * 6), *([P()] * 8)),
        check_vma=False,
    )
```
